32 devices in a mesh: rep: 4 (over x, core), ep: 8 (over z, y).
Axes of the slice: x: 2, y: 2, z: 4, core: 2. Of those that a mesh axis runs over, the one named last changes fastest.
Arguments:
- tokens: bfloat16 [63040, 512], P(('rep', 'ep')), may hold values from -6 to 6
- cotangent: bfloat16 [63040, 512], P(('rep', 'ep')), may hold values from -6 to 6
- expert_ids: int32 [63040, 2], P(('rep', 'ep')), may hold values from 0 to 7, all different within a row
- priority: int32 [32, 1970], P(('rep', 'ep')), may hold values from 0 to 1969, each once within a row
- heads_in: float32 [512, 1536], P(('rep', 'ep')), may hold values from -0.25 to 0.25
- heads_in_first: float32 [512, 1536], P(('rep', 'ep')), may hold values from -448 to 448
- heads_in_second: float32 [512, 1536], P(('rep', 'ep')), may hold values from 5673.6 to 22694.4
- heads_out: float32 [512, 512], P(('rep', 'ep')), may hold values from -0.75 to 0.75
- heads_out_first: float32 [512, 512], P(('rep', 'ep')), may hold values from -448 to 448
- heads_out_second: float32 [512, 512], P(('rep', 'ep')), may hold values from 5673.6 to 22694.4
- router: float32 [512, 8], P(('rep', 'ep')), may hold values from -0.1875 to 0.1875
- router_first: float32 [512, 8], P(('rep', 'ep')), may hold values from -8192 to 8192
- router_second: float32 [512, 8], P(('rep', 'ep')), may hold values from 2017280 to 8069120
- scales: float32 [512, 5], P(('rep', 'ep')), may hold values from -0.5 to 1.4
- scales_first: float32 [512, 5], P(('rep', 'ep')), may hold values from -1536 to 1536
- scales_second: float32 [512, 5], P(('rep', 'ep')), may hold values from 63040 to 252160
- expert_in: float32 [8, 512, 2048], P('ep', None, 'rep'), may hold values from -0.25 to 0.25
- expert_in_first: float32 [8, 512, 2048], P('ep', None, 'rep'), may hold values from -224 to 224
- expert_in_second: float32 [8, 512, 2048], P('ep', None, 'rep'), may hold values from 1418.4 to 5673.6
- bias_in: float32 [8, 2048], P('ep', 'rep'), may hold values from -0.625 to 0.625
- bias_in_first: float32 [8, 2048], P('ep', 'rep'), may hold values from -224 to 224
- bias_in_second: float32 [8, 2048], P('ep', 'rep'), may hold values from 1418.4 to 5673.6
- expert_out: float32 [8, 2048, 512], P('ep', 'rep'), may hold values from -0.1875 to 0.1875
- expert_out_first: float32 [8, 2048, 512], P('ep', 'rep'), may hold values from -224 to 224
- expert_out_second: float32 [8, 2048, 512], P('ep', 'rep'), may hold values from 1418.4 to 5673.6
- bias_out: float32 [8, 512], P('ep', 'rep'), may hold values from -0.625 to 0.625
- bias_out_first: float32 [8, 512], P('ep', 'rep'), may hold values from -384 to 384
- bias_out_second: float32 [8, 512], P('ep', 'rep'), may hold values from 3940 to 15760
Outputs:
- output: float32 [63040, 512], P(('rep', 'ep'))
- input_grad: float32 [63040, 512], P(('rep', 'ep'))
- heads_in_first_new: float32 [512, 1536], P(('rep', 'ep'))
- heads_in_second_new: float32 [512, 1536], P(('rep', 'ep'))
- heads_in_new: float32 [512, 1536], P(('rep', 'ep'))
- heads_out_first_new: float32 [512, 512], P(('rep', 'ep'))
- heads_out_second_new: float32 [512, 512], P(('rep', 'ep'))
- heads_out_new: float32 [512, 512], P(('rep', 'ep'))
- router_first_new: float32 [512, 8], P(('rep', 'ep'))
- router_second_new: float32 [512, 8], P(('rep', 'ep'))
- router_new: float32 [512, 8], P(('rep', 'ep'))
- scales_first_new: float32 [512, 5], P(('rep', 'ep'))
- scales_second_new: float32 [512, 5], P(('rep', 'ep'))
- scales_new: float32 [512, 5], P(('rep', 'ep'))
- expert_in_first_new: float32 [8, 512, 2048], P('ep', None, 'rep')
- expert_in_second_new: float32 [8, 512, 2048], P('ep', None, 'rep')
- expert_in_new: float32 [8, 512, 2048], P('ep', None, 'rep')
- bias_in_first_new: float32 [8, 2048], P('ep', 'rep')
- bias_in_second_new: float32 [8, 2048], P('ep', 'rep')
- bias_in_new: float32 [8, 2048], P('ep', 'rep')
- expert_out_first_new: float32 [8, 2048, 512], P('ep', 'rep')
- expert_out_second_new: float32 [8, 2048, 512], P('ep', 'rep')
- expert_out_new: float32 [8, 2048, 512], P('ep', 'rep')
- bias_out_first_new: float32 [8, 512], P('ep', 'rep')
- bias_out_second_new: float32 [8, 512], P('ep', 'rep')
- bias_out_new: float32 [8, 512], P('ep', 'rep')
- norms: float32 [3, 12], replicated
The draws below stay inside these ranges and needn't reach their ends.
Inputs may be any that keep to these rules, and one draw needn't show every extreme that they name: `expert_ids`: each token names 2 different experts. `priority`: each row is a permutation of its device's 1970 token positions.
All inputs are finite; a program needn't handle non-finite values.
Results may differ from the reference program's by a relative error of at most 0.014.
Values may be sent and summed in bfloat16 or wider, within the bound.
No kernel may reach another device: no remote copies, remote signals or barrier semaphores. Data moves between devices by JAX's collectives and lax.ppermute only.
A program may use at most 256 MiB of HBM per device.

```python
import math
import jax
import jax.numpy as jnp
from jax import lax

D = 512
HEADS = 8
HEAD = 64
FF = 2048
SEQ = 197
TOP = 2
STEP = 5
TOK_DEV = 1970
TOKENS = 63040
EXPERTS = 8
CAP = 616
N_REP = 4
N_EP = 8


def draw_scales(key, part):
    key = jax.random.fold_in(key, 11)
    gain_key, shift_key = jax.random.split(key)
    gains = jax.random.uniform(gain_key, (D, 2), jnp.float32, 0.7, 1.3)
    shifts = jnp.clip(0.1 * jax.random.normal(shift_key, (D, 3), jnp.float32), -0.5, 0.5)
    return jnp.stack([gains[:, 0], shifts[:, 0], gains[:, 1], shifts[:, 1], shifts[:, 2]], axis=1)


def shard_levels(rng, extent, cuts, smallest, largest):
    loudness = 1.0
    for dim, parts in cuts:
        draws = jax.random.uniform(jax.random.fold_in(jax.random.fold_in(rng, 6), dim), (parts,), jnp.float32, smallest / len(cuts), largest / len(cuts))
        loudness = loudness * jnp.repeat(jnp.exp(draws), extent[dim] // parts).reshape((-1,) + (1,) * (len(extent) - 1 - dim))
    return loudness


def choose_distinct(own_key, rows, count, top, lift):
    sequence = jax.random.permutation(jax.random.fold_in(own_key, 1), count)
    pull = sequence
    for power in range(3):
        pull = pull * pull // count
    pull = pull * lift // count
    tickets = jax.random.randint(jax.random.fold_in(own_key, 2), (rows, count), 0, 4096) + pull
    fixed_rows = jax.random.permutation(jax.random.fold_in(own_key, 3), rows)[jnp.arange(count) % rows]
    tickets = jnp.where(jnp.arange(rows)[:, None] == fixed_rows[None, :], 1 << 14, tickets)
    merit = tickets * count + jnp.arange(count)
    return lax.top_k(merit.astype(jnp.int32), top)[1].astype(jnp.int32)


def bell_draw(own_key, extent, scale, limit, pieces=(), kind=jnp.bfloat16):
    entries = scale * jax.random.normal(own_key, extent, jnp.float32)
    if pieces:
        entries = entries * shard_levels(own_key, extent, pieces, -0.22, 0.18)
    return jnp.clip(entries, -limit, limit).astype(kind)


def setup_inputs(seed: int = 0) -> dict:
    seeds = jax.random.split(jax.random.key(seed), 29)
    return {
        "tokens": bell_draw(seeds[0], (TOKENS, D), 1.0, 6.0, ((0, 32),)),
        "cotangent": bell_draw(seeds[1], (TOKENS, D), 1.0, 6.0, ((0, 32),)),
        "expert_ids": choose_distinct(seeds[2], TOKENS, EXPERTS, TOP, 4096),
        "priority": jax.vmap(lambda own: jax.random.permutation(own, TOK_DEV))(jax.random.split(seeds[3], (N_REP * N_EP))).reshape((N_REP * N_EP, TOK_DEV)).astype(jnp.int32),
        "heads_in": bell_draw(seeds[4], (D, 3 * D), D ** -0.5, 0.25, ((0, 32),), jnp.float32),
        "heads_in_first": bell_draw(seeds[5], (D, 3 * D), (0.3 * TOKENS ** 0.5), 448.0, ((0, 32),), jnp.float32),
        "heads_in_second": jnp.clip(jnp.exp(math.log(22694.4) - 1.3862944 * jax.random.uniform(seeds[6], (D, 3 * D), jnp.float32) ** shard_levels(seeds[6], (D, 3 * D), ((0, 32),), -0.2, 0.2)), 5673.6, 22694.4),
        "heads_out": bell_draw(seeds[7], (D, D), (D // 8) ** -0.5, 0.75, ((0, 32),), jnp.float32),
        "heads_out_first": bell_draw(seeds[8], (D, D), (0.3 * TOKENS ** 0.5), 448.0, ((0, 32),), jnp.float32),
        "heads_out_second": jnp.clip(jnp.exp(math.log(22694.4) - 1.3862944 * jax.random.uniform(seeds[9], (D, D), jnp.float32) ** shard_levels(seeds[9], (D, D), ((0, 32),), -0.2, 0.2)), 5673.6, 22694.4),
        "router": bell_draw(seeds[10], (D, EXPERTS), (2 * D) ** -0.5, 0.1875, ((0, 32),), jnp.float32),
        "router_first": bell_draw(seeds[11], (D, EXPERTS), (0.25 * (D * TOKENS) ** 0.5), 8192.0, ((0, 32),), jnp.float32),
        "router_second": jnp.clip(jnp.exp(math.log(8069120) - 1.3862944 * jax.random.uniform(seeds[12], (D, EXPERTS), jnp.float32) ** shard_levels(seeds[12], (D, EXPERTS), ((0, 32),), -0.2, 0.2)), 2017280, 8069120),
        "scales": draw_scales(jax.random.fold_in(seeds[28], 71), 0),
        "scales_first": bell_draw(seeds[14], (D, 5), (TOKENS ** 0.5), 1536.0, ((0, 32),), jnp.float32),
        "scales_second": jnp.clip(jnp.exp(math.log(252160.0) - 1.3862944 * jax.random.uniform(seeds[15], (D, 5), jnp.float32) ** shard_levels(seeds[15], (D, 5), ((0, 32),), -0.2, 0.2)), 63040.0, 252160.0),
        "expert_in": bell_draw(seeds[16], (EXPERTS, D, FF), D ** -0.5, 0.25, ((0, 8), (2, 4)), jnp.float32),
        "expert_in_first": bell_draw(seeds[17], (EXPERTS, D, FF), (0.3 * (2 * TOKENS // EXPERTS) ** 0.5), 224.0, ((0, 8), (2, 4)), jnp.float32),
        "expert_in_second": jnp.clip(jnp.exp(math.log(5673.6) - 1.3862944 * jax.random.uniform(seeds[18], (EXPERTS, D, FF), jnp.float32) ** shard_levels(seeds[18], (EXPERTS, D, FF), ((0, 8), (2, 4)), -0.2, 0.2)), 1418.4, 5673.6),
        "bias_in": bell_draw(seeds[19], (EXPERTS, FF), 0.1, 0.625, ((0, 8), (1, 4)), jnp.float32),
        "bias_in_first": bell_draw(seeds[20], (EXPERTS, FF), (0.3 * (2 * TOKENS // EXPERTS) ** 0.5), 224.0, ((0, 8), (1, 4)), jnp.float32),
        "bias_in_second": jnp.clip(jnp.exp(math.log(5673.6) - 1.3862944 * jax.random.uniform(seeds[21], (EXPERTS, FF), jnp.float32) ** shard_levels(seeds[21], (EXPERTS, FF), ((0, 8), (1, 4)), -0.2, 0.2)), 1418.4, 5673.6),
        "expert_out": bell_draw(seeds[22], (EXPERTS, FF, D), (FF // 2) ** -0.5, 0.1875, ((0, 8), (1, 4)), jnp.float32),
        "expert_out_first": bell_draw(seeds[23], (EXPERTS, FF, D), (0.3 * (2 * TOKENS // EXPERTS) ** 0.5), 224.0, ((0, 8), (1, 4)), jnp.float32),
        "expert_out_second": jnp.clip(jnp.exp(math.log(5673.6) - 1.3862944 * jax.random.uniform(seeds[24], (EXPERTS, FF, D), jnp.float32) ** shard_levels(seeds[24], (EXPERTS, FF, D), ((0, 8), (1, 4)), -0.2, 0.2)), 1418.4, 5673.6),
        "bias_out": bell_draw(seeds[25], (EXPERTS, D), 0.1, 0.625, ((0, 8), (1, 4)), jnp.float32),
        "bias_out_first": bell_draw(seeds[26], (EXPERTS, D), (0.5 * (2 * TOKENS // EXPERTS) ** 0.5), 384.0, ((0, 8), (1, 4)), jnp.float32),
        "bias_out_second": jnp.clip(jnp.exp(math.log(15760.0) - 1.3862944 * jax.random.uniform(seeds[27], (EXPERTS, D), jnp.float32) ** shard_levels(seeds[27], (EXPERTS, D), ((0, 8), (1, 4)), -0.2, 0.2)), 3940.0, 15760.0),
    }


BETA = 0.5
RATE = 0.3
DECAY = 0.01
EPSILON = 1e-06

@jax.custom_vjp
def low(v):
    return lax.optimization_barrier(v.astype(jnp.bfloat16)).astype(jnp.float32)

@jax.custom_vjp
def low_back(v):
    return v

def low_keep(v):
    return (low(v), None)

def low_pass(kept, grad):
    return (grad,)

def back_keep(v):
    return (v, None)

def back_low(kept, grad):
    return (low(grad),)
low.defvjp(low_keep, low_pass)
low_back.defvjp(back_keep, back_low)

def matmul(left, right):
    return jnp.dot(left, right, precision=lax.Precision.HIGHEST, preferred_element_type=jnp.float32)

def layer_norm(rows, gain, shift):
    centred = rows - lax.optimization_barrier(jnp.mean(rows, axis=-1, keepdims=True))
    inverse = lax.rsqrt(lax.optimization_barrier(jnp.mean(centred * centred, axis=-1, keepdims=True)) + 1e-06)
    return centred * inverse * gain + shift

def route_places(block_ids, ranking, experts):
    count = block_ids.shape[0]
    keys = jnp.arange(block_ids.shape[1], dtype=jnp.int32)[None, :] * count + ranking[:, None]
    ordered = jnp.zeros((block_ids.size,), jnp.int32).at[keys.reshape(-1)].set(block_ids.reshape(-1))
    hits = (ordered[:, None] == jnp.arange(experts, dtype=jnp.int32)[None, :]).astype(jnp.int32)
    before = jnp.cumsum(hits, axis=0) - hits
    place = lax.optimization_barrier(jnp.sum(before * hits, axis=1))
    return place[keys]

def attend(rows, in_low, out_low):
    count = rows.shape[0]
    projected = low(low_back(matmul(rows, in_low)))
    grid = projected.reshape(count // SEQ, SEQ, 3, HEADS, HEAD)
    scores = jnp.einsum('bqhd,bkhd->bhqk', grid[:, :, 0], grid[:, :, 1], precision=lax.Precision.HIGHEST)
    scores = low_back(scores * HEAD ** (-0.5))
    probs = jax.nn.softmax(scores, axis=-1)
    mixed = jnp.einsum('bhqk,bkhd->bqhd', low(probs), grid[:, :, 2], precision=lax.Precision.HIGHEST)
    mixed = low(low_back(mixed.reshape(count, HEADS * HEAD)))
    return low_back(matmul(mixed, out_low))

def forward(inputs, heads_in, heads_out, router, scales, expert_in, bias_in, expert_out, bias_out, pair_slot, table, expert_ids):
    gains = low(scales)
    entry = low(layer_norm(inputs, gains[:, 0], gains[:, 1]))
    in_low = low(heads_in)
    out_low = low(heads_out)
    attend_block = jax.checkpoint(attend)

    def scan_step(carry, block):
        return (carry, attend_block(block, in_low, out_low))
    _, attended = lax.scan(scan_step, jnp.zeros((), jnp.float32), entry.reshape(N_REP * N_EP, TOK_DEV, D))
    hidden = inputs + attended.reshape(TOKENS, D) + gains[:, 4]
    routed = low(layer_norm(hidden, gains[:, 2], gains[:, 3]))
    logits = low_back(matmul(routed, low(router)))
    choose = (expert_ids[:, :, None] == jnp.arange(EXPERTS, dtype=jnp.int32)[None, None, :]).astype(jnp.float32)
    picked = lax.optimization_barrier(jnp.sum(choose * logits[:, None, :], axis=2))
    gates = jax.nn.softmax(picked, axis=1)
    padded_rows = jnp.concatenate([routed, jnp.zeros((1, D), jnp.float32)], axis=0)

    def one_expert(item):
        index, first, first_bias, second, second_bias = item
        rows = low_back(padded_rows[index])
        pre = low_back(matmul(rows, first) + first_bias)
        act = low(jax.nn.gelu(pre, approximate=False))
        return low(low_back(matmul(act, second) + second_bias))
    results = lax.map(jax.checkpoint(one_expert), (table, low(expert_in), low(bias_in), low(expert_out), low(bias_out)))
    flat = jnp.concatenate([results.reshape(-1, D), jnp.zeros((1, D), jnp.float32)], axis=0)
    return hidden + lax.optimization_barrier(jnp.sum(gates[:, :, None] * flat[pair_slot], axis=1))

def moments(weight, grad, first, second):
    first_new = BETA * first + (1.0 - BETA) * grad
    second_new = BETA * second + (1.0 - BETA) * grad * grad
    step = first_new / (1.0 - BETA ** STEP) / (jnp.sqrt(second_new / (1.0 - BETA ** STEP)) + EPSILON) + DECAY * weight
    return (first_new, second_new, step)

def squares(array, per_column):
    if per_column:
        return lax.optimization_barrier(jnp.sum(array * array, axis=0))
    return jnp.sum(array * array)[None]

def reference(tokens, cotangent, expert_ids, priority, heads_in, heads_in_first, heads_in_second, heads_out, heads_out_first, heads_out_second, router, router_first, router_second, scales, scales_first, scales_second, expert_in, expert_in_first, expert_in_second, bias_in, bias_in_first, bias_in_second, expert_out, expert_out_first, expert_out_second, bias_out, bias_out_first, bias_out_second):
    devices = N_REP * N_EP

    def route_block(block_ids, ranking):
        return route_places(block_ids, ranking, EXPERTS)
    places = jax.vmap(route_block)(expert_ids.reshape(devices, TOK_DEV, TOP), priority).reshape(TOKENS, TOP)
    per_expert = devices * CAP
    source = (jnp.arange(TOKENS, dtype=jnp.int32) // TOK_DEV)[:, None]
    slot = expert_ids * per_expert + source * CAP + places
    pair_slot = jnp.where(places < CAP, slot, EXPERTS * per_expert).astype(jnp.int32)
    owners = jnp.broadcast_to(jnp.arange(TOKENS, dtype=jnp.int32)[:, None], (TOKENS, TOP))
    table = jnp.full((EXPERTS * per_expert,), TOKENS, jnp.int32)
    table = table.at[pair_slot.reshape(-1)].set(owners.reshape(-1), mode='drop').reshape(EXPERTS, per_expert)

    def forward_all(*params):
        return forward(*params, pair_slot, table, expert_ids)
    primals = (tokens.astype(jnp.float32), heads_in, heads_out, router, scales, expert_in, bias_in, expert_out, bias_out)
    output, pullback = jax.vjp(forward_all, *primals)
    grads = pullback(cotangent.astype(jnp.float32))
    firsts = (heads_in_first, heads_out_first, router_first, scales_first, expert_in_first, bias_in_first, expert_out_first, bias_out_first)
    seconds = (heads_in_second, heads_out_second, router_second, scales_second, expert_in_second, bias_in_second, expert_out_second, bias_out_second)
    states = [moments(w, g, f, s) for w, g, f, s in zip(primals[1:], grads[1:], firsts, seconds)]
    weight_terms = jnp.concatenate([squares(w, index == 3) for index, w in enumerate(primals[1:])])
    step_terms = jnp.concatenate([squares(state[2], index == 3) for index, state in enumerate(states)])
    counts = jnp.array([3 * D * D, D * D, D * EXPERTS] + [D] * 5 + [EXPERTS * D * FF, EXPERTS * FF, EXPERTS * FF * D, EXPERTS * D], jnp.float32)
    weight_rms = jnp.sqrt(weight_terms / counts)
    step_rms = jnp.sqrt(step_terms / counts)
    trust = weight_rms / step_rms
    bounds = [(0, 1), (1, 2), (2, 3), (3, 8), (8, 9), (9, 10), (10, 11), (11, 12)]
    results = [output, grads[0]]
    for weight, state, bound in zip(primals[1:], states, bounds):
        results.extend([state[0], state[1], weight - RATE * trust[bound[0]:bound[1]] * state[2]])
    results.append(jnp.stack([weight_rms, step_rms, trust]))
    return tuple(results)
```

```python
import functools

import jax
import jax.numpy as jnp
from jax import lax
from jax.experimental import pallas as pl
from jax.experimental.pallas import tpu as pltpu
from jax.sharding import PartitionSpec as P

HEADS = 8
HEAD = 64
FF = 2048
SEQ = 197
STEP = 5


BETA = 0.5
RATE = 0.3
DECAY = 0.01
EPSILON = 1e-06


def normalize(rows):
    centred = rows - jnp.mean(rows, axis=-1, keepdims=True)
    inverse = lax.rsqrt(jnp.mean(centred * centred, axis=-1, keepdims=True) + 1e-06)
    return (centred * inverse, inverse)


def norm_back(grad_rows, normed, inverse, gain):
    scaled = grad_rows * gain
    return inverse * (
        scaled
        - jnp.mean(scaled, axis=-1, keepdims=True)
        - normed * jnp.mean(scaled * normed, axis=-1, keepdims=True)
    )


def exact_gelu(values):
    return jax.nn.gelu(values, approximate=False)


def route_places(block_ids, ranking, experts):
    count = block_ids.shape[0]
    keys = jnp.arange(block_ids.shape[1], dtype=jnp.int32)[None, :] * count + ranking[:, None]
    ordered = (
        jnp.zeros((block_ids.size,), jnp.int32).at[keys.reshape(-1)].set(block_ids.reshape(-1))
    )
    hits = (ordered[:, None] == jnp.arange(experts, dtype=jnp.int32)[None, :]).astype(jnp.int32)
    before = jnp.cumsum(hits, axis=0) - hits
    place = jnp.sum(before * hits, axis=1)
    return place[keys]


def attention_scores(query, keyed, factor):
    return jnp.einsum("bqhd,bkhd->bhqk", query, keyed, preferred_element_type=jnp.float32) * factor


def moments(weight, grad, first, second):
    first_new = BETA * first + (1.0 - BETA) * grad
    second_new = BETA * second + (1.0 - BETA) * grad * grad
    step = (
        first_new / (1.0 - BETA**STEP) / (jnp.sqrt(second_new / (1.0 - BETA**STEP)) + EPSILON)
        + DECAY * weight
    )
    return (first_new, second_new, step)


def squares(array, per_column):
    if per_column:
        return jnp.sum(array * array, axis=0)
    return jnp.sum(array * array)[None]


def finish(totals, weights_now, states, width, experts):
    counts = jnp.array(
        [3 * width * width, width * width, width * experts]
        + [width] * 5
        + [experts * width * FF, experts * FF, experts * FF * width, experts * width],
        jnp.float32,
    )
    weight_rms = jnp.sqrt(totals[0] / counts)
    step_rms = jnp.sqrt(totals[1] / counts)
    trust = weight_rms / step_rms
    bounds = [(0, 1), (1, 2), (2, 3), (3, 8), (8, 9), (9, 10), (10, 11), (11, 12)]
    results = []
    for weight, state, bound in zip(weights_now, states, bounds):
        results.extend([state[0], state[1], weight - RATE * trust[bound[0] : bound[1]] * state[2]])
    results.append(jnp.stack([weight_rms, step_rms, trust]))
    return tuple(results)


PAD = 208
WIN = 96
VMEM = 60 * 1024 * 1024
BF = jnp.bfloat16
F32 = jnp.float32


def dot_nn(a, b):
    return lax.dot_general(a, b, (((1,), (0,)), ((), ())), preferred_element_type=F32)


def dot_nt(a, b):
    return lax.dot_general(a, b, (((1,), (1,)), ((), ())), preferred_element_type=F32)


def dot_tn(a, b):
    return lax.dot_general(a, b, (((0,), (0,)), ((), ())), preferred_element_type=F32)


def lane_iota(rows, lanes):
    return lax.broadcasted_iota(jnp.int32, (rows, lanes), 1)


def row_iota(rows, lanes):
    return lax.broadcasted_iota(jnp.int32, (rows, lanes), 0)


def whole(shape):
    return pl.BlockSpec(shape, lambda *_: (0,) * len(shape))


def params(semantics=None, **kw):
    return pltpu.CompilerParams(vmem_limit_bytes=VMEM, **kw)


def assemble_kernel(place_ref, got_ref, in_ref, out_ref, router_ref, gains_ref, small_ref):
    copies, rows = got_ref.shape[0], got_ref.shape[1]
    width = out_ref.shape[1]

    def body(j, carry):
        place = pl.multiple_of(place_ref[j] * rows, rows)
        in_ref[pl.ds(place, rows), :] = got_ref[j, :, : 3 * width]
        out_ref[pl.ds(place, rows), :] = got_ref[j, :, 3 * width : 4 * width]
        small_ref[pl.ds(place, rows), :] = got_ref[j, :, 4 * width :]
        return carry

    lax.fori_loop(0, copies, body, 0)
    turned = small_ref[:, :128].astype(F32).T
    experts = router_ref.shape[0]
    router_ref[...] = turned[:experts].astype(BF)
    gains_ref[...] = turned[experts : experts + 8]


def assemble(place, got, experts):
    copies, rows, lanes = got.shape
    width = copies * rows
    return pl.pallas_call(
        assemble_kernel,
        grid_spec=pltpu.PrefetchScalarGridSpec(
            num_scalar_prefetch=1,
            grid=(1,),
            in_specs=[whole(got.shape)],
            out_specs=[
                whole((width, 3 * width)),
                whole((width, width)),
                whole((experts, width)),
                whole((8, width)),
                whole((width, lanes - 4 * width)),
            ],
        ),
        out_shape=[
            jax.ShapeDtypeStruct((width, 3 * width), BF),
            jax.ShapeDtypeStruct((width, width), BF),
            jax.ShapeDtypeStruct((experts, width), BF),
            jax.ShapeDtypeStruct((8, width), F32),
            jax.ShapeDtypeStruct((width, lanes - 4 * width), BF),
        ],
        compiler_params=params(),
        name="assemble",
    )(place, got)


def places_kernel(capacity, rows_ref, cols_ref, lrow_ref, lcol_ref, meta_ref):
    count = cols_ref.shape[0]
    images = count // PAD
    experts = lcol_ref.shape[1]
    expert = lane_iota(count, experts).astype(F32)
    first = (cols_ref[:, 1:2] == expert).astype(F32)
    second = (cols_ref[:, 2:3] == expert).astype(F32)
    first_low = first.astype(BF)
    second_low = second.astype(BF)
    total_first = jnp.sum(first, axis=0, keepdims=True)
    lower = (lane_iota(PAD, PAD) < row_iota(PAD, PAD)).astype(F32).astype(BF)
    ranking = rows_ref[0:1, :]
    begin = jnp.zeros((1, experts), F32)
    for i in range(images):
        span = slice(i * PAD, (i + 1) * PAD)
        ahead = (ranking < cols_ref[span, 0:1]).astype(F32).astype(BF)
        rank_first = dot_nn(ahead, first_low)
        rank_second = dot_nn(ahead, second_low) + total_first
        place = first[span] * rank_first + second[span] * rank_second
        kept = (first[span] + second[span]) * (place < capacity).astype(F32)
        local = dot_nn(lower, kept.astype(BF))
        local = jnp.where(kept > 0.0, local, -1.0)
        lcol_ref[span, :] = local
        lrow_ref[i] = local.T
        here = jnp.sum(kept, axis=0, keepdims=True)
        meta_ref[i : i + 1, :] = begin.astype(jnp.int32)
        meta_ref[images + i : images + i + 1, :] = here.astype(jnp.int32)
        begin = begin + here


def find_places(rows, cols, capacity, experts):
    count = cols.shape[0]
    images = count // PAD
    return pl.pallas_call(
        functools.partial(places_kernel, capacity),
        out_shape=[
            jax.ShapeDtypeStruct((images, experts, PAD), F32),
            jax.ShapeDtypeStruct((count, experts), F32),
            jax.ShapeDtypeStruct((2 * images, experts), jnp.int32),
        ],
        compiler_params=params(),
        name="places",
    )(rows, cols)


def spread_kernel(tok_ref, cot_ref, tpad_ref, cpad_ref):
    count, width = tok_ref.shape
    for source, target in ((tok_ref, tpad_ref), (cot_ref, cpad_ref)):
        for i in range(count // SEQ):
            rows = source[SEQ * i : SEQ * (i + 1), :].astype(F32)
            rows = jnp.concatenate([rows, jnp.zeros((PAD - SEQ, width), F32)], axis=0)
            target[PAD * i : PAD * (i + 1), :] = rows.astype(BF)


def spread_rows(tokens, cotangent):
    count, width = tokens.shape
    shape = jax.ShapeDtypeStruct((count // SEQ * PAD, width), BF)
    return pl.pallas_call(
        spread_kernel, out_shape=[shape, shape], compiler_params=params(), name="spread_rows"
    )(tokens, cotangent)


def store_image(target, i, values):
    for image in range(target.shape[0] // SEQ):

        @pl.when(i == image)
        def _(image=image):
            target[SEQ * image : SEQ * (image + 1), :] = values[0:SEQ, :]


def attention_kernel(
    tok_ref, in_ref, out_ref, router_ref, gains_ref, ids_ref,
    proj_ref, prob_ref, mixed_ref, hidden_ref, routed_ref, gcol_ref, grow_ref, mixed_all,
):
    width = tok_ref.shape[1]
    x = tok_ref[...].astype(F32)
    normed, _ = normalize(x)
    entry = (normed * gains_ref[0:1, :] + gains_ref[1:2, :]).astype(BF)
    proj_ref[...] = dot_nn(entry, in_ref[...]).astype(BF)
    pair = 2 * HEAD
    halves = lane_iota(PAD, pair) < HEAD
    key_there = lane_iota(PAD, PAD) < SEQ
    for p in range(HEADS // 2):
        q = proj_ref[:, pair * p : pair * (p + 1)] * jnp.asarray(HEAD ** -0.5, BF)
        k = proj_ref[:, width + pair * p : width + pair * (p + 1)]
        v = proj_ref[:, 2 * width + pair * p : 2 * width + pair * (p + 1)]
        sides = []
        for s in range(2):
            mine = halves if s == 0 else jnp.logical_not(halves)
            scores = dot_nt(jnp.where(mine, q, jnp.zeros_like(q)), k)
            scores = jnp.where(key_there, scores, -1e30)
            peak = jnp.max(scores, axis=1, keepdims=True)
            raised = jnp.exp(scores - peak)
            total = jnp.sum(raised, axis=1, keepdims=True)
            weights = (raised * (1.0 / total)).astype(BF)
            prob_ref[0, 2 * p + s] = weights
            sides.append(dot_nn(weights, v))
        mixed_all[:, pair * p : pair * (p + 1)] = jnp.where(halves, sides[0], sides[1]).astype(BF)
    mixed = mixed_all[...]
    mixed_ref[...] = mixed
    hidden = x + dot_nn(mixed, out_ref[...]) + gains_ref[4:5, :]
    hidden_ref[...] = hidden
    normed_two, _ = normalize(hidden)
    routed = (normed_two * gains_ref[2:3, :] + gains_ref[3:4, :]).astype(BF)
    routed_ref[...] = routed
    logits = dot_nt(routed, router_ref[...])
    experts = logits.shape[1]
    expert = lane_iota(PAD, experts)
    chosen = jnp.logical_or(ids_ref[:, 0:1] == expert, ids_ref[:, 1:2] == expert)
    top = jnp.max(jnp.where(chosen, logits, -1e30), axis=1, keepdims=True)
    raised = jnp.where(chosen, jnp.exp(jnp.where(chosen, logits - top, 0.0)), 0.0)
    total = jnp.sum(raised, axis=1, keepdims=True)
    gates = raised / jnp.where(total > 0.0, total, 1.0)
    gcol_ref[...] = gates
    grow_ref[0] = gates.T


def attention(tok_pad, in_matrix, out_matrix, router, gains, ids_col):
    padded, width = tok_pad.shape
    images = padded // PAD
    experts = router.shape[0]
    row = lambda lanes: pl.BlockSpec((PAD, lanes), lambda i: (i, 0))
    once = lambda a: pl.BlockSpec(a.shape, lambda i: (0, 0), pipeline_mode=pl.Buffered(1))
    return pl.pallas_call(
        attention_kernel,
        grid=(images,),
        in_specs=[row(width), once(in_matrix), once(out_matrix), once(router), once(gains), row(2)],
        out_specs=[
            row(3 * width),
            pl.BlockSpec((1, HEADS, PAD, PAD), lambda i: (i, 0, 0, 0)),
            row(width), row(width), row(width), row(experts),
            pl.BlockSpec((1, experts, PAD), lambda i: (i, 0, 0)),
        ],
        out_shape=[
            jax.ShapeDtypeStruct((padded, 3 * width), BF),
            jax.ShapeDtypeStruct((images, HEADS, PAD, PAD), BF),
            jax.ShapeDtypeStruct((padded, width), BF),
            jax.ShapeDtypeStruct((padded, width), F32),
            jax.ShapeDtypeStruct((padded, width), BF),
            jax.ShapeDtypeStruct((padded, experts), F32),
            jax.ShapeDtypeStruct((images, experts, PAD), F32),
        ],
        scratch_shapes=[pltpu.VMEM((PAD, width), BF)],
        compiler_params=params(),
        name="attention",
    )(tok_pad, in_matrix, out_matrix, router, gains, ids_col)


def window_count():
    return -(-(15 + SEQ) // WIN)


def gather_kernel(meta_ref, routed_ref, cot_ref, lrow_ref, grow_ref, r_ref, g_ref, rt_ref, gt_ref, r_all, g_all):
    e = pl.program_id(0)
    images = lrow_ref.shape[0]
    listed = r_ref.shape[1]
    r_all[...] = jnp.zeros_like(r_all)
    g_all[...] = jnp.zeros_like(g_all)
    row = row_iota(WIN, PAD).astype(F32)
    for i in range(images):
        start, here = meta_ref[i, e], meta_ref[images + i, e]
        base = lax.shift_left(lax.shift_right_logical(start, 4), 4)
        shift = (start - base).astype(F32)
        local = lrow_ref[i, pl.ds(e, 1), :]
        gate = grow_ref[i, pl.ds(e, 1), :]
        for q in range(window_count()):
            @pl.when(jnp.logical_and(here > 0, base + q * WIN < start + here))
            def _(i=i, q=q, base=base, shift=shift, local=local, gate=gate):
                pick = jnp.logical_and(local >= 0.0, local + (shift - q * WIN) == row)
                low = pick.astype(F32).astype(BF)
                slot_gate = jnp.sum(jnp.where(pick, gate, 0.0), axis=1, keepdims=True)
                where = pl.ds(pl.multiple_of(base + q * WIN, 16), WIN)
                r_all[where, :] += dot_nn(low, routed_ref[i * PAD : (i + 1) * PAD, :])
                g_all[where, :] += slot_gate * dot_nn(low, cot_ref[i * PAD : (i + 1) * PAD, :])
    r_ref[0] = r_all[0:listed, :].astype(BF)
    g_ref[0] = g_all[0:listed, :].astype(BF)
    rt_ref[0] = r_all[0:listed, :].T.astype(BF)
    gt_ref[0] = g_all[0:listed, :].astype(BF).astype(F32).T.astype(BF)


def gather(meta, routed, cot_pad, lrow, grow, listed):
    width = routed.shape[1]
    experts = lrow.shape[1]
    once = lambda a: pl.BlockSpec(a.shape, lambda e, m: (0,) * a.ndim, pipeline_mode=pl.Buffered(1))
    block = pl.BlockSpec((1, listed, width), lambda e, m: (e, 0, 0))
    turned = pl.BlockSpec((1, width, listed), lambda e, m: (e, 0, 0))
    return pl.pallas_call(
        gather_kernel,
        grid_spec=pltpu.PrefetchScalarGridSpec(
            num_scalar_prefetch=1,
            grid=(experts,),
            in_specs=[once(routed), once(cot_pad), once(lrow), once(grow)],
            out_specs=[block, block, turned, turned],
            scratch_shapes=[pltpu.VMEM((listed + WIN, width), F32)] * 2,
        ),
        out_shape=[jax.ShapeDtypeStruct((experts, listed, width), BF)] * 2
        + [jax.ShapeDtypeStruct((experts, width, listed), BF)] * 2,
        compiler_params=params(),
        name="gather",
    )(meta, routed, cot_pad, lrow, grow)


def gelu_both(pre):
    bell = jnp.exp(-0.5 * (pre * pre))
    t = pl.reciprocal(1.0 + (0.3275911 * 2.0**-0.5) * jnp.abs(pre))
    tail = t * (0.127414796 + t * (-0.142248368 + t * (0.7107068705 + t * (-0.7265760135 + t * 0.5307027145))))
    tail = tail * bell
    phi = jnp.where(pre < 0.0, tail, 1.0 - tail)
    return pre * phi, phi + pre * bell * 0.3989422804014327


def expert_kernel(last, at_ref, *refs):
    if last:
        (r_ref, g_ref, rt_ref, gt_ref, w_ref, b_ref, ob_ref, y_in, d_in,
         y_ref, d_ref, near_ref, far_ref, db_ref, y_all, d_all) = refs
    else:
        (r_ref, g_ref, rt_ref, gt_ref, w_ref, b_ref,
         y_ref, d_ref, near_ref, far_ref, db_ref, obg_ref, y_all, d_all) = refs
    rep = w_ref.shape[0]
    rows, grads = r_ref[0], g_ref[0]
    rows_t, grads_t = rt_ref[0], gt_ref[0]
    if not last:
        obg_ref[0] = jnp.sum(grads.astype(F32), axis=0, keepdims=True)
    for r in range(rep):
        place = lax.bitwise_xor(at_ref[0], r)
        enter, leave = w_ref[place, 0, 0], w_ref[place, 0, 1]
        pre = dot_nn(rows, enter) + b_ref[0, pl.ds(place, 1), :]
        act, slope = gelu_both(pre)
        act = act.astype(BF)
        grad_pre = (dot_nn(grads, leave) * slope).astype(BF)
        out = far_ref if r % 2 else near_ref
        out[r // 2, 0, 0] = dot_nn(rows_t, grad_pre).astype(BF)
        out[r // 2, 0, 1] = dot_nn(grads_t, act).astype(BF)
        db_ref[0, pl.ds(place, 1), :] = jnp.sum(grad_pre.astype(F32), axis=0, keepdims=True)
        y_part = dot_nt(act, leave)
        d_part = dot_nt(grad_pre, enter)
        if r == 0:
            y_all[...] = y_part + y_in[0] if last else y_part
            d_all[...] = d_part + d_in[0] if last else d_part
        else:
            y_all[...] += y_part
            d_all[...] += d_part
    if last:
        y_ref[0] = (y_all[...] + ob_ref[0]).astype(BF)
        d_ref[0] = d_all[...].astype(BF)
    else:
        y_ref[0] = y_all[...]
        d_ref[0] = d_all[...]


def expert_pass(at, lists, weights, bias, out_bias=None, carried=None):
    last = carried is not None
    rows = lists[0]
    experts, listed, width = rows.shape
    rep, _, _, _, cols = weights.shape
    here = lambda e, at: lax.bitwise_xor(e, at[1])
    block = pl.BlockSpec((1, listed, width), lambda e, at: (here(e, at), 0, 0))
    turned = pl.BlockSpec((1, width, listed), lambda e, at: (here(e, at), 0, 0))
    out_w = pl.BlockSpec((rep // 2, 1, 2, width, cols), lambda e, at: (0, e, 0, 0, 0))
    in_specs = [
        block, block, turned, turned,
        pl.BlockSpec((rep, 1, 2, width, cols), lambda e, at: (0, here(e, at), 0, 0, 0)),
        pl.BlockSpec((1, rep, cols), lambda e, at: (here(e, at), 0, 0)),
    ]
    args = list(lists) + [weights, bias]
    kind = BF if last else F32
    out_specs = [block, block, out_w, out_w, pl.BlockSpec((1, rep, cols), lambda e, at: (here(e, at), 0, 0))]
    out_shape = [
        jax.ShapeDtypeStruct(rows.shape, kind),
        jax.ShapeDtypeStruct(rows.shape, kind),
        jax.ShapeDtypeStruct((rep // 2, experts, 2, width, cols), BF),
        jax.ShapeDtypeStruct((rep // 2, experts, 2, width, cols), BF),
        jax.ShapeDtypeStruct((experts, rep, cols), F32),
    ]
    if last:
        in_specs += [pl.BlockSpec((1, 1, width), lambda e, at: (here(e, at), 0, 0)), block, block]
        args += [out_bias, *carried]
    else:
        out_specs.append(pl.BlockSpec((1, 1, width), lambda e, at: (here(e, at), 0, 0)))
        out_shape.append(jax.ShapeDtypeStruct((experts, 1, width), F32))
    flops = 12 * experts * listed * width * rep * cols
    return pl.pallas_call(
        functools.partial(expert_kernel, last),
        grid_spec=pltpu.PrefetchScalarGridSpec(
            num_scalar_prefetch=1,
            grid=(experts,),
            in_specs=in_specs,
            out_specs=out_specs,
            scratch_shapes=[pltpu.VMEM((listed, width), F32)] * 2,
        ),
        out_shape=out_shape,
        compiler_params=params(),
        cost_estimate=pl.CostEstimate(flops=flops, bytes_accessed=60_000_000, transcendentals=0),
        name="experts_last" if last else "experts_first",
    )(at, *args)


def combine_kernel(
    meta_ref, y_ref, d_ref, lcol_ref, gcol_ref, hidden_ref, cot_ref, mixed_ref, out_w_ref, router_ref, gains_ref,
    out_ref, gh_ref, gm_ref, dout_ref, drouter_ref, dscale_ref, y_acc, g_acc, d_acc,
):
    i = pl.program_id(0)
    images = pl.num_programs(0)
    experts, listed, width = y_ref.shape
    gates = gcol_ref[...]
    local = lcol_ref[...]
    go = cot_ref[...].astype(F32)
    lane = lane_iota(PAD, WIN).astype(F32)
    expert = lane_iota(PAD, experts)

    def window(e, q, base, shift):
        at = jnp.minimum(base + q * WIN, listed - WIN)
        moved = (at - base).astype(F32)
        spot = local[:, e : e + 1] + shift
        pick = jnp.logical_and(spot == lane + moved, local[:, e : e + 1] >= 0.0)
        pick = jnp.logical_and(pick, spot >= q * WIN)
        low = pick.astype(F32).astype(BF)
        where = pl.ds(pl.multiple_of(at, 16), WIN)
        return dot_nn(low, y_ref[e, where, :]), dot_nn(low, d_ref[e, where, :])

    y_sum = jnp.zeros((PAD, width), F32)
    d_sum = jnp.zeros((PAD, width), F32)
    grad_gates = jnp.zeros((PAD, experts), F32)
    bases = []
    for e in range(experts):
        start = meta_ref[i, e]
        base = lax.shift_left(lax.shift_right_logical(start, 4), 4)
        bases.append((start, base))
        y_tok, d_tok = window(e, 0, base, (start - base).astype(F32))
        y_sum += gates[:, e : e + 1] * y_tok
        d_sum += d_tok
        gg = jnp.sum(go * y_tok, axis=1, keepdims=True)
        grad_gates += jnp.where(expert == e, gg, 0.0)
    y_acc[...] = y_sum
    d_acc[...] = d_sum
    g_acc[...] = grad_gates
    for e in range(experts):
        start, base = bases[e]
        here = meta_ref[images + i, e]
        for q in range(1, window_count()):
            @pl.when(base + q * WIN < start + here)
            def _(e=e, q=q, base=base, start=start):
                y_tok, d_tok = window(e, q, base, (start - base).astype(F32))
                y_acc[...] += gates[:, e : e + 1] * y_tok
                d_acc[...] += d_tok
                gg = jnp.sum(go * y_tok, axis=1, keepdims=True)
                g_acc[...] += jnp.where(expert == e, gg, 0.0)
    hidden = hidden_ref[...]
    y_acc[...] += hidden
    store_image(out_ref, i, y_acc)
    grad_gates = g_acc[...]
    pick = gates * (grad_gates - jnp.sum(gates * grad_gates, axis=1, keepdims=True))
    logit_low = pick.astype(BF)
    grad_routed = d_acc[...] + dot_nn(logit_low, router_ref[...])
    normed, inverse = normalize(hidden)
    routed = (normed * gains_ref[2:3, :] + gains_ref[3:4, :]).astype(BF)
    grad_hidden = go + norm_back(grad_routed, normed, inverse, gains_ref[2:3, :])
    gh_ref[...] = grad_hidden
    grad_mix = grad_hidden.astype(BF)
    gm_ref[...] = dot_nt(grad_mix, out_w_ref[...]).astype(BF)

    @pl.when(i == 0)
    def _():
        dout_ref[...] = jnp.zeros_like(dout_ref)
        drouter_ref[...] = jnp.zeros_like(drouter_ref)
        dscale_ref[...] = jnp.zeros_like(dscale_ref)

    dout_ref[...] += dot_tn(mixed_ref[...], grad_mix)
    drouter_ref[...] += dot_tn(logit_low, routed)
    dscale_ref[2:3, :] += jnp.sum(grad_routed * normed, axis=0, keepdims=True)
    dscale_ref[3:4, :] += jnp.sum(grad_routed, axis=0, keepdims=True)
    dscale_ref[4:5, :] += jnp.sum(grad_hidden, axis=0, keepdims=True)


def combine(meta, y, d, lcol, gcol, hidden, cot_pad, mixed, out_matrix, router, gains):
    padded, width = hidden.shape
    images = padded // PAD
    experts = y.shape[0]
    row = lambda lanes: pl.BlockSpec((PAD, lanes), lambda i, m: (i, 0))
    once = lambda a: pl.BlockSpec(a.shape, lambda i, m: (0,) * a.ndim, pipeline_mode=pl.Buffered(1))
    return pl.pallas_call(
        combine_kernel,
        grid_spec=pltpu.PrefetchScalarGridSpec(
            num_scalar_prefetch=1,
            grid=(images,),
            in_specs=[
                once(y), once(d), row(experts), row(experts), row(width), row(width), row(width),
                once(out_matrix), once(router), once(gains),
            ],
            out_specs=[
                whole((images * SEQ, width)), row(width), row(width), whole((width, width)), whole((experts, width)),
                whole((8, width)),
            ],
            scratch_shapes=[
                pltpu.VMEM((PAD, width), F32), pltpu.VMEM((PAD, experts), F32), pltpu.VMEM((PAD, width), F32),
            ],
        ),
        out_shape=[
            jax.ShapeDtypeStruct((images * SEQ, width), F32),
            jax.ShapeDtypeStruct((padded, width), F32),
            jax.ShapeDtypeStruct((padded, width), BF),
            jax.ShapeDtypeStruct((width, width), F32),
            jax.ShapeDtypeStruct((experts, width), F32),
            jax.ShapeDtypeStruct((8, width), F32),
        ],
        compiler_params=params(),
        name="combine",
    )(meta, y, d, lcol, gcol, hidden, cot_pad, mixed, out_matrix, router, gains)


def attention_back_kernel(
    place_ref, proj_ref, prob_ref, gm_ref, gh_ref, tpad_ref, in_ref, gains_ref, dout_ref, small_ref,
    grad_ref, near_ref, far_ref, din_ref, dscale_ref, line_ref, dproj, grad_all,
):
    i = pl.program_id(0)
    width = gm_ref.shape[1]
    pair = 2 * HEAD
    halves = lane_iota(PAD, pair) < HEAD
    factor = HEAD ** -0.5
    for p in range(HEADS // 2):
        cut = slice(pair * p, pair * (p + 1))
        q = proj_ref[:, cut]
        k = proj_ref[:, width + pair * p : width + pair * (p + 1)]
        v = proj_ref[:, 2 * width + pair * p : 2 * width + pair * (p + 1)]
        gm = gm_ref[:, cut]
        both = []
        for s in range(2):
            mine = halves if s == 0 else jnp.logical_not(halves)
            low = prob_ref[0, 2 * p + s]
            probs = low.astype(F32)
            grad_probs = dot_nt(jnp.where(mine, gm, jnp.zeros_like(gm)), v)
            middle = jnp.sum(probs * grad_probs, axis=1, keepdims=True)
            grad_scores = (probs * (grad_probs - middle)).astype(BF)
            both.append((dot_nn(grad_scores, k), dot_tn(grad_scores, q), dot_tn(low, gm)))
        dproj[:, cut] = (jnp.where(halves, both[0][0], both[1][0]) * factor).astype(BF)
        dproj[:, width + pair * p : width + pair * (p + 1)] = (
            jnp.where(halves, both[0][1], both[1][1]) * factor
        ).astype(BF)
        dproj[:, 2 * width + pair * p : 2 * width + pair * (p + 1)] = jnp.where(
            halves, both[0][2], both[1][2]
        ).astype(BF)
    normed, inverse = normalize(tpad_ref[...].astype(F32))
    entry = (normed * gains_ref[0:1, :] + gains_ref[1:2, :]).astype(BF)
    grads = dproj[...]
    grad_entry = dot_nt(grads, in_ref[...])

    @pl.when(i == 0)
    def _():
        din_ref[...] = jnp.zeros_like(din_ref)
        dscale_ref[...] = jnp.zeros_like(dscale_ref)

    din_ref[...] += dot_tn(entry, grads)
    dscale_ref[0:1, :] += jnp.sum(grad_entry * normed, axis=0, keepdims=True)
    dscale_ref[1:2, :] += jnp.sum(grad_entry, axis=0, keepdims=True)
    grad = gh_ref[...] + norm_back(grad_entry, normed, inverse, gains_ref[0:1, :])
    grad_all[...] = grad
    store_image(grad_ref, i, grad_all)

    @pl.when(i == pl.num_programs(0) - 1)
    def _():
        blocks, rows = 2 * near_ref.shape[0], near_ref.shape[1]
        owner = lane_iota(blocks, width) // rows == row_iota(blocks, width)
        spot = row_iota(width, 128) % rows
        line = jnp.zeros((blocks, 128), F32)
        for s in range(2):
            spread = jnp.where(owner, dscale_ref[s : s + 1, :], 0.0)
            chosen = (lane_iota(width, 128) == spot + s * rows).astype(F32)
            line += lax.dot_general(
                spread, chosen, (((1,), (0,)), ((), ())),
                preferred_element_type=F32, precision=lax.Precision.HIGHEST,
            )
        line_ref[...] = line
        scale_row = row_iota(8, 128) == 6
        for side, out in ((0, near_ref), (1, far_ref)):
            def body(j, carry, side=side, out=out):
                place = place_ref[side * (blocks // 2) + j]
                here = pl.ds(pl.multiple_of(place * rows, rows), rows)
                out[j, :, : 3 * width] = din_ref[here, :].astype(BF)
                out[j, :, 3 * width : 4 * width] = dout_ref[here, :].astype(BF)
                small = small_ref[place] + jnp.where(scale_row, line_ref[pl.ds(place, 1), :], 0.0)
                out[j, :, 4 * width :] = resplit(small)
                return carry

            lax.fori_loop(0, blocks // 2, body, 0)


def attention_back(place, proj, probs, grad_mixed, grad_hidden, tok_pad, in_matrix, gains, grad_out, small):
    padded, width = grad_hidden.shape
    images = padded // PAD
    blocks = small.shape[0]
    rows = width // blocks
    row = lambda lanes: pl.BlockSpec((PAD, lanes), lambda i, m: (i, 0))
    once = lambda a: pl.BlockSpec(a.shape, lambda i, m: (0,) * a.ndim, pipeline_mode=pl.Buffered(1))
    half = (blocks // 2, rows, 4 * width + 128)
    return pl.pallas_call(
        attention_back_kernel,
        grid_spec=pltpu.PrefetchScalarGridSpec(
            num_scalar_prefetch=1,
            grid=(images,),
            in_specs=[
                row(3 * width), pl.BlockSpec((1, HEADS, PAD, PAD), lambda i, m: (i, 0, 0, 0)), row(width), row(width),
                row(width), once(in_matrix), once(gains), once(grad_out), once(small),
            ],
            out_specs=[whole((images * SEQ, width)), whole(half), whole(half)],
            scratch_shapes=[
                pltpu.VMEM((width, 3 * width), F32), pltpu.VMEM((8, width), F32), pltpu.VMEM((blocks, 128), F32),
                pltpu.VMEM((PAD, 3 * width), BF), pltpu.VMEM((PAD, width), F32),
            ],
        ),
        out_shape=[
            jax.ShapeDtypeStruct((images * SEQ, width), F32),
            jax.ShapeDtypeStruct(half, BF),
            jax.ShapeDtypeStruct(half, BF),
        ],
        compiler_params=params(),
        name="attention_back",
    )(place, proj, probs, grad_mixed, grad_hidden, tok_pad, in_matrix, gains, grad_out, small)


X_BIT, CORE_BIT, Y_BIT = 16, 8, 1
Z_BITS = (2, 4, 6)
AXES = ("rep", "ep")


def swap(array, bits):
    devices = lax.axis_size("rep") * lax.axis_size("ep")
    return lax.ppermute(array, AXES, [(d, d ^ bits) for d in range(devices)])


def relative(position):
    c, x, y, z = position >> 4 & 1, position >> 3 & 1, position >> 2 & 1, position & 3
    return x * X_BIT + c * CORE_BIT + z * 2 + y * Y_BIT


def gather_all(block):
    zs = jnp.stack([block] + [swap(block, bits) for bits in Z_BITS])
    others = [swap(zs, bits) for bits in (Y_BIT, X_BIT, X_BIT | Y_BIT)]
    plane = jnp.stack([zs] + others)
    return jnp.stack([plane, swap(plane, CORE_BIT)]).reshape((32,) + block.shape)


def sum_everywhere(values):
    for bits in (CORE_BIT, Y_BIT, X_BIT, 2, 4):
        values = values + swap(values, bits)
    return values


def unsplit(block):
    return block[:8] + block[8:]


def resplit(small):
    twice = jnp.concatenate([small, small], axis=0)
    high = twice.astype(BF).astype(F32)
    return jnp.where(row_iota(16, 128) < 8, high, twice - high).astype(BF)


def block_sum_kernel(parts, terms, *refs):
    ins, outs = refs[:terms], refs[terms:]
    size = ins[0].shape[0] // parts
    lanes = ins[0].shape[2]
    for p in range(parts):
        for j in range(size):
            at = p * size + j
            total = ins[0][at].astype(F32)
            for t in ins[1:]:
                total = total + t[at].astype(F32)
            small = unsplit(total[:, lanes - 128 :])
            outs[p][j, :, : lanes - 128] = total[:, : lanes - 128].astype(BF)
            outs[p][j, :, lanes - 128 :] = resplit(small)


def block_sum(terms, parts):
    size = terms[0].shape[0] // parts
    shape = (size,) + terms[0].shape[1:]
    return pl.pallas_call(
        functools.partial(block_sum_kernel, parts, len(terms)),
        out_shape=[jax.ShapeDtypeStruct(shape, BF)] * parts,
        compiler_params=params(),
        name="block_sum",
    )(*terms)


def last_sum_kernel(*refs):
    ins, (big_ref, small_ref) = refs[:-2], refs[-2:]
    lanes = ins[0].shape[2]
    total = ins[0][0].astype(F32)
    for t in ins[1:]:
        total = total + t[0].astype(F32)
    big_ref[...] = total[:, : lanes - 128]
    small_ref[...] = unsplit(total[:, lanes - 128 :])


def last_sum(terms):
    lanes = terms[0].shape[2]
    return pl.pallas_call(
        last_sum_kernel,
        out_shape=[jax.ShapeDtypeStruct((16, lanes - 128), F32), jax.ShapeDtypeStruct((8, 128), F32)],
        compiler_params=params(),
        name="last_sum",
    )(*terms)


def scatter_dense(near, far):
    parts = block_sum([near, swap(far, CORE_BIT)], 4)
    got = [swap(parts[1], Y_BIT), swap(parts[2], X_BIT), swap(parts[3], X_BIT | Y_BIT)]
    parts = block_sum([parts[0]] + got, 4)
    return last_sum([parts[0]] + [swap(parts[z], Z_BITS[z - 1]) for z in (1, 2, 3)])


def scatter_expert(near, far):
    got = swap(far, CORE_BIT)
    shape = (2, 4, 2) + near.shape[2:]
    near, got = near.reshape(shape), got.reshape(shape)
    add = lambda cut: near[cut] + got[cut]
    every = slice(None)
    a_keep, a_send = add((every, every, 0, 0)), add((every, every, 1, 0))
    b_keep, b_send = add((0, every, every, 1)), add((1, every, every, 1))
    a_got, b_got = swap(a_send, Y_BIT), swap(b_send, X_BIT)
    a_far, b_far = a_keep[1] + a_got[1], b_keep[:, 1] + b_got[:, 1]
    a_got2, b_got2 = swap(a_far, X_BIT), swap(b_far, Y_BIT)
    total = lambda z: jnp.stack(
        [a_keep[0, z] + a_got[0, z] + a_got2[z], b_keep[z, 0] + b_got[z, 0] + b_got2[z]]
    )
    result = total(0).astype(F32)
    for z in (1, 2, 3):
        result = result + swap(total(z), Z_BITS[z - 1]).astype(F32)
    return result


CHUNKS = 2


def replicate_plan(
    tokens, cotangent, expert_ids, priority,
    heads_in, heads_in_first, heads_in_second, heads_out, heads_out_first, heads_out_second,
    router, router_first, router_second, scales, scales_first, scales_second,
    expert_in, expert_in_first, expert_in_second, bias_in, bias_in_first, bias_in_second,
    expert_out, expert_out_first, expert_out_second, bias_out, bias_out_first, bias_out_second,
):
    count, width = tokens.shape
    images = count // SEQ
    experts = router.shape[1]
    rep, ep = lax.axis_size("rep"), lax.axis_size("ep")
    rep_me, ep_me = lax.axis_index("rep"), lax.axis_index("ep")
    me = (rep_me * ep + ep_me).astype(jnp.int32)
    at = jnp.stack([rep_me, ep_me]).astype(jnp.int32)
    capacity = (5 * expert_ids.shape[1] * count + 4 * experts - 1) // (4 * experts)
    listed = -(-capacity // 16) * 16
    hidden_part = FF // rep
    cols = hidden_part // CHUNKS

    enter_low = expert_in[0].astype(BF)
    leave_low = expert_out[0].astype(BF).T
    pieces = [
        jnp.stack([enter_low[:, k * cols : (k + 1) * cols], leave_low[:, k * cols : (k + 1) * cols]])
        for k in range(CHUNKS)
    ]
    wide = [
        lax.all_gather(piece[None], AXES, axis=0, tiled=True).reshape(rep, ep, 2, width, cols) for piece in pieces
    ]

    rows_here = heads_in.shape[0]
    small = jnp.concatenate([router, scales], axis=1)
    small = jnp.pad(small, ((0, 0), (0, 128 - small.shape[1])))
    biases = jnp.concatenate([bias_in.reshape(-1, 128), bias_out.reshape(-1, 128)], axis=0)
    biases = jnp.pad(biases, ((0, rows_here - biases.shape[0]), (0, 0)))
    dense = jnp.concatenate([heads_in, heads_out, small, biases], axis=1).astype(BF)
    order = jnp.array([relative(p) for p in range(rep * ep)], jnp.int32)
    place = jnp.bitwise_xor(order, me)
    in_matrix, out_matrix, router_matrix, gains, small_all = assemble(place, gather_all(dense), experts)
    bias_all = small_all[:, 128:].reshape(rep, ep, rows_here, 128)
    in_rows = hidden_part // 128
    enter_bias = bias_all[:, :, :in_rows].reshape(rep, ep, hidden_part).astype(F32).transpose(1, 0, 2)
    leave_bias = bias_all[:, :, in_rows].astype(F32).transpose(1, 0, 2).reshape(ep, 1, width)

    spread = lambda a, fill: jnp.pad(
        a.reshape(-1, images, SEQ), ((0, 0), (0, 0), (0, PAD - SEQ)), constant_values=fill
    ).reshape(-1, images * PAD)
    ids_rows = spread(expert_ids.T, -1)
    rows = jnp.concatenate([spread(priority, count), ids_rows], axis=0).astype(F32)
    rows = jnp.pad(rows, ((0, 5), (0, 0)))
    lrow, lcol, meta = find_places(rows, rows.T, capacity, experts)

    tok_pad, cot_pad = spread_rows(tokens, cotangent)
    proj, probs, mixed, hidden, routed, gcol, grow = attention(
        tok_pad, in_matrix, out_matrix, router_matrix, gains, ids_rows.T
    )
    lists = gather(meta, routed, cot_pad, lrow, grow, listed)

    bias_cut = lambda k: enter_bias[:, :, k * cols : (k + 1) * cols]
    near, far, grad_bias = [], [], []
    y, d, n, f, b, grad_leave_bias = expert_pass(at, lists, wide[0], bias_cut(0))
    near.append(n), far.append(f), grad_bias.append(b)
    y, d, n, f, b = expert_pass(at, lists, wide[1], bias_cut(1), leave_bias, (y, d))
    near.append(n), far.append(f), grad_bias.append(b)
    expert_sums = [scatter_expert(n, f) for n, f in zip(near, far)]

    output, grad_hidden, grad_mixed, grad_out, grad_router, grad_scale = combine(
        meta, y, d, lcol, gcol, hidden, cot_pad, mixed, out_matrix, router_matrix, gains
    )
    devices = rep * ep
    by_device = lambda a: jnp.pad(
        a.reshape(a.shape[0], devices, rows_here).transpose(1, 0, 2).reshape(devices, 1, -1),
        ((0, 0), (0, 0), (0, 128 - a.shape[0] * rows_here)),
    )
    small_grads = jnp.concatenate(
        [
            jnp.concatenate(grad_bias, axis=2).transpose(1, 0, 2).reshape(devices, in_rows, 128),
            grad_leave_bias.reshape(ep, rep, 128).transpose(1, 0, 2).reshape(devices, 1, 128),
            by_device(grad_router),
            by_device(grad_scale[:5]),
        ],
        axis=1,
    )
    small_grads = jnp.pad(small_grads, ((0, 0), (0, 8 - small_grads.shape[1]), (0, 0)))
    input_grad, near_dense, far_dense = attention_back(
        place, proj, probs, grad_mixed, grad_hidden, tok_pad, in_matrix, gains, grad_out, small_grads
    )
    big, small = scatter_dense(near_dense, far_dense)
    grads_now = (
        big[:, : 3 * width],
        big[:, 3 * width :],
        small[in_rows + 1].reshape(experts, rows_here).T,
        small[in_rows + 2, : 5 * rows_here].reshape(5, rows_here).T,
        jnp.concatenate([total[0] for total in expert_sums], axis=1)[None],
        small[:in_rows].reshape(1, hidden_part),
        jnp.concatenate([total[1] for total in expert_sums], axis=1).T[None],
        small[in_rows][None],
    )
    weights_now = (heads_in, heads_out, router, scales, expert_in, bias_in, expert_out, bias_out)
    firsts = (
        heads_in_first, heads_out_first, router_first, scales_first,
        expert_in_first, bias_in_first, expert_out_first, bias_out_first,
    )
    seconds = (
        heads_in_second, heads_out_second, router_second, scales_second,
        expert_in_second, bias_in_second, expert_out_second, bias_out_second,
    )
    states = [moments(w, g, f, s) for w, g, f, s in zip(weights_now, grads_now, firsts, seconds)]
    weight_terms = jnp.concatenate([squares(w, index == 3) for index, w in enumerate(weights_now)])
    step_terms = jnp.concatenate([squares(state[2], index == 3) for index, state in enumerate(states)])
    totals = sum_everywhere(jnp.stack([weight_terms, step_terms]))
    return (output, input_grad) + finish(totals, weights_now, states, width, experts)


def expert_front(rows, enter_weight, enter_bias):
    pre = jnp.einsum("sjcd,jdf->sjcf", rows, enter_weight, preferred_element_type=jnp.float32)
    return pre + enter_bias.astype(jnp.float32)[None, :, None, :]


def exchange_plan(
    tokens,
    cotangent,
    expert_ids,
    priority,
    heads_in,
    heads_in_first,
    heads_in_second,
    heads_out,
    heads_out_first,
    heads_out_second,
    router,
    router_first,
    router_second,
    scales,
    scales_first,
    scales_second,
    expert_in,
    expert_in_first,
    expert_in_second,
    bias_in,
    bias_in_first,
    bias_in_second,
    expert_out,
    expert_out_first,
    expert_out_second,
    bias_out,
    bias_out_first,
    bias_out_second,
):
    in_matrix, out_matrix, router_matrix, scale_table = (
        lax.all_gather(heads_in.astype(jnp.bfloat16), ("rep", "ep"), axis=0, tiled=True),
        lax.all_gather(heads_out.astype(jnp.bfloat16), ("rep", "ep"), axis=0, tiled=True),
        lax.all_gather(router.astype(jnp.bfloat16), ("rep", "ep"), axis=0, tiled=True),
        lax.all_gather(scales.astype(jnp.bfloat16), ("rep", "ep"), axis=0, tiled=True),
    )
    enter_weight, enter_bias, leave_weight, leave_bias = (
        lax.all_gather(expert_in.astype(jnp.bfloat16), "rep", axis=2, tiled=True),
        lax.all_gather(bias_in.astype(jnp.bfloat16), "rep", axis=1, tiled=True),
        lax.all_gather(expert_out.astype(jnp.bfloat16), "rep", axis=1, tiled=True),
        lax.all_gather(bias_out.astype(jnp.bfloat16), "rep", axis=1, tiled=True),
    )
    gains = scale_table.astype(jnp.float32)
    inputs = tokens.astype(jnp.float32)
    count, width = inputs.shape
    images = count // SEQ
    factor = HEAD ** (-0.5)
    normed_one, inverse_one = normalize(inputs)
    entry = (normed_one * gains[:, 0] + gains[:, 1]).astype(jnp.bfloat16)
    projected = jnp.dot(entry, in_matrix, preferred_element_type=jnp.float32).astype(jnp.bfloat16)
    grid = projected.reshape(images, SEQ, 3, HEADS, HEAD)
    query = grid[:, :, 0]
    keyed = grid[:, :, 1]
    valued = grid[:, :, 2]
    scores = attention_scores(query, keyed, factor)
    peak = jnp.max(scores, axis=-1, keepdims=True)
    log_total = peak + jnp.log(jnp.sum(jnp.exp(scores - peak), axis=-1, keepdims=True))
    weights = jnp.exp(scores - log_total).astype(jnp.bfloat16)
    mixed = jnp.einsum("bhqk,bkhd->bqhd", weights, valued, preferred_element_type=jnp.float32)
    mixed = mixed.reshape(count, width).astype(jnp.bfloat16)
    hidden = inputs + jnp.dot(mixed, out_matrix, preferred_element_type=jnp.float32) + gains[:, 4]
    normed_two, inverse_two = normalize(hidden)
    routed = (normed_two * gains[:, 2] + gains[:, 3]).astype(jnp.bfloat16)
    logits = jnp.dot(routed, router_matrix, preferred_element_type=jnp.float32)
    experts = logits.shape[1]
    top = expert_ids.shape[1]
    choose = (expert_ids[:, :, None] == jnp.arange(experts, dtype=jnp.int32)[None, None, :]).astype(
        jnp.float32
    )
    picked = jnp.sum(choose * logits[:, None, :], axis=2)
    gates = jax.nn.softmax(picked, axis=1)
    places = route_places(expert_ids, priority[0], experts)
    capacity = (5 * top * count + 4 * experts - 1) // (4 * experts)
    groups = lax.axis_size("ep")
    local = experts // groups
    slots = experts * capacity
    slot = jnp.where(places < capacity, expert_ids * capacity + places, slots)
    pair_of_slot = (
        jnp.full((slots,), count * top, jnp.int32)
        .at[slot.reshape(-1)]
        .set(jnp.arange(count * top, dtype=jnp.int32), mode="drop")
    )
    token_of_slot = pair_of_slot // top
    padded_rows = jnp.concatenate([routed, jnp.zeros((1, width), jnp.bfloat16)], axis=0)
    outgoing = padded_rows[token_of_slot].reshape(groups, local, capacity, width)
    arrived = lax.all_to_all(outgoing, "ep", split_axis=0, concat_axis=0, tiled=True)
    pre = expert_front(arrived, enter_weight, enter_bias)
    act, gelu_back = jax.vjp(exact_gelu, pre)
    act_low = act.astype(jnp.bfloat16)
    result = jnp.einsum("sjcf,jfd->sjcd", act_low, leave_weight, preferred_element_type=jnp.float32)
    result = (result + leave_bias.astype(jnp.float32)[None, :, None, :]).astype(jnp.bfloat16)
    returned = lax.all_to_all(result, "ep", split_axis=0, concat_axis=0, tiled=True).reshape(
        slots, width
    )
    padded_back = jnp.concatenate([returned, jnp.zeros((1, width), jnp.bfloat16)], axis=0)
    picked_rows = padded_back[slot].astype(jnp.float32)
    output = hidden + jnp.sum(gates[:, :, None] * picked_rows, axis=1)
    grad_output = cotangent.astype(jnp.float32)
    grad_gates = jnp.sum(picked_rows * grad_output[:, None, :], axis=2)
    gate_list = jnp.concatenate([gates.reshape(-1), jnp.zeros((1,), jnp.float32)])
    padded_grad = jnp.concatenate([grad_output, jnp.zeros((1, width), jnp.float32)], axis=0)
    grad_slots = (padded_grad[token_of_slot] * gate_list[pair_of_slot][:, None]).astype(
        jnp.bfloat16
    )
    grad_arrived = lax.all_to_all(
        grad_slots.reshape(groups, local, capacity, width),
        "ep",
        split_axis=0,
        concat_axis=0,
        tiled=True,
    )
    grad_act = jnp.einsum(
        "sjcd,jfd->sjcf", grad_arrived, leave_weight, preferred_element_type=jnp.float32
    )
    grad_pre = gelu_back(grad_act)[0].astype(jnp.bfloat16)
    grad_leave = jnp.einsum(
        "sjcf,sjcd->jfd", act_low, grad_arrived, preferred_element_type=jnp.float32
    )
    grad_leave_bias = jnp.sum(grad_arrived, axis=(0, 2), dtype=jnp.float32)
    grad_enter = jnp.einsum("sjcd,sjcf->jdf", arrived, grad_pre, preferred_element_type=jnp.float32)
    grad_enter_bias = jnp.sum(grad_pre, axis=(0, 2), dtype=jnp.float32)
    grad_rows = jnp.einsum(
        "sjcf,jdf->sjcd", grad_pre, enter_weight, preferred_element_type=jnp.float32
    ).astype(jnp.bfloat16)
    grad_back = lax.all_to_all(grad_rows, "ep", split_axis=0, concat_axis=0, tiled=True).reshape(
        slots, width
    )
    padded_grad_back = jnp.concatenate([grad_back, jnp.zeros((1, width), jnp.bfloat16)], axis=0)
    grad_routed = jnp.sum(padded_grad_back[slot], axis=1, dtype=jnp.float32)
    grad_picked = gates * (grad_gates - jnp.sum(gates * grad_gates, axis=1, keepdims=True))
    grad_logits = jnp.sum(choose * grad_picked[:, :, None], axis=1).astype(jnp.bfloat16)
    grad_router = jnp.einsum("td,te->de", routed, grad_logits, preferred_element_type=jnp.float32)
    grad_routed = grad_routed + jnp.einsum(
        "te,de->td", grad_logits, router_matrix, preferred_element_type=jnp.float32
    )
    grad_gain_two = jnp.sum(grad_routed * normed_two, axis=0)
    grad_shift_two = jnp.sum(grad_routed, axis=0)
    grad_hidden = grad_output + norm_back(grad_routed, normed_two, inverse_two, gains[:, 2])
    grad_shift_out = jnp.sum(grad_hidden, axis=0)
    grad_mix_out = grad_hidden.astype(jnp.bfloat16)
    grad_out_matrix = jnp.einsum(
        "td,te->de", mixed, grad_mix_out, preferred_element_type=jnp.float32
    )
    grad_mixed = jnp.einsum(
        "te,de->td", grad_mix_out, out_matrix, preferred_element_type=jnp.float32
    )
    grad_mixed = grad_mixed.astype(jnp.bfloat16).reshape(images, SEQ, HEADS, HEAD)
    probs = jnp.exp(attention_scores(query, keyed, factor) - log_total)
    weights_again = probs.astype(jnp.bfloat16)
    grad_valued = jnp.einsum(
        "bhqk,bqhd->bkhd", weights_again, grad_mixed, preferred_element_type=jnp.float32
    )
    grad_probs = jnp.einsum(
        "bqhd,bkhd->bhqk", grad_mixed, valued, preferred_element_type=jnp.float32
    )
    grad_scores = (
        probs * (grad_probs - jnp.sum(probs * grad_probs, axis=-1, keepdims=True))
    ).astype(jnp.bfloat16)
    grad_query = (
        jnp.einsum("bhqk,bkhd->bqhd", grad_scores, keyed, preferred_element_type=jnp.float32)
        * factor
    )
    grad_keyed = (
        jnp.einsum("bhqk,bqhd->bkhd", grad_scores, query, preferred_element_type=jnp.float32)
        * factor
    )
    grad_projected = (
        jnp.stack([grad_query, grad_keyed, grad_valued], axis=2)
        .reshape(count, 3 * width)
        .astype(jnp.bfloat16)
    )
    grad_in_matrix = jnp.einsum(
        "td,te->de", entry, grad_projected, preferred_element_type=jnp.float32
    )
    grad_entry = jnp.einsum(
        "te,de->td", grad_projected, in_matrix, preferred_element_type=jnp.float32
    )
    grad_gain_one = jnp.sum(grad_entry * normed_one, axis=0)
    grad_shift_one = jnp.sum(grad_entry, axis=0)
    input_grad = grad_hidden + norm_back(grad_entry, normed_one, inverse_one, gains[:, 0])
    grad_scales = jnp.stack(
        [grad_gain_one, grad_shift_one, grad_gain_two, grad_shift_two, grad_shift_out], axis=1
    )
    summed_dense = (
        lax.psum_scatter(grad_in_matrix, ("rep", "ep"), scatter_dimension=0, tiled=True),
        lax.psum_scatter(grad_out_matrix, ("rep", "ep"), scatter_dimension=0, tiled=True),
        lax.psum_scatter(grad_router, ("rep", "ep"), scatter_dimension=0, tiled=True),
        lax.psum_scatter(grad_scales, ("rep", "ep"), scatter_dimension=0, tiled=True),
    )
    summed_expert = (
        lax.psum_scatter(
            grad_enter.astype(jnp.bfloat16), "rep", scatter_dimension=2, tiled=True
        ).astype(jnp.float32),
        lax.psum_scatter(
            grad_enter_bias.astype(jnp.bfloat16), "rep", scatter_dimension=1, tiled=True
        ).astype(jnp.float32),
        lax.psum_scatter(
            grad_leave.astype(jnp.bfloat16), "rep", scatter_dimension=1, tiled=True
        ).astype(jnp.float32),
        lax.psum_scatter(
            grad_leave_bias.astype(jnp.bfloat16), "rep", scatter_dimension=1, tiled=True
        ).astype(jnp.float32),
    )
    weights_now = (heads_in, heads_out, router, scales, expert_in, bias_in, expert_out, bias_out)
    grads_now = tuple(summed_dense) + tuple(summed_expert)
    firsts = (
        heads_in_first,
        heads_out_first,
        router_first,
        scales_first,
        expert_in_first,
        bias_in_first,
        expert_out_first,
        bias_out_first,
    )
    seconds = (
        heads_in_second,
        heads_out_second,
        router_second,
        scales_second,
        expert_in_second,
        bias_in_second,
        expert_out_second,
        bias_out_second,
    )
    states = [moments(w, g, f, s) for w, g, f, s in zip(weights_now, grads_now, firsts, seconds)]
    weight_terms = jnp.concatenate([squares(w, index == 3) for index, w in enumerate(weights_now)])
    step_terms = jnp.concatenate(
        [squares(state[2], index == 3) for index, state in enumerate(states)]
    )
    totals = lax.psum(jnp.stack([weight_terms, step_terms]), ("rep", "ep"))
    return (output, input_grad) + finish(totals, weights_now, states, width, experts)


def solution(mesh):
    in_specs = (
        P(("rep", "ep"), None),
        P(("rep", "ep"), None),
        P(("rep", "ep"), None),
        P(("rep", "ep"), None),
        P(("rep", "ep"), None),
        P(("rep", "ep"), None),
        P(("rep", "ep"), None),
        P(("rep", "ep"), None),
        P(("rep", "ep"), None),
        P(("rep", "ep"), None),
        P(("rep", "ep"), None),
        P(("rep", "ep"), None),
        P(("rep", "ep"), None),
        P(("rep", "ep"), None),
        P(("rep", "ep"), None),
        P(("rep", "ep"), None),
        P("ep", None, "rep"),
        P("ep", None, "rep"),
        P("ep", None, "rep"),
        P("ep", "rep"),
        P("ep", "rep"),
        P("ep", "rep"),
        P("ep", "rep", None),
        P("ep", "rep", None),
        P("ep", "rep", None),
        P("ep", "rep"),
        P("ep", "rep"),
        P("ep", "rep"),
    )
    out_specs = (
        P(("rep", "ep"), None),
        P(("rep", "ep"), None),
        P(("rep", "ep"), None),
        P(("rep", "ep"), None),
        P(("rep", "ep"), None),
        P(("rep", "ep"), None),
        P(("rep", "ep"), None),
        P(("rep", "ep"), None),
        P(("rep", "ep"), None),
        P(("rep", "ep"), None),
        P(("rep", "ep"), None),
        P(("rep", "ep"), None),
        P(("rep", "ep"), None),
        P(("rep", "ep"), None),
        P("ep", None, "rep"),
        P("ep", None, "rep"),
        P("ep", None, "rep"),
        P("ep", "rep"),
        P("ep", "rep"),
        P("ep", "rep"),
        P("ep", "rep", None),
        P("ep", "rep", None),
        P("ep", "rep", None),
        P("ep", "rep"),
        P("ep", "rep"),
        P("ep", "rep"),
        P(),
    )
    replicated = mesh.shape["rep"] == 4 and mesh.shape["ep"] == 8
    return jax.shard_map(
        replicate_plan if replicated else exchange_plan,
        mesh=mesh,
        in_specs=in_specs,
        out_specs=out_specs,
        check_vma=False,
    )
```

```python
import functools

import jax
import jax.numpy as jnp
from jax import lax
from jax.experimental import pallas as pl
from jax.experimental.pallas import tpu as pltpu
from jax.sharding import PartitionSpec as P

HEADS = 8
HEAD = 64
FF = 2048
SEQ = 197
STEP = 5


BETA = 0.5
RATE = 0.3
DECAY = 0.01
EPSILON = 1e-06


def normalize(rows):
    centred = rows - jnp.mean(rows, axis=-1, keepdims=True)
    inverse = lax.rsqrt(jnp.mean(centred * centred, axis=-1, keepdims=True) + 1e-06)
    return (centred * inverse, inverse)


def norm_back(grad_rows, normed, inverse, gain):
    scaled = grad_rows * gain
    return inverse * (
        scaled
        - jnp.mean(scaled, axis=-1, keepdims=True)
        - normed * jnp.mean(scaled * normed, axis=-1, keepdims=True)
    )


def exact_gelu(values):
    return jax.nn.gelu(values, approximate=False)


def route_places(block_ids, ranking, experts):
    count = block_ids.shape[0]
    keys = jnp.arange(block_ids.shape[1], dtype=jnp.int32)[None, :] * count + ranking[:, None]
    ordered = (
        jnp.zeros((block_ids.size,), jnp.int32).at[keys.reshape(-1)].set(block_ids.reshape(-1))
    )
    hits = (ordered[:, None] == jnp.arange(experts, dtype=jnp.int32)[None, :]).astype(jnp.int32)
    before = jnp.cumsum(hits, axis=0) - hits
    place = jnp.sum(before * hits, axis=1)
    return place[keys]


def attention_scores(query, keyed, factor):
    return jnp.einsum("bqhd,bkhd->bhqk", query, keyed, preferred_element_type=jnp.float32) * factor


def moments(weight, grad, first, second):
    first_new = BETA * first + (1.0 - BETA) * grad
    second_new = BETA * second + (1.0 - BETA) * grad * grad
    step = (
        first_new / (1.0 - BETA**STEP) / (jnp.sqrt(second_new / (1.0 - BETA**STEP)) + EPSILON)
        + DECAY * weight
    )
    return (first_new, second_new, step)


def squares(array, per_column):
    if per_column:
        return jnp.sum(array * array, axis=0)
    return jnp.sum(array * array)[None]


def finish(totals, weights_now, states, width, experts):
    counts = jnp.array(
        [3 * width * width, width * width, width * experts]
        + [width] * 5
        + [experts * width * FF, experts * FF, experts * FF * width, experts * width],
        jnp.float32,
    )
    weight_rms = jnp.sqrt(totals[0] / counts)
    step_rms = jnp.sqrt(totals[1] / counts)
    trust = weight_rms / step_rms
    bounds = [(0, 1), (1, 2), (2, 3), (3, 8), (8, 9), (9, 10), (10, 11), (11, 12)]
    results = []
    for weight, state, bound in zip(weights_now, states, bounds):
        results.extend([state[0], state[1], weight - RATE * trust[bound[0] : bound[1]] * state[2]])
    results.append(jnp.stack([weight_rms, step_rms, trust]))
    return tuple(results)


PAD = 208
WIN = 96
VMEM = 60 * 1024 * 1024
BF = jnp.bfloat16
F32 = jnp.float32


def dot_nn(a, b):
    return lax.dot_general(a, b, (((1,), (0,)), ((), ())), preferred_element_type=F32)


def dot_nt(a, b):
    return lax.dot_general(a, b, (((1,), (1,)), ((), ())), preferred_element_type=F32)


def dot_tn(a, b):
    return lax.dot_general(a, b, (((0,), (0,)), ((), ())), preferred_element_type=F32)


def lane_iota(rows, lanes):
    return lax.broadcasted_iota(jnp.int32, (rows, lanes), 1)


def row_iota(rows, lanes):
    return lax.broadcasted_iota(jnp.int32, (rows, lanes), 0)


def whole(shape):
    return pl.BlockSpec(shape, lambda *_: (0,) * len(shape))


def cost(micros):
    return pl.CostEstimate(flops=int(micros * 1e9), bytes_accessed=int(micros * 1e5), transcendentals=0)


def params(**kw):
    return pltpu.CompilerParams(vmem_limit_bytes=VMEM, **kw)


def behind(kernel, inputs, after):
    def body(*refs):
        return kernel(*refs[:inputs], *refs[inputs + len(after) :])

    return body


def unread(after):
    return [pl.BlockSpec(memory_space=pl.ANY)] * len(after)


def assemble_kernel(place_ref, near_ref, far_ref, in_ref, out_ref, router_ref, gains_ref, small_ref):
    copies, rows = near_ref.shape[0], near_ref.shape[1]
    width = out_ref.shape[1]
    for side, got_ref in enumerate((near_ref, far_ref)):
        for j in range(copies):
            place = pl.multiple_of(place_ref[side * copies + j] * rows, rows)
            in_ref[pl.ds(place, rows), :] = got_ref[j, :, : 3 * width]
            out_ref[pl.ds(place, rows), :] = got_ref[j, :, 3 * width : 4 * width]
            small_ref[pl.ds(place, rows), :] = got_ref[j, :, 4 * width :]
    turned = small_ref[:, :128].astype(F32).T
    experts = router_ref.shape[0]
    router_ref[...] = turned[:experts].astype(BF)
    gains_ref[...] = turned[experts : experts + 8]


def assemble(place, near, far, experts):
    copies, rows, lanes = near.shape
    width = 2 * copies * rows
    return pl.pallas_call(
        assemble_kernel,
        grid_spec=pltpu.PrefetchScalarGridSpec(
            num_scalar_prefetch=1,
            grid=(1,),
            in_specs=[whole(near.shape)] * 2,
            out_specs=[
                whole((width, 3 * width)),
                whole((width, width)),
                whole((experts, width)),
                whole((8, width)),
                whole((width, lanes - 4 * width)),
            ],
        ),
        out_shape=[
            jax.ShapeDtypeStruct((width, 3 * width), BF),
            jax.ShapeDtypeStruct((width, width), BF),
            jax.ShapeDtypeStruct((experts, width), BF),
            jax.ShapeDtypeStruct((8, width), F32),
            jax.ShapeDtypeStruct((width, lanes - 4 * width), BF),
        ],
        compiler_params=params(),
        cost_estimate=cost(5),
        name="assemble",
    )(place, near, far)


def places_kernel(capacity, rows_ref, cols_ref, lrow_ref, lcol_ref, meta_ref):
    count = cols_ref.shape[0]
    images = count // PAD
    experts = lcol_ref.shape[1]
    expert = lane_iota(count, experts).astype(F32)
    first = (cols_ref[:, 1:2] == expert).astype(F32)
    second = (cols_ref[:, 2:3] == expert).astype(F32)
    first_low = first.astype(BF)
    second_low = second.astype(BF)
    total_first = jnp.sum(first, axis=0, keepdims=True)
    lower = (lane_iota(PAD, PAD) < row_iota(PAD, PAD)).astype(F32).astype(BF)
    ranking = rows_ref[0:1, :]
    begin = jnp.zeros((1, experts), F32)
    for i in range(images):
        span = slice(i * PAD, (i + 1) * PAD)
        ahead = (ranking < cols_ref[span, 0:1]).astype(F32).astype(BF)
        rank_first = dot_nn(ahead, first_low)
        rank_second = dot_nn(ahead, second_low) + total_first
        place = first[span] * rank_first + second[span] * rank_second
        kept = (first[span] + second[span]) * (place < capacity).astype(F32)
        local = dot_nn(lower, kept.astype(BF))
        local = jnp.where(kept > 0.0, local, -1.0)
        lcol_ref[span, :] = local
        lrow_ref[i] = local.T
        here = jnp.sum(kept, axis=0, keepdims=True)
        meta_ref[i : i + 1, :] = begin.astype(jnp.int32)
        meta_ref[images + i : images + i + 1, :] = here.astype(jnp.int32)
        begin = begin + here


def find_places(rows, cols, capacity, experts):
    count = cols.shape[0]
    images = count // PAD
    return pl.pallas_call(
        functools.partial(places_kernel, capacity),
        out_shape=[
            jax.ShapeDtypeStruct((images, experts, PAD), F32),
            jax.ShapeDtypeStruct((count, experts), F32),
            jax.ShapeDtypeStruct((2 * images, experts), jnp.int32),
        ],
        compiler_params=params(),
        cost_estimate=cost(9),
        name="places",
    )(rows, cols)


def spread_kernel(tok_ref, cot_ref, tpad_ref, cpad_ref):
    count, width = tok_ref.shape
    for source, target in ((tok_ref, tpad_ref), (cot_ref, cpad_ref)):
        for i in range(count // SEQ):
            rows = source[SEQ * i : SEQ * (i + 1), :].astype(F32)
            rows = jnp.concatenate([rows, jnp.zeros((PAD - SEQ, width), F32)], axis=0)
            target[PAD * i : PAD * (i + 1), :] = rows.astype(BF)


def spread_rows(tokens, cotangent):
    count, width = tokens.shape
    shape = jax.ShapeDtypeStruct((count // SEQ * PAD, width), BF)
    return pl.pallas_call(
        spread_kernel, out_shape=[shape, shape], compiler_params=params(), cost_estimate=cost(5), name="spread_rows"
    )(tokens, cotangent)


def store_image(target, i, values):
    for image in range(target.shape[0] // SEQ):

        @pl.when(i == image)
        def _(image=image):
            target[SEQ * image : SEQ * (image + 1), :] = values[0:SEQ, :]


def attention_kernel(
    tok_ref, in_ref, out_ref, router_ref, gains_ref, ids_ref,
    proj_ref, prob_ref, mixed_ref, hidden_ref, routed_ref, gcol_ref, grow_ref, mixed_all,
):
    width = tok_ref.shape[1]
    x = tok_ref[...].astype(F32)
    normed, _ = normalize(x)
    entry = (normed * gains_ref[0:1, :] + gains_ref[1:2, :]).astype(BF)
    proj_ref[...] = dot_nn(entry, in_ref[...]).astype(BF)
    pair = 2 * HEAD
    halves = lane_iota(PAD, pair) < HEAD
    key_there = lane_iota(PAD, PAD) < SEQ
    for p in range(HEADS // 2):
        q = proj_ref[:, pair * p : pair * (p + 1)] * jnp.asarray(HEAD ** -0.5, BF)
        k = proj_ref[:, width + pair * p : width + pair * (p + 1)]
        v = proj_ref[:, 2 * width + pair * p : 2 * width + pair * (p + 1)]
        sides = []
        for s in range(2):
            mine = halves if s == 0 else jnp.logical_not(halves)
            scores = dot_nt(jnp.where(mine, q, jnp.zeros_like(q)), k)
            scores = jnp.where(key_there, scores, -1e30)
            peak = jnp.max(scores, axis=1, keepdims=True)
            raised = jnp.exp(scores - peak)
            total = jnp.sum(raised, axis=1, keepdims=True)
            weights = (raised * (1.0 / total)).astype(BF)
            prob_ref[0, 2 * p + s] = weights
            sides.append(dot_nn(weights, v))
        mixed_all[:, pair * p : pair * (p + 1)] = jnp.where(halves, sides[0], sides[1]).astype(BF)
    mixed = mixed_all[...]
    mixed_ref[...] = mixed
    hidden = x + dot_nn(mixed, out_ref[...]) + gains_ref[4:5, :]
    hidden_ref[...] = hidden
    normed_two, _ = normalize(hidden)
    routed = (normed_two * gains_ref[2:3, :] + gains_ref[3:4, :]).astype(BF)
    routed_ref[...] = routed
    logits = dot_nt(routed, router_ref[...])
    experts = logits.shape[1]
    expert = lane_iota(PAD, experts)
    chosen = jnp.logical_or(ids_ref[:, 0:1] == expert, ids_ref[:, 1:2] == expert)
    top = jnp.max(jnp.where(chosen, logits, -1e30), axis=1, keepdims=True)
    raised = jnp.where(chosen, jnp.exp(jnp.where(chosen, logits - top, 0.0)), 0.0)
    total = jnp.sum(raised, axis=1, keepdims=True)
    gates = raised / jnp.where(total > 0.0, total, 1.0)
    gcol_ref[...] = gates
    grow_ref[0] = gates.T


def attention(tok_pad, in_matrix, out_matrix, router, gains, ids_col, after=()):
    padded, width = tok_pad.shape
    images = padded // PAD
    experts = router.shape[0]
    row = lambda lanes: pl.BlockSpec((PAD, lanes), lambda i: (i, 0))
    once = lambda a: pl.BlockSpec(a.shape, lambda i: (0, 0), pipeline_mode=pl.Buffered(1))
    return pl.pallas_call(
        behind(attention_kernel, 6, after),
        grid=(images,),
        in_specs=[row(width), once(in_matrix), once(out_matrix), once(router), once(gains), row(2)] + unread(after),
        out_specs=[
            row(3 * width),
            pl.BlockSpec((1, HEADS, PAD, PAD), lambda i: (i, 0, 0, 0)),
            row(width), row(width), row(width), row(experts),
            pl.BlockSpec((1, experts, PAD), lambda i: (i, 0, 0)),
        ],
        out_shape=[
            jax.ShapeDtypeStruct((padded, 3 * width), BF),
            jax.ShapeDtypeStruct((images, HEADS, PAD, PAD), BF),
            jax.ShapeDtypeStruct((padded, width), BF),
            jax.ShapeDtypeStruct((padded, width), F32),
            jax.ShapeDtypeStruct((padded, width), BF),
            jax.ShapeDtypeStruct((padded, experts), F32),
            jax.ShapeDtypeStruct((images, experts, PAD), F32),
        ],
        scratch_shapes=[pltpu.VMEM((PAD, width), BF)],
        compiler_params=params(),
        cost_estimate=cost(28),
        name="attention",
    )(tok_pad, in_matrix, out_matrix, router, gains, ids_col, *after)


def window_count():
    return -(-(15 + SEQ) // WIN)


def gather_kernel(meta_ref, routed_ref, cot_ref, lrow_ref, grow_ref, r_ref, g_ref, rt_ref, gt_ref, r_all, g_all):
    e = pl.program_id(0)
    images = lrow_ref.shape[0]
    listed = r_ref.shape[1]
    r_all[...] = jnp.zeros_like(r_all)
    g_all[...] = jnp.zeros_like(g_all)
    row = row_iota(WIN, PAD).astype(F32)
    for i in range(images):
        start, here = meta_ref[i, e], meta_ref[images + i, e]
        base = lax.shift_left(lax.shift_right_logical(start, 4), 4)
        shift = (start - base).astype(F32)
        local = lrow_ref[i, pl.ds(e, 1), :]
        gate = grow_ref[i, pl.ds(e, 1), :]
        for q in range(window_count()):
            @pl.when(jnp.logical_and(here > 0, base + q * WIN < start + here))
            def _(i=i, q=q, base=base, shift=shift, local=local, gate=gate):
                pick = jnp.logical_and(local >= 0.0, local + (shift - q * WIN) == row)
                low = pick.astype(F32).astype(BF)
                slot_gate = jnp.sum(jnp.where(pick, gate, 0.0), axis=1, keepdims=True)
                where = pl.ds(pl.multiple_of(base + q * WIN, 16), WIN)
                r_all[where, :] += dot_nn(low, routed_ref[i * PAD : (i + 1) * PAD, :])
                g_all[where, :] += slot_gate * dot_nn(low, cot_ref[i * PAD : (i + 1) * PAD, :])
    r_ref[0] = r_all[0:listed, :].astype(BF)
    g_ref[0] = g_all[0:listed, :].astype(BF)
    rt_ref[0] = r_all[0:listed, :].T.astype(BF)
    gt_ref[0] = g_all[0:listed, :].astype(BF).astype(F32).T.astype(BF)


def gather(meta, routed, cot_pad, lrow, grow, listed, after=()):
    width = routed.shape[1]
    experts = lrow.shape[1]
    once = lambda a: pl.BlockSpec(a.shape, lambda e, m: (0,) * a.ndim, pipeline_mode=pl.Buffered(1))
    block = pl.BlockSpec((1, listed, width), lambda e, m: (e, 0, 0))
    turned = pl.BlockSpec((1, width, listed), lambda e, m: (e, 0, 0))
    return pl.pallas_call(
        behind(gather_kernel, 5, after),
        grid_spec=pltpu.PrefetchScalarGridSpec(
            num_scalar_prefetch=1,
            grid=(experts,),
            in_specs=[once(routed), once(cot_pad), once(lrow), once(grow)] + unread(after),
            out_specs=[block, block, turned, turned],
            scratch_shapes=[pltpu.VMEM((listed + WIN, width), F32)] * 2,
        ),
        out_shape=[jax.ShapeDtypeStruct((experts, listed, width), BF)] * 2
        + [jax.ShapeDtypeStruct((experts, width, listed), BF)] * 2,
        compiler_params=params(),
        cost_estimate=cost(25),
        name="gather",
    )(meta, routed, cot_pad, lrow, grow, *after)


def gelu_both(pre):
    bell = jnp.exp(-0.5 * (pre * pre))
    t = pl.reciprocal(1.0 + (0.3275911 * 2.0**-0.5) * jnp.abs(pre))
    tail = t * (0.127414796 + t * (-0.142248368 + t * (0.7107068705 + t * (-0.7265760135 + t * 0.5307027145))))
    tail = tail * bell
    phi = jnp.where(pre < 0.0, tail, 1.0 - tail)
    return pre * phi, phi + pre * bell * 0.3989422804014327


def expert_kernel(first, last, half, at_ref, *refs):
    rep = 4
    if first:
        (r_ref, g_ref, rt_ref, gt_ref, w_ref, b_ref), refs = refs[:6], refs[6 + 2 * (half > 0) :]
        y_ref, d_ref, near_ref, far_ref, db_ref, obg_ref, y_all, d_all = refs
    else:
        (r_ref, g_ref, rt_ref, gt_ref), w_refs, refs = refs[:4], refs[4:12], refs[12:]
        (b_ref, ob_ref, y_in, d_in), refs = refs[:4], refs[4 + 2 * (half > 0) :]
        y_ref, d_ref, near_ref, far_ref, db_ref, y_all, d_all = refs
    listed = r_ref.shape[1]
    step = pl.program_id(0)
    count = at_ref[2 + lax.bitwise_xor(expert_rank(step, half), at_ref[1])]

    def run(n):
        rows_t, grads_t = rt_ref[0, :, :n], gt_ref[0, :, :n]

        def weights(r):
            place = lax.bitwise_xor(at_ref[0], r)
            if first:
                return place, w_ref[place, 0, 0], w_ref[place, 0, 1]
            return place, w_refs[r][0], w_refs[rep + r][0]

        def enter_part(r):
            place, enter, leave = weights(r)
            pre = dot_nn(r_ref[0, :n, :], enter) + b_ref[0, pl.ds(place, 1), :]
            return pre, dot_nn(g_ref[0, :n, :], leave)

        def middle_part(pre, grad_act):
            act, slope = gelu_both(pre)
            return act.astype(BF), (grad_act * slope).astype(BF)

        def leave_part(r, act, grad_pre):
            place, enter, leave = weights(r)
            out = far_ref if r % 2 else near_ref
            out[r // 2, 0, 0] = dot_nn(rows_t, grad_pre).astype(BF)
            out[r // 2, 0, 1] = dot_nn(grads_t, act).astype(BF)
            db_ref[0, pl.ds(place, 1), :] = jnp.sum(grad_pre.astype(F32), axis=0, keepdims=True)
            y_part = dot_nt(act, leave)
            d_part = dot_nt(grad_pre, enter)
            if r == 0:
                y_all[:n, :] = y_part if first else y_part + y_in[0, :n, :]
                d_all[:n, :] = d_part if first else d_part + d_in[0, :n, :]
            else:
                y_all[:n, :] += y_part
                d_all[:n, :] += d_part

        held = enter_part(0)
        ready = None
        for r in range(rep):
            now = middle_part(*held)
            if r + 1 < rep:
                held = enter_part(r + 1)
            if ready is not None:
                leave_part(r - 1, *ready)
            ready = now
        leave_part(rep - 1, *ready)
        if last:
            y_ref[0, :n, :] = (y_all[:n, :] + ob_ref[0]).astype(BF)
            d_ref[0, :n, :] = d_all[:n, :].astype(BF)
        else:
            y_ref[0, :n, :] = y_all[:n, :]
            d_ref[0, :n, :] = d_all[:n, :]
        if n < listed:
            y_ref[0, n:, :] = jnp.zeros((listed - n, y_ref.shape[2]), y_ref.dtype)
            d_ref[0, n:, :] = jnp.zeros((listed - n, y_ref.shape[2]), y_ref.dtype)

    if first:
        obg_ref[0] = jnp.sum(g_ref[0].astype(F32), axis=0, keepdims=True)
    short = listed * 3 // 4 // 16 * 16
    pl.when(count <= short)(lambda: run(short))
    pl.when(count > short)(lambda: run(listed))


def expert_rank(step, half):
    return lax.shift_left(lax.bitwise_and(step, 3), 1) + lax.shift_right_logical(step, 2) + half


def expert_pass(at, lists, weights, bias, out_bias=None, carried=None, half=0, done=None, after=()):
    first = carried is None
    rows = lists[0]
    experts, listed, width = rows.shape
    rep, cols = bias.shape[1], bias.shape[2]
    steps = experts // 2
    here = lambda e, at: lax.bitwise_xor(expert_rank(e, half), at[1])
    block = pl.BlockSpec((1, listed, width), lambda e, at: (here(e, at), 0, 0))
    turned = pl.BlockSpec((1, width, listed), lambda e, at: (here(e, at), 0, 0))
    out_w = pl.BlockSpec((rep // 2, 1, 2, width, cols), lambda e, at: (0, e, 0, 0, 0))
    in_specs = [
        block, block, turned, turned,
        *(
            [pl.BlockSpec((rep, 1, 2, width, cols), lambda e, at: (0, here(e, at), 0, 0, 0))]
            if first
            else [pl.BlockSpec((1, width, cols), lambda e, at: (e, 0, 0))] * len(weights)
        ),
        pl.BlockSpec((1, rep, cols), lambda e, at: (here(e, at), 0, 0)),
    ]
    args = list(lists) + ([weights] if first else list(weights)) + [bias]
    kind = F32 if first else BF
    out_specs = [block, block, out_w, out_w, pl.BlockSpec((1, rep, cols), lambda e, at: (here(e, at), 0, 0))]
    out_shape = [
        jax.ShapeDtypeStruct(rows.shape, kind),
        jax.ShapeDtypeStruct(rows.shape, kind),
        jax.ShapeDtypeStruct((rep // 2, steps, 2, width, cols), BF),
        jax.ShapeDtypeStruct((rep // 2, steps, 2, width, cols), BF),
        jax.ShapeDtypeStruct((experts, rep, cols), F32),
    ]
    aliases = {}
    if first:
        out_specs.append(pl.BlockSpec((1, 1, width), lambda e, at: (here(e, at), 0, 0)))
        out_shape.append(jax.ShapeDtypeStruct((experts, 1, width), F32))
    else:
        in_specs += [pl.BlockSpec((1, 1, width), lambda e, at: (here(e, at), 0, 0)), block, block]
        args += [out_bias, *carried]
    if half:
        aliases = {len(args) + 1: 0, len(args) + 2: 1}
        in_specs += unread(done)
        args += list(done)
    kernel = behind(functools.partial(expert_kernel, first, not first, half), len(args) + 1, after)
    return pl.pallas_call(
        kernel,
        grid_spec=pltpu.PrefetchScalarGridSpec(
            num_scalar_prefetch=1,
            grid=(steps,),
            in_specs=in_specs + unread(after),
            out_specs=out_specs,
            scratch_shapes=[pltpu.VMEM((listed, width), F32)] * 2,
        ),
        out_shape=out_shape,
        input_output_aliases=aliases,
        compiler_params=params(),
        cost_estimate=cost(6 * steps),
        name=f"experts_{0 if first else 1}{half}",
    )(at, *args, *after)


def combine_kernel(
    meta_ref, y_ref, d_ref, lcol_ref, gcol_ref, hidden_ref, cot_ref, mixed_ref, out_w_ref, router_ref, gains_ref,
    out_ref, gh_ref, gm_ref, dout_ref, drouter_ref, dscale_ref, y_acc, g_acc, d_acc,
):
    i = pl.program_id(0)
    images = pl.num_programs(0)
    experts, listed, width = y_ref.shape
    gates = gcol_ref[...]
    local = lcol_ref[...]
    go = cot_ref[...].astype(F32)
    lane = lane_iota(PAD, WIN).astype(F32)
    expert = lane_iota(PAD, experts)

    def window(e, q, base, shift):
        at = jnp.minimum(base + q * WIN, listed - WIN)
        moved = (at - base).astype(F32)
        spot = local[:, e : e + 1] + shift
        pick = jnp.logical_and(spot == lane + moved, local[:, e : e + 1] >= 0.0)
        pick = jnp.logical_and(pick, spot >= q * WIN)
        low = pick.astype(F32).astype(BF)
        where = pl.ds(pl.multiple_of(at, 16), WIN)
        return dot_nn(low, y_ref[e, where, :]), dot_nn(low, d_ref[e, where, :])

    y_sum = jnp.zeros((PAD, width), F32)
    d_sum = jnp.zeros((PAD, width), F32)
    grad_gates = jnp.zeros((PAD, experts), F32)
    bases = []
    for e in range(experts):
        start = meta_ref[i, e]
        base = lax.shift_left(lax.shift_right_logical(start, 4), 4)
        bases.append((start, base))
        y_tok, d_tok = window(e, 0, base, (start - base).astype(F32))
        y_sum += gates[:, e : e + 1] * y_tok
        d_sum += d_tok
        gg = jnp.sum(go * y_tok, axis=1, keepdims=True)
        grad_gates += jnp.where(expert == e, gg, 0.0)
    y_acc[...] = y_sum
    d_acc[...] = d_sum
    g_acc[...] = grad_gates
    for e in range(experts):
        start, base = bases[e]
        here = meta_ref[images + i, e]
        for q in range(1, window_count()):
            @pl.when(base + q * WIN < start + here)
            def _(e=e, q=q, base=base, start=start):
                y_tok, d_tok = window(e, q, base, (start - base).astype(F32))
                y_acc[...] += gates[:, e : e + 1] * y_tok
                d_acc[...] += d_tok
                gg = jnp.sum(go * y_tok, axis=1, keepdims=True)
                g_acc[...] += jnp.where(expert == e, gg, 0.0)
    hidden = hidden_ref[...]
    y_acc[...] += hidden
    store_image(out_ref, i, y_acc)
    grad_gates = g_acc[...]
    pick = gates * (grad_gates - jnp.sum(gates * grad_gates, axis=1, keepdims=True))
    logit_low = pick.astype(BF)
    grad_routed = d_acc[...] + dot_nn(logit_low, router_ref[...])
    normed, inverse = normalize(hidden)
    routed = (normed * gains_ref[2:3, :] + gains_ref[3:4, :]).astype(BF)
    grad_hidden = go + norm_back(grad_routed, normed, inverse, gains_ref[2:3, :])
    gh_ref[...] = grad_hidden
    grad_mix = grad_hidden.astype(BF)
    gm_ref[...] = dot_nt(grad_mix, out_w_ref[...]).astype(BF)

    @pl.when(i == 0)
    def _():
        dout_ref[...] = jnp.zeros_like(dout_ref)
        drouter_ref[...] = jnp.zeros_like(drouter_ref)
        dscale_ref[...] = jnp.zeros_like(dscale_ref)

    dout_ref[...] += dot_tn(mixed_ref[...], grad_mix)
    drouter_ref[...] += dot_tn(logit_low, routed)
    dscale_ref[2:3, :] += jnp.sum(grad_routed * normed, axis=0, keepdims=True)
    dscale_ref[3:4, :] += jnp.sum(grad_routed, axis=0, keepdims=True)
    dscale_ref[4:5, :] += jnp.sum(grad_hidden, axis=0, keepdims=True)


def combine(meta, y, d, lcol, gcol, hidden, cot_pad, mixed, out_matrix, router, gains, after=()):
    padded, width = hidden.shape
    images = padded // PAD
    experts = y.shape[0]
    row = lambda lanes: pl.BlockSpec((PAD, lanes), lambda i, m: (i, 0))
    once = lambda a: pl.BlockSpec(a.shape, lambda i, m: (0,) * a.ndim, pipeline_mode=pl.Buffered(1))
    return pl.pallas_call(
        behind(combine_kernel, 11, after),
        grid_spec=pltpu.PrefetchScalarGridSpec(
            num_scalar_prefetch=1,
            grid=(images,),
            in_specs=[
                once(y), once(d), row(experts), row(experts), row(width), row(width), row(width),
                once(out_matrix), once(router), once(gains), *unread(after),
            ],
            out_specs=[
                whole((images * SEQ, width)), row(width), row(width), whole((width, width)), whole((experts, width)),
                whole((8, width)),
            ],
            scratch_shapes=[
                pltpu.VMEM((PAD, width), F32), pltpu.VMEM((PAD, experts), F32), pltpu.VMEM((PAD, width), F32),
            ],
        ),
        out_shape=[
            jax.ShapeDtypeStruct((images * SEQ, width), F32),
            jax.ShapeDtypeStruct((padded, width), F32),
            jax.ShapeDtypeStruct((padded, width), BF),
            jax.ShapeDtypeStruct((width, width), F32),
            jax.ShapeDtypeStruct((experts, width), F32),
            jax.ShapeDtypeStruct((8, width), F32),
        ],
        compiler_params=params(),
        cost_estimate=cost(40),
        name="combine",
    )(meta, y, d, lcol, gcol, hidden, cot_pad, mixed, out_matrix, router, gains, *after)


def attention_back_kernel(
    place_ref, proj_ref, prob_ref, gm_ref, gh_ref, tpad_ref, in_ref, gains_ref, dout_ref, small_ref,
    grad_ref, near_ref, far_ref, din_ref, dscale_ref, line_ref, dproj, grad_all,
):
    i = pl.program_id(0)
    width = gm_ref.shape[1]
    pair = 2 * HEAD
    halves = lane_iota(PAD, pair) < HEAD
    factor = HEAD ** -0.5
    for p in range(HEADS // 2):
        cut = slice(pair * p, pair * (p + 1))
        q = proj_ref[:, cut]
        k = proj_ref[:, width + pair * p : width + pair * (p + 1)]
        v = proj_ref[:, 2 * width + pair * p : 2 * width + pair * (p + 1)]
        gm = gm_ref[:, cut]
        both = []
        for s in range(2):
            mine = halves if s == 0 else jnp.logical_not(halves)
            low = prob_ref[0, 2 * p + s]
            probs = low.astype(F32)
            grad_probs = dot_nt(jnp.where(mine, gm, jnp.zeros_like(gm)), v)
            middle = jnp.sum(probs * grad_probs, axis=1, keepdims=True)
            grad_scores = (probs * (grad_probs - middle)).astype(BF)
            both.append((dot_nn(grad_scores, k), dot_tn(grad_scores, q), dot_tn(low, gm)))
        dproj[:, cut] = (jnp.where(halves, both[0][0], both[1][0]) * factor).astype(BF)
        dproj[:, width + pair * p : width + pair * (p + 1)] = (
            jnp.where(halves, both[0][1], both[1][1]) * factor
        ).astype(BF)
        dproj[:, 2 * width + pair * p : 2 * width + pair * (p + 1)] = jnp.where(
            halves, both[0][2], both[1][2]
        ).astype(BF)
    normed, inverse = normalize(tpad_ref[...].astype(F32))
    entry = (normed * gains_ref[0:1, :] + gains_ref[1:2, :]).astype(BF)
    grads = dproj[...]
    grad_entry = dot_nt(grads, in_ref[...])

    @pl.when(i == 0)
    def _():
        din_ref[...] = jnp.zeros_like(din_ref)
        dscale_ref[...] = jnp.zeros_like(dscale_ref)

    din_ref[...] += dot_tn(entry, grads)
    dscale_ref[0:1, :] += jnp.sum(grad_entry * normed, axis=0, keepdims=True)
    dscale_ref[1:2, :] += jnp.sum(grad_entry, axis=0, keepdims=True)
    grad = gh_ref[...] + norm_back(grad_entry, normed, inverse, gains_ref[0:1, :])
    grad_all[...] = grad
    store_image(grad_ref, i, grad_all)

    @pl.when(i == pl.num_programs(0) - 1)
    def _():
        blocks, rows = 2 * near_ref.shape[0], near_ref.shape[1]
        owner = lane_iota(blocks, width) // rows == row_iota(blocks, width)
        spot = row_iota(width, 128) % rows
        line = jnp.zeros((blocks, 128), F32)
        for s in range(2):
            spread = jnp.where(owner, dscale_ref[s : s + 1, :], 0.0)
            chosen = (lane_iota(width, 128) == spot + s * rows).astype(F32)
            line += lax.dot_general(
                spread, chosen, (((1,), (0,)), ((), ())),
                preferred_element_type=F32, precision=lax.Precision.HIGHEST,
            )
        line_ref[...] = line
        scale_row = row_iota(8, 128) == 6
        for side, out in ((0, near_ref), (1, far_ref)):
            def body(j, carry, side=side, out=out):
                place = place_ref[side * (blocks // 2) + j]
                here = pl.ds(pl.multiple_of(place * rows, rows), rows)
                out[j, :, : 3 * width] = din_ref[here, :].astype(BF)
                out[j, :, 3 * width : 4 * width] = dout_ref[here, :].astype(BF)
                small = small_ref[place] + jnp.where(scale_row, line_ref[pl.ds(place, 1), :], 0.0)
                out[j, :, 4 * width :] = resplit(small)
                return carry

            lax.fori_loop(0, blocks // 2, body, 0)


def attention_back(place, proj, probs, grad_mixed, grad_hidden, tok_pad, in_matrix, gains, grad_out, small, after=()):
    padded, width = grad_hidden.shape
    images = padded // PAD
    blocks = small.shape[0]
    rows = width // blocks
    row = lambda lanes: pl.BlockSpec((PAD, lanes), lambda i, m: (i, 0))
    once = lambda a: pl.BlockSpec(a.shape, lambda i, m: (0,) * a.ndim, pipeline_mode=pl.Buffered(1))
    half = (blocks // 2, rows, 4 * width + 128)
    return pl.pallas_call(
        behind(attention_back_kernel, 10, after),
        grid_spec=pltpu.PrefetchScalarGridSpec(
            num_scalar_prefetch=1,
            grid=(images,),
            in_specs=[
                row(3 * width), pl.BlockSpec((1, HEADS, PAD, PAD), lambda i, m: (i, 0, 0, 0)), row(width), row(width),
                row(width), once(in_matrix), once(gains), once(grad_out), once(small),
                *unread(after),
            ],
            out_specs=[whole((images * SEQ, width)), whole(half), whole(half)],
            scratch_shapes=[
                pltpu.VMEM((width, 3 * width), F32), pltpu.VMEM((8, width), F32), pltpu.VMEM((blocks, 128), F32),
                pltpu.VMEM((PAD, 3 * width), BF), pltpu.VMEM((PAD, width), F32),
            ],
        ),
        out_shape=[
            jax.ShapeDtypeStruct((images * SEQ, width), F32),
            jax.ShapeDtypeStruct(half, BF),
            jax.ShapeDtypeStruct(half, BF),
        ],
        compiler_params=params(),
        cost_estimate=cost(50),
        name="attention_back",
    )(place, proj, probs, grad_mixed, grad_hidden, tok_pad, in_matrix, gains, grad_out, small, *after)


X_BIT, CORE_BIT, Y_BIT = 16, 8, 1
Z_BITS = (2, 4, 6)
AXES = ("rep", "ep")


def swap(array, bits):
    devices = lax.axis_size("rep") * lax.axis_size("ep")
    return lax.ppermute(array, AXES, [(d, d ^ bits) for d in range(devices)])


def relative(position):
    c, x, y, z = position >> 4 & 1, position >> 3 & 1, position >> 2 & 1, position & 3
    return x * X_BIT + c * CORE_BIT + z * 2 + y * Y_BIT


def stack_kernel(count, *refs):
    for j in range(count):
        refs[count][j] = refs[j][...]


def stack(arrays, after=()):
    count = len(arrays)
    return pl.pallas_call(
        behind(functools.partial(stack_kernel, count), count, after),
        in_specs=[pl.BlockSpec(memory_space=pltpu.VMEM)] * count + unread(after),
        out_shape=jax.ShapeDtypeStruct((count,) + arrays[0].shape, arrays[0].dtype),
        compiler_params=params(),
        cost_estimate=cost(1),
        name="stack",
    )(*arrays, *after)


def split_stack_kernel(*refs):
    for j in range(4):
        refs[4][j] = refs[j][0]
        refs[5][j] = refs[j][1]


def split_stack(arrays, after=()):
    shape = jax.ShapeDtypeStruct((4,) + arrays[0].shape[1:], arrays[0].dtype)
    return pl.pallas_call(
        behind(split_stack_kernel, 4, after),
        in_specs=[pl.BlockSpec(memory_space=pltpu.VMEM)] * 4 + unread(after),
        out_shape=[shape, shape],
        compiler_params=params(),
        cost_estimate=cost(2),
        name="split_stack",
    )(*arrays, *after)


def sum_everywhere(values):
    for bits in (CORE_BIT, Y_BIT, X_BIT, 2, 4):
        values = values + swap(values, bits)
    return values


def unsplit(block):
    return block[:8] + block[8:]


def resplit(small):
    twice = jnp.concatenate([small, small], axis=0)
    high = twice.astype(BF).astype(F32)
    return jnp.where(row_iota(16, 128) < 8, high, twice - high).astype(BF)


def block_sum_kernel(parts, terms, *refs):
    ins, outs = refs[:terms], refs[terms:]
    size = ins[0].shape[0] // parts
    lanes = ins[0].shape[2]
    for p in range(parts):
        for j in range(size):
            at = p * size + j
            total = ins[0][at].astype(F32)
            for t in ins[1:]:
                total = total + t[at].astype(F32)
            small = unsplit(total[:, lanes - 128 :])
            outs[p][j, :, : lanes - 128] = total[:, : lanes - 128].astype(BF)
            outs[p][j, :, lanes - 128 :] = resplit(small)


def block_sum(terms, parts):
    size = terms[0].shape[0] // parts
    shape = (size,) + terms[0].shape[1:]
    return pl.pallas_call(
        functools.partial(block_sum_kernel, parts, len(terms)),
        out_shape=[jax.ShapeDtypeStruct(shape, BF)] * parts,
        compiler_params=params(),
        name="block_sum",
    )(*terms)


def scatter_dense(near, far):
    parts = block_sum([near, swap(far, CORE_BIT)], 4)
    got = [swap(parts[1], Y_BIT), swap(parts[2], X_BIT), swap(parts[3], X_BIT | Y_BIT)]
    parts = block_sum([parts[0]] + got, 4)
    return [parts[0]] + [swap(parts[z], Z_BITS[z - 1]) for z in (1, 2, 3)]


def fold_cores_kernel(n0, n1, g0, g1, a_keep, b_keep, a_send, b_send):
    for x in range(2):
        a_keep[x, 0] = n0[x, 0, 0] + g0[x, 0, 0]
        a_send[x, 0] = n1[x, 0, 0] + g1[x, 0, 0]
        out = b_send if x else b_keep
        out[0, 0] = n0[x, 0, 1] + g0[x, 0, 1]
        out[1, 0] = n1[x, 0, 1] + g1[x, 0, 1]


def fold_cores(near, got):
    rows, cols = near[0].shape[3:]
    out = jax.ShapeDtypeStruct((2, 4, rows, cols), BF)
    return pl.pallas_call(
        fold_cores_kernel,
        grid=(4,),
        in_specs=[pl.BlockSpec((2, 1, 2, rows, cols), lambda z: (0, z, 0, 0, 0))] * 4,
        out_specs=[pl.BlockSpec((2, 1, rows, cols), lambda z: (0, z, 0, 0))] * 4,
        out_shape=[out] * 4,
        compiler_params=params(),
        cost_estimate=cost(7),
        name="fold_cores",
    )(*near, *got)


def fold_first_kernel(a_keep, b_keep, a_got, b_got, a_near, b_near, a_far, b_far):
    a_near[0] = a_keep[0, 0] + a_got[0, 0]
    b_near[0] = b_keep[0, 0] + b_got[0, 0]
    a_far[0] = a_keep[1, 0] + a_got[1, 0]
    b_far[0] = b_keep[1, 0] + b_got[1, 0]


def fold_first(a_keep, b_keep, a_got, b_got, after=()):
    rows, cols = a_keep.shape[2:]
    return pl.pallas_call(
        behind(fold_first_kernel, 4, after),
        grid=(4,),
        in_specs=[pl.BlockSpec((2, 1, rows, cols), lambda z: (0, z, 0, 0))] * 4 + unread(after),
        out_specs=[pl.BlockSpec((1, rows, cols), lambda z: (z, 0, 0))] * 4,
        out_shape=[jax.ShapeDtypeStruct((4, rows, cols), BF)] * 4,
        compiler_params=params(),
        cost_estimate=cost(4),
        name="fold_first",
    )(a_keep, b_keep, a_got, b_got, *after)


def fold_second_kernel(a_keep, b_keep, a_got, b_got, *parts):
    for z in range(4):
        parts[z][0] = a_keep[z] + a_got[z]
        parts[z][1] = b_keep[z] + b_got[z]


def fold_second(a_keep, b_keep, a_got, b_got):
    return pl.pallas_call(
        fold_second_kernel,
        out_shape=[jax.ShapeDtypeStruct((2,) + a_keep.shape[1:], BF)] * 4,
        compiler_params=params(),
        cost_estimate=cost(3),
        name="fold_second",
    )(a_keep, b_keep, a_got, b_got)


def total_of(array):
    return jnp.sum(jnp.sum(array, axis=1, keepdims=True), axis=0, keepdims=True)


def expert_update_kernel(*refs):
    parts, (wi, fi, si, wo, fo, so), outs = refs[:8], refs[8:14], refs[14:]
    sums = outs[6]
    lane = lane_iota(1, 128)
    kept = jnp.zeros((1, 128), F32)
    moved = jnp.zeros((1, 128), F32)
    cols = parts[0].shape[2]
    for m, (weight, first, second, new) in enumerate(((wi, fi, si, outs[0:3]), (wo, fo, so, outs[3:6]))):
        for k in range(2):
            grad = parts[4 * k][m].astype(F32)
            for part in parts[4 * k + 1 : 4 * k + 4]:
                grad = grad + part[m].astype(F32)
            span = slice(k * cols, (k + 1) * cols)
            if m == 0:
                at = (0, slice(None), span)
            else:
                grad = grad.T
                at = (0, span, slice(None))
            state = moments(weight[at], grad, first[at], second[at])
            for ref, value in zip(new, state):
                ref[at] = value
            slot = lane == (8 if m == 0 else 10)
            kept += jnp.where(slot, total_of(weight[at] * weight[at]), 0.0)
            moved += jnp.where(slot, total_of(state[2] * state[2]), 0.0)
    sums[...] = jnp.zeros_like(sums)
    sums[0:1, :] = kept
    sums[1:2, :] = moved


def expert_update(parts, arrays):
    shape = jax.ShapeDtypeStruct(arrays[0].shape, F32)
    return pl.pallas_call(
        expert_update_kernel,
        out_shape=[shape] * 6 + [jax.ShapeDtypeStruct((8, 128), F32)],
        compiler_params=params(),
        cost_estimate=cost(6),
        name="expert_update",
    )(*parts, *arrays)


def narrow(row, columns, rows):
    spread = jnp.where(lane_iota(rows, 128) % rows == row_iota(rows, 128), row, 0.0)
    chosen = (row_iota(128, columns) // rows == lane_iota(128, columns)).astype(F32)
    return lax.dot_general(
        spread, chosen, (((1,), (0,)), ((), ())), preferred_element_type=F32, precision=lax.Precision.HIGHEST
    )


def dense_update_kernel(*refs):
    ins, sums, states, outs = refs[:4], refs[4], refs[5:23], refs[23:]
    width = ins[0].shape[2] - 128
    total = ins[0][0].astype(F32)
    for t in ins[1:]:
        total = total + t[0].astype(F32)
    small = unsplit(total[:, width:])
    experts, rows = states[6].shape[1], states[6].shape[0]
    bias_rows = states[12].shape[1] // 128
    grads = (
        total[:, : width * 3 // 4],
        total[:, width * 3 // 4 : width],
        narrow(small[bias_rows + 1 : bias_rows + 2], experts, rows),
        narrow(small[bias_rows + 2 : bias_rows + 3], 5, rows),
        jnp.concatenate([small[j : j + 1] for j in range(bias_rows)], axis=1),
        small[bias_rows : bias_rows + 1],
    )
    lane = lane_iota(1, 128)
    kept, moved = sums[0:1, :], sums[1:2, :]
    for j, grad in enumerate(grads):
        weight, first, second = (states[3 * j + k][...] for k in range(3))
        state = moments(weight, grad, first, second)
        for k in range(3):
            outs[3 * j + k][...] = state[k]
        for c, slot in enumerate({0: (0,), 1: (1,), 2: (2,), 3: (3, 4, 5, 6, 7), 4: (9,), 5: (11,)}[j]):
            cut = (slice(None), slice(c, c + 1)) if j == 3 else (slice(None), slice(None))
            kept += jnp.where(lane == slot, total_of(weight[cut] * weight[cut]), 0.0)
            moved += jnp.where(lane == slot, total_of(state[2][cut] * state[2][cut]), 0.0)
    outs[18][...] = jnp.zeros_like(outs[18])
    outs[18][0:1, :] = kept
    outs[18][1:2, :] = moved


def dense_update(terms, sums, states):
    return pl.pallas_call(
        dense_update_kernel,
        out_shape=[jax.ShapeDtypeStruct(a.shape, F32) for a in states] + [jax.ShapeDtypeStruct((8, 128), F32)],
        compiler_params=params(),
        cost_estimate=cost(3),
        name="dense_update",
    )(*terms, sums, *states)


def new_weights_kernel(sums, counts, *refs):
    weights, steps, outs, norms = refs[:8], refs[8:16], refs[16:24], refs[24]
    weight_rms = jnp.sqrt(sums[0:1, :] / counts[...])
    step_rms = jnp.sqrt(sums[1:2, :] / counts[...])
    trust = weight_rms / step_rms
    norms[...] = jnp.zeros_like(norms)
    norms[0:1, :] = weight_rms
    norms[1:2, :] = step_rms
    norms[2:3, :] = trust
    for j, begin in enumerate((0, 1, 2, 3, 8, 9, 10, 11)):
        scale = trust[:, 3:8] if j == 3 else trust[:, begin : begin + 1]
        if len(outs[j].shape) == 3:
            outs[j][0] = weights[j][0] - RATE * scale * steps[j][0]
        else:
            outs[j][...] = weights[j][...] - RATE * scale * steps[j][...]


def new_weights(sums, counts, weights, steps):
    return pl.pallas_call(
        new_weights_kernel,
        out_shape=[jax.ShapeDtypeStruct(a.shape, F32) for a in weights] + [jax.ShapeDtypeStruct((8, 128), F32)],
        compiler_params=params(),
        cost_estimate=cost(5),
        name="new_weights",
    )(sums, counts, *weights, *steps)


CHUNKS = 2


def replicate_plan(
    tokens, cotangent, expert_ids, priority,
    heads_in, heads_in_first, heads_in_second, heads_out, heads_out_first, heads_out_second,
    router, router_first, router_second, scales, scales_first, scales_second,
    expert_in, expert_in_first, expert_in_second, bias_in, bias_in_first, bias_in_second,
    expert_out, expert_out_first, expert_out_second, bias_out, bias_out_first, bias_out_second,
):
    count, width = tokens.shape
    images = count // SEQ
    experts = router.shape[1]
    rep, ep = lax.axis_size("rep"), lax.axis_size("ep")
    rep_me, ep_me = lax.axis_index("rep"), lax.axis_index("ep")
    me = (rep_me * ep + ep_me).astype(jnp.int32)
    at = jnp.stack([rep_me, ep_me]).astype(jnp.int32)
    capacity = (5 * expert_ids.shape[1] * count + 4 * experts - 1) // (4 * experts)
    listed = -(-capacity // 16) * 16
    hidden_part = FF // rep
    cols = hidden_part // CHUNKS

    enter_low = expert_in[0].astype(BF)
    leave_low = expert_out[0].astype(BF).T
    pieces = [
        jnp.stack([enter_low[:, k * cols : (k + 1) * cols], leave_low[:, k * cols : (k + 1) * cols]])
        for k in range(CHUNKS)
    ]
    wide = lax.all_gather(pieces[0][None], AXES, axis=0, tiled=True).reshape(rep, ep, 2, width, cols)

    rows_here = heads_in.shape[0]
    small = jnp.concatenate([router, scales], axis=1)
    small = jnp.pad(small, ((0, 0), (0, 128 - small.shape[1])))
    biases = jnp.concatenate([bias_in.reshape(-1, 128), bias_out.reshape(-1, 128)], axis=0)
    biases = jnp.pad(biases, ((0, rows_here - biases.shape[0]), (0, 0)))
    dense = jnp.concatenate([heads_in, heads_out, small, biases], axis=1).astype(BF)
    order = jnp.array([relative(p) for p in range(rep * ep)], jnp.int32)
    place = jnp.bitwise_xor(order, me)
    spread = lambda a, fill: jnp.pad(
        a.reshape(-1, images, SEQ), ((0, 0), (0, 0), (0, PAD - SEQ)), constant_values=fill
    ).reshape(-1, images * PAD)
    ids_rows = spread(expert_ids.T, -1)
    rows = jnp.concatenate([spread(priority, count), ids_rows], axis=0).astype(F32)
    rows = jnp.pad(rows, ((0, 5), (0, 0)))

    zs_got = [swap(dense, bits) for bits in Z_BITS]
    tok_pad, cot_pad = spread_rows(tokens, cotangent)
    zs = stack([dense] + zs_got, after=(tok_pad,))
    others = [swap(zs, bits) for bits in (Y_BIT, X_BIT, X_BIT | Y_BIT)]
    lrow, lcol, meta = find_places(rows, rows.T, capacity, experts)
    plane = stack([zs] + others, after=(lrow,))
    in_matrix, out_matrix, router_matrix, gains, small_all = assemble(
        place, plane.reshape((16,) + dense.shape), swap(plane, CORE_BIT).reshape((16,) + dense.shape), experts
    )
    bias_all = small_all[:, 128:].reshape(rep, ep, rows_here, 128)
    in_rows = hidden_part // 128
    enter_bias = bias_all[:, :, :in_rows].reshape(rep, ep, hidden_part).astype(F32).transpose(1, 0, 2)
    leave_bias = bias_all[:, :, in_rows].astype(F32).transpose(1, 0, 2).reshape(ep, 1, width)

    piece_got = [swap(pieces[1], bits) for bits in Z_BITS]
    proj, probs, mixed, hidden, routed, gcol, grow = attention(
        tok_pad, in_matrix, out_matrix, router_matrix, gains, ids_rows.T
    )
    halves = split_stack([pieces[1]] + piece_got, after=(gcol,))
    far_x = [swap(h, X_BIT) for h in halves]
    far_y = [swap(h, Y_BIT) for h in halves]
    lists = gather(meta, routed, cot_pad, lrow, grow, listed, after=halves)

    totals_here = meta[images - 1] + meta[2 * images - 1]
    at = jnp.concatenate([at, totals_here])
    bias_cut = lambda k: enter_bias[:, :, k * cols : (k + 1) * cols]
    cross = lambda arrays: [swap(a, CORE_BIT) for a in arrays]
    mingle = lambda near, far: [a for pair in zip(near, far) for a in pair]
    far_xy = swap(far_x[0], Y_BIT), swap(far_y[1], X_BIT)
    y_part, d_part, near_a, far_a, bias_a, leave_a = expert_pass(
        at, lists, wide, bias_cut(0), after=far_x + far_y
    )
    near_half = [halves[0], far_x[0], halves[1], far_x[1]]
    far_half = [far_y[0], far_xy[0], far_y[1], far_xy[1]]
    crossed = cross(near_half)
    got_a = swap(far_a, CORE_BIT)
    y_half, d_half, near_b, far_b, bias_b, leave_b = expert_pass(
        at, lists, wide, bias_cut(0), half=1, done=(y_part, d_part), after=list(far_xy) + crossed
    )
    got_b = swap(far_b, CORE_BIT)
    one = fold_cores((near_a, near_b), (got_a, got_b))
    even = lax.bitwise_xor(jnp.arange(ep, dtype=jnp.int32), ep_me)[:, None, None] % 2 == 0
    grad_bias = [jnp.where(even, bias_a, bias_b)]
    grad_leave_bias = jnp.where(even, leave_a, leave_b)
    one_got = swap(one[2], Y_BIT), swap(one[3], X_BIT)
    crossed_far = cross(far_half)
    y_part, d_part, near_a, far_a, bias_a = expert_pass(
        at, lists, mingle(near_half, crossed), bias_cut(1), leave_bias, (y_half, d_half)
    )
    got_a = swap(far_a, CORE_BIT)
    y, d, near_b, far_b, bias_b = expert_pass(
        at, lists, mingle(far_half, crossed_far), bias_cut(1), leave_bias, (y_half, d_half), half=1,
        done=(y_part, d_part), after=list(one_got),
    )
    one = fold_first(*one[:2], *one_got)
    one_got = swap(one[2], X_BIT), swap(one[3], Y_BIT)
    got_b = swap(far_b, CORE_BIT)
    output, grad_hidden, grad_mixed, grad_out, grad_router, grad_scale = combine(
        meta, y, d, lcol, gcol, hidden, cot_pad, mixed, out_matrix, router_matrix, gains
    )
    one = fold_second(*one[:2], *one_got)
    two = fold_cores((near_a, near_b), (got_a, got_b))
    grad_bias.append(jnp.where(even, bias_a, bias_b))
    devices = rep * ep
    by_device = lambda a: jnp.pad(
        a.reshape(a.shape[0], devices, rows_here).transpose(1, 0, 2).reshape(devices, 1, -1),
        ((0, 0), (0, 0), (0, 128 - a.shape[0] * rows_here)),
    )
    small_grads = jnp.concatenate(
        [
            jnp.concatenate(grad_bias, axis=2).transpose(1, 0, 2).reshape(devices, in_rows, 128),
            grad_leave_bias.reshape(ep, rep, 128).transpose(1, 0, 2).reshape(devices, 1, 128),
            by_device(grad_router),
            by_device(grad_scale[:5]),
        ],
        axis=1,
    )
    small_grads = jnp.pad(small_grads, ((0, 0), (0, 8 - small_grads.shape[1]), (0, 0)))
    one_got = [swap(one[z], Z_BITS[z - 1]) for z in (1, 2, 3)]
    two_got = swap(two[2], Y_BIT), swap(two[3], X_BIT)
    input_grad, near_dense, far_dense = attention_back(
        place, proj, probs, grad_mixed, grad_hidden, tok_pad, in_matrix, gains, grad_out, small_grads,
        after=list(one[1:]) + list(two[2:]),
    )
    two = fold_first(*two[:2], *two_got, after=one_got)
    two_got = swap(two[2], X_BIT), swap(two[3], Y_BIT)
    dense_terms = scatter_dense(near_dense, far_dense)
    two = fold_second(*two[:2], *two_got)
    two_got = [swap(two[z], Z_BITS[z - 1]) for z in (1, 2, 3)]
    parts = [one[0]] + one_got + [two[0]] + two_got
    (in_first, in_second, in_step, out_first, out_second, out_step, sums) = expert_update(
        parts, (expert_in, expert_in_first, expert_in_second, expert_out, expert_out_first, expert_out_second)
    )
    dense_states = (
        heads_in, heads_in_first, heads_in_second, heads_out, heads_out_first, heads_out_second,
        router, router_first, router_second, scales, scales_first, scales_second,
        bias_in, bias_in_first, bias_in_second, bias_out, bias_out_first, bias_out_second,
    )
    *dense_new, sums = dense_update(dense_terms, sums, dense_states)
    sums = sum_everywhere(sums)
    counts = jnp.array(
        [3 * width * width, width * width, width * experts]
        + [width] * 5
        + [experts * width * FF, experts * FF, experts * FF * width, experts * width]
        + [1] * (128 - 12),
        jnp.float32,
    )[None]
    trio = lambda j: tuple(dense_new[3 * j : 3 * j + 3])
    states = [
        trio(0), trio(1), trio(2), trio(3), (in_first, in_second, in_step), trio(4),
        (out_first, out_second, out_step), trio(5),
    ]
    weights_now = (heads_in, heads_out, router, scales, expert_in, bias_in, expert_out, bias_out)
    *fresh, norms = new_weights(sums, counts, weights_now, [state[2] for state in states])
    results = [output, input_grad]
    for state, weight in zip(states, fresh):
        results.extend([state[0], state[1], weight])
    results.append(norms[:3, :12])
    return tuple(results)


def expert_front(rows, enter_weight, enter_bias):
    pre = jnp.einsum("sjcd,jdf->sjcf", rows, enter_weight, preferred_element_type=jnp.float32)
    return pre + enter_bias.astype(jnp.float32)[None, :, None, :]


def exchange_plan(
    tokens,
    cotangent,
    expert_ids,
    priority,
    heads_in,
    heads_in_first,
    heads_in_second,
    heads_out,
    heads_out_first,
    heads_out_second,
    router,
    router_first,
    router_second,
    scales,
    scales_first,
    scales_second,
    expert_in,
    expert_in_first,
    expert_in_second,
    bias_in,
    bias_in_first,
    bias_in_second,
    expert_out,
    expert_out_first,
    expert_out_second,
    bias_out,
    bias_out_first,
    bias_out_second,
):
    in_matrix, out_matrix, router_matrix, scale_table = (
        lax.all_gather(heads_in.astype(jnp.bfloat16), ("rep", "ep"), axis=0, tiled=True),
        lax.all_gather(heads_out.astype(jnp.bfloat16), ("rep", "ep"), axis=0, tiled=True),
        lax.all_gather(router.astype(jnp.bfloat16), ("rep", "ep"), axis=0, tiled=True),
        lax.all_gather(scales.astype(jnp.bfloat16), ("rep", "ep"), axis=0, tiled=True),
    )
    enter_weight, enter_bias, leave_weight, leave_bias = (
        lax.all_gather(expert_in.astype(jnp.bfloat16), "rep", axis=2, tiled=True),
        lax.all_gather(bias_in.astype(jnp.bfloat16), "rep", axis=1, tiled=True),
        lax.all_gather(expert_out.astype(jnp.bfloat16), "rep", axis=1, tiled=True),
        lax.all_gather(bias_out.astype(jnp.bfloat16), "rep", axis=1, tiled=True),
    )
    gains = scale_table.astype(jnp.float32)
    inputs = tokens.astype(jnp.float32)
    count, width = inputs.shape
    images = count // SEQ
    factor = HEAD ** (-0.5)
    normed_one, inverse_one = normalize(inputs)
    entry = (normed_one * gains[:, 0] + gains[:, 1]).astype(jnp.bfloat16)
    projected = jnp.dot(entry, in_matrix, preferred_element_type=jnp.float32).astype(jnp.bfloat16)
    grid = projected.reshape(images, SEQ, 3, HEADS, HEAD)
    query = grid[:, :, 0]
    keyed = grid[:, :, 1]
    valued = grid[:, :, 2]
    scores = attention_scores(query, keyed, factor)
    peak = jnp.max(scores, axis=-1, keepdims=True)
    log_total = peak + jnp.log(jnp.sum(jnp.exp(scores - peak), axis=-1, keepdims=True))
    weights = jnp.exp(scores - log_total).astype(jnp.bfloat16)
    mixed = jnp.einsum("bhqk,bkhd->bqhd", weights, valued, preferred_element_type=jnp.float32)
    mixed = mixed.reshape(count, width).astype(jnp.bfloat16)
    hidden = inputs + jnp.dot(mixed, out_matrix, preferred_element_type=jnp.float32) + gains[:, 4]
    normed_two, inverse_two = normalize(hidden)
    routed = (normed_two * gains[:, 2] + gains[:, 3]).astype(jnp.bfloat16)
    logits = jnp.dot(routed, router_matrix, preferred_element_type=jnp.float32)
    experts = logits.shape[1]
    top = expert_ids.shape[1]
    choose = (expert_ids[:, :, None] == jnp.arange(experts, dtype=jnp.int32)[None, None, :]).astype(
        jnp.float32
    )
    picked = jnp.sum(choose * logits[:, None, :], axis=2)
    gates = jax.nn.softmax(picked, axis=1)
    places = route_places(expert_ids, priority[0], experts)
    capacity = (5 * top * count + 4 * experts - 1) // (4 * experts)
    groups = lax.axis_size("ep")
    local = experts // groups
    slots = experts * capacity
    slot = jnp.where(places < capacity, expert_ids * capacity + places, slots)
    pair_of_slot = (
        jnp.full((slots,), count * top, jnp.int32)
        .at[slot.reshape(-1)]
        .set(jnp.arange(count * top, dtype=jnp.int32), mode="drop")
    )
    token_of_slot = pair_of_slot // top
    padded_rows = jnp.concatenate([routed, jnp.zeros((1, width), jnp.bfloat16)], axis=0)
    outgoing = padded_rows[token_of_slot].reshape(groups, local, capacity, width)
    arrived = lax.all_to_all(outgoing, "ep", split_axis=0, concat_axis=0, tiled=True)
    pre = expert_front(arrived, enter_weight, enter_bias)
    act, gelu_back = jax.vjp(exact_gelu, pre)
    act_low = act.astype(jnp.bfloat16)
    result = jnp.einsum("sjcf,jfd->sjcd", act_low, leave_weight, preferred_element_type=jnp.float32)
    result = (result + leave_bias.astype(jnp.float32)[None, :, None, :]).astype(jnp.bfloat16)
    returned = lax.all_to_all(result, "ep", split_axis=0, concat_axis=0, tiled=True).reshape(
        slots, width
    )
    padded_back = jnp.concatenate([returned, jnp.zeros((1, width), jnp.bfloat16)], axis=0)
    picked_rows = padded_back[slot].astype(jnp.float32)
    output = hidden + jnp.sum(gates[:, :, None] * picked_rows, axis=1)
    grad_output = cotangent.astype(jnp.float32)
    grad_gates = jnp.sum(picked_rows * grad_output[:, None, :], axis=2)
    gate_list = jnp.concatenate([gates.reshape(-1), jnp.zeros((1,), jnp.float32)])
    padded_grad = jnp.concatenate([grad_output, jnp.zeros((1, width), jnp.float32)], axis=0)
    grad_slots = (padded_grad[token_of_slot] * gate_list[pair_of_slot][:, None]).astype(
        jnp.bfloat16
    )
    grad_arrived = lax.all_to_all(
        grad_slots.reshape(groups, local, capacity, width),
        "ep",
        split_axis=0,
        concat_axis=0,
        tiled=True,
    )
    grad_act = jnp.einsum(
        "sjcd,jfd->sjcf", grad_arrived, leave_weight, preferred_element_type=jnp.float32
    )
    grad_pre = gelu_back(grad_act)[0].astype(jnp.bfloat16)
    grad_leave = jnp.einsum(
        "sjcf,sjcd->jfd", act_low, grad_arrived, preferred_element_type=jnp.float32
    )
    grad_leave_bias = jnp.sum(grad_arrived, axis=(0, 2), dtype=jnp.float32)
    grad_enter = jnp.einsum("sjcd,sjcf->jdf", arrived, grad_pre, preferred_element_type=jnp.float32)
    grad_enter_bias = jnp.sum(grad_pre, axis=(0, 2), dtype=jnp.float32)
    grad_rows = jnp.einsum(
        "sjcf,jdf->sjcd", grad_pre, enter_weight, preferred_element_type=jnp.float32
    ).astype(jnp.bfloat16)
    grad_back = lax.all_to_all(grad_rows, "ep", split_axis=0, concat_axis=0, tiled=True).reshape(
        slots, width
    )
    padded_grad_back = jnp.concatenate([grad_back, jnp.zeros((1, width), jnp.bfloat16)], axis=0)
    grad_routed = jnp.sum(padded_grad_back[slot], axis=1, dtype=jnp.float32)
    grad_picked = gates * (grad_gates - jnp.sum(gates * grad_gates, axis=1, keepdims=True))
    grad_logits = jnp.sum(choose * grad_picked[:, :, None], axis=1).astype(jnp.bfloat16)
    grad_router = jnp.einsum("td,te->de", routed, grad_logits, preferred_element_type=jnp.float32)
    grad_routed = grad_routed + jnp.einsum(
        "te,de->td", grad_logits, router_matrix, preferred_element_type=jnp.float32
    )
    grad_gain_two = jnp.sum(grad_routed * normed_two, axis=0)
    grad_shift_two = jnp.sum(grad_routed, axis=0)
    grad_hidden = grad_output + norm_back(grad_routed, normed_two, inverse_two, gains[:, 2])
    grad_shift_out = jnp.sum(grad_hidden, axis=0)
    grad_mix_out = grad_hidden.astype(jnp.bfloat16)
    grad_out_matrix = jnp.einsum(
        "td,te->de", mixed, grad_mix_out, preferred_element_type=jnp.float32
    )
    grad_mixed = jnp.einsum(
        "te,de->td", grad_mix_out, out_matrix, preferred_element_type=jnp.float32
    )
    grad_mixed = grad_mixed.astype(jnp.bfloat16).reshape(images, SEQ, HEADS, HEAD)
    probs = jnp.exp(attention_scores(query, keyed, factor) - log_total)
    weights_again = probs.astype(jnp.bfloat16)
    grad_valued = jnp.einsum(
        "bhqk,bqhd->bkhd", weights_again, grad_mixed, preferred_element_type=jnp.float32
    )
    grad_probs = jnp.einsum(
        "bqhd,bkhd->bhqk", grad_mixed, valued, preferred_element_type=jnp.float32
    )
    grad_scores = (
        probs * (grad_probs - jnp.sum(probs * grad_probs, axis=-1, keepdims=True))
    ).astype(jnp.bfloat16)
    grad_query = (
        jnp.einsum("bhqk,bkhd->bqhd", grad_scores, keyed, preferred_element_type=jnp.float32)
        * factor
    )
    grad_keyed = (
        jnp.einsum("bhqk,bqhd->bkhd", grad_scores, query, preferred_element_type=jnp.float32)
        * factor
    )
    grad_projected = (
        jnp.stack([grad_query, grad_keyed, grad_valued], axis=2)
        .reshape(count, 3 * width)
        .astype(jnp.bfloat16)
    )
    grad_in_matrix = jnp.einsum(
        "td,te->de", entry, grad_projected, preferred_element_type=jnp.float32
    )
    grad_entry = jnp.einsum(
        "te,de->td", grad_projected, in_matrix, preferred_element_type=jnp.float32
    )
    grad_gain_one = jnp.sum(grad_entry * normed_one, axis=0)
    grad_shift_one = jnp.sum(grad_entry, axis=0)
    input_grad = grad_hidden + norm_back(grad_entry, normed_one, inverse_one, gains[:, 0])
    grad_scales = jnp.stack(
        [grad_gain_one, grad_shift_one, grad_gain_two, grad_shift_two, grad_shift_out], axis=1
    )
    summed_dense = (
        lax.psum_scatter(grad_in_matrix, ("rep", "ep"), scatter_dimension=0, tiled=True),
        lax.psum_scatter(grad_out_matrix, ("rep", "ep"), scatter_dimension=0, tiled=True),
        lax.psum_scatter(grad_router, ("rep", "ep"), scatter_dimension=0, tiled=True),
        lax.psum_scatter(grad_scales, ("rep", "ep"), scatter_dimension=0, tiled=True),
    )
    summed_expert = (
        lax.psum_scatter(
            grad_enter.astype(jnp.bfloat16), "rep", scatter_dimension=2, tiled=True
        ).astype(jnp.float32),
        lax.psum_scatter(
            grad_enter_bias.astype(jnp.bfloat16), "rep", scatter_dimension=1, tiled=True
        ).astype(jnp.float32),
        lax.psum_scatter(
            grad_leave.astype(jnp.bfloat16), "rep", scatter_dimension=1, tiled=True
        ).astype(jnp.float32),
        lax.psum_scatter(
            grad_leave_bias.astype(jnp.bfloat16), "rep", scatter_dimension=1, tiled=True
        ).astype(jnp.float32),
    )
    weights_now = (heads_in, heads_out, router, scales, expert_in, bias_in, expert_out, bias_out)
    grads_now = tuple(summed_dense) + tuple(summed_expert)
    firsts = (
        heads_in_first,
        heads_out_first,
        router_first,
        scales_first,
        expert_in_first,
        bias_in_first,
        expert_out_first,
        bias_out_first,
    )
    seconds = (
        heads_in_second,
        heads_out_second,
        router_second,
        scales_second,
        expert_in_second,
        bias_in_second,
        expert_out_second,
        bias_out_second,
    )
    states = [moments(w, g, f, s) for w, g, f, s in zip(weights_now, grads_now, firsts, seconds)]
    weight_terms = jnp.concatenate([squares(w, index == 3) for index, w in enumerate(weights_now)])
    step_terms = jnp.concatenate(
        [squares(state[2], index == 3) for index, state in enumerate(states)]
    )
    totals = lax.psum(jnp.stack([weight_terms, step_terms]), ("rep", "ep"))
    return (output, input_grad) + finish(totals, weights_now, states, width, experts)


def solution(mesh):
    in_specs = (
        P(("rep", "ep"), None),
        P(("rep", "ep"), None),
        P(("rep", "ep"), None),
        P(("rep", "ep"), None),
        P(("rep", "ep"), None),
        P(("rep", "ep"), None),
        P(("rep", "ep"), None),
        P(("rep", "ep"), None),
        P(("rep", "ep"), None),
        P(("rep", "ep"), None),
        P(("rep", "ep"), None),
        P(("rep", "ep"), None),
        P(("rep", "ep"), None),
        P(("rep", "ep"), None),
        P(("rep", "ep"), None),
        P(("rep", "ep"), None),
        P("ep", None, "rep"),
        P("ep", None, "rep"),
        P("ep", None, "rep"),
        P("ep", "rep"),
        P("ep", "rep"),
        P("ep", "rep"),
        P("ep", "rep", None),
        P("ep", "rep", None),
        P("ep", "rep", None),
        P("ep", "rep"),
        P("ep", "rep"),
        P("ep", "rep"),
    )
    out_specs = (
        P(("rep", "ep"), None),
        P(("rep", "ep"), None),
        P(("rep", "ep"), None),
        P(("rep", "ep"), None),
        P(("rep", "ep"), None),
        P(("rep", "ep"), None),
        P(("rep", "ep"), None),
        P(("rep", "ep"), None),
        P(("rep", "ep"), None),
        P(("rep", "ep"), None),
        P(("rep", "ep"), None),
        P(("rep", "ep"), None),
        P(("rep", "ep"), None),
        P(("rep", "ep"), None),
        P("ep", None, "rep"),
        P("ep", None, "rep"),
        P("ep", None, "rep"),
        P("ep", "rep"),
        P("ep", "rep"),
        P("ep", "rep"),
        P("ep", "rep", None),
        P("ep", "rep", None),
        P("ep", "rep", None),
        P("ep", "rep"),
        P("ep", "rep"),
        P("ep", "rep"),
        P(),
    )
    replicated = mesh.shape["rep"] == 4 and mesh.shape["ep"] == 8
    return jax.shard_map(
        replicate_plan if replicated else exchange_plan,
        mesh=mesh,
        in_specs=in_specs,
        out_specs=out_specs,
        check_vma=False,
    )
```

```python
import functools

import jax
import jax.numpy as jnp
from jax import lax
from jax.experimental import pallas as pl
from jax.experimental.pallas import tpu as pltpu
from jax.sharding import PartitionSpec as P

HEADS = 8
HEAD = 64
FF = 2048
SEQ = 197
STEP = 5


BETA = 0.5
RATE = 0.3
DECAY = 0.01
EPSILON = 1e-06


def normalize(rows):
    centred = rows - jnp.mean(rows, axis=-1, keepdims=True)
    inverse = lax.rsqrt(jnp.mean(centred * centred, axis=-1, keepdims=True) + 1e-06)
    return (centred * inverse, inverse)


def norm_back(grad_rows, normed, inverse, gain):
    scaled = grad_rows * gain
    return inverse * (
        scaled
        - jnp.mean(scaled, axis=-1, keepdims=True)
        - normed * jnp.mean(scaled * normed, axis=-1, keepdims=True)
    )


def exact_gelu(values):
    return jax.nn.gelu(values, approximate=False)


def route_places(block_ids, ranking, experts):
    count = block_ids.shape[0]
    keys = jnp.arange(block_ids.shape[1], dtype=jnp.int32)[None, :] * count + ranking[:, None]
    ordered = (
        jnp.zeros((block_ids.size,), jnp.int32).at[keys.reshape(-1)].set(block_ids.reshape(-1))
    )
    hits = (ordered[:, None] == jnp.arange(experts, dtype=jnp.int32)[None, :]).astype(jnp.int32)
    before = jnp.cumsum(hits, axis=0) - hits
    place = jnp.sum(before * hits, axis=1)
    return place[keys]


def attention_scores(query, keyed, factor):
    return jnp.einsum("bqhd,bkhd->bhqk", query, keyed, preferred_element_type=jnp.float32) * factor


def moments(weight, grad, first, second):
    first_new = BETA * first + (1.0 - BETA) * grad
    second_new = BETA * second + (1.0 - BETA) * grad * grad
    step = (
        first_new / (1.0 - BETA**STEP) / (jnp.sqrt(second_new / (1.0 - BETA**STEP)) + EPSILON)
        + DECAY * weight
    )
    return (first_new, second_new, step)


def squares(array, per_column):
    if per_column:
        return jnp.sum(array * array, axis=0)
    return jnp.sum(array * array)[None]


def finish(totals, weights_now, states, width, experts):
    counts = jnp.array(
        [3 * width * width, width * width, width * experts]
        + [width] * 5
        + [experts * width * FF, experts * FF, experts * FF * width, experts * width],
        jnp.float32,
    )
    weight_rms = jnp.sqrt(totals[0] / counts)
    step_rms = jnp.sqrt(totals[1] / counts)
    trust = weight_rms / step_rms
    bounds = [(0, 1), (1, 2), (2, 3), (3, 8), (8, 9), (9, 10), (10, 11), (11, 12)]
    results = []
    for weight, state, bound in zip(weights_now, states, bounds):
        results.extend([state[0], state[1], weight - RATE * trust[bound[0] : bound[1]] * state[2]])
    results.append(jnp.stack([weight_rms, step_rms, trust]))
    return tuple(results)


PAD = 208
WIN = 96
VMEM = 60 * 1024 * 1024
BF = jnp.bfloat16
F32 = jnp.float32


def dot_nn(a, b):
    return lax.dot_general(a, b, (((1,), (0,)), ((), ())), preferred_element_type=F32)


def dot_nt(a, b):
    return lax.dot_general(a, b, (((1,), (1,)), ((), ())), preferred_element_type=F32)


def dot_tn(a, b):
    return lax.dot_general(a, b, (((0,), (0,)), ((), ())), preferred_element_type=F32)


def lane_iota(rows, lanes):
    return lax.broadcasted_iota(jnp.int32, (rows, lanes), 1)


def row_iota(rows, lanes):
    return lax.broadcasted_iota(jnp.int32, (rows, lanes), 0)


def whole(shape):
    return pl.BlockSpec(shape, lambda *_: (0,) * len(shape))


def cost(micros):
    return pl.CostEstimate(flops=int(micros * 1e9), bytes_accessed=int(micros * 1e5), transcendentals=0)


def params(**kw):
    return pltpu.CompilerParams(vmem_limit_bytes=VMEM, **kw)


def behind(kernel, inputs, after):
    def body(*refs):
        return kernel(*refs[:inputs], *refs[inputs + len(after) :])

    return body


def unread(after):
    return [pl.BlockSpec(memory_space=pl.ANY)] * len(after)


def assemble_kernel(place_ref, near_ref, far_ref, in_ref, out_ref, router_ref, gains_ref, small_ref):
    copies, rows = near_ref.shape[0], near_ref.shape[1]
    width = out_ref.shape[1]
    for side, got_ref in enumerate((near_ref, far_ref)):
        for j in range(copies):
            place = pl.multiple_of(place_ref[side * copies + j] * rows, rows)
            in_ref[pl.ds(place, rows), :] = got_ref[j, :, : 3 * width]
            out_ref[pl.ds(place, rows), :] = got_ref[j, :, 3 * width : 4 * width]
            small_ref[pl.ds(place, rows), :] = got_ref[j, :, 4 * width :]
    turned = small_ref[:, :128].astype(F32).T
    experts = router_ref.shape[0]
    router_ref[...] = turned[:experts].astype(BF)
    gains_ref[...] = turned[experts : experts + 8]


def assemble(place, near, far, experts):
    copies, rows, lanes = near.shape
    width = 2 * copies * rows
    return pl.pallas_call(
        assemble_kernel,
        grid_spec=pltpu.PrefetchScalarGridSpec(
            num_scalar_prefetch=1,
            grid=(1,),
            in_specs=[whole(near.shape)] * 2,
            out_specs=[
                whole((width, 3 * width)),
                whole((width, width)),
                whole((experts, width)),
                whole((8, width)),
                whole((width, lanes - 4 * width)),
            ],
        ),
        out_shape=[
            jax.ShapeDtypeStruct((width, 3 * width), BF),
            jax.ShapeDtypeStruct((width, width), BF),
            jax.ShapeDtypeStruct((experts, width), BF),
            jax.ShapeDtypeStruct((8, width), F32),
            jax.ShapeDtypeStruct((width, lanes - 4 * width), BF),
        ],
        compiler_params=params(),
        cost_estimate=cost(1),
        name="assemble",
    )(place, near, far)


def places_kernel(capacity, rows_ref, cols_ref, lrow_ref, lcol_ref, meta_ref):
    count = cols_ref.shape[0]
    images = count // PAD
    experts = lcol_ref.shape[1]
    expert = lane_iota(count, experts).astype(F32)
    first = (cols_ref[:, 1:2] == expert).astype(F32)
    second = (cols_ref[:, 2:3] == expert).astype(F32)
    first_low = first.astype(BF)
    second_low = second.astype(BF)
    total_first = jnp.sum(first, axis=0, keepdims=True)
    lower = (lane_iota(PAD, PAD) < row_iota(PAD, PAD)).astype(F32).astype(BF)
    ranking = rows_ref[0:1, :]
    begin = jnp.zeros((1, experts), F32)
    for i in range(images):
        span = slice(i * PAD, (i + 1) * PAD)
        ahead = (ranking < cols_ref[span, 0:1]).astype(F32).astype(BF)
        rank_first = dot_nn(ahead, first_low)
        rank_second = dot_nn(ahead, second_low) + total_first
        place = first[span] * rank_first + second[span] * rank_second
        kept = (first[span] + second[span]) * (place < capacity).astype(F32)
        local = dot_nn(lower, kept.astype(BF))
        local = jnp.where(kept > 0.0, local, -1.0)
        lcol_ref[span, :] = local
        lrow_ref[i] = local.T
        here = jnp.sum(kept, axis=0, keepdims=True)
        meta_ref[i : i + 1, :] = begin.astype(jnp.int32)
        meta_ref[images + i : images + i + 1, :] = here.astype(jnp.int32)
        begin = begin + here


def find_places(rows, cols, capacity, experts):
    count = cols.shape[0]
    images = count // PAD
    return pl.pallas_call(
        functools.partial(places_kernel, capacity),
        out_shape=[
            jax.ShapeDtypeStruct((images, experts, PAD), F32),
            jax.ShapeDtypeStruct((count, experts), F32),
            jax.ShapeDtypeStruct((2 * images, experts), jnp.int32),
        ],
        compiler_params=params(),
        cost_estimate=cost(2),
        name="places",
    )(rows, cols)


def spread_kernel(tok_ref, cot_ref, tpad_ref, cpad_ref):
    count, width = tok_ref.shape
    for source, target in ((tok_ref, tpad_ref), (cot_ref, cpad_ref)):
        for i in range(count // SEQ):
            rows = source[SEQ * i : SEQ * (i + 1), :].astype(F32)
            rows = jnp.concatenate([rows, jnp.zeros((PAD - SEQ, width), F32)], axis=0)
            target[PAD * i : PAD * (i + 1), :] = rows.astype(BF)


def spread_rows(tokens, cotangent):
    count, width = tokens.shape
    shape = jax.ShapeDtypeStruct((count // SEQ * PAD, width), BF)
    return pl.pallas_call(
        spread_kernel, out_shape=[shape, shape], compiler_params=params(), cost_estimate=cost(5), name="spread_rows"
    )(tokens, cotangent)


def store_image(target, i, values):
    for image in range(target.shape[0] // SEQ):

        @pl.when(i == image)
        def _(image=image):
            target[SEQ * image : SEQ * (image + 1), :] = values[0:SEQ, :]


def split_halves(block, halves):
    zero = jnp.zeros_like(block)
    return jnp.concatenate([jnp.where(halves, block, zero), jnp.where(halves, zero, block)], axis=0)


def attention_kernel(
    tok_ref, in_ref, out_ref, router_ref, gains_ref, ids_ref,
    proj_ref, prob_ref, mixed_ref, hidden_ref, routed_ref, gcol_ref, grow_ref, mixed_all,
):
    width = tok_ref.shape[1]
    x = tok_ref[...].astype(F32)
    normed, _ = normalize(x)
    entry = (normed * gains_ref[0:1, :] + gains_ref[1:2, :]).astype(BF)
    proj_ref[...] = dot_nn(entry, in_ref[...]).astype(BF)
    pair = 2 * HEAD
    halves = lane_iota(PAD, pair) < HEAD
    key_there = lane_iota(2 * PAD, PAD) < SEQ
    for p in range(HEADS // 2):
        q = proj_ref[:, pair * p : pair * (p + 1)] * jnp.asarray(HEAD ** -0.5, BF)
        k = proj_ref[:, width + pair * p : width + pair * (p + 1)]
        v = proj_ref[:, 2 * width + pair * p : 2 * width + pair * (p + 1)]
        scores = dot_nt(split_halves(q, halves), k)
        scores = jnp.where(key_there, scores, -1e30)
        peak = jnp.max(scores, axis=1, keepdims=True)
        raised = jnp.exp(scores - peak)
        total = jnp.sum(raised, axis=1, keepdims=True)
        weights = (raised * (1.0 / total)).astype(BF)
        prob_ref[0, 2 * p] = weights[:PAD]
        prob_ref[0, 2 * p + 1] = weights[PAD:]
        out = dot_nn(weights, v)
        mixed_all[:, pair * p : pair * (p + 1)] = jnp.where(halves, out[:PAD], out[PAD:]).astype(BF)
    mixed = mixed_all[...]
    mixed_ref[...] = mixed
    hidden = x + dot_nn(mixed, out_ref[...]) + gains_ref[4:5, :]
    hidden_ref[...] = hidden
    normed_two, _ = normalize(hidden)
    routed = (normed_two * gains_ref[2:3, :] + gains_ref[3:4, :]).astype(BF)
    routed_ref[...] = routed
    logits = dot_nt(routed, router_ref[...])
    experts = logits.shape[1]
    expert = lane_iota(PAD, experts)
    chosen = jnp.logical_or(ids_ref[:, 0:1] == expert, ids_ref[:, 1:2] == expert)
    top = jnp.max(jnp.where(chosen, logits, -1e30), axis=1, keepdims=True)
    raised = jnp.where(chosen, jnp.exp(jnp.where(chosen, logits - top, 0.0)), 0.0)
    total = jnp.sum(raised, axis=1, keepdims=True)
    gates = raised / jnp.where(total > 0.0, total, 1.0)
    gcol_ref[...] = gates
    grow_ref[0] = gates.T


def attention(tok_pad, in_matrix, out_matrix, router, gains, ids_col, after=()):
    padded, width = tok_pad.shape
    images = padded // PAD
    experts = router.shape[0]
    row = lambda lanes: pl.BlockSpec((PAD, lanes), lambda i: (i, 0))
    once = lambda a: pl.BlockSpec(a.shape, lambda i: (0, 0), pipeline_mode=pl.Buffered(1))
    return pl.pallas_call(
        behind(attention_kernel, 6, after),
        grid=(images,),
        in_specs=[row(width), once(in_matrix), once(out_matrix), once(router), once(gains), row(2)] + unread(after),
        out_specs=[
            row(3 * width),
            pl.BlockSpec((1, HEADS, PAD, PAD), lambda i: (i, 0, 0, 0)),
            row(width), row(width), row(width), row(experts),
            pl.BlockSpec((1, experts, PAD), lambda i: (i, 0, 0)),
        ],
        out_shape=[
            jax.ShapeDtypeStruct((padded, 3 * width), BF),
            jax.ShapeDtypeStruct((images, HEADS, PAD, PAD), BF),
            jax.ShapeDtypeStruct((padded, width), BF),
            jax.ShapeDtypeStruct((padded, width), F32),
            jax.ShapeDtypeStruct((padded, width), BF),
            jax.ShapeDtypeStruct((padded, experts), F32),
            jax.ShapeDtypeStruct((images, experts, PAD), F32),
        ],
        scratch_shapes=[pltpu.VMEM((PAD, width), BF)],
        compiler_params=params(),
        cost_estimate=cost(8),
        name="attention",
    )(tok_pad, in_matrix, out_matrix, router, gains, ids_col, *after)


def window_count():
    return -(-(15 + SEQ) // WIN)


def gather_kernel(meta_ref, routed_ref, cot_ref, lrow_ref, grow_ref, r_ref, g_ref, rt_ref, gt_ref, r_all, g_all):
    e = pl.program_id(0)
    images = lrow_ref.shape[0]
    listed = r_ref.shape[1]
    r_all[...] = jnp.zeros_like(r_all)
    g_all[...] = jnp.zeros_like(g_all)
    row = row_iota(WIN, PAD).astype(F32)
    for i in range(images):
        start, here = meta_ref[i, e], meta_ref[images + i, e]
        base = lax.shift_left(lax.shift_right_logical(start, 4), 4)
        shift = (start - base).astype(F32)
        local = lrow_ref[i, pl.ds(e, 1), :]
        gate = grow_ref[i, pl.ds(e, 1), :]
        for q in range(window_count()):
            @pl.when(jnp.logical_and(here > 0, base + q * WIN < start + here))
            def _(i=i, q=q, base=base, shift=shift, local=local, gate=gate):
                pick = jnp.logical_and(local >= 0.0, local + (shift - q * WIN) == row)
                low = pick.astype(F32).astype(BF)
                slot_gate = jnp.sum(jnp.where(pick, gate, 0.0), axis=1, keepdims=True)
                where = pl.ds(pl.multiple_of(base + q * WIN, 16), WIN)
                r_all[where, :] += dot_nn(low, routed_ref[i * PAD : (i + 1) * PAD, :])
                g_all[where, :] += slot_gate * dot_nn(low, cot_ref[i * PAD : (i + 1) * PAD, :])
    r_ref[0] = r_all[0:listed, :].astype(BF)
    g_ref[0] = g_all[0:listed, :].astype(BF)
    rt_ref[0] = r_all[0:listed, :].T.astype(BF)
    gt_ref[0] = g_all[0:listed, :].astype(BF).astype(F32).T.astype(BF)


def gather(meta, routed, cot_pad, lrow, grow, listed, after=()):
    width = routed.shape[1]
    experts = lrow.shape[1]
    once = lambda a: pl.BlockSpec(a.shape, lambda e, m: (0,) * a.ndim, pipeline_mode=pl.Buffered(1))
    block = pl.BlockSpec((1, listed, width), lambda e, m: (e, 0, 0))
    turned = pl.BlockSpec((1, width, listed), lambda e, m: (e, 0, 0))
    return pl.pallas_call(
        behind(gather_kernel, 5, after),
        grid_spec=pltpu.PrefetchScalarGridSpec(
            num_scalar_prefetch=1,
            grid=(experts,),
            in_specs=[once(routed), once(cot_pad), once(lrow), once(grow)] + unread(after),
            out_specs=[block, block, turned, turned],
            scratch_shapes=[pltpu.VMEM((listed + WIN, width), F32)] * 2,
        ),
        out_shape=[jax.ShapeDtypeStruct((experts, listed, width), BF)] * 2
        + [jax.ShapeDtypeStruct((experts, width, listed), BF)] * 2,
        compiler_params=params(),
        cost_estimate=cost(8),
        name="gather",
    )(meta, routed, cot_pad, lrow, grow, *after)


def gelu_both(pre):
    bell = jnp.exp(-0.5 * (pre * pre))
    t = pl.reciprocal(1.0 + (0.3275911 * 2.0**-0.5) * jnp.abs(pre))
    tail = t * (0.127414796 + t * (-0.142248368 + t * (0.7107068705 + t * (-0.7265760135 + t * 0.5307027145))))
    tail = tail * bell
    phi = jnp.where(pre < 0.0, tail, 1.0 - tail)
    return pre * phi, phi + pre * bell * 0.3989422804014327


def expert_kernel(first, half, at_ref, *refs):
    rep = 4
    (r_ref, g_ref, rt_ref, gt_ref), w_refs, b_ref, refs = refs[:4], refs[4:12], refs[12], refs[13:]
    if first:
        refs = refs[2 * (half > 0) :]
        y_ref, d_ref, near_ref, far_ref, db_ref, obg_ref, y_all, d_all = refs
    else:
        (ob_ref, y_in, d_in), refs = refs[:3], refs[3 + 2 * (half > 0) :]
        y_ref, d_ref, near_ref, far_ref, db_ref, y_all, d_all = refs
    listed = r_ref.shape[1]
    step = pl.program_id(0)
    count = at_ref[2 + lax.bitwise_xor(expert_rank(step, half), at_ref[1])]

    def run(n):
        rows_t, grads_t = rt_ref[0, :, :n], gt_ref[0, :, :n]

        def weights(r):
            place = lax.bitwise_xor(at_ref[0], r)
            return place, w_refs[r][0, 0], w_refs[rep + r][0, 0]

        def enter_part(r):
            place, enter, leave = weights(r)
            pre = dot_nn(r_ref[0, :n, :], enter) + b_ref[0, pl.ds(place, 1), :]
            return pre, dot_nn(g_ref[0, :n, :], leave)

        def middle_part(pre, grad_act):
            act, slope = gelu_both(pre)
            return act.astype(BF), (grad_act * slope).astype(BF)

        def leave_part(r, act, grad_pre):
            place, enter, leave = weights(r)
            out = far_ref if r % 2 else near_ref
            out[r // 2, 0, 0] = dot_nn(rows_t, grad_pre).astype(BF)
            out[r // 2, 0, 1] = dot_nn(grads_t, act).astype(BF)
            db_ref[0, pl.ds(place, 1), :] = jnp.sum(grad_pre.astype(F32), axis=0, keepdims=True)
            y_part = dot_nt(act, leave)
            d_part = dot_nt(grad_pre, enter)
            if r == 0:
                y_all[:n, :] = y_part if first else y_part + y_in[0, :n, :]
                d_all[:n, :] = d_part if first else d_part + d_in[0, :n, :]
            else:
                y_all[:n, :] += y_part
                d_all[:n, :] += d_part

        held = enter_part(0)
        ready = None
        for r in range(rep):
            now = middle_part(*held)
            if r + 1 < rep:
                held = enter_part(r + 1)
            if ready is not None:
                leave_part(r - 1, *ready)
            ready = now
        leave_part(rep - 1, *ready)
        if not first:
            y_ref[0, :n, :] = (y_all[:n, :] + ob_ref[0]).astype(BF)
            d_ref[0, :n, :] = d_all[:n, :].astype(BF)
        else:
            y_ref[0, :n, :] = y_all[:n, :]
            d_ref[0, :n, :] = d_all[:n, :]
        if n < listed:
            y_ref[0, n:, :] = jnp.zeros((listed - n, y_ref.shape[2]), y_ref.dtype)
            d_ref[0, n:, :] = jnp.zeros((listed - n, y_ref.shape[2]), y_ref.dtype)

    if first:
        obg_ref[0] = jnp.sum(g_ref[0].astype(F32), axis=0, keepdims=True)
    short = listed * 3 // 4 // 16 * 16
    pl.when(count <= short)(lambda: run(short))
    pl.when(count > short)(lambda: run(listed))


def expert_rank(step, half):
    return lax.shift_left(lax.bitwise_and(step, 3), 1) + lax.shift_right_logical(step, 2) + half


def expert_pass(at, lists, weights, bias, out_bias=None, carried=None, half=0, done=None, after=()):
    first = carried is None
    rows = lists[0]
    experts, listed, width = rows.shape
    rep, cols = bias.shape[1], bias.shape[2]
    steps = experts // 2
    here = lambda e, at: lax.bitwise_xor(expert_rank(e, half), at[1])
    block = pl.BlockSpec((1, listed, width), lambda e, at: (here(e, at), 0, 0))
    turned = pl.BlockSpec((1, width, listed), lambda e, at: (here(e, at), 0, 0))
    out_w = pl.BlockSpec((rep // 2, 1, 2, width, cols), lambda e, at: (0, e, 0, 0, 0))
    in_specs = [
        block, block, turned, turned,
        *[pl.BlockSpec((1, 1, width, cols), lambda e, at, m=m: (m, e, 0, 0)) for _, m in weights],
        pl.BlockSpec((1, rep, cols), lambda e, at: (here(e, at), 0, 0)),
    ]
    args = list(lists) + [a for a, _ in weights] + [bias]
    kind = F32 if first else BF
    out_specs = [block, block, out_w, out_w, pl.BlockSpec((1, rep, cols), lambda e, at: (here(e, at), 0, 0))]
    out_shape = [
        jax.ShapeDtypeStruct(rows.shape, kind),
        jax.ShapeDtypeStruct(rows.shape, kind),
        jax.ShapeDtypeStruct((rep // 2, steps, 2, width, cols), BF),
        jax.ShapeDtypeStruct((rep // 2, steps, 2, width, cols), BF),
        jax.ShapeDtypeStruct((experts, rep, cols), F32),
    ]
    aliases = {}
    if first:
        out_specs.append(pl.BlockSpec((1, 1, width), lambda e, at: (here(e, at), 0, 0)))
        out_shape.append(jax.ShapeDtypeStruct((experts, 1, width), F32))
    else:
        in_specs += [pl.BlockSpec((1, 1, width), lambda e, at: (here(e, at), 0, 0)), block, block]
        args += [out_bias, *carried]
    if half:
        aliases = {len(args) + 1: 0, len(args) + 2: 1}
        in_specs += unread(done)
        args += list(done)
    kernel = behind(functools.partial(expert_kernel, first, half), len(args) + 1, after)
    return pl.pallas_call(
        kernel,
        grid_spec=pltpu.PrefetchScalarGridSpec(
            num_scalar_prefetch=1,
            grid=(steps,),
            in_specs=in_specs + unread(after),
            out_specs=out_specs,
            scratch_shapes=[pltpu.VMEM((listed, width), F32)] * 2,
        ),
        out_shape=out_shape,
        input_output_aliases=aliases,
        compiler_params=params(),
        cost_estimate=cost(10),
        name=f"experts_{0 if first else 1}{half}",
    )(at, *args, *after)


def combine_kernel(
    meta_ref, y_ref, d_ref, lcol_ref, gcol_ref, hidden_ref, cot_ref, mixed_ref, out_w_ref, router_ref, gains_ref,
    out_ref, gh_ref, gm_ref, dout_ref, drouter_ref, dscale_ref, y_acc, g_acc, d_acc,
):
    i = pl.program_id(0)
    images = pl.num_programs(0)
    experts, listed, width = y_ref.shape
    gates = gcol_ref[...]
    local = lcol_ref[...]
    go = cot_ref[...].astype(F32)
    lane = lane_iota(PAD, WIN).astype(F32)
    expert = lane_iota(PAD, experts)

    def window(e, q, base, shift):
        at = jnp.minimum(base + q * WIN, listed - WIN)
        moved = (at - base).astype(F32)
        spot = local[:, e : e + 1] + shift
        pick = jnp.logical_and(spot == lane + moved, local[:, e : e + 1] >= 0.0)
        pick = jnp.logical_and(pick, spot >= q * WIN)
        low = pick.astype(F32).astype(BF)
        where = pl.ds(pl.multiple_of(at, 16), WIN)
        return dot_nn(low, y_ref[e, where, :]), dot_nn(low, d_ref[e, where, :])

    y_sum = jnp.zeros((PAD, width), F32)
    d_sum = jnp.zeros((PAD, width), F32)
    grad_gates = jnp.zeros((PAD, experts), F32)
    bases = []
    for e in range(experts):
        start = meta_ref[i, e]
        base = lax.shift_left(lax.shift_right_logical(start, 4), 4)
        bases.append((start, base))
        y_tok, d_tok = window(e, 0, base, (start - base).astype(F32))
        y_sum += gates[:, e : e + 1] * y_tok
        d_sum += d_tok
        gg = jnp.sum(go * y_tok, axis=1, keepdims=True)
        grad_gates += jnp.where(expert == e, gg, 0.0)
    y_acc[...] = y_sum
    d_acc[...] = d_sum
    g_acc[...] = grad_gates
    for e in range(experts):
        start, base = bases[e]
        here = meta_ref[images + i, e]
        for q in range(1, window_count()):
            @pl.when(base + q * WIN < start + here)
            def _(e=e, q=q, base=base, start=start):
                y_tok, d_tok = window(e, q, base, (start - base).astype(F32))
                y_acc[...] += gates[:, e : e + 1] * y_tok
                d_acc[...] += d_tok
                gg = jnp.sum(go * y_tok, axis=1, keepdims=True)
                g_acc[...] += jnp.where(expert == e, gg, 0.0)
    hidden = hidden_ref[...]
    y_acc[...] += hidden
    store_image(out_ref, i, y_acc)
    grad_gates = g_acc[...]
    pick = gates * (grad_gates - jnp.sum(gates * grad_gates, axis=1, keepdims=True))
    logit_low = pick.astype(BF)
    grad_routed = d_acc[...] + dot_nn(logit_low, router_ref[...])
    normed, inverse = normalize(hidden)
    routed = (normed * gains_ref[2:3, :] + gains_ref[3:4, :]).astype(BF)
    grad_hidden = go + norm_back(grad_routed, normed, inverse, gains_ref[2:3, :])
    gh_ref[...] = grad_hidden
    grad_mix = grad_hidden.astype(BF)
    gm_ref[...] = dot_nt(grad_mix, out_w_ref[...]).astype(BF)

    @pl.when(i == 0)
    def _():
        dout_ref[...] = jnp.zeros_like(dout_ref)
        drouter_ref[...] = jnp.zeros_like(drouter_ref)
        dscale_ref[...] = jnp.zeros_like(dscale_ref)

    dout_ref[...] += dot_tn(mixed_ref[...], grad_mix)
    drouter_ref[...] += dot_tn(logit_low, routed)
    dscale_ref[2:3, :] += jnp.sum(grad_routed * normed, axis=0, keepdims=True)
    dscale_ref[3:4, :] += jnp.sum(grad_routed, axis=0, keepdims=True)
    dscale_ref[4:5, :] += jnp.sum(grad_hidden, axis=0, keepdims=True)


def combine(meta, y, d, lcol, gcol, hidden, cot_pad, mixed, out_matrix, router, gains, after=()):
    padded, width = hidden.shape
    images = padded // PAD
    experts = y.shape[0]
    row = lambda lanes: pl.BlockSpec((PAD, lanes), lambda i, m: (i, 0))
    once = lambda a: pl.BlockSpec(a.shape, lambda i, m: (0,) * a.ndim, pipeline_mode=pl.Buffered(1))
    return pl.pallas_call(
        behind(combine_kernel, 11, after),
        grid_spec=pltpu.PrefetchScalarGridSpec(
            num_scalar_prefetch=1,
            grid=(images,),
            in_specs=[
                once(y), once(d), row(experts), row(experts), row(width), row(width), row(width),
                once(out_matrix), once(router), once(gains), *unread(after),
            ],
            out_specs=[
                whole((images * SEQ, width)), row(width), row(width), whole((width, width)), whole((experts, width)),
                whole((8, width)),
            ],
            scratch_shapes=[
                pltpu.VMEM((PAD, width), F32), pltpu.VMEM((PAD, experts), F32), pltpu.VMEM((PAD, width), F32),
            ],
        ),
        out_shape=[
            jax.ShapeDtypeStruct((images * SEQ, width), F32),
            jax.ShapeDtypeStruct((padded, width), F32),
            jax.ShapeDtypeStruct((padded, width), BF),
            jax.ShapeDtypeStruct((width, width), F32),
            jax.ShapeDtypeStruct((experts, width), F32),
            jax.ShapeDtypeStruct((8, width), F32),
        ],
        compiler_params=params(),
        cost_estimate=cost(40),
        name="combine",
    )(meta, y, d, lcol, gcol, hidden, cot_pad, mixed, out_matrix, router, gains, *after)


def attention_back_kernel(
    place_ref, proj_ref, prob_ref, gm_ref, gh_ref, tpad_ref, in_ref, gains_ref, dout_ref, small_ref,
    grad_ref, near_ref, far_ref, din_ref, dscale_ref, line_ref, dproj, grad_all,
):
    i = pl.program_id(0)
    width = gm_ref.shape[1]
    pair = 2 * HEAD
    halves = lane_iota(PAD, pair) < HEAD
    factor = HEAD ** -0.5
    for p in range(HEADS // 2):
        cut = slice(pair * p, pair * (p + 1))
        q = proj_ref[:, cut]
        k = proj_ref[:, width + pair * p : width + pair * (p + 1)]
        v = proj_ref[:, 2 * width + pair * p : 2 * width + pair * (p + 1)]
        gm = gm_ref[:, cut]
        gms = split_halves(gm, halves)
        low = jnp.concatenate([prob_ref[0, 2 * p], prob_ref[0, 2 * p + 1]], axis=0)
        probs = low.astype(F32)
        grad_probs = dot_nt(gms, v)
        middle = jnp.sum(probs * grad_probs, axis=1, keepdims=True)
        grad_scores = (probs * (grad_probs - middle)).astype(BF)
        grad_q = dot_nn(grad_scores, k)
        dproj[:, cut] = (jnp.where(halves, grad_q[:PAD], grad_q[PAD:]) * factor).astype(BF)
        dproj[:, width + pair * p : width + pair * (p + 1)] = (
            dot_tn(grad_scores, split_halves(q, halves)) * factor
        ).astype(BF)
        dproj[:, 2 * width + pair * p : 2 * width + pair * (p + 1)] = dot_tn(low, gms).astype(BF)
    normed, inverse = normalize(tpad_ref[...].astype(F32))
    entry = (normed * gains_ref[0:1, :] + gains_ref[1:2, :]).astype(BF)
    grads = dproj[...]
    grad_entry = dot_nt(grads, in_ref[...])

    @pl.when(i == 0)
    def _():
        din_ref[...] = jnp.zeros_like(din_ref)
        dscale_ref[...] = jnp.zeros_like(dscale_ref)

    din_ref[...] += dot_tn(entry, grads)
    dscale_ref[0:1, :] += jnp.sum(grad_entry * normed, axis=0, keepdims=True)
    dscale_ref[1:2, :] += jnp.sum(grad_entry, axis=0, keepdims=True)
    grad = gh_ref[...] + norm_back(grad_entry, normed, inverse, gains_ref[0:1, :])
    grad_all[...] = grad
    store_image(grad_ref, i, grad_all)

    @pl.when(i == pl.num_programs(0) - 1)
    def _():
        blocks, rows = 2 * near_ref.shape[0], near_ref.shape[1]
        owner = lane_iota(blocks, width) // rows == row_iota(blocks, width)
        spot = row_iota(width, 128) % rows
        line = jnp.zeros((blocks, 128), F32)
        for s in range(2):
            spread = jnp.where(owner, dscale_ref[s : s + 1, :], 0.0)
            chosen = (lane_iota(width, 128) == spot + s * rows).astype(F32)
            line += lax.dot_general(
                spread, chosen, (((1,), (0,)), ((), ())),
                preferred_element_type=F32, precision=lax.Precision.HIGHEST,
            )
        line_ref[...] = line
        scale_row = row_iota(8, 128) == 6
        for side, out in ((0, near_ref), (1, far_ref)):
            def body(j, carry, side=side, out=out):
                place = place_ref[side * (blocks // 2) + j]
                here = pl.ds(pl.multiple_of(place * rows, rows), rows)
                out[j, :, : 3 * width] = din_ref[here, :].astype(BF)
                out[j, :, 3 * width : 4 * width] = dout_ref[here, :].astype(BF)
                small = small_ref[place] + jnp.where(scale_row, line_ref[pl.ds(place, 1), :], 0.0)
                out[j, :, 4 * width :] = resplit(small)
                return carry

            lax.fori_loop(0, blocks // 2, body, 0)


def attention_back(place, proj, probs, grad_mixed, grad_hidden, tok_pad, in_matrix, gains, grad_out, small, after=()):
    padded, width = grad_hidden.shape
    images = padded // PAD
    blocks = small.shape[0]
    rows = width // blocks
    row = lambda lanes: pl.BlockSpec((PAD, lanes), lambda i, m: (i, 0))
    once = lambda a: pl.BlockSpec(a.shape, lambda i, m: (0,) * a.ndim, pipeline_mode=pl.Buffered(1))
    half = (blocks // 2, rows, 4 * width + 128)
    return pl.pallas_call(
        behind(attention_back_kernel, 10, after),
        grid_spec=pltpu.PrefetchScalarGridSpec(
            num_scalar_prefetch=1,
            grid=(images,),
            in_specs=[
                row(3 * width), pl.BlockSpec((1, HEADS, PAD, PAD), lambda i, m: (i, 0, 0, 0)), row(width), row(width),
                row(width), once(in_matrix), once(gains), once(grad_out), once(small),
                *unread(after),
            ],
            out_specs=[whole((images * SEQ, width)), whole(half), whole(half)],
            scratch_shapes=[
                pltpu.VMEM((width, 3 * width), F32), pltpu.VMEM((8, width), F32), pltpu.VMEM((blocks, 128), F32),
                pltpu.VMEM((PAD, 3 * width), BF), pltpu.VMEM((PAD, width), F32),
            ],
        ),
        out_shape=[
            jax.ShapeDtypeStruct((images * SEQ, width), F32),
            jax.ShapeDtypeStruct(half, BF),
            jax.ShapeDtypeStruct(half, BF),
        ],
        compiler_params=params(),
        cost_estimate=cost(50),
        name="attention_back",
    )(place, proj, probs, grad_mixed, grad_hidden, tok_pad, in_matrix, gains, grad_out, small, *after)


X_BIT, CORE_BIT, Y_BIT = 16, 8, 1
Z_BITS = (2, 4, 6)
AXES = ("rep", "ep")


def swap(array, bits):
    devices = lax.axis_size("rep") * lax.axis_size("ep")
    return lax.ppermute(array, AXES, [(d, d ^ bits) for d in range(devices)])


def relative(position):
    c, x, y, z = position >> 4 & 1, position >> 3 & 1, position >> 2 & 1, position & 3
    return x * X_BIT + c * CORE_BIT + z * 2 + y * Y_BIT


def stack_kernel(count, *refs):
    for j in range(count):
        refs[count][j] = refs[j][...]


def stack(arrays, after=()):
    count = len(arrays)
    return pl.pallas_call(
        behind(functools.partial(stack_kernel, count), count, after),
        in_specs=[pl.BlockSpec(memory_space=pltpu.VMEM)] * count + unread(after),
        out_shape=jax.ShapeDtypeStruct((count,) + arrays[0].shape, arrays[0].dtype),
        compiler_params=params(),
        cost_estimate=cost(1),
        name="stack",
    )(*arrays, *after)


def turn_stack_kernel(*refs):
    for m in range(2):
        for j in range(4):
            refs[4][m, j] = refs[j][m]


def turn_stack(arrays, after=()):
    piece = arrays[0].shape
    return pl.pallas_call(
        behind(turn_stack_kernel, 4, after),
        in_specs=[pl.BlockSpec(memory_space=pltpu.VMEM)] * 4 + unread(after),
        out_shape=jax.ShapeDtypeStruct((2, 4) + piece[1:], arrays[0].dtype),
        compiler_params=params(),
        cost_estimate=cost(2),
        name="turn_stack",
    )(*arrays, *after)


def pick_kernel(far_x, far_y, x_in, x_out, y_out):
    x_in[0] = far_x[0]
    x_out[0] = far_x[1]
    y_out[0] = far_y[1]


def pick(far_x, far_y, after=()):
    shape = (1,) + far_x.shape[1:]
    return pl.pallas_call(
        behind(pick_kernel, 2, after),
        in_specs=[pl.BlockSpec(memory_space=pltpu.VMEM)] * 2 + unread(after),
        out_shape=[jax.ShapeDtypeStruct(shape, far_x.dtype)] * 3,
        compiler_params=params(),
        cost_estimate=cost(3),
        name="pick",
    )(far_x, far_y, *after)


def sum_everywhere(values):
    for bits in (CORE_BIT, Y_BIT, X_BIT, 2, 4):
        values = values + swap(values, bits)
    return values


def unsplit(block):
    return block[:8] + block[8:]


def resplit(small):
    twice = jnp.concatenate([small, small], axis=0)
    high = twice.astype(BF).astype(F32)
    return jnp.where(row_iota(16, 128) < 8, high, twice - high).astype(BF)


def block_sum_kernel(parts, terms, *refs):
    ins, outs = refs[:terms], refs[terms:]
    size = ins[0].shape[0] // parts
    lanes = ins[0].shape[2]
    for p in range(parts):
        for j in range(size):
            at = p * size + j
            total = ins[0][at].astype(F32)
            for t in ins[1:]:
                total = total + t[at].astype(F32)
            small = unsplit(total[:, lanes - 128 :])
            outs[p][j, :, : lanes - 128] = total[:, : lanes - 128].astype(BF)
            outs[p][j, :, lanes - 128 :] = resplit(small)


def block_sum(terms, parts):
    size = terms[0].shape[0] // parts
    shape = (size,) + terms[0].shape[1:]
    return pl.pallas_call(
        functools.partial(block_sum_kernel, parts, len(terms)),
        out_shape=[jax.ShapeDtypeStruct(shape, BF)] * parts,
        compiler_params=params(),
        name="block_sum",
    )(*terms)


def scatter_dense(near, far):
    parts = block_sum([near, swap(far, CORE_BIT)], 4)
    got = [swap(parts[1], Y_BIT), swap(parts[2], X_BIT), swap(parts[3], X_BIT | Y_BIT)]
    parts = block_sum([parts[0]] + got, 4)
    return [parts[0]] + [swap(parts[z], Z_BITS[z - 1]) for z in (1, 2, 3)]


def fold_cores_kernel(n0, n1, g0, g1, a_keep, b_keep, a_send, b_send):
    for x in range(2):
        a_keep[x, 0] = n0[x, 0, 0] + g0[x, 0, 0]
        a_send[x, 0] = n1[x, 0, 0] + g1[x, 0, 0]
        out = b_send if x else b_keep
        out[0, 0] = n0[x, 0, 1] + g0[x, 0, 1]
        out[1, 0] = n1[x, 0, 1] + g1[x, 0, 1]


def fold_cores(near, got):
    rows, cols = near[0].shape[3:]
    out = jax.ShapeDtypeStruct((2, 4, rows, cols), BF)
    return pl.pallas_call(
        fold_cores_kernel,
        grid=(4,),
        in_specs=[pl.BlockSpec((2, 1, 2, rows, cols), lambda z: (0, z, 0, 0, 0))] * 4,
        out_specs=[pl.BlockSpec((2, 1, rows, cols), lambda z: (0, z, 0, 0))] * 4,
        out_shape=[out] * 4,
        compiler_params=params(),
        cost_estimate=cost(7),
        name="fold_cores",
    )(*near, *got)


def fold_first_kernel(a_keep, b_keep, a_got, b_got, a_near, b_near, a_far, b_far):
    a_near[0] = a_keep[0, 0] + a_got[0, 0]
    b_near[0] = b_keep[0, 0] + b_got[0, 0]
    a_far[0] = a_keep[1, 0] + a_got[1, 0]
    b_far[0] = b_keep[1, 0] + b_got[1, 0]


def fold_first(a_keep, b_keep, a_got, b_got, after=()):
    rows, cols = a_keep.shape[2:]
    return pl.pallas_call(
        behind(fold_first_kernel, 4, after),
        grid=(4,),
        in_specs=[pl.BlockSpec((2, 1, rows, cols), lambda z: (0, z, 0, 0))] * 4 + unread(after),
        out_specs=[pl.BlockSpec((1, rows, cols), lambda z: (z, 0, 0))] * 4,
        out_shape=[jax.ShapeDtypeStruct((4, rows, cols), BF)] * 4,
        compiler_params=params(),
        cost_estimate=cost(4),
        name="fold_first",
    )(a_keep, b_keep, a_got, b_got, *after)


def fold_second_kernel(a_keep, b_keep, a_got, b_got, *parts):
    for z in range(4):
        parts[z][0] = a_keep[z] + a_got[z]
        parts[z][1] = b_keep[z] + b_got[z]


def fold_second(a_keep, b_keep, a_got, b_got):
    return pl.pallas_call(
        fold_second_kernel,
        out_shape=[jax.ShapeDtypeStruct((2,) + a_keep.shape[1:], BF)] * 4,
        compiler_params=params(),
        cost_estimate=cost(3),
        name="fold_second",
    )(a_keep, b_keep, a_got, b_got)


def total_of(array):
    return jnp.sum(jnp.sum(array, axis=1, keepdims=True), axis=0, keepdims=True)


def expert_update_kernel(*refs):
    parts, (wi, fi, si, wo, fo, so), outs = refs[:8], refs[8:14], refs[14:]
    sums = outs[6]
    lane = lane_iota(1, 128)
    kept = jnp.zeros((1, 128), F32)
    moved = jnp.zeros((1, 128), F32)
    cols = parts[0].shape[2]
    for m, (weight, first, second, new) in enumerate(((wi, fi, si, outs[0:3]), (wo, fo, so, outs[3:6]))):
        for k in range(2):
            grad = parts[4 * k][m].astype(F32)
            for part in parts[4 * k + 1 : 4 * k + 4]:
                grad = grad + part[m].astype(F32)
            span = slice(k * cols, (k + 1) * cols)
            if m == 0:
                at = (0, slice(None), span)
            else:
                grad = grad.T
                at = (0, span, slice(None))
            state = moments(weight[at], grad, first[at], second[at])
            for ref, value in zip(new, state):
                ref[at] = value
            slot = lane == (8 if m == 0 else 10)
            kept += jnp.where(slot, total_of(weight[at] * weight[at]), 0.0)
            moved += jnp.where(slot, total_of(state[2] * state[2]), 0.0)
    sums[...] = jnp.zeros_like(sums)
    sums[0:1, :] = kept
    sums[1:2, :] = moved


def expert_update(parts, arrays):
    shape = jax.ShapeDtypeStruct(arrays[0].shape, F32)
    return pl.pallas_call(
        expert_update_kernel,
        out_shape=[shape] * 6 + [jax.ShapeDtypeStruct((8, 128), F32)],
        compiler_params=params(),
        cost_estimate=cost(6),
        name="expert_update",
    )(*parts, *arrays)


def narrow(row, columns, rows):
    spread = jnp.where(lane_iota(rows, 128) % rows == row_iota(rows, 128), row, 0.0)
    chosen = (row_iota(128, columns) // rows == lane_iota(128, columns)).astype(F32)
    return lax.dot_general(
        spread, chosen, (((1,), (0,)), ((), ())), preferred_element_type=F32, precision=lax.Precision.HIGHEST
    )


def dense_update_kernel(*refs):
    ins, sums, states, outs = refs[:4], refs[4], refs[5:23], refs[23:]
    width = ins[0].shape[2] - 128
    total = ins[0][0].astype(F32)
    for t in ins[1:]:
        total = total + t[0].astype(F32)
    small = unsplit(total[:, width:])
    experts, rows = states[6].shape[1], states[6].shape[0]
    bias_rows = states[12].shape[1] // 128
    grads = (
        total[:, : width * 3 // 4],
        total[:, width * 3 // 4 : width],
        narrow(small[bias_rows + 1 : bias_rows + 2], experts, rows),
        narrow(small[bias_rows + 2 : bias_rows + 3], 5, rows),
        jnp.concatenate([small[j : j + 1] for j in range(bias_rows)], axis=1),
        small[bias_rows : bias_rows + 1],
    )
    lane = lane_iota(1, 128)
    kept, moved = sums[0:1, :], sums[1:2, :]
    for j, grad in enumerate(grads):
        weight, first, second = (states[3 * j + k][...] for k in range(3))
        state = moments(weight, grad, first, second)
        for k in range(3):
            outs[3 * j + k][...] = state[k]
        for c, slot in enumerate({0: (0,), 1: (1,), 2: (2,), 3: (3, 4, 5, 6, 7), 4: (9,), 5: (11,)}[j]):
            cut = (slice(None), slice(c, c + 1)) if j == 3 else (slice(None), slice(None))
            kept += jnp.where(lane == slot, total_of(weight[cut] * weight[cut]), 0.0)
            moved += jnp.where(lane == slot, total_of(state[2][cut] * state[2][cut]), 0.0)
    outs[18][...] = jnp.zeros_like(outs[18])
    outs[18][0:1, :] = kept
    outs[18][1:2, :] = moved


def dense_update(terms, sums, states):
    return pl.pallas_call(
        dense_update_kernel,
        out_shape=[jax.ShapeDtypeStruct(a.shape, F32) for a in states] + [jax.ShapeDtypeStruct((8, 128), F32)],
        compiler_params=params(),
        cost_estimate=cost(3),
        name="dense_update",
    )(*terms, sums, *states)


def new_weights_kernel(sums, counts, *refs):
    weights, steps, outs, norms = refs[:8], refs[8:16], refs[16:24], refs[24]
    weight_rms = jnp.sqrt(sums[0:1, :] / counts[...])
    step_rms = jnp.sqrt(sums[1:2, :] / counts[...])
    trust = weight_rms / step_rms
    norms[...] = jnp.zeros_like(norms)
    norms[0:1, :] = weight_rms
    norms[1:2, :] = step_rms
    norms[2:3, :] = trust
    for j, begin in enumerate((0, 1, 2, 3, 8, 9, 10, 11)):
        scale = trust[:, 3:8] if j == 3 else trust[:, begin : begin + 1]
        if len(outs[j].shape) == 3:
            outs[j][0] = weights[j][0] - RATE * scale * steps[j][0]
        else:
            outs[j][...] = weights[j][...] - RATE * scale * steps[j][...]


def new_weights(sums, counts, weights, steps):
    return pl.pallas_call(
        new_weights_kernel,
        out_shape=[jax.ShapeDtypeStruct(a.shape, F32) for a in weights] + [jax.ShapeDtypeStruct((8, 128), F32)],
        compiler_params=params(),
        cost_estimate=cost(5),
        name="new_weights",
    )(sums, counts, *weights, *steps)


CHUNKS = 2


def replicate_plan(
    tokens, cotangent, expert_ids, priority,
    heads_in, heads_in_first, heads_in_second, heads_out, heads_out_first, heads_out_second,
    router, router_first, router_second, scales, scales_first, scales_second,
    expert_in, expert_in_first, expert_in_second, bias_in, bias_in_first, bias_in_second,
    expert_out, expert_out_first, expert_out_second, bias_out, bias_out_first, bias_out_second,
):
    count, width = tokens.shape
    images = count // SEQ
    experts = router.shape[1]
    rep, ep = lax.axis_size("rep"), lax.axis_size("ep")
    rep_me, ep_me = lax.axis_index("rep"), lax.axis_index("ep")
    me = (rep_me * ep + ep_me).astype(jnp.int32)
    at = jnp.stack([rep_me, ep_me]).astype(jnp.int32)
    capacity = (5 * expert_ids.shape[1] * count + 4 * experts - 1) // (4 * experts)
    listed = -(-capacity // 16) * 16
    hidden_part = FF // rep
    cols = hidden_part // CHUNKS

    enter_low = expert_in[0].astype(BF)
    leave_low = expert_out[0].astype(BF).T
    pieces = [
        jnp.stack([enter_low[:, k * cols : (k + 1) * cols], leave_low[:, k * cols : (k + 1) * cols]])
        for k in range(CHUNKS)
    ]

    rows_here = heads_in.shape[0]
    small = jnp.concatenate([router, scales], axis=1)
    small = jnp.pad(small, ((0, 0), (0, 128 - small.shape[1])))
    biases = jnp.concatenate([bias_in.reshape(-1, 128), bias_out.reshape(-1, 128)], axis=0)
    biases = jnp.pad(biases, ((0, rows_here - biases.shape[0]), (0, 0)))
    dense = jnp.concatenate([heads_in, heads_out, small, biases], axis=1).astype(BF)
    order = jnp.array([relative(p) for p in range(rep * ep)], jnp.int32)
    place = jnp.bitwise_xor(order, me)
    spread = lambda a, fill: jnp.pad(
        a.reshape(-1, images, SEQ), ((0, 0), (0, 0), (0, PAD - SEQ)), constant_values=fill
    ).reshape(-1, images * PAD)
    ids_rows = spread(expert_ids.T, -1)
    rows = jnp.concatenate([spread(priority, count), ids_rows], axis=0).astype(F32)
    rows = jnp.pad(rows, ((0, 5), (0, 0)))

    zs_got = [swap(dense, bits) for bits in Z_BITS]
    tok_pad, cot_pad = spread_rows(tokens, cotangent)
    zs = stack([dense] + zs_got, after=(tok_pad,))
    zs, pieces[0] = lax.optimization_barrier((zs, pieces[0]))
    others = [swap(zs, bits) for bits in (Y_BIT, X_BIT, X_BIT | Y_BIT)]
    lrow, lcol, meta = find_places(rows, rows.T, capacity, experts)
    piece_got = [swap(pieces[0], bits) for bits in Z_BITS]
    plane = stack([zs] + others, after=(lrow, piece_got[0]))
    in_matrix, out_matrix, router_matrix, gains, small_all = assemble(
        place, plane.reshape((16,) + dense.shape), swap(plane, CORE_BIT).reshape((16,) + dense.shape), experts
    )
    bias_all = small_all[:, 128:].reshape(rep, ep, rows_here, 128)
    in_rows = hidden_part // 128
    enter_bias = bias_all[:, :, :in_rows].reshape(rep, ep, hidden_part).astype(F32).transpose(1, 0, 2)
    leave_bias = bias_all[:, :, in_rows].astype(F32).transpose(1, 0, 2).reshape(ep, 1, width)

    proj, probs, mixed, hidden, routed, gcol, grow = attention(
        tok_pad, in_matrix, out_matrix, router_matrix, gains, ids_rows.T
    )
    near = turn_stack([pieces[0]] + piece_got, after=(gcol,))
    far_x, far_y = swap(near, X_BIT), swap(near, Y_BIT)
    near, pieces[1] = lax.optimization_barrier((near, pieces[1]))
    lists = gather(meta, routed, cot_pad, lrow, grow, listed, after=(near,))
    near_two = turn_stack([pieces[1]] + [swap(pieces[1], bits) for bits in Z_BITS], after=(lists[0],))

    totals_here = meta[images - 1] + meta[2 * images - 1]
    at = jnp.concatenate([at, totals_here])
    bias_cut = lambda k: enter_bias[:, :, k * cols : (k + 1) * cols]
    cross = lambda a: swap(a, CORE_BIT)

    def first_half(near, far_x, crossed):
        pairs = []
        for m in range(2):
            other = (crossed[1][m], 0) if isinstance(crossed[1], tuple) else (crossed[1], m)
            pairs += [(near, m), (crossed[0], m), (far_x, m), other]
        return pairs

    def other_half(far_y, far_xy, crossed):
        return [
            pair
            for m in range(2)
            for pair in ((far_y, m), (crossed[0], m), (far_xy[m], 0), (crossed[1 + m], 0))
        ]

    x_in, x_out, y_out = pick(far_x, far_y, after=(near_two,))
    far_xy = swap(x_in, Y_BIT), swap(y_out, X_BIT)
    near, x_in = lax.optimization_barrier((near, x_in))
    crossed = cross(near), (cross(x_in), cross(x_out))
    y_part, d_part, near_a, far_a, bias_a, leave_a = expert_pass(
        at, lists, first_half(near, far_x, crossed), bias_cut(0), after=far_xy
    )
    near_two, *far_xy = lax.optimization_barrier((near_two, *far_xy))
    far_x_two, far_y_two = swap(near_two, X_BIT), swap(near_two, Y_BIT)
    crossed = cross(far_y), cross(far_xy[0]), cross(far_xy[1])
    y_half, d_half, near_b, far_b, bias_b, leave_b = expert_pass(
        at, lists, other_half(far_y, far_xy, crossed), bias_cut(0), half=1, done=(y_part, d_part),
    )
    got_a = swap(far_a, CORE_BIT)
    far_b, far_x_two, far_y_two = lax.optimization_barrier((far_b, far_x_two, far_y_two))
    crossed = cross(near_two), cross(far_x_two)
    got_b = swap(far_b, CORE_BIT)
    one = fold_cores((near_a, near_b), (got_a, got_b))
    a_send, far_x_two, far_y_two = lax.optimization_barrier((one[2], far_x_two, far_y_two))
    one = (*one[:2], a_send, one[3])
    far_xy_two = swap(far_x_two[0:1], Y_BIT), swap(far_y_two[1:2], X_BIT)
    even = lax.bitwise_xor(jnp.arange(ep, dtype=jnp.int32), ep_me)[:, None, None] % 2 == 0
    grad_bias = [jnp.where(even, bias_a, bias_b)]
    grad_leave_bias = jnp.where(even, leave_a, leave_b)
    one_got = swap(one[2], Y_BIT), swap(one[3], X_BIT)
    y_part, d_part, near_a, far_a, bias_a = expert_pass(
        at, lists, first_half(near_two, far_x_two, crossed), bias_cut(1), leave_bias, (y_half, d_half),
        after=one[2:],
    )
    y_part, *far_xy_two = lax.optimization_barrier((y_part, *far_xy_two))
    crossed = cross(far_y_two), cross(far_xy_two[0]), cross(far_xy_two[1])
    got_a = swap(far_a, CORE_BIT)
    y, d, near_b, far_b, bias_b = expert_pass(
        at, lists, other_half(far_y_two, far_xy_two, crossed), bias_cut(1), leave_bias, (y_half, d_half), half=1,
        done=(y_part, d_part),
    )
    one = fold_first(*one[:2], *one_got)
    one_got = swap(one[2], X_BIT), swap(one[3], Y_BIT)
    got_b = swap(far_b, CORE_BIT)
    output, grad_hidden, grad_mixed, grad_out, grad_router, grad_scale = combine(
        meta, y, d, lcol, gcol, hidden, cot_pad, mixed, out_matrix, router_matrix, gains,
        after=one,
    )
    one = fold_second(*one[:2], *one_got)
    two = fold_cores((near_a, near_b), (got_a, got_b))
    grad_bias.append(jnp.where(even, bias_a, bias_b))
    devices = rep * ep
    by_device = lambda a: jnp.pad(
        a.reshape(a.shape[0], devices, rows_here).transpose(1, 0, 2).reshape(devices, 1, -1),
        ((0, 0), (0, 0), (0, 128 - a.shape[0] * rows_here)),
    )
    small_grads = jnp.concatenate(
        [
            jnp.concatenate(grad_bias, axis=2).transpose(1, 0, 2).reshape(devices, in_rows, 128),
            grad_leave_bias.reshape(ep, rep, 128).transpose(1, 0, 2).reshape(devices, 1, 128),
            by_device(grad_router),
            by_device(grad_scale[:5]),
        ],
        axis=1,
    )
    small_grads = jnp.pad(small_grads, ((0, 0), (0, 8 - small_grads.shape[1]), (0, 0)))
    one_got = [swap(one[z], Z_BITS[z - 1]) for z in (1, 2, 3)]
    two_got = swap(two[2], Y_BIT), swap(two[3], X_BIT)
    input_grad, near_dense, far_dense = attention_back(
        place, proj, probs, grad_mixed, grad_hidden, tok_pad, in_matrix, gains, grad_out, small_grads,
        after=list(one[1:]) + list(two[2:]),
    )
    two = fold_first(*two[:2], *two_got, after=one_got)
    two_got = swap(two[2], X_BIT), swap(two[3], Y_BIT)
    dense_terms = scatter_dense(near_dense, far_dense)
    two = fold_second(*two[:2], *two_got)
    two_got = [swap(two[z], Z_BITS[z - 1]) for z in (1, 2, 3)]
    parts = [one[0]] + one_got + [two[0]] + two_got
    (in_first, in_second, in_step, out_first, out_second, out_step, sums) = expert_update(
        parts, (expert_in, expert_in_first, expert_in_second, expert_out, expert_out_first, expert_out_second)
    )
    dense_states = (
        heads_in, heads_in_first, heads_in_second, heads_out, heads_out_first, heads_out_second,
        router, router_first, router_second, scales, scales_first, scales_second,
        bias_in, bias_in_first, bias_in_second, bias_out, bias_out_first, bias_out_second,
    )
    *dense_new, sums = dense_update(dense_terms, sums, dense_states)
    sums = sum_everywhere(sums)
    counts = jnp.array(
        [3 * width * width, width * width, width * experts]
        + [width] * 5
        + [experts * width * FF, experts * FF, experts * FF * width, experts * width]
        + [1] * (128 - 12),
        jnp.float32,
    )[None]
    trio = lambda j: tuple(dense_new[3 * j : 3 * j + 3])
    states = [
        trio(0), trio(1), trio(2), trio(3), (in_first, in_second, in_step), trio(4),
        (out_first, out_second, out_step), trio(5),
    ]
    weights_now = (heads_in, heads_out, router, scales, expert_in, bias_in, expert_out, bias_out)
    *fresh, norms = new_weights(sums, counts, weights_now, [state[2] for state in states])
    results = [output, input_grad]
    for state, weight in zip(states, fresh):
        results.extend([state[0], state[1], weight])
    results.append(norms[:3, :12])
    return tuple(results)


def expert_front(rows, enter_weight, enter_bias):
    pre = jnp.einsum("sjcd,jdf->sjcf", rows, enter_weight, preferred_element_type=jnp.float32)
    return pre + enter_bias.astype(jnp.float32)[None, :, None, :]


def exchange_plan(
    tokens,
    cotangent,
    expert_ids,
    priority,
    heads_in,
    heads_in_first,
    heads_in_second,
    heads_out,
    heads_out_first,
    heads_out_second,
    router,
    router_first,
    router_second,
    scales,
    scales_first,
    scales_second,
    expert_in,
    expert_in_first,
    expert_in_second,
    bias_in,
    bias_in_first,
    bias_in_second,
    expert_out,
    expert_out_first,
    expert_out_second,
    bias_out,
    bias_out_first,
    bias_out_second,
):
    in_matrix, out_matrix, router_matrix, scale_table = (
        lax.all_gather(heads_in.astype(jnp.bfloat16), ("rep", "ep"), axis=0, tiled=True),
        lax.all_gather(heads_out.astype(jnp.bfloat16), ("rep", "ep"), axis=0, tiled=True),
        lax.all_gather(router.astype(jnp.bfloat16), ("rep", "ep"), axis=0, tiled=True),
        lax.all_gather(scales.astype(jnp.bfloat16), ("rep", "ep"), axis=0, tiled=True),
    )
    enter_weight, enter_bias, leave_weight, leave_bias = (
        lax.all_gather(expert_in.astype(jnp.bfloat16), "rep", axis=2, tiled=True),
        lax.all_gather(bias_in.astype(jnp.bfloat16), "rep", axis=1, tiled=True),
        lax.all_gather(expert_out.astype(jnp.bfloat16), "rep", axis=1, tiled=True),
        lax.all_gather(bias_out.astype(jnp.bfloat16), "rep", axis=1, tiled=True),
    )
    gains = scale_table.astype(jnp.float32)
    inputs = tokens.astype(jnp.float32)
    count, width = inputs.shape
    images = count // SEQ
    factor = HEAD ** (-0.5)
    normed_one, inverse_one = normalize(inputs)
    entry = (normed_one * gains[:, 0] + gains[:, 1]).astype(jnp.bfloat16)
    projected = jnp.dot(entry, in_matrix, preferred_element_type=jnp.float32).astype(jnp.bfloat16)
    grid = projected.reshape(images, SEQ, 3, HEADS, HEAD)
    query = grid[:, :, 0]
    keyed = grid[:, :, 1]
    valued = grid[:, :, 2]
    scores = attention_scores(query, keyed, factor)
    peak = jnp.max(scores, axis=-1, keepdims=True)
    log_total = peak + jnp.log(jnp.sum(jnp.exp(scores - peak), axis=-1, keepdims=True))
    weights = jnp.exp(scores - log_total).astype(jnp.bfloat16)
    mixed = jnp.einsum("bhqk,bkhd->bqhd", weights, valued, preferred_element_type=jnp.float32)
    mixed = mixed.reshape(count, width).astype(jnp.bfloat16)
    hidden = inputs + jnp.dot(mixed, out_matrix, preferred_element_type=jnp.float32) + gains[:, 4]
    normed_two, inverse_two = normalize(hidden)
    routed = (normed_two * gains[:, 2] + gains[:, 3]).astype(jnp.bfloat16)
    logits = jnp.dot(routed, router_matrix, preferred_element_type=jnp.float32)
    experts = logits.shape[1]
    top = expert_ids.shape[1]
    choose = (expert_ids[:, :, None] == jnp.arange(experts, dtype=jnp.int32)[None, None, :]).astype(
        jnp.float32
    )
    picked = jnp.sum(choose * logits[:, None, :], axis=2)
    gates = jax.nn.softmax(picked, axis=1)
    places = route_places(expert_ids, priority[0], experts)
    capacity = (5 * top * count + 4 * experts - 1) // (4 * experts)
    groups = lax.axis_size("ep")
    local = experts // groups
    slots = experts * capacity
    slot = jnp.where(places < capacity, expert_ids * capacity + places, slots)
    pair_of_slot = (
        jnp.full((slots,), count * top, jnp.int32)
        .at[slot.reshape(-1)]
        .set(jnp.arange(count * top, dtype=jnp.int32), mode="drop")
    )
    token_of_slot = pair_of_slot // top
    padded_rows = jnp.concatenate([routed, jnp.zeros((1, width), jnp.bfloat16)], axis=0)
    outgoing = padded_rows[token_of_slot].reshape(groups, local, capacity, width)
    arrived = lax.all_to_all(outgoing, "ep", split_axis=0, concat_axis=0, tiled=True)
    pre = expert_front(arrived, enter_weight, enter_bias)
    act, gelu_back = jax.vjp(exact_gelu, pre)
    act_low = act.astype(jnp.bfloat16)
    result = jnp.einsum("sjcf,jfd->sjcd", act_low, leave_weight, preferred_element_type=jnp.float32)
    result = (result + leave_bias.astype(jnp.float32)[None, :, None, :]).astype(jnp.bfloat16)
    returned = lax.all_to_all(result, "ep", split_axis=0, concat_axis=0, tiled=True).reshape(
        slots, width
    )
    padded_back = jnp.concatenate([returned, jnp.zeros((1, width), jnp.bfloat16)], axis=0)
    picked_rows = padded_back[slot].astype(jnp.float32)
    output = hidden + jnp.sum(gates[:, :, None] * picked_rows, axis=1)
    grad_output = cotangent.astype(jnp.float32)
    grad_gates = jnp.sum(picked_rows * grad_output[:, None, :], axis=2)
    gate_list = jnp.concatenate([gates.reshape(-1), jnp.zeros((1,), jnp.float32)])
    padded_grad = jnp.concatenate([grad_output, jnp.zeros((1, width), jnp.float32)], axis=0)
    grad_slots = (padded_grad[token_of_slot] * gate_list[pair_of_slot][:, None]).astype(
        jnp.bfloat16
    )
    grad_arrived = lax.all_to_all(
        grad_slots.reshape(groups, local, capacity, width),
        "ep",
        split_axis=0,
        concat_axis=0,
        tiled=True,
    )
    grad_act = jnp.einsum(
        "sjcd,jfd->sjcf", grad_arrived, leave_weight, preferred_element_type=jnp.float32
    )
    grad_pre = gelu_back(grad_act)[0].astype(jnp.bfloat16)
    grad_leave = jnp.einsum(
        "sjcf,sjcd->jfd", act_low, grad_arrived, preferred_element_type=jnp.float32
    )
    grad_leave_bias = jnp.sum(grad_arrived, axis=(0, 2), dtype=jnp.float32)
    grad_enter = jnp.einsum("sjcd,sjcf->jdf", arrived, grad_pre, preferred_element_type=jnp.float32)
    grad_enter_bias = jnp.sum(grad_pre, axis=(0, 2), dtype=jnp.float32)
    grad_rows = jnp.einsum(
        "sjcf,jdf->sjcd", grad_pre, enter_weight, preferred_element_type=jnp.float32
    ).astype(jnp.bfloat16)
    grad_back = lax.all_to_all(grad_rows, "ep", split_axis=0, concat_axis=0, tiled=True).reshape(
        slots, width
    )
    padded_grad_back = jnp.concatenate([grad_back, jnp.zeros((1, width), jnp.bfloat16)], axis=0)
    grad_routed = jnp.sum(padded_grad_back[slot], axis=1, dtype=jnp.float32)
    grad_picked = gates * (grad_gates - jnp.sum(gates * grad_gates, axis=1, keepdims=True))
    grad_logits = jnp.sum(choose * grad_picked[:, :, None], axis=1).astype(jnp.bfloat16)
    grad_router = jnp.einsum("td,te->de", routed, grad_logits, preferred_element_type=jnp.float32)
    grad_routed = grad_routed + jnp.einsum(
        "te,de->td", grad_logits, router_matrix, preferred_element_type=jnp.float32
    )
    grad_gain_two = jnp.sum(grad_routed * normed_two, axis=0)
    grad_shift_two = jnp.sum(grad_routed, axis=0)
    grad_hidden = grad_output + norm_back(grad_routed, normed_two, inverse_two, gains[:, 2])
    grad_shift_out = jnp.sum(grad_hidden, axis=0)
    grad_mix_out = grad_hidden.astype(jnp.bfloat16)
    grad_out_matrix = jnp.einsum(
        "td,te->de", mixed, grad_mix_out, preferred_element_type=jnp.float32
    )
    grad_mixed = jnp.einsum(
        "te,de->td", grad_mix_out, out_matrix, preferred_element_type=jnp.float32
    )
    grad_mixed = grad_mixed.astype(jnp.bfloat16).reshape(images, SEQ, HEADS, HEAD)
    probs = jnp.exp(attention_scores(query, keyed, factor) - log_total)
    weights_again = probs.astype(jnp.bfloat16)
    grad_valued = jnp.einsum(
        "bhqk,bqhd->bkhd", weights_again, grad_mixed, preferred_element_type=jnp.float32
    )
    grad_probs = jnp.einsum(
        "bqhd,bkhd->bhqk", grad_mixed, valued, preferred_element_type=jnp.float32
    )
    grad_scores = (
        probs * (grad_probs - jnp.sum(probs * grad_probs, axis=-1, keepdims=True))
    ).astype(jnp.bfloat16)
    grad_query = (
        jnp.einsum("bhqk,bkhd->bqhd", grad_scores, keyed, preferred_element_type=jnp.float32)
        * factor
    )
    grad_keyed = (
        jnp.einsum("bhqk,bqhd->bkhd", grad_scores, query, preferred_element_type=jnp.float32)
        * factor
    )
    grad_projected = (
        jnp.stack([grad_query, grad_keyed, grad_valued], axis=2)
        .reshape(count, 3 * width)
        .astype(jnp.bfloat16)
    )
    grad_in_matrix = jnp.einsum(
        "td,te->de", entry, grad_projected, preferred_element_type=jnp.float32
    )
    grad_entry = jnp.einsum(
        "te,de->td", grad_projected, in_matrix, preferred_element_type=jnp.float32
    )
    grad_gain_one = jnp.sum(grad_entry * normed_one, axis=0)
    grad_shift_one = jnp.sum(grad_entry, axis=0)
    input_grad = grad_hidden + norm_back(grad_entry, normed_one, inverse_one, gains[:, 0])
    grad_scales = jnp.stack(
        [grad_gain_one, grad_shift_one, grad_gain_two, grad_shift_two, grad_shift_out], axis=1
    )
    summed_dense = (
        lax.psum_scatter(grad_in_matrix, ("rep", "ep"), scatter_dimension=0, tiled=True),
        lax.psum_scatter(grad_out_matrix, ("rep", "ep"), scatter_dimension=0, tiled=True),
        lax.psum_scatter(grad_router, ("rep", "ep"), scatter_dimension=0, tiled=True),
        lax.psum_scatter(grad_scales, ("rep", "ep"), scatter_dimension=0, tiled=True),
    )
    summed_expert = (
        lax.psum_scatter(
            grad_enter.astype(jnp.bfloat16), "rep", scatter_dimension=2, tiled=True
        ).astype(jnp.float32),
        lax.psum_scatter(
            grad_enter_bias.astype(jnp.bfloat16), "rep", scatter_dimension=1, tiled=True
        ).astype(jnp.float32),
        lax.psum_scatter(
            grad_leave.astype(jnp.bfloat16), "rep", scatter_dimension=1, tiled=True
        ).astype(jnp.float32),
        lax.psum_scatter(
            grad_leave_bias.astype(jnp.bfloat16), "rep", scatter_dimension=1, tiled=True
        ).astype(jnp.float32),
    )
    weights_now = (heads_in, heads_out, router, scales, expert_in, bias_in, expert_out, bias_out)
    grads_now = tuple(summed_dense) + tuple(summed_expert)
    firsts = (
        heads_in_first,
        heads_out_first,
        router_first,
        scales_first,
        expert_in_first,
        bias_in_first,
        expert_out_first,
        bias_out_first,
    )
    seconds = (
        heads_in_second,
        heads_out_second,
        router_second,
        scales_second,
        expert_in_second,
        bias_in_second,
        expert_out_second,
        bias_out_second,
    )
    states = [moments(w, g, f, s) for w, g, f, s in zip(weights_now, grads_now, firsts, seconds)]
    weight_terms = jnp.concatenate([squares(w, index == 3) for index, w in enumerate(weights_now)])
    step_terms = jnp.concatenate(
        [squares(state[2], index == 3) for index, state in enumerate(states)]
    )
    totals = lax.psum(jnp.stack([weight_terms, step_terms]), ("rep", "ep"))
    return (output, input_grad) + finish(totals, weights_now, states, width, experts)


def solution(mesh):
    in_specs = (
        P(("rep", "ep"), None),
        P(("rep", "ep"), None),
        P(("rep", "ep"), None),
        P(("rep", "ep"), None),
        P(("rep", "ep"), None),
        P(("rep", "ep"), None),
        P(("rep", "ep"), None),
        P(("rep", "ep"), None),
        P(("rep", "ep"), None),
        P(("rep", "ep"), None),
        P(("rep", "ep"), None),
        P(("rep", "ep"), None),
        P(("rep", "ep"), None),
        P(("rep", "ep"), None),
        P(("rep", "ep"), None),
        P(("rep", "ep"), None),
        P("ep", None, "rep"),
        P("ep", None, "rep"),
        P("ep", None, "rep"),
        P("ep", "rep"),
        P("ep", "rep"),
        P("ep", "rep"),
        P("ep", "rep", None),
        P("ep", "rep", None),
        P("ep", "rep", None),
        P("ep", "rep"),
        P("ep", "rep"),
        P("ep", "rep"),
    )
    out_specs = (
        P(("rep", "ep"), None),
        P(("rep", "ep"), None),
        P(("rep", "ep"), None),
        P(("rep", "ep"), None),
        P(("rep", "ep"), None),
        P(("rep", "ep"), None),
        P(("rep", "ep"), None),
        P(("rep", "ep"), None),
        P(("rep", "ep"), None),
        P(("rep", "ep"), None),
        P(("rep", "ep"), None),
        P(("rep", "ep"), None),
        P(("rep", "ep"), None),
        P(("rep", "ep"), None),
        P("ep", None, "rep"),
        P("ep", None, "rep"),
        P("ep", None, "rep"),
        P("ep", "rep"),
        P("ep", "rep"),
        P("ep", "rep"),
        P("ep", "rep", None),
        P("ep", "rep", None),
        P("ep", "rep", None),
        P("ep", "rep"),
        P("ep", "rep"),
        P("ep", "rep"),
        P(),
    )
    replicated = mesh.shape["rep"] == 4 and mesh.shape["ep"] == 8
    return jax.shard_map(
        replicate_plan if replicated else exchange_plan,
        mesh=mesh,
        in_specs=in_specs,
        out_specs=out_specs,
        check_vma=False,
    )
```

```python
import functools

import jax
import jax.numpy as jnp
from jax import lax
from jax.experimental import pallas as pl
from jax.experimental.pallas import tpu as pltpu
from jax.sharding import PartitionSpec as P

HEADS = 8
HEAD = 64
FF = 2048
SEQ = 197
STEP = 5


BETA = 0.5
RATE = 0.3
DECAY = 0.01
EPSILON = 1e-06


def normalize(rows):
    centred = rows - jnp.mean(rows, axis=-1, keepdims=True)
    inverse = lax.rsqrt(jnp.mean(centred * centred, axis=-1, keepdims=True) + 1e-06)
    return (centred * inverse, inverse)


def norm_back(grad_rows, normed, inverse, gain):
    scaled = grad_rows * gain
    return inverse * (
        scaled
        - jnp.mean(scaled, axis=-1, keepdims=True)
        - normed * jnp.mean(scaled * normed, axis=-1, keepdims=True)
    )


def exact_gelu(values):
    return jax.nn.gelu(values, approximate=False)


def route_places(block_ids, ranking, experts):
    count = block_ids.shape[0]
    keys = jnp.arange(block_ids.shape[1], dtype=jnp.int32)[None, :] * count + ranking[:, None]
    ordered = (
        jnp.zeros((block_ids.size,), jnp.int32).at[keys.reshape(-1)].set(block_ids.reshape(-1))
    )
    hits = (ordered[:, None] == jnp.arange(experts, dtype=jnp.int32)[None, :]).astype(jnp.int32)
    before = jnp.cumsum(hits, axis=0) - hits
    place = jnp.sum(before * hits, axis=1)
    return place[keys]


def attention_scores(query, keyed, factor):
    return jnp.einsum("bqhd,bkhd->bhqk", query, keyed, preferred_element_type=jnp.float32) * factor


def moments(weight, grad, first, second):
    first_new = BETA * first + (1.0 - BETA) * grad
    second_new = BETA * second + (1.0 - BETA) * grad * grad
    step = (
        first_new / (1.0 - BETA**STEP) / (jnp.sqrt(second_new / (1.0 - BETA**STEP)) + EPSILON)
        + DECAY * weight
    )
    return (first_new, second_new, step)


def squares(array, per_column):
    if per_column:
        return jnp.sum(array * array, axis=0)
    return jnp.sum(array * array)[None]


def finish(totals, weights_now, states, width, experts):
    counts = jnp.array(
        [3 * width * width, width * width, width * experts]
        + [width] * 5
        + [experts * width * FF, experts * FF, experts * FF * width, experts * width],
        jnp.float32,
    )
    weight_rms = jnp.sqrt(totals[0] / counts)
    step_rms = jnp.sqrt(totals[1] / counts)
    trust = weight_rms / step_rms
    bounds = [(0, 1), (1, 2), (2, 3), (3, 8), (8, 9), (9, 10), (10, 11), (11, 12)]
    results = []
    for weight, state, bound in zip(weights_now, states, bounds):
        results.extend([state[0], state[1], weight - RATE * trust[bound[0] : bound[1]] * state[2]])
    results.append(jnp.stack([weight_rms, step_rms, trust]))
    return tuple(results)


PAD = 208
WIN = 96
VMEM = 60 * 1024 * 1024
BF = jnp.bfloat16
F32 = jnp.float32


def dot_nn(a, b):
    return lax.dot_general(a, b, (((1,), (0,)), ((), ())), preferred_element_type=F32)


def dot_nt(a, b):
    return lax.dot_general(a, b, (((1,), (1,)), ((), ())), preferred_element_type=F32)


def dot_tn(a, b):
    return lax.dot_general(a, b, (((0,), (0,)), ((), ())), preferred_element_type=F32)


def lane_iota(rows, lanes):
    return lax.broadcasted_iota(jnp.int32, (rows, lanes), 1)


def row_iota(rows, lanes):
    return lax.broadcasted_iota(jnp.int32, (rows, lanes), 0)


def whole(shape):
    return pl.BlockSpec(shape, lambda *_: (0,) * len(shape))


def cost(micros):
    return pl.CostEstimate(flops=int(micros * 1e9), bytes_accessed=int(micros * 1e5), transcendentals=0)


def params(**kw):
    return pltpu.CompilerParams(vmem_limit_bytes=VMEM, **kw)


def behind(kernel, inputs, after):
    def body(*refs):
        return kernel(*refs[:inputs], *refs[inputs + len(after) :])

    return body


def unread(after):
    return [pl.BlockSpec(memory_space=pl.ANY)] * len(after)


def assemble_kernel(place_ref, near_ref, far_ref, in_ref, out_ref, router_ref, gains_ref, small_ref):
    copies, rows = near_ref.shape[0], near_ref.shape[1]
    width = out_ref.shape[1]
    for side, got_ref in enumerate((near_ref, far_ref)):
        for j in range(copies):
            place = pl.multiple_of(place_ref[side * copies + j] * rows, rows)
            in_ref[pl.ds(place, rows), :] = got_ref[j, :, : 3 * width]
            out_ref[pl.ds(place, rows), :] = got_ref[j, :, 3 * width : 4 * width]
            small_ref[pl.ds(place, rows), :] = got_ref[j, :, 4 * width :]
    turned = small_ref[:, :128].astype(F32).T
    experts = router_ref.shape[0]
    router_ref[...] = turned[:experts].astype(BF)
    gains_ref[...] = turned[experts : experts + 8]


def assemble(place, near, far, experts):
    copies, rows, lanes = near.shape
    width = 2 * copies * rows
    return pl.pallas_call(
        assemble_kernel,
        grid_spec=pltpu.PrefetchScalarGridSpec(
            num_scalar_prefetch=1,
            grid=(1,),
            in_specs=[whole(near.shape)] * 2,
            out_specs=[
                whole((width, 3 * width)),
                whole((width, width)),
                whole((experts, width)),
                whole((8, width)),
                whole((width, lanes - 4 * width)),
            ],
        ),
        out_shape=[
            jax.ShapeDtypeStruct((width, 3 * width), BF),
            jax.ShapeDtypeStruct((width, width), BF),
            jax.ShapeDtypeStruct((experts, width), BF),
            jax.ShapeDtypeStruct((8, width), F32),
            jax.ShapeDtypeStruct((width, lanes - 4 * width), BF),
        ],
        compiler_params=params(),
        cost_estimate=cost(1),
        name="assemble",
    )(place, near, far)


def places_kernel(capacity, rows_ref, cols_ref, lrow_ref, lcol_ref, meta_ref):
    count = cols_ref.shape[0]
    images = count // PAD
    experts = lcol_ref.shape[1]
    expert = lane_iota(count, experts).astype(F32)
    first = (cols_ref[:, 1:2] == expert).astype(F32)
    second = (cols_ref[:, 2:3] == expert).astype(F32)
    first_low = first.astype(BF)
    second_low = second.astype(BF)
    total_first = jnp.sum(first, axis=0, keepdims=True)
    lower = (lane_iota(PAD, PAD) < row_iota(PAD, PAD)).astype(F32).astype(BF)
    ranking = rows_ref[0:1, :]
    begin = jnp.zeros((1, experts), F32)
    for i in range(images):
        span = slice(i * PAD, (i + 1) * PAD)
        ahead = (ranking < cols_ref[span, 0:1]).astype(F32).astype(BF)
        rank_first = dot_nn(ahead, first_low)
        rank_second = dot_nn(ahead, second_low) + total_first
        place = first[span] * rank_first + second[span] * rank_second
        kept = (first[span] + second[span]) * (place < capacity).astype(F32)
        local = dot_nn(lower, kept.astype(BF))
        local = jnp.where(kept > 0.0, local, -1.0)
        lcol_ref[span, :] = local
        lrow_ref[i] = local.T
        here = jnp.sum(kept, axis=0, keepdims=True)
        meta_ref[i : i + 1, :] = begin.astype(jnp.int32)
        meta_ref[images + i : images + i + 1, :] = here.astype(jnp.int32)
        begin = begin + here


def find_places(rows, cols, capacity, experts):
    count = cols.shape[0]
    images = count // PAD
    return pl.pallas_call(
        functools.partial(places_kernel, capacity),
        out_shape=[
            jax.ShapeDtypeStruct((images, experts, PAD), F32),
            jax.ShapeDtypeStruct((count, experts), F32),
            jax.ShapeDtypeStruct((2 * images, experts), jnp.int32),
        ],
        compiler_params=params(),
        cost_estimate=cost(2),
        name="places",
    )(rows, cols)


def spread_kernel(tok_ref, cot_ref, tpad_ref, cpad_ref):
    count, width = tok_ref.shape
    for source, target in ((tok_ref, tpad_ref), (cot_ref, cpad_ref)):
        for i in range(count // SEQ):
            rows = source[SEQ * i : SEQ * (i + 1), :].astype(F32)
            rows = jnp.concatenate([rows, jnp.zeros((PAD - SEQ, width), F32)], axis=0)
            target[PAD * i : PAD * (i + 1), :] = rows.astype(BF)


def spread_rows(tokens, cotangent):
    count, width = tokens.shape
    shape = jax.ShapeDtypeStruct((count // SEQ * PAD, width), BF)
    return pl.pallas_call(
        spread_kernel, out_shape=[shape, shape], compiler_params=params(), cost_estimate=cost(5), name="spread_rows"
    )(tokens, cotangent)


def store_image(target, i, values):
    for image in range(target.shape[0] // SEQ):

        @pl.when(i == image)
        def _(image=image):
            target[SEQ * image : SEQ * (image + 1), :] = values[0:SEQ, :]


def split_halves(block, halves):
    zero = jnp.zeros_like(block)
    return jnp.concatenate([jnp.where(halves, block, zero), jnp.where(halves, zero, block)], axis=0)


def attention_kernel(
    tok_ref, in_ref, out_ref, router_ref, gains_ref, ids_ref,
    proj_ref, prob_ref, mixed_ref, hidden_ref, routed_ref, gcol_ref, grow_ref, mixed_all,
):
    width = tok_ref.shape[1]
    x = tok_ref[...].astype(F32)
    normed, _ = normalize(x)
    entry = (normed * gains_ref[0:1, :] + gains_ref[1:2, :]).astype(BF)
    proj_ref[...] = dot_nn(entry, in_ref[...]).astype(BF)
    pair = 2 * HEAD
    halves = lane_iota(PAD, pair) < HEAD
    key_there = lane_iota(2 * PAD, PAD) < SEQ
    for p in range(HEADS // 2):
        q = proj_ref[:, pair * p : pair * (p + 1)] * jnp.asarray(HEAD ** -0.5, BF)
        k = proj_ref[:, width + pair * p : width + pair * (p + 1)]
        v = proj_ref[:, 2 * width + pair * p : 2 * width + pair * (p + 1)]
        scores = dot_nt(split_halves(q, halves), k)
        scores = jnp.where(key_there, scores, -1e30)
        peak = jnp.max(scores, axis=1, keepdims=True)
        raised = jnp.exp(scores - peak)
        total = jnp.sum(raised, axis=1, keepdims=True)
        weights = (raised * (1.0 / total)).astype(BF)
        prob_ref[0, 2 * p] = weights[:PAD]
        prob_ref[0, 2 * p + 1] = weights[PAD:]
        out = dot_nn(weights, v)
        mixed_all[:, pair * p : pair * (p + 1)] = jnp.where(halves, out[:PAD], out[PAD:]).astype(BF)
    mixed = mixed_all[...]
    mixed_ref[...] = mixed
    hidden = x + dot_nn(mixed, out_ref[...]) + gains_ref[4:5, :]
    hidden_ref[...] = hidden
    normed_two, _ = normalize(hidden)
    routed = (normed_two * gains_ref[2:3, :] + gains_ref[3:4, :]).astype(BF)
    routed_ref[...] = routed
    logits = dot_nt(routed, router_ref[...])
    experts = logits.shape[1]
    expert = lane_iota(PAD, experts)
    chosen = jnp.logical_or(ids_ref[:, 0:1] == expert, ids_ref[:, 1:2] == expert)
    top = jnp.max(jnp.where(chosen, logits, -1e30), axis=1, keepdims=True)
    raised = jnp.where(chosen, jnp.exp(jnp.where(chosen, logits - top, 0.0)), 0.0)
    total = jnp.sum(raised, axis=1, keepdims=True)
    gates = raised / jnp.where(total > 0.0, total, 1.0)
    gcol_ref[...] = gates
    grow_ref[0] = gates.T


def attention(tok_pad, in_matrix, out_matrix, router, gains, ids_col, after=()):
    padded, width = tok_pad.shape
    images = padded // PAD
    experts = router.shape[0]
    row = lambda lanes: pl.BlockSpec((PAD, lanes), lambda i: (i, 0))
    once = lambda a: pl.BlockSpec(a.shape, lambda i: (0, 0), pipeline_mode=pl.Buffered(1))
    return pl.pallas_call(
        behind(attention_kernel, 6, after),
        grid=(images,),
        in_specs=[row(width), once(in_matrix), once(out_matrix), once(router), once(gains), row(2)] + unread(after),
        out_specs=[
            row(3 * width),
            pl.BlockSpec((1, HEADS, PAD, PAD), lambda i: (i, 0, 0, 0)),
            row(width), row(width), row(width), row(experts),
            pl.BlockSpec((1, experts, PAD), lambda i: (i, 0, 0)),
        ],
        out_shape=[
            jax.ShapeDtypeStruct((padded, 3 * width), BF),
            jax.ShapeDtypeStruct((images, HEADS, PAD, PAD), BF),
            jax.ShapeDtypeStruct((padded, width), BF),
            jax.ShapeDtypeStruct((padded, width), F32),
            jax.ShapeDtypeStruct((padded, width), BF),
            jax.ShapeDtypeStruct((padded, experts), F32),
            jax.ShapeDtypeStruct((images, experts, PAD), F32),
        ],
        scratch_shapes=[pltpu.VMEM((PAD, width), BF)],
        compiler_params=params(),
        cost_estimate=cost(8),
        name="attention",
    )(tok_pad, in_matrix, out_matrix, router, gains, ids_col, *after)


def window_count():
    return -(-(15 + SEQ) // WIN)


def gather_kernel(meta_ref, routed_ref, cot_ref, lrow_ref, grow_ref, r_ref, g_ref, rt_ref, gt_ref, r_all, g_all):
    e = pl.program_id(0)
    images = lrow_ref.shape[0]
    listed = r_ref.shape[1]
    r_all[...] = jnp.zeros_like(r_all)
    g_all[...] = jnp.zeros_like(g_all)
    row = row_iota(WIN, PAD).astype(F32)
    for i in range(images):
        start, here = meta_ref[i, e], meta_ref[images + i, e]
        base = lax.shift_left(lax.shift_right_logical(start, 4), 4)
        shift = (start - base).astype(F32)
        local = lrow_ref[i, pl.ds(e, 1), :]
        gate = grow_ref[i, pl.ds(e, 1), :]
        for q in range(window_count()):
            @pl.when(jnp.logical_and(here > 0, base + q * WIN < start + here))
            def _(i=i, q=q, base=base, shift=shift, local=local, gate=gate):
                pick = jnp.logical_and(local >= 0.0, local + (shift - q * WIN) == row)
                low = pick.astype(F32).astype(BF)
                slot_gate = jnp.sum(jnp.where(pick, gate, 0.0), axis=1, keepdims=True)
                where = pl.ds(pl.multiple_of(base + q * WIN, 16), WIN)
                r_all[where, :] += dot_nn(low, routed_ref[i * PAD : (i + 1) * PAD, :])
                g_all[where, :] += slot_gate * dot_nn(low, cot_ref[i * PAD : (i + 1) * PAD, :])
    r_ref[0] = r_all[0:listed, :].astype(BF)
    g_ref[0] = g_all[0:listed, :].astype(BF)
    rt_ref[0] = r_all[0:listed, :].T.astype(BF)
    gt_ref[0] = g_all[0:listed, :].astype(BF).astype(F32).T.astype(BF)


def gather(meta, routed, cot_pad, lrow, grow, listed, after=()):
    width = routed.shape[1]
    experts = lrow.shape[1]
    once = lambda a: pl.BlockSpec(a.shape, lambda e, m: (0,) * a.ndim, pipeline_mode=pl.Buffered(1))
    block = pl.BlockSpec((1, listed, width), lambda e, m: (e, 0, 0))
    turned = pl.BlockSpec((1, width, listed), lambda e, m: (e, 0, 0))
    return pl.pallas_call(
        behind(gather_kernel, 5, after),
        grid_spec=pltpu.PrefetchScalarGridSpec(
            num_scalar_prefetch=1,
            grid=(experts,),
            in_specs=[once(routed), once(cot_pad), once(lrow), once(grow)] + unread(after),
            out_specs=[block, block, turned, turned],
            scratch_shapes=[pltpu.VMEM((listed + WIN, width), F32)] * 2,
        ),
        out_shape=[jax.ShapeDtypeStruct((experts, listed, width), BF)] * 2
        + [jax.ShapeDtypeStruct((experts, width, listed), BF)] * 2,
        compiler_params=params(),
        cost_estimate=cost(8),
        name="gather",
    )(meta, routed, cot_pad, lrow, grow, *after)


def gelu_both(pre):
    bell = jnp.exp(-0.5 * (pre * pre))
    t = pl.reciprocal(1.0 + (0.3275911 * 2.0**-0.5) * jnp.abs(pre))
    tail = t * (0.127414796 + t * (-0.142248368 + t * (0.7107068705 + t * (-0.7265760135 + t * 0.5307027145))))
    tail = tail * bell
    phi = jnp.where(pre < 0.0, tail, 1.0 - tail)
    return pre * phi, phi + pre * bell * 0.3989422804014327


def expert_kernel(first, half, at_ref, *refs):
    rep = 4
    (r_ref, g_ref, rt_ref, gt_ref), w_refs, b_ref, refs = refs[:4], refs[4:12], refs[12], refs[13:]
    if first:
        refs = refs[2 * (half > 0) :]
        y_ref, d_ref, near_ref, far_ref, db_ref, obg_ref, y_all, d_all = refs
    else:
        (ob_ref, y_in, d_in), refs = refs[:3], refs[3 + 2 * (half > 0) :]
        y_ref, d_ref, near_ref, far_ref, db_ref, y_all, d_all = refs
    listed = r_ref.shape[1]
    step = pl.program_id(0)
    count = at_ref[2 + lax.bitwise_xor(expert_rank(step, half), at_ref[1])]

    def run(n):
        rows_t, grads_t = rt_ref[0, :, :n], gt_ref[0, :, :n]

        def weights(r):
            place = lax.bitwise_xor(at_ref[0], r)
            return place, w_refs[r][0, 0], w_refs[rep + r][0, 0]

        def enter_part(r):
            place, enter, leave = weights(r)
            pre = dot_nn(r_ref[0, :n, :], enter) + b_ref[0, pl.ds(place, 1), :]
            return pre, dot_nn(g_ref[0, :n, :], leave)

        def middle_part(pre, grad_act):
            act, slope = gelu_both(pre)
            return act.astype(BF), (grad_act * slope).astype(BF)

        def leave_part(r, act, grad_pre):
            place, enter, leave = weights(r)
            out = far_ref if r % 2 else near_ref
            out[r // 2, 0, 0] = dot_nn(rows_t, grad_pre).astype(BF)
            out[r // 2, 0, 1] = dot_nn(grads_t, act).astype(BF)
            db_ref[0, pl.ds(place, 1), :] = jnp.sum(grad_pre.astype(F32), axis=0, keepdims=True)
            y_part = dot_nt(act, leave)
            d_part = dot_nt(grad_pre, enter)
            if r == 0:
                y_all[:n, :] = y_part if first else y_part + y_in[0, :n, :]
                d_all[:n, :] = d_part if first else d_part + d_in[0, :n, :]
            else:
                y_all[:n, :] += y_part
                d_all[:n, :] += d_part

        held = enter_part(0)
        ready = None
        for r in range(rep):
            now = middle_part(*held)
            if r + 1 < rep:
                held = enter_part(r + 1)
            if ready is not None:
                leave_part(r - 1, *ready)
            ready = now
        leave_part(rep - 1, *ready)
        if not first:
            y_ref[0, :n, :] = (y_all[:n, :] + ob_ref[0]).astype(BF)
            d_ref[0, :n, :] = d_all[:n, :].astype(BF)
        else:
            y_ref[0, :n, :] = y_all[:n, :]
            d_ref[0, :n, :] = d_all[:n, :]
        if n < listed:
            y_ref[0, n:, :] = jnp.zeros((listed - n, y_ref.shape[2]), y_ref.dtype)
            d_ref[0, n:, :] = jnp.zeros((listed - n, y_ref.shape[2]), y_ref.dtype)

    if first:
        obg_ref[0] = jnp.sum(g_ref[0].astype(F32), axis=0, keepdims=True)
    short = listed * 3 // 4 // 16 * 16
    pl.when(count <= short)(lambda: run(short))
    pl.when(count > short)(lambda: run(listed))


def expert_rank(step, half):
    return lax.shift_left(lax.bitwise_and(step, 3), 1) + lax.shift_right_logical(step, 2) + half


def expert_pass(at, lists, weights, bias, out_bias=None, carried=None, half=0, done=None, after=()):
    first = carried is None
    rows = lists[0]
    experts, listed, width = rows.shape
    rep, cols = bias.shape[1], bias.shape[2]
    steps = experts // 2
    here = lambda e, at: lax.bitwise_xor(expert_rank(e, half), at[1])
    block = pl.BlockSpec((1, listed, width), lambda e, at: (here(e, at), 0, 0))
    turned = pl.BlockSpec((1, width, listed), lambda e, at: (here(e, at), 0, 0))
    out_w = pl.BlockSpec((rep // 2, 1, 2, width, cols), lambda e, at: (0, e, 0, 0, 0))
    in_specs = [
        block, block, turned, turned,
        *[pl.BlockSpec((1, 1, width, cols), lambda e, at, m=m: (m, e, 0, 0)) for _, m in weights],
        pl.BlockSpec((1, rep, cols), lambda e, at: (here(e, at), 0, 0)),
    ]
    args = list(lists) + [a for a, _ in weights] + [bias]
    kind = F32 if first else BF
    out_specs = [block, block, out_w, out_w, pl.BlockSpec((1, rep, cols), lambda e, at: (here(e, at), 0, 0))]
    out_shape = [
        jax.ShapeDtypeStruct(rows.shape, kind),
        jax.ShapeDtypeStruct(rows.shape, kind),
        jax.ShapeDtypeStruct((rep // 2, steps, 2, width, cols), BF),
        jax.ShapeDtypeStruct((rep // 2, steps, 2, width, cols), BF),
        jax.ShapeDtypeStruct((experts, rep, cols), F32),
    ]
    aliases = {}
    if first:
        out_specs.append(pl.BlockSpec((1, 1, width), lambda e, at: (here(e, at), 0, 0)))
        out_shape.append(jax.ShapeDtypeStruct((experts, 1, width), F32))
    else:
        in_specs += [pl.BlockSpec((1, 1, width), lambda e, at: (here(e, at), 0, 0)), block, block]
        args += [out_bias, *carried]
    if half:
        aliases = {len(args) + 1: 0, len(args) + 2: 1}
        in_specs += unread(done)
        args += list(done)
    kernel = behind(functools.partial(expert_kernel, first, half), len(args) + 1, after)
    return pl.pallas_call(
        kernel,
        grid_spec=pltpu.PrefetchScalarGridSpec(
            num_scalar_prefetch=1,
            grid=(steps,),
            in_specs=in_specs + unread(after),
            out_specs=out_specs,
            scratch_shapes=[pltpu.VMEM((listed, width), F32)] * 2,
        ),
        out_shape=out_shape,
        input_output_aliases=aliases,
        compiler_params=params(),
        cost_estimate=cost(4),
        name=f"experts_{0 if first else 1}{half}",
    )(at, *args, *after)


def combine_kernel(
    meta_ref, y_ref, d_ref, lcol_ref, gcol_ref, hidden_ref, cot_ref, mixed_ref, out_w_ref, router_ref, gains_ref,
    out_ref, gh_ref, gm_ref, dout_ref, drouter_ref, dscale_ref, y_acc, g_acc, d_acc,
):
    i = pl.program_id(0)
    images = pl.num_programs(0)
    experts, listed, width = y_ref.shape
    gates = gcol_ref[...]
    local = lcol_ref[...]
    go = cot_ref[...].astype(F32)
    lane = lane_iota(PAD, WIN).astype(F32)
    expert = lane_iota(PAD, experts)

    def window(e, q, base, shift):
        at = jnp.minimum(base + q * WIN, listed - WIN)
        moved = (at - base).astype(F32)
        spot = local[:, e : e + 1] + shift
        pick = jnp.logical_and(spot == lane + moved, local[:, e : e + 1] >= 0.0)
        pick = jnp.logical_and(pick, spot >= q * WIN)
        low = pick.astype(F32).astype(BF)
        where = pl.ds(pl.multiple_of(at, 16), WIN)
        return dot_nn(low, y_ref[e, where, :]), dot_nn(low, d_ref[e, where, :])

    y_sum = jnp.zeros((PAD, width), F32)
    d_sum = jnp.zeros((PAD, width), F32)
    grad_gates = jnp.zeros((PAD, experts), F32)
    bases = []
    for e in range(experts):
        start = meta_ref[i, e]
        base = lax.shift_left(lax.shift_right_logical(start, 4), 4)
        bases.append((start, base))
        y_tok, d_tok = window(e, 0, base, (start - base).astype(F32))
        y_sum += gates[:, e : e + 1] * y_tok
        d_sum += d_tok
        gg = jnp.sum(go * y_tok, axis=1, keepdims=True)
        grad_gates += jnp.where(expert == e, gg, 0.0)
    y_acc[...] = y_sum
    d_acc[...] = d_sum
    g_acc[...] = grad_gates
    for e in range(experts):
        start, base = bases[e]
        here = meta_ref[images + i, e]
        for q in range(1, window_count()):
            @pl.when(base + q * WIN < start + here)
            def _(e=e, q=q, base=base, start=start):
                y_tok, d_tok = window(e, q, base, (start - base).astype(F32))
                y_acc[...] += gates[:, e : e + 1] * y_tok
                d_acc[...] += d_tok
                gg = jnp.sum(go * y_tok, axis=1, keepdims=True)
                g_acc[...] += jnp.where(expert == e, gg, 0.0)
    hidden = hidden_ref[...]
    y_acc[...] += hidden
    store_image(out_ref, i, y_acc)
    grad_gates = g_acc[...]
    pick = gates * (grad_gates - jnp.sum(gates * grad_gates, axis=1, keepdims=True))
    logit_low = pick.astype(BF)
    grad_routed = d_acc[...] + dot_nn(logit_low, router_ref[...])
    normed, inverse = normalize(hidden)
    routed = (normed * gains_ref[2:3, :] + gains_ref[3:4, :]).astype(BF)
    grad_hidden = go + norm_back(grad_routed, normed, inverse, gains_ref[2:3, :])
    gh_ref[...] = grad_hidden
    grad_mix = grad_hidden.astype(BF)
    gm_ref[...] = dot_nt(grad_mix, out_w_ref[...]).astype(BF)

    @pl.when(i == 0)
    def _():
        dout_ref[...] = jnp.zeros_like(dout_ref)
        drouter_ref[...] = jnp.zeros_like(drouter_ref)
        dscale_ref[...] = jnp.zeros_like(dscale_ref)

    dout_ref[...] += dot_tn(mixed_ref[...], grad_mix)
    drouter_ref[...] += dot_tn(logit_low, routed)
    dscale_ref[2:3, :] += jnp.sum(grad_routed * normed, axis=0, keepdims=True)
    dscale_ref[3:4, :] += jnp.sum(grad_routed, axis=0, keepdims=True)
    dscale_ref[4:5, :] += jnp.sum(grad_hidden, axis=0, keepdims=True)


def combine(meta, y, d, lcol, gcol, hidden, cot_pad, mixed, out_matrix, router, gains, after=()):
    padded, width = hidden.shape
    images = padded // PAD
    experts = y.shape[0]
    row = lambda lanes: pl.BlockSpec((PAD, lanes), lambda i, m: (i, 0))
    once = lambda a: pl.BlockSpec(a.shape, lambda i, m: (0,) * a.ndim, pipeline_mode=pl.Buffered(1))
    return pl.pallas_call(
        behind(combine_kernel, 11, after),
        grid_spec=pltpu.PrefetchScalarGridSpec(
            num_scalar_prefetch=1,
            grid=(images,),
            in_specs=[
                once(y), once(d), row(experts), row(experts), row(width), row(width), row(width),
                once(out_matrix), once(router), once(gains), *unread(after),
            ],
            out_specs=[
                whole((images * SEQ, width)), row(width), row(width), whole((width, width)), whole((experts, width)),
                whole((8, width)),
            ],
            scratch_shapes=[
                pltpu.VMEM((PAD, width), F32), pltpu.VMEM((PAD, experts), F32), pltpu.VMEM((PAD, width), F32),
            ],
        ),
        out_shape=[
            jax.ShapeDtypeStruct((images * SEQ, width), F32),
            jax.ShapeDtypeStruct((padded, width), F32),
            jax.ShapeDtypeStruct((padded, width), BF),
            jax.ShapeDtypeStruct((width, width), F32),
            jax.ShapeDtypeStruct((experts, width), F32),
            jax.ShapeDtypeStruct((8, width), F32),
        ],
        compiler_params=params(),
        cost_estimate=cost(40),
        name="combine",
    )(meta, y, d, lcol, gcol, hidden, cot_pad, mixed, out_matrix, router, gains, *after)


def attention_back_kernel(
    place_ref, proj_ref, prob_ref, gm_ref, gh_ref, tpad_ref, in_ref, gains_ref, dout_ref, small_ref,
    grad_ref, near_ref, far_ref, din_ref, dscale_ref, line_ref, dproj, grad_all,
):
    i = pl.program_id(0)
    width = gm_ref.shape[1]
    pair = 2 * HEAD
    halves = lane_iota(PAD, pair) < HEAD
    factor = HEAD ** -0.5
    for p in range(HEADS // 2):
        cut = slice(pair * p, pair * (p + 1))
        q = proj_ref[:, cut]
        k = proj_ref[:, width + pair * p : width + pair * (p + 1)]
        v = proj_ref[:, 2 * width + pair * p : 2 * width + pair * (p + 1)]
        gm = gm_ref[:, cut]
        gms = split_halves(gm, halves)
        low = jnp.concatenate([prob_ref[0, 2 * p], prob_ref[0, 2 * p + 1]], axis=0)
        probs = low.astype(F32)
        grad_probs = dot_nt(gms, v)
        middle = jnp.sum(probs * grad_probs, axis=1, keepdims=True)
        grad_scores = (probs * (grad_probs - middle)).astype(BF)
        grad_q = dot_nn(grad_scores, k)
        dproj[:, cut] = (jnp.where(halves, grad_q[:PAD], grad_q[PAD:]) * factor).astype(BF)
        dproj[:, width + pair * p : width + pair * (p + 1)] = (
            dot_tn(grad_scores, split_halves(q, halves)) * factor
        ).astype(BF)
        dproj[:, 2 * width + pair * p : 2 * width + pair * (p + 1)] = dot_tn(low, gms).astype(BF)
    normed, inverse = normalize(tpad_ref[...].astype(F32))
    entry = (normed * gains_ref[0:1, :] + gains_ref[1:2, :]).astype(BF)
    grads = dproj[...]
    grad_entry = dot_nt(grads, in_ref[...])

    @pl.when(i == 0)
    def _():
        din_ref[...] = jnp.zeros_like(din_ref)
        dscale_ref[...] = jnp.zeros_like(dscale_ref)

    din_ref[...] += dot_tn(entry, grads)
    dscale_ref[0:1, :] += jnp.sum(grad_entry * normed, axis=0, keepdims=True)
    dscale_ref[1:2, :] += jnp.sum(grad_entry, axis=0, keepdims=True)
    grad = gh_ref[...] + norm_back(grad_entry, normed, inverse, gains_ref[0:1, :])
    grad_all[...] = grad
    store_image(grad_ref, i, grad_all)

    @pl.when(i == pl.num_programs(0) - 1)
    def _():
        blocks, rows = 2 * near_ref.shape[0], near_ref.shape[1]
        owner = lane_iota(blocks, width) // rows == row_iota(blocks, width)
        spot = row_iota(width, 128) % rows
        line = jnp.zeros((blocks, 128), F32)
        for s in range(2):
            spread = jnp.where(owner, dscale_ref[s : s + 1, :], 0.0)
            chosen = (lane_iota(width, 128) == spot + s * rows).astype(F32)
            line += lax.dot_general(
                spread, chosen, (((1,), (0,)), ((), ())),
                preferred_element_type=F32, precision=lax.Precision.HIGHEST,
            )
        line_ref[...] = line
        scale_row = row_iota(8, 128) == 6
        for side, out in ((0, near_ref), (1, far_ref)):
            def body(j, carry, side=side, out=out):
                place = place_ref[side * (blocks // 2) + j]
                here = pl.ds(pl.multiple_of(place * rows, rows), rows)
                out[j, :, : 3 * width] = din_ref[here, :].astype(BF)
                out[j, :, 3 * width : 4 * width] = dout_ref[here, :].astype(BF)
                small = small_ref[place] + jnp.where(scale_row, line_ref[pl.ds(place, 1), :], 0.0)
                out[j, :, 4 * width :] = resplit(small)
                return carry

            lax.fori_loop(0, blocks // 2, body, 0)


def attention_back(place, proj, probs, grad_mixed, grad_hidden, tok_pad, in_matrix, gains, grad_out, small, after=()):
    padded, width = grad_hidden.shape
    images = padded // PAD
    blocks = small.shape[0]
    rows = width // blocks
    row = lambda lanes: pl.BlockSpec((PAD, lanes), lambda i, m: (i, 0))
    once = lambda a: pl.BlockSpec(a.shape, lambda i, m: (0,) * a.ndim, pipeline_mode=pl.Buffered(1))
    half = (blocks // 2, rows, 4 * width + 128)
    return pl.pallas_call(
        behind(attention_back_kernel, 10, after),
        grid_spec=pltpu.PrefetchScalarGridSpec(
            num_scalar_prefetch=1,
            grid=(images,),
            in_specs=[
                row(3 * width), pl.BlockSpec((1, HEADS, PAD, PAD), lambda i, m: (i, 0, 0, 0)), row(width), row(width),
                row(width), once(in_matrix), once(gains), once(grad_out), once(small),
                *unread(after),
            ],
            out_specs=[whole((images * SEQ, width)), whole(half), whole(half)],
            scratch_shapes=[
                pltpu.VMEM((width, 3 * width), F32), pltpu.VMEM((8, width), F32), pltpu.VMEM((blocks, 128), F32),
                pltpu.VMEM((PAD, 3 * width), BF), pltpu.VMEM((PAD, width), F32),
            ],
        ),
        out_shape=[
            jax.ShapeDtypeStruct((images * SEQ, width), F32),
            jax.ShapeDtypeStruct(half, BF),
            jax.ShapeDtypeStruct(half, BF),
        ],
        compiler_params=params(),
        cost_estimate=cost(50),
        name="attention_back",
    )(place, proj, probs, grad_mixed, grad_hidden, tok_pad, in_matrix, gains, grad_out, small, *after)


X_BIT, CORE_BIT, Y_BIT = 16, 8, 1
Z_BITS = (2, 4, 6)
AXES = ("rep", "ep")


def swap(array, bits):
    devices = lax.axis_size("rep") * lax.axis_size("ep")
    return lax.ppermute(array, AXES, [(d, d ^ bits) for d in range(devices)])


def relative(position):
    c, x, y, z = position >> 4 & 1, position >> 3 & 1, position >> 2 & 1, position & 3
    return x * X_BIT + c * CORE_BIT + z * 2 + y * Y_BIT


def stack_kernel(count, *refs):
    for j in range(count):
        refs[count][j] = refs[j][...]


def stack(arrays, after=()):
    count = len(arrays)
    return pl.pallas_call(
        behind(functools.partial(stack_kernel, count), count, after),
        in_specs=[pl.BlockSpec(memory_space=pltpu.VMEM)] * count + unread(after),
        out_shape=jax.ShapeDtypeStruct((count,) + arrays[0].shape, arrays[0].dtype),
        compiler_params=params(),
        cost_estimate=cost(1),
        name="stack",
    )(*arrays, *after)


def turn_stack_kernel(*refs):
    for m in range(2):
        for j in range(4):
            refs[4][m, j] = refs[j][m]


def turn_stack(arrays, after=()):
    piece = arrays[0].shape
    return pl.pallas_call(
        behind(turn_stack_kernel, 4, after),
        in_specs=[pl.BlockSpec(memory_space=pltpu.VMEM)] * 4 + unread(after),
        out_shape=jax.ShapeDtypeStruct((2, 4) + piece[1:], arrays[0].dtype),
        compiler_params=params(),
        cost_estimate=cost(2),
        name="turn_stack",
    )(*arrays, *after)


def pick_kernel(far_x, far_y, x_in, x_out, y_out):
    x_in[0] = far_x[0]
    x_out[0] = far_x[1]
    y_out[0] = far_y[1]


def pick(far_x, far_y, after=()):
    shape = (1,) + far_x.shape[1:]
    return pl.pallas_call(
        behind(pick_kernel, 2, after),
        in_specs=[pl.BlockSpec(memory_space=pltpu.VMEM)] * 2 + unread(after),
        out_shape=[jax.ShapeDtypeStruct(shape, far_x.dtype)] * 3,
        compiler_params=params(),
        cost_estimate=cost(3),
        name="pick",
    )(far_x, far_y, *after)


def sum_everywhere(values):
    for bits in (CORE_BIT, Y_BIT, X_BIT, 2, 4):
        values = values + swap(values, bits)
    return values


def unsplit(block):
    return block[:8] + block[8:]


def resplit(small):
    twice = jnp.concatenate([small, small], axis=0)
    high = twice.astype(BF).astype(F32)
    return jnp.where(row_iota(16, 128) < 8, high, twice - high).astype(BF)


def block_sum_kernel(parts, terms, *refs):
    ins, outs = refs[:terms], refs[terms:]
    size = ins[0].shape[0] // parts
    lanes = ins[0].shape[2]
    for p in range(parts):
        for j in range(size):
            at = p * size + j
            total = ins[0][at].astype(F32)
            for t in ins[1:]:
                total = total + t[at].astype(F32)
            small = unsplit(total[:, lanes - 128 :])
            outs[p][j, :, : lanes - 128] = total[:, : lanes - 128].astype(BF)
            outs[p][j, :, lanes - 128 :] = resplit(small)


def block_sum(terms, parts):
    size = terms[0].shape[0] // parts
    shape = (size,) + terms[0].shape[1:]
    return pl.pallas_call(
        functools.partial(block_sum_kernel, parts, len(terms)),
        out_shape=[jax.ShapeDtypeStruct(shape, BF)] * parts,
        compiler_params=params(),
        cost_estimate=cost(0.1),
        name="block_sum",
    )(*terms)


def scatter_dense(near, far, beside):
    parts = block_sum([near, swap(far, CORE_BIT)], 4)
    got = [swap(parts[1], Y_BIT), swap(parts[2], X_BIT), swap(parts[3], X_BIT | Y_BIT)]
    keep, beside = lax.optimization_barrier((parts[0], beside))
    parts = block_sum([keep] + got, 4)
    return beside, [parts[0]] + [swap(parts[z], Z_BITS[z - 1]) for z in (1, 2, 3)]


def fold_cores_kernel(n0, n1, g0, g1, a_keep, b_keep, a_send, b_send):
    for x in range(2):
        a_keep[x, 0] = n0[x, 0, 0] + g0[x, 0, 0]
        a_send[x, 0] = n1[x, 0, 0] + g1[x, 0, 0]
        out = b_send if x else b_keep
        out[0, 0] = n0[x, 0, 1] + g0[x, 0, 1]
        out[1, 0] = n1[x, 0, 1] + g1[x, 0, 1]


def fold_cores(near, got):
    rows, cols = near[0].shape[3:]
    out = jax.ShapeDtypeStruct((2, 4, rows, cols), BF)
    return pl.pallas_call(
        fold_cores_kernel,
        grid=(4,),
        in_specs=[pl.BlockSpec((2, 1, 2, rows, cols), lambda z: (0, z, 0, 0, 0))] * 4,
        out_specs=[pl.BlockSpec((2, 1, rows, cols), lambda z: (0, z, 0, 0))] * 4,
        out_shape=[out] * 4,
        compiler_params=params(),
        cost_estimate=cost(7),
        name="fold_cores",
    )(*near, *got)


def fold_first_kernel(a_keep, b_keep, a_got, b_got, a_near, b_near, a_far, b_far):
    a_near[0] = a_keep[0, 0] + a_got[0, 0]
    b_near[0] = b_keep[0, 0] + b_got[0, 0]
    a_far[0] = a_keep[1, 0] + a_got[1, 0]
    b_far[0] = b_keep[1, 0] + b_got[1, 0]


def fold_first(a_keep, b_keep, a_got, b_got, after=()):
    rows, cols = a_keep.shape[2:]
    return pl.pallas_call(
        behind(fold_first_kernel, 4, after),
        grid=(4,),
        in_specs=[pl.BlockSpec((2, 1, rows, cols), lambda z: (0, z, 0, 0))] * 4 + unread(after),
        out_specs=[pl.BlockSpec((1, rows, cols), lambda z: (z, 0, 0))] * 4,
        out_shape=[jax.ShapeDtypeStruct((4, rows, cols), BF)] * 4,
        compiler_params=params(),
        cost_estimate=cost(4),
        name="fold_first",
    )(a_keep, b_keep, a_got, b_got, *after)


def fold_second_kernel(a_keep, b_keep, a_got, b_got, *parts):
    for z in range(4):
        parts[z][0] = a_keep[z] + a_got[z]
        parts[z][1] = b_keep[z] + b_got[z]


def fold_second(a_keep, b_keep, a_got, b_got):
    return pl.pallas_call(
        fold_second_kernel,
        out_shape=[jax.ShapeDtypeStruct((2,) + a_keep.shape[1:], BF)] * 4,
        compiler_params=params(),
        cost_estimate=cost(3),
        name="fold_second",
    )(a_keep, b_keep, a_got, b_got)


def total_of(array):
    return jnp.sum(jnp.sum(array, axis=1, keepdims=True), axis=0, keepdims=True)


def expert_update_kernel(given, *refs):
    parts, (wi, fi, si, wo, fo, so, before), refs = refs[:4], refs[4:11], refs[11:]
    outs, sums = refs[given : given + 6], refs[given + 6]
    lane = lane_iota(1, 128)
    kept, moved = before[0:1, :], before[1:2, :]
    for m, (weight, first, second, new) in enumerate(((wi, fi, si, outs[0:3]), (wo, fo, so, outs[3:6]))):
        grad = parts[0][m].astype(F32)
        for part in parts[1:]:
            grad = grad + part[m].astype(F32)
        if m:
            grad = grad.T
        state = moments(weight[0], grad, first[0], second[0])
        for ref, value in zip(new, state):
            ref[0] = value
        slot = lane == (10 if m else 8)
        kept += jnp.where(slot, total_of(weight[0] * weight[0]), 0.0)
        moved += jnp.where(slot, total_of(state[2] * state[2]), 0.0)
    sums[...] = jnp.zeros_like(sums)
    sums[0:1, :] = kept
    sums[1:2, :] = moved


def expert_update(parts, arrays, sums, slice_index, done=()):
    rows, cols = parts[0].shape[1:]
    part = pl.BlockSpec(parts[0].shape, lambda i: (0, 0, 0))
    enter = pl.BlockSpec((1, rows, cols), lambda i: (0, 0, slice_index))
    leave = pl.BlockSpec((1, cols, rows), lambda i: (0, slice_index, 0))
    total = pl.BlockSpec((8, 128), lambda i: (0, 0))
    shape = jax.ShapeDtypeStruct(arrays[0].shape, F32)
    return pl.pallas_call(
        functools.partial(expert_update_kernel, len(done)),
        grid=(1,),
        in_specs=[part] * 4 + [enter] * 3 + [leave] * 3 + [total] + unread(done),
        out_specs=[enter] * 3 + [leave] * 3 + [total],
        out_shape=[shape] * 6 + [jax.ShapeDtypeStruct((8, 128), F32)],
        input_output_aliases={11 + j: j for j in range(len(done))},
        compiler_params=params(),
        cost_estimate=cost(0.1),
        name=f"expert_update_{slice_index}",
    )(*parts, *arrays, sums, *done)


def narrow(row, columns, rows):
    spread = jnp.where(lane_iota(rows, 128) % rows == row_iota(rows, 128), row, 0.0)
    chosen = (row_iota(128, columns) // rows == lane_iota(128, columns)).astype(F32)
    return lax.dot_general(
        spread, chosen, (((1,), (0,)), ((), ())), preferred_element_type=F32, precision=lax.Precision.HIGHEST
    )


def dense_update_kernel(*refs):
    ins, sums, states, outs = refs[:4], refs[4], refs[5:23], refs[23:]
    width = ins[0].shape[2] - 128
    total = ins[0][0].astype(F32)
    for t in ins[1:]:
        total = total + t[0].astype(F32)
    small = unsplit(total[:, width:])
    experts, rows = states[6].shape[1], states[6].shape[0]
    bias_rows = states[12].shape[1] // 128
    grads = (
        total[:, : width * 3 // 4],
        total[:, width * 3 // 4 : width],
        narrow(small[bias_rows + 1 : bias_rows + 2], experts, rows),
        narrow(small[bias_rows + 2 : bias_rows + 3], 5, rows),
        jnp.concatenate([small[j : j + 1] for j in range(bias_rows)], axis=1),
        small[bias_rows : bias_rows + 1],
    )
    lane = lane_iota(1, 128)
    kept, moved = sums[0:1, :], sums[1:2, :]
    for j, grad in enumerate(grads):
        weight, first, second = (states[3 * j + k][...] for k in range(3))
        state = moments(weight, grad, first, second)
        for k in range(3):
            outs[3 * j + k][...] = state[k]
        for c, slot in enumerate({0: (0,), 1: (1,), 2: (2,), 3: (3, 4, 5, 6, 7), 4: (9,), 5: (11,)}[j]):
            cut = (slice(None), slice(c, c + 1)) if j == 3 else (slice(None), slice(None))
            kept += jnp.where(lane == slot, total_of(weight[cut] * weight[cut]), 0.0)
            moved += jnp.where(lane == slot, total_of(state[2][cut] * state[2][cut]), 0.0)
    outs[18][...] = jnp.zeros_like(outs[18])
    outs[18][0:1, :] = kept
    outs[18][1:2, :] = moved


def dense_update(terms, sums, states):
    return pl.pallas_call(
        dense_update_kernel,
        out_shape=[jax.ShapeDtypeStruct(a.shape, F32) for a in states] + [jax.ShapeDtypeStruct((8, 128), F32)],
        compiler_params=params(),
        cost_estimate=cost(0.1),
        name="dense_update",
    )(*terms, sums, *states)


def new_weights_kernel(sums, counts, *refs):
    weights, steps, outs, norms = refs[:8], refs[8:16], refs[16:24], refs[24]
    weight_rms = jnp.sqrt(sums[0:1, :] / counts[...])
    step_rms = jnp.sqrt(sums[1:2, :] / counts[...])
    trust = weight_rms / step_rms
    norms[...] = jnp.zeros_like(norms)
    norms[0:1, :] = weight_rms
    norms[1:2, :] = step_rms
    norms[2:3, :] = trust
    for j, begin in enumerate((0, 1, 2, 3, 8, 9, 10, 11)):
        scale = trust[:, 3:8] if j == 3 else trust[:, begin : begin + 1]
        if len(outs[j].shape) == 3:
            outs[j][0] = weights[j][0] - RATE * scale * steps[j][0]
        else:
            outs[j][...] = weights[j][...] - RATE * scale * steps[j][...]


def new_weights(sums, counts, weights, steps):
    return pl.pallas_call(
        new_weights_kernel,
        out_shape=[jax.ShapeDtypeStruct(a.shape, F32) for a in weights] + [jax.ShapeDtypeStruct((8, 128), F32)],
        compiler_params=params(),
        cost_estimate=cost(5),
        name="new_weights",
    )(sums, counts, *weights, *steps)


CHUNKS = 2


def replicate_plan(
    tokens, cotangent, expert_ids, priority,
    heads_in, heads_in_first, heads_in_second, heads_out, heads_out_first, heads_out_second,
    router, router_first, router_second, scales, scales_first, scales_second,
    expert_in, expert_in_first, expert_in_second, bias_in, bias_in_first, bias_in_second,
    expert_out, expert_out_first, expert_out_second, bias_out, bias_out_first, bias_out_second,
):
    count, width = tokens.shape
    images = count // SEQ
    experts = router.shape[1]
    rep, ep = lax.axis_size("rep"), lax.axis_size("ep")
    rep_me, ep_me = lax.axis_index("rep"), lax.axis_index("ep")
    me = (rep_me * ep + ep_me).astype(jnp.int32)
    at = jnp.stack([rep_me, ep_me]).astype(jnp.int32)
    capacity = (5 * expert_ids.shape[1] * count + 4 * experts - 1) // (4 * experts)
    listed = -(-capacity // 16) * 16
    hidden_part = FF // rep
    cols = hidden_part // CHUNKS

    enter_low = expert_in[0].astype(BF)
    leave_low = expert_out[0].astype(BF).T
    pieces = [
        jnp.stack([enter_low[:, k * cols : (k + 1) * cols], leave_low[:, k * cols : (k + 1) * cols]])
        for k in range(CHUNKS)
    ]

    rows_here = heads_in.shape[0]
    small = jnp.concatenate([router, scales], axis=1)
    small = jnp.pad(small, ((0, 0), (0, 128 - small.shape[1])))
    biases = jnp.concatenate([bias_in.reshape(-1, 128), bias_out.reshape(-1, 128)], axis=0)
    biases = jnp.pad(biases, ((0, rows_here - biases.shape[0]), (0, 0)))
    dense = jnp.concatenate([heads_in, heads_out, small, biases], axis=1).astype(BF)
    order = jnp.array([relative(p) for p in range(rep * ep)], jnp.int32)
    place = jnp.bitwise_xor(order, me)
    spread = lambda a, fill: jnp.pad(
        a.reshape(-1, images, SEQ), ((0, 0), (0, 0), (0, PAD - SEQ)), constant_values=fill
    ).reshape(-1, images * PAD)
    ids_rows = spread(expert_ids.T, -1)
    rows = jnp.concatenate([spread(priority, count), ids_rows], axis=0).astype(F32)
    rows = jnp.pad(rows, ((0, 5), (0, 0)))

    zs_got = [swap(dense, bits) for bits in Z_BITS]
    tok_pad, cot_pad = spread_rows(tokens, cotangent)
    zs = stack([dense] + zs_got, after=(tok_pad,))
    zs, pieces[0] = lax.optimization_barrier((zs, pieces[0]))
    others = [swap(zs, bits) for bits in (Y_BIT, X_BIT, X_BIT | Y_BIT)]
    lrow, lcol, meta = find_places(rows, rows.T, capacity, experts)
    piece_got = [swap(pieces[0], bits) for bits in Z_BITS]
    plane = stack([zs] + others, after=(lrow, piece_got[0]))
    in_matrix, out_matrix, router_matrix, gains, small_all = assemble(
        place, plane.reshape((16,) + dense.shape), swap(plane, CORE_BIT).reshape((16,) + dense.shape), experts
    )
    bias_all = small_all[:, 128:].reshape(rep, ep, rows_here, 128)
    in_rows = hidden_part // 128
    enter_bias = bias_all[:, :, :in_rows].reshape(rep, ep, hidden_part).astype(F32).transpose(1, 0, 2)
    leave_bias = bias_all[:, :, in_rows].astype(F32).transpose(1, 0, 2).reshape(ep, 1, width)

    proj, probs, mixed, hidden, routed, gcol, grow = attention(
        tok_pad, in_matrix, out_matrix, router_matrix, gains, ids_rows.T
    )
    near = turn_stack([pieces[0]] + piece_got, after=(gcol,))
    far_x, far_y = swap(near, X_BIT), swap(near, Y_BIT)
    near, pieces[1] = lax.optimization_barrier((near, pieces[1]))
    lists = gather(meta, routed, cot_pad, lrow, grow, listed, after=(near,))
    near_two = turn_stack([pieces[1]] + [swap(pieces[1], bits) for bits in Z_BITS], after=(lists[0],))

    totals_here = meta[images - 1] + meta[2 * images - 1]
    at = jnp.concatenate([at, totals_here])
    bias_cut = lambda k: enter_bias[:, :, k * cols : (k + 1) * cols]
    cross = lambda a: swap(a, CORE_BIT)

    def first_half(near, far_x, crossed):
        pairs = []
        for m in range(2):
            other = (crossed[1][m], 0) if isinstance(crossed[1], tuple) else (crossed[1], m)
            pairs += [(near, m), (crossed[0], m), (far_x, m), other]
        return pairs

    def other_half(far_y, far_xy, crossed):
        return [
            pair
            for m in range(2)
            for pair in ((far_y, m), (crossed[0], m), (far_xy[m], 0), (crossed[1 + m], 0))
        ]

    x_in, x_out, y_out = pick(far_x, far_y, after=(near_two,))
    far_xy = swap(x_in, Y_BIT), swap(y_out, X_BIT)
    near, x_in = lax.optimization_barrier((near, x_in))
    crossed = cross(near), (cross(x_in), cross(x_out))
    y_part, d_part, near_a, far_a, bias_a, leave_a = expert_pass(
        at, lists, first_half(near, far_x, crossed), bias_cut(0)
    )
    y_part, *far_xy = lax.optimization_barrier((y_part, *far_xy))
    far_x_two, far_y_two = swap(near_two, X_BIT), swap(near_two, Y_BIT)
    crossed = cross(far_y), cross(far_xy[0]), cross(far_xy[1])
    y_half, d_half, near_b, far_b, bias_b, leave_b = expert_pass(
        at, lists, other_half(far_y, far_xy, crossed), bias_cut(0), half=1, done=(y_part, d_part),
    )
    got_a = swap(far_a, CORE_BIT)
    far_b, far_x_two, far_y_two = lax.optimization_barrier((far_b, far_x_two, far_y_two))
    diagonal = far_x_two[0:1], far_y_two[1:2]
    crossed = cross(near_two), cross(far_x_two)
    got_b = swap(far_b, CORE_BIT)
    one = fold_cores((near_a, near_b), (got_a, got_b))
    far_y_crossed = cross(far_y_two)
    a_send, far_y_crossed, *diagonal = lax.optimization_barrier((one[2], far_y_crossed, *diagonal))
    one = (*one[:2], a_send, one[3])
    far_xy_two = swap(diagonal[0], Y_BIT), swap(diagonal[1], X_BIT)
    even = lax.bitwise_xor(jnp.arange(ep, dtype=jnp.int32), ep_me)[:, None, None] % 2 == 0
    grad_bias = [jnp.where(even, bias_a, bias_b)]
    grad_leave_bias = jnp.where(even, leave_a, leave_b)
    one_got = swap(one[2], Y_BIT), swap(one[3], X_BIT)
    y_part, d_part, near_a, far_a, bias_a = expert_pass(
        at, lists, first_half(near_two, far_x_two, crossed), bias_cut(1), leave_bias, (y_half, d_half),
        after=one[2:],
    )
    y_part, *far_xy_two = lax.optimization_barrier((y_part, *far_xy_two))
    crossed = far_y_crossed, cross(far_xy_two[0]), cross(far_xy_two[1])
    got_a = swap(far_a, CORE_BIT)
    y, d, near_b, far_b, bias_b = expert_pass(
        at, lists, other_half(far_y_two, far_xy_two, crossed), bias_cut(1), leave_bias, (y_half, d_half), half=1,
        done=(y_part, d_part),
    )
    far_b, *one_got = lax.optimization_barrier((far_b, *one_got))
    one = fold_first(*one[:2], *one_got)
    one_got = swap(one[2], X_BIT), swap(one[3], Y_BIT)
    got_b = swap(far_b, CORE_BIT)
    two = fold_cores((near_a, near_b), (got_a, got_b))
    two_got = swap(two[2], Y_BIT), swap(two[3], X_BIT)
    output, grad_hidden, grad_mixed, grad_out, grad_router, grad_scale = combine(
        meta, y, d, lcol, gcol, hidden, cot_pad, mixed, out_matrix, router_matrix, gains,
        after=list(one) + list(two[2:]),
    )
    grad_mixed, *one_got = lax.optimization_barrier((grad_mixed, *one_got))
    one = fold_second(*one[:2], *one_got)
    one_got = [swap(one[z], Z_BITS[z - 1]) for z in (1, 2, 3)]
    two = fold_first(*two[:2], *two_got)
    two_got = swap(two[2], X_BIT), swap(two[3], Y_BIT)
    grad_bias.append(jnp.where(even, bias_a, bias_b))
    devices = rep * ep
    by_device = lambda a: jnp.pad(
        a.reshape(a.shape[0], devices, rows_here).transpose(1, 0, 2).reshape(devices, 1, -1),
        ((0, 0), (0, 0), (0, 128 - a.shape[0] * rows_here)),
    )
    small_grads = jnp.concatenate(
        [
            jnp.concatenate(grad_bias, axis=2).transpose(1, 0, 2).reshape(devices, in_rows, 128),
            grad_leave_bias.reshape(ep, rep, 128).transpose(1, 0, 2).reshape(devices, 1, 128),
            by_device(grad_router),
            by_device(grad_scale[:5]),
        ],
        axis=1,
    )
    small_grads = jnp.pad(small_grads, ((0, 0), (0, 8 - small_grads.shape[1]), (0, 0)))
    input_grad, near_dense, far_dense = attention_back(
        place, proj, probs, grad_mixed, grad_hidden, tok_pad, in_matrix, gains, grad_out, small_grads,
        after=list(one[1:]) + list(two[2:]),
    )
    far_dense, *got = lax.optimization_barrier((far_dense, *one_got, *two_got))
    one_got, two_got = got[:3], got[3:]
    two = fold_second(*two[:2], *two_got)
    far_dense, *two = lax.optimization_barrier((far_dense, *two))
    two_got = [swap(two[z], Z_BITS[z - 1]) for z in (1, 2, 3)]
    expert_states = (expert_in, expert_in_first, expert_in_second, expert_out, expert_out_first, expert_out_second)
    *expert_new, sums = expert_update([one[0]] + list(one_got), expert_states, jnp.zeros((8, 128), F32), 0)
    sums, dense_terms = scatter_dense(near_dense, far_dense, sums)
    dense_states = (
        heads_in, heads_in_first, heads_in_second, heads_out, heads_out_first, heads_out_second,
        router, router_first, router_second, scales, scales_first, scales_second,
        bias_in, bias_in_first, bias_in_second, bias_out, bias_out_first, bias_out_second,
    )
    *dense_new, sums = dense_update(dense_terms, sums, dense_states)
    sums, *two_got = lax.optimization_barrier((sums, *two_got))
    *expert_new, sums = expert_update([two[0]] + two_got, expert_states, sums, 1, done=expert_new)
    in_first, in_second, in_step, out_first, out_second, out_step = expert_new
    sums = sum_everywhere(sums)
    counts = jnp.array(
        [3 * width * width, width * width, width * experts]
        + [width] * 5
        + [experts * width * FF, experts * FF, experts * FF * width, experts * width]
        + [1] * (128 - 12),
        jnp.float32,
    )[None]
    trio = lambda j: tuple(dense_new[3 * j : 3 * j + 3])
    states = [
        trio(0), trio(1), trio(2), trio(3), (in_first, in_second, in_step), trio(4),
        (out_first, out_second, out_step), trio(5),
    ]
    weights_now = (heads_in, heads_out, router, scales, expert_in, bias_in, expert_out, bias_out)
    *fresh, norms = new_weights(sums, counts, weights_now, [state[2] for state in states])
    results = [output, input_grad]
    for state, weight in zip(states, fresh):
        results.extend([state[0], state[1], weight])
    results.append(norms[:3, :12])
    return tuple(results)


def expert_front(rows, enter_weight, enter_bias):
    pre = jnp.einsum("sjcd,jdf->sjcf", rows, enter_weight, preferred_element_type=jnp.float32)
    return pre + enter_bias.astype(jnp.float32)[None, :, None, :]


def exchange_plan(
    tokens,
    cotangent,
    expert_ids,
    priority,
    heads_in,
    heads_in_first,
    heads_in_second,
    heads_out,
    heads_out_first,
    heads_out_second,
    router,
    router_first,
    router_second,
    scales,
    scales_first,
    scales_second,
    expert_in,
    expert_in_first,
    expert_in_second,
    bias_in,
    bias_in_first,
    bias_in_second,
    expert_out,
    expert_out_first,
    expert_out_second,
    bias_out,
    bias_out_first,
    bias_out_second,
):
    in_matrix, out_matrix, router_matrix, scale_table = (
        lax.all_gather(heads_in.astype(jnp.bfloat16), ("rep", "ep"), axis=0, tiled=True),
        lax.all_gather(heads_out.astype(jnp.bfloat16), ("rep", "ep"), axis=0, tiled=True),
        lax.all_gather(router.astype(jnp.bfloat16), ("rep", "ep"), axis=0, tiled=True),
        lax.all_gather(scales.astype(jnp.bfloat16), ("rep", "ep"), axis=0, tiled=True),
    )
    enter_weight, enter_bias, leave_weight, leave_bias = (
        lax.all_gather(expert_in.astype(jnp.bfloat16), "rep", axis=2, tiled=True),
        lax.all_gather(bias_in.astype(jnp.bfloat16), "rep", axis=1, tiled=True),
        lax.all_gather(expert_out.astype(jnp.bfloat16), "rep", axis=1, tiled=True),
        lax.all_gather(bias_out.astype(jnp.bfloat16), "rep", axis=1, tiled=True),
    )
    gains = scale_table.astype(jnp.float32)
    inputs = tokens.astype(jnp.float32)
    count, width = inputs.shape
    images = count // SEQ
    factor = HEAD ** (-0.5)
    normed_one, inverse_one = normalize(inputs)
    entry = (normed_one * gains[:, 0] + gains[:, 1]).astype(jnp.bfloat16)
    projected = jnp.dot(entry, in_matrix, preferred_element_type=jnp.float32).astype(jnp.bfloat16)
    grid = projected.reshape(images, SEQ, 3, HEADS, HEAD)
    query = grid[:, :, 0]
    keyed = grid[:, :, 1]
    valued = grid[:, :, 2]
    scores = attention_scores(query, keyed, factor)
    peak = jnp.max(scores, axis=-1, keepdims=True)
    log_total = peak + jnp.log(jnp.sum(jnp.exp(scores - peak), axis=-1, keepdims=True))
    weights = jnp.exp(scores - log_total).astype(jnp.bfloat16)
    mixed = jnp.einsum("bhqk,bkhd->bqhd", weights, valued, preferred_element_type=jnp.float32)
    mixed = mixed.reshape(count, width).astype(jnp.bfloat16)
    hidden = inputs + jnp.dot(mixed, out_matrix, preferred_element_type=jnp.float32) + gains[:, 4]
    normed_two, inverse_two = normalize(hidden)
    routed = (normed_two * gains[:, 2] + gains[:, 3]).astype(jnp.bfloat16)
    logits = jnp.dot(routed, router_matrix, preferred_element_type=jnp.float32)
    experts = logits.shape[1]
    top = expert_ids.shape[1]
    choose = (expert_ids[:, :, None] == jnp.arange(experts, dtype=jnp.int32)[None, None, :]).astype(
        jnp.float32
    )
    picked = jnp.sum(choose * logits[:, None, :], axis=2)
    gates = jax.nn.softmax(picked, axis=1)
    places = route_places(expert_ids, priority[0], experts)
    capacity = (5 * top * count + 4 * experts - 1) // (4 * experts)
    groups = lax.axis_size("ep")
    local = experts // groups
    slots = experts * capacity
    slot = jnp.where(places < capacity, expert_ids * capacity + places, slots)
    pair_of_slot = (
        jnp.full((slots,), count * top, jnp.int32)
        .at[slot.reshape(-1)]
        .set(jnp.arange(count * top, dtype=jnp.int32), mode="drop")
    )
    token_of_slot = pair_of_slot // top
    padded_rows = jnp.concatenate([routed, jnp.zeros((1, width), jnp.bfloat16)], axis=0)
    outgoing = padded_rows[token_of_slot].reshape(groups, local, capacity, width)
    arrived = lax.all_to_all(outgoing, "ep", split_axis=0, concat_axis=0, tiled=True)
    pre = expert_front(arrived, enter_weight, enter_bias)
    act, gelu_back = jax.vjp(exact_gelu, pre)
    act_low = act.astype(jnp.bfloat16)
    result = jnp.einsum("sjcf,jfd->sjcd", act_low, leave_weight, preferred_element_type=jnp.float32)
    result = (result + leave_bias.astype(jnp.float32)[None, :, None, :]).astype(jnp.bfloat16)
    returned = lax.all_to_all(result, "ep", split_axis=0, concat_axis=0, tiled=True).reshape(
        slots, width
    )
    padded_back = jnp.concatenate([returned, jnp.zeros((1, width), jnp.bfloat16)], axis=0)
    picked_rows = padded_back[slot].astype(jnp.float32)
    output = hidden + jnp.sum(gates[:, :, None] * picked_rows, axis=1)
    grad_output = cotangent.astype(jnp.float32)
    grad_gates = jnp.sum(picked_rows * grad_output[:, None, :], axis=2)
    gate_list = jnp.concatenate([gates.reshape(-1), jnp.zeros((1,), jnp.float32)])
    padded_grad = jnp.concatenate([grad_output, jnp.zeros((1, width), jnp.float32)], axis=0)
    grad_slots = (padded_grad[token_of_slot] * gate_list[pair_of_slot][:, None]).astype(
        jnp.bfloat16
    )
    grad_arrived = lax.all_to_all(
        grad_slots.reshape(groups, local, capacity, width),
        "ep",
        split_axis=0,
        concat_axis=0,
        tiled=True,
    )
    grad_act = jnp.einsum(
        "sjcd,jfd->sjcf", grad_arrived, leave_weight, preferred_element_type=jnp.float32
    )
    grad_pre = gelu_back(grad_act)[0].astype(jnp.bfloat16)
    grad_leave = jnp.einsum(
        "sjcf,sjcd->jfd", act_low, grad_arrived, preferred_element_type=jnp.float32
    )
    grad_leave_bias = jnp.sum(grad_arrived, axis=(0, 2), dtype=jnp.float32)
    grad_enter = jnp.einsum("sjcd,sjcf->jdf", arrived, grad_pre, preferred_element_type=jnp.float32)
    grad_enter_bias = jnp.sum(grad_pre, axis=(0, 2), dtype=jnp.float32)
    grad_rows = jnp.einsum(
        "sjcf,jdf->sjcd", grad_pre, enter_weight, preferred_element_type=jnp.float32
    ).astype(jnp.bfloat16)
    grad_back = lax.all_to_all(grad_rows, "ep", split_axis=0, concat_axis=0, tiled=True).reshape(
        slots, width
    )
    padded_grad_back = jnp.concatenate([grad_back, jnp.zeros((1, width), jnp.bfloat16)], axis=0)
    grad_routed = jnp.sum(padded_grad_back[slot], axis=1, dtype=jnp.float32)
    grad_picked = gates * (grad_gates - jnp.sum(gates * grad_gates, axis=1, keepdims=True))
    grad_logits = jnp.sum(choose * grad_picked[:, :, None], axis=1).astype(jnp.bfloat16)
    grad_router = jnp.einsum("td,te->de", routed, grad_logits, preferred_element_type=jnp.float32)
    grad_routed = grad_routed + jnp.einsum(
        "te,de->td", grad_logits, router_matrix, preferred_element_type=jnp.float32
    )
    grad_gain_two = jnp.sum(grad_routed * normed_two, axis=0)
    grad_shift_two = jnp.sum(grad_routed, axis=0)
    grad_hidden = grad_output + norm_back(grad_routed, normed_two, inverse_two, gains[:, 2])
    grad_shift_out = jnp.sum(grad_hidden, axis=0)
    grad_mix_out = grad_hidden.astype(jnp.bfloat16)
    grad_out_matrix = jnp.einsum(
        "td,te->de", mixed, grad_mix_out, preferred_element_type=jnp.float32
    )
    grad_mixed = jnp.einsum(
        "te,de->td", grad_mix_out, out_matrix, preferred_element_type=jnp.float32
    )
    grad_mixed = grad_mixed.astype(jnp.bfloat16).reshape(images, SEQ, HEADS, HEAD)
    probs = jnp.exp(attention_scores(query, keyed, factor) - log_total)
    weights_again = probs.astype(jnp.bfloat16)
    grad_valued = jnp.einsum(
        "bhqk,bqhd->bkhd", weights_again, grad_mixed, preferred_element_type=jnp.float32
    )
    grad_probs = jnp.einsum(
        "bqhd,bkhd->bhqk", grad_mixed, valued, preferred_element_type=jnp.float32
    )
    grad_scores = (
        probs * (grad_probs - jnp.sum(probs * grad_probs, axis=-1, keepdims=True))
    ).astype(jnp.bfloat16)
    grad_query = (
        jnp.einsum("bhqk,bkhd->bqhd", grad_scores, keyed, preferred_element_type=jnp.float32)
        * factor
    )
    grad_keyed = (
        jnp.einsum("bhqk,bqhd->bkhd", grad_scores, query, preferred_element_type=jnp.float32)
        * factor
    )
    grad_projected = (
        jnp.stack([grad_query, grad_keyed, grad_valued], axis=2)
        .reshape(count, 3 * width)
        .astype(jnp.bfloat16)
    )
    grad_in_matrix = jnp.einsum(
        "td,te->de", entry, grad_projected, preferred_element_type=jnp.float32
    )
    grad_entry = jnp.einsum(
        "te,de->td", grad_projected, in_matrix, preferred_element_type=jnp.float32
    )
    grad_gain_one = jnp.sum(grad_entry * normed_one, axis=0)
    grad_shift_one = jnp.sum(grad_entry, axis=0)
    input_grad = grad_hidden + norm_back(grad_entry, normed_one, inverse_one, gains[:, 0])
    grad_scales = jnp.stack(
        [grad_gain_one, grad_shift_one, grad_gain_two, grad_shift_two, grad_shift_out], axis=1
    )
    summed_dense = (
        lax.psum_scatter(grad_in_matrix, ("rep", "ep"), scatter_dimension=0, tiled=True),
        lax.psum_scatter(grad_out_matrix, ("rep", "ep"), scatter_dimension=0, tiled=True),
        lax.psum_scatter(grad_router, ("rep", "ep"), scatter_dimension=0, tiled=True),
        lax.psum_scatter(grad_scales, ("rep", "ep"), scatter_dimension=0, tiled=True),
    )
    summed_expert = (
        lax.psum_scatter(
            grad_enter.astype(jnp.bfloat16), "rep", scatter_dimension=2, tiled=True
        ).astype(jnp.float32),
        lax.psum_scatter(
            grad_enter_bias.astype(jnp.bfloat16), "rep", scatter_dimension=1, tiled=True
        ).astype(jnp.float32),
        lax.psum_scatter(
            grad_leave.astype(jnp.bfloat16), "rep", scatter_dimension=1, tiled=True
        ).astype(jnp.float32),
        lax.psum_scatter(
            grad_leave_bias.astype(jnp.bfloat16), "rep", scatter_dimension=1, tiled=True
        ).astype(jnp.float32),
    )
    weights_now = (heads_in, heads_out, router, scales, expert_in, bias_in, expert_out, bias_out)
    grads_now = tuple(summed_dense) + tuple(summed_expert)
    firsts = (
        heads_in_first,
        heads_out_first,
        router_first,
        scales_first,
        expert_in_first,
        bias_in_first,
        expert_out_first,
        bias_out_first,
    )
    seconds = (
        heads_in_second,
        heads_out_second,
        router_second,
        scales_second,
        expert_in_second,
        bias_in_second,
        expert_out_second,
        bias_out_second,
    )
    states = [moments(w, g, f, s) for w, g, f, s in zip(weights_now, grads_now, firsts, seconds)]
    weight_terms = jnp.concatenate([squares(w, index == 3) for index, w in enumerate(weights_now)])
    step_terms = jnp.concatenate(
        [squares(state[2], index == 3) for index, state in enumerate(states)]
    )
    totals = lax.psum(jnp.stack([weight_terms, step_terms]), ("rep", "ep"))
    return (output, input_grad) + finish(totals, weights_now, states, width, experts)


def solution(mesh):
    in_specs = (
        P(("rep", "ep"), None),
        P(("rep", "ep"), None),
        P(("rep", "ep"), None),
        P(("rep", "ep"), None),
        P(("rep", "ep"), None),
        P(("rep", "ep"), None),
        P(("rep", "ep"), None),
        P(("rep", "ep"), None),
        P(("rep", "ep"), None),
        P(("rep", "ep"), None),
        P(("rep", "ep"), None),
        P(("rep", "ep"), None),
        P(("rep", "ep"), None),
        P(("rep", "ep"), None),
        P(("rep", "ep"), None),
        P(("rep", "ep"), None),
        P("ep", None, "rep"),
        P("ep", None, "rep"),
        P("ep", None, "rep"),
        P("ep", "rep"),
        P("ep", "rep"),
        P("ep", "rep"),
        P("ep", "rep", None),
        P("ep", "rep", None),
        P("ep", "rep", None),
        P("ep", "rep"),
        P("ep", "rep"),
        P("ep", "rep"),
    )
    out_specs = (
        P(("rep", "ep"), None),
        P(("rep", "ep"), None),
        P(("rep", "ep"), None),
        P(("rep", "ep"), None),
        P(("rep", "ep"), None),
        P(("rep", "ep"), None),
        P(("rep", "ep"), None),
        P(("rep", "ep"), None),
        P(("rep", "ep"), None),
        P(("rep", "ep"), None),
        P(("rep", "ep"), None),
        P(("rep", "ep"), None),
        P(("rep", "ep"), None),
        P(("rep", "ep"), None),
        P("ep", None, "rep"),
        P("ep", None, "rep"),
        P("ep", None, "rep"),
        P("ep", "rep"),
        P("ep", "rep"),
        P("ep", "rep"),
        P("ep", "rep", None),
        P("ep", "rep", None),
        P("ep", "rep", None),
        P("ep", "rep"),
        P("ep", "rep"),
        P("ep", "rep"),
        P(),
    )
    replicated = mesh.shape["rep"] == 4 and mesh.shape["ep"] == 8
    return jax.shard_map(
        replicate_plan if replicated else exchange_plan,
        mesh=mesh,
        in_specs=in_specs,
        out_specs=out_specs,
        check_vma=False,
    )
```

```python
import functools

import jax
import jax.numpy as jnp
from jax import lax
from jax.experimental import pallas as pl
from jax.experimental.pallas import tpu as pltpu
from jax.sharding import PartitionSpec as P

HEADS = 8
HEAD = 64
FF = 2048
SEQ = 197
STEP = 5


BETA = 0.5
RATE = 0.3
DECAY = 0.01
EPSILON = 1e-06


def normalize(rows):
    centred = rows - jnp.mean(rows, axis=-1, keepdims=True)
    inverse = lax.rsqrt(jnp.mean(centred * centred, axis=-1, keepdims=True) + 1e-06)
    return (centred * inverse, inverse)


def norm_back(grad_rows, normed, inverse, gain):
    scaled = grad_rows * gain
    return inverse * (
        scaled
        - jnp.mean(scaled, axis=-1, keepdims=True)
        - normed * jnp.mean(scaled * normed, axis=-1, keepdims=True)
    )


def exact_gelu(values):
    return jax.nn.gelu(values, approximate=False)


def route_places(block_ids, ranking, experts):
    count = block_ids.shape[0]
    keys = jnp.arange(block_ids.shape[1], dtype=jnp.int32)[None, :] * count + ranking[:, None]
    ordered = (
        jnp.zeros((block_ids.size,), jnp.int32).at[keys.reshape(-1)].set(block_ids.reshape(-1))
    )
    hits = (ordered[:, None] == jnp.arange(experts, dtype=jnp.int32)[None, :]).astype(jnp.int32)
    before = jnp.cumsum(hits, axis=0) - hits
    place = jnp.sum(before * hits, axis=1)
    return place[keys]


def attention_scores(query, keyed, factor):
    return jnp.einsum("bqhd,bkhd->bhqk", query, keyed, preferred_element_type=jnp.float32) * factor


def moments(weight, grad, first, second):
    first_new = BETA * first + (1.0 - BETA) * grad
    second_new = BETA * second + (1.0 - BETA) * grad * grad
    step = (
        first_new / (1.0 - BETA**STEP) / (jnp.sqrt(second_new / (1.0 - BETA**STEP)) + EPSILON)
        + DECAY * weight
    )
    return (first_new, second_new, step)


def squares(array, per_column):
    if per_column:
        return jnp.sum(array * array, axis=0)
    return jnp.sum(array * array)[None]


def finish(totals, weights_now, states, width, experts):
    counts = jnp.array(
        [3 * width * width, width * width, width * experts]
        + [width] * 5
        + [experts * width * FF, experts * FF, experts * FF * width, experts * width],
        jnp.float32,
    )
    weight_rms = jnp.sqrt(totals[0] / counts)
    step_rms = jnp.sqrt(totals[1] / counts)
    trust = weight_rms / step_rms
    bounds = [(0, 1), (1, 2), (2, 3), (3, 8), (8, 9), (9, 10), (10, 11), (11, 12)]
    results = []
    for weight, state, bound in zip(weights_now, states, bounds):
        results.extend([state[0], state[1], weight - RATE * trust[bound[0] : bound[1]] * state[2]])
    results.append(jnp.stack([weight_rms, step_rms, trust]))
    return tuple(results)


PAD = 208
WIN = 96
VMEM = 60 * 1024 * 1024
BF = jnp.bfloat16
F32 = jnp.float32


def dot_nn(a, b):
    return lax.dot_general(a, b, (((1,), (0,)), ((), ())), preferred_element_type=F32)


def dot_nt(a, b):
    return lax.dot_general(a, b, (((1,), (1,)), ((), ())), preferred_element_type=F32)


def dot_tn(a, b):
    return lax.dot_general(a, b, (((0,), (0,)), ((), ())), preferred_element_type=F32)


def lane_iota(rows, lanes):
    return lax.broadcasted_iota(jnp.int32, (rows, lanes), 1)


def row_iota(rows, lanes):
    return lax.broadcasted_iota(jnp.int32, (rows, lanes), 0)


def whole(shape):
    return pl.BlockSpec(shape, lambda *_: (0,) * len(shape))


def cost(micros):
    return pl.CostEstimate(flops=int(micros * 1e9), bytes_accessed=int(micros * 1e5), transcendentals=0)


def params(**kw):
    return pltpu.CompilerParams(vmem_limit_bytes=VMEM, **kw)


def behind(kernel, inputs, after):
    def body(*refs):
        return kernel(*refs[:inputs], *refs[inputs + len(after) :])

    return body


def unread(after):
    return [pl.BlockSpec(memory_space=pl.ANY)] * len(after)


def assemble_kernel(place_ref, near_ref, far_ref, in_ref, out_ref, router_ref, gains_ref, small_ref):
    copies, rows = near_ref.shape[0], near_ref.shape[1]
    width = out_ref.shape[1]
    for side, got_ref in enumerate((near_ref, far_ref)):
        for j in range(copies):
            place = pl.multiple_of(place_ref[side * copies + j] * rows, rows)
            in_ref[pl.ds(place, rows), :] = got_ref[j, :, : 3 * width]
            out_ref[pl.ds(place, rows), :] = got_ref[j, :, 3 * width : 4 * width]
            small_ref[pl.ds(place, rows), :] = got_ref[j, :, 4 * width :]
    turned = small_ref[:, :128].astype(F32).T
    experts = router_ref.shape[0]
    router_ref[...] = turned[:experts].astype(BF)
    gains_ref[...] = turned[experts : experts + 8]


def assemble(place, near, far, experts):
    copies, rows, lanes = near.shape
    width = 2 * copies * rows
    return pl.pallas_call(
        assemble_kernel,
        grid_spec=pltpu.PrefetchScalarGridSpec(
            num_scalar_prefetch=1,
            grid=(1,),
            in_specs=[whole(near.shape)] * 2,
            out_specs=[
                whole((width, 3 * width)),
                whole((width, width)),
                whole((experts, width)),
                whole((8, width)),
                whole((width, lanes - 4 * width)),
            ],
        ),
        out_shape=[
            jax.ShapeDtypeStruct((width, 3 * width), BF),
            jax.ShapeDtypeStruct((width, width), BF),
            jax.ShapeDtypeStruct((experts, width), BF),
            jax.ShapeDtypeStruct((8, width), F32),
            jax.ShapeDtypeStruct((width, lanes - 4 * width), BF),
        ],
        compiler_params=params(),
        cost_estimate=cost(1),
        name="assemble",
    )(place, near, far)


def places_kernel(capacity, rows_ref, cols_ref, lrow_ref, lcol_ref, meta_ref):
    count = cols_ref.shape[0]
    images = count // PAD
    experts = lcol_ref.shape[1]
    expert = lane_iota(count, experts).astype(F32)
    first = (cols_ref[:, 1:2] == expert).astype(F32)
    second = (cols_ref[:, 2:3] == expert).astype(F32)
    first_low = first.astype(BF)
    second_low = second.astype(BF)
    total_first = jnp.sum(first, axis=0, keepdims=True)
    lower = (lane_iota(PAD, PAD) < row_iota(PAD, PAD)).astype(F32).astype(BF)
    ranking = rows_ref[0:1, :]
    begin = jnp.zeros((1, experts), F32)
    for i in range(images):
        span = slice(i * PAD, (i + 1) * PAD)
        ahead = (ranking < cols_ref[span, 0:1]).astype(F32).astype(BF)
        rank_first = dot_nn(ahead, first_low)
        rank_second = dot_nn(ahead, second_low) + total_first
        place = first[span] * rank_first + second[span] * rank_second
        kept = (first[span] + second[span]) * (place < capacity).astype(F32)
        local = dot_nn(lower, kept.astype(BF))
        local = jnp.where(kept > 0.0, local, -1.0)
        lcol_ref[span, :] = local
        lrow_ref[i] = local.T
        here = jnp.sum(kept, axis=0, keepdims=True)
        meta_ref[i : i + 1, :] = begin.astype(jnp.int32)
        meta_ref[images + i : images + i + 1, :] = here.astype(jnp.int32)
        begin = begin + here


def find_places(rows, cols, capacity, experts):
    count = cols.shape[0]
    images = count // PAD
    return pl.pallas_call(
        functools.partial(places_kernel, capacity),
        out_shape=[
            jax.ShapeDtypeStruct((images, experts, PAD), F32),
            jax.ShapeDtypeStruct((count, experts), F32),
            jax.ShapeDtypeStruct((2 * images, experts), jnp.int32),
        ],
        compiler_params=params(),
        cost_estimate=cost(2),
        name="places",
    )(rows, cols)


def spread_kernel(tok_ref, cot_ref, tpad_ref, cpad_ref):
    count, width = tok_ref.shape
    for source, target in ((tok_ref, tpad_ref), (cot_ref, cpad_ref)):
        for i in range(count // SEQ):
            rows = source[SEQ * i : SEQ * (i + 1), :].astype(F32)
            rows = jnp.concatenate([rows, jnp.zeros((PAD - SEQ, width), F32)], axis=0)
            target[PAD * i : PAD * (i + 1), :] = rows.astype(BF)


def spread_rows(tokens, cotangent):
    count, width = tokens.shape
    shape = jax.ShapeDtypeStruct((count // SEQ * PAD, width), BF)
    return pl.pallas_call(
        spread_kernel, out_shape=[shape, shape], compiler_params=params(), cost_estimate=cost(5), name="spread_rows"
    )(tokens, cotangent)


def store_image(target, i, values):
    for image in range(target.shape[0] // SEQ):

        @pl.when(i == image)
        def _(image=image):
            target[SEQ * image : SEQ * (image + 1), :] = values[0:SEQ, :]


def split_halves(block, halves):
    zero = jnp.zeros_like(block)
    return jnp.concatenate([jnp.where(halves, block, zero), jnp.where(halves, zero, block)], axis=0)


def attention_kernel(
    tok_ref, in_ref, out_ref, router_ref, gains_ref, ids_ref,
    proj_ref, prob_ref, mixed_ref, hidden_ref, routed_ref, gcol_ref, grow_ref, mixed_all,
):
    width = tok_ref.shape[1]
    x = tok_ref[...].astype(F32)
    normed, _ = normalize(x)
    entry = (normed * gains_ref[0:1, :] + gains_ref[1:2, :]).astype(BF)
    proj_ref[...] = dot_nn(entry, in_ref[...]).astype(BF)
    pair = 2 * HEAD
    halves = lane_iota(PAD, pair) < HEAD
    key_there = lane_iota(2 * PAD, PAD) < SEQ
    for p in range(HEADS // 2):
        q = proj_ref[:, pair * p : pair * (p + 1)] * jnp.asarray(HEAD ** -0.5, BF)
        k = proj_ref[:, width + pair * p : width + pair * (p + 1)]
        v = proj_ref[:, 2 * width + pair * p : 2 * width + pair * (p + 1)]
        scores = dot_nt(split_halves(q, halves), k)
        scores = jnp.where(key_there, scores, -1e30)
        peak = jnp.max(scores, axis=1, keepdims=True)
        raised = jnp.exp(scores - peak)
        total = jnp.sum(raised, axis=1, keepdims=True)
        weights = (raised * (1.0 / total)).astype(BF)
        prob_ref[0, 2 * p] = weights[:PAD]
        prob_ref[0, 2 * p + 1] = weights[PAD:]
        out = dot_nn(weights, v)
        mixed_all[:, pair * p : pair * (p + 1)] = jnp.where(halves, out[:PAD], out[PAD:]).astype(BF)
    mixed = mixed_all[...]
    mixed_ref[...] = mixed
    hidden = x + dot_nn(mixed, out_ref[...]) + gains_ref[4:5, :]
    hidden_ref[...] = hidden
    normed_two, _ = normalize(hidden)
    routed = (normed_two * gains_ref[2:3, :] + gains_ref[3:4, :]).astype(BF)
    routed_ref[...] = routed
    logits = dot_nt(routed, router_ref[...])
    experts = logits.shape[1]
    expert = lane_iota(PAD, experts)
    chosen = jnp.logical_or(ids_ref[:, 0:1] == expert, ids_ref[:, 1:2] == expert)
    top = jnp.max(jnp.where(chosen, logits, -1e30), axis=1, keepdims=True)
    raised = jnp.where(chosen, jnp.exp(jnp.where(chosen, logits - top, 0.0)), 0.0)
    total = jnp.sum(raised, axis=1, keepdims=True)
    gates = raised / jnp.where(total > 0.0, total, 1.0)
    gcol_ref[...] = gates
    grow_ref[0] = gates.T


def attention(tok_pad, in_matrix, out_matrix, router, gains, ids_col, after=()):
    padded, width = tok_pad.shape
    images = padded // PAD
    experts = router.shape[0]
    row = lambda lanes: pl.BlockSpec((PAD, lanes), lambda i: (i, 0))
    once = lambda a: pl.BlockSpec(a.shape, lambda i: (0, 0), pipeline_mode=pl.Buffered(1))
    return pl.pallas_call(
        behind(attention_kernel, 6, after),
        grid=(images,),
        in_specs=[row(width), once(in_matrix), once(out_matrix), once(router), once(gains), row(2)] + unread(after),
        out_specs=[
            row(3 * width),
            pl.BlockSpec((1, HEADS, PAD, PAD), lambda i: (i, 0, 0, 0)),
            row(width), row(width), row(width), row(experts),
            pl.BlockSpec((1, experts, PAD), lambda i: (i, 0, 0)),
        ],
        out_shape=[
            jax.ShapeDtypeStruct((padded, 3 * width), BF),
            jax.ShapeDtypeStruct((images, HEADS, PAD, PAD), BF),
            jax.ShapeDtypeStruct((padded, width), BF),
            jax.ShapeDtypeStruct((padded, width), F32),
            jax.ShapeDtypeStruct((padded, width), BF),
            jax.ShapeDtypeStruct((padded, experts), F32),
            jax.ShapeDtypeStruct((images, experts, PAD), F32),
        ],
        scratch_shapes=[pltpu.VMEM((PAD, width), BF)],
        compiler_params=params(),
        cost_estimate=cost(8),
        name="attention",
    )(tok_pad, in_matrix, out_matrix, router, gains, ids_col, *after)


def window_count():
    return -(-(15 + SEQ) // WIN)


def gather_kernel(meta_ref, routed_ref, cot_ref, lrow_ref, grow_ref, r_ref, g_ref, rt_ref, gt_ref, r_all, g_all):
    e = pl.program_id(0)
    images = lrow_ref.shape[0]
    listed = r_ref.shape[1]
    r_all[...] = jnp.zeros_like(r_all)
    g_all[...] = jnp.zeros_like(g_all)
    row = row_iota(WIN, PAD).astype(F32)
    for i in range(images):
        start, here = meta_ref[i, e], meta_ref[images + i, e]
        base = lax.shift_left(lax.shift_right_logical(start, 4), 4)
        shift = (start - base).astype(F32)
        local = lrow_ref[i, pl.ds(e, 1), :]
        gate = grow_ref[i, pl.ds(e, 1), :]
        for q in range(window_count()):
            @pl.when(jnp.logical_and(here > 0, base + q * WIN < start + here))
            def _(i=i, q=q, base=base, shift=shift, local=local, gate=gate):
                pick = jnp.logical_and(local >= 0.0, local + (shift - q * WIN) == row)
                low = pick.astype(F32).astype(BF)
                slot_gate = jnp.sum(jnp.where(pick, gate, 0.0), axis=1, keepdims=True)
                where = pl.ds(pl.multiple_of(base + q * WIN, 16), WIN)
                r_all[where, :] += dot_nn(low, routed_ref[i * PAD : (i + 1) * PAD, :])
                g_all[where, :] += slot_gate * dot_nn(low, cot_ref[i * PAD : (i + 1) * PAD, :])
    r_ref[0] = r_all[0:listed, :].astype(BF)
    g_ref[0] = g_all[0:listed, :].astype(BF)
    rt_ref[0] = r_all[0:listed, :].T.astype(BF)
    gt_ref[0] = g_all[0:listed, :].astype(BF).astype(F32).T.astype(BF)


def gather(meta, routed, cot_pad, lrow, grow, listed, after=()):
    width = routed.shape[1]
    experts = lrow.shape[1]
    once = lambda a: pl.BlockSpec(a.shape, lambda e, m: (0,) * a.ndim, pipeline_mode=pl.Buffered(1))
    block = pl.BlockSpec((1, listed, width), lambda e, m: (e, 0, 0))
    turned = pl.BlockSpec((1, width, listed), lambda e, m: (e, 0, 0))
    return pl.pallas_call(
        behind(gather_kernel, 5, after),
        grid_spec=pltpu.PrefetchScalarGridSpec(
            num_scalar_prefetch=1,
            grid=(experts,),
            in_specs=[once(routed), once(cot_pad), once(lrow), once(grow)] + unread(after),
            out_specs=[block, block, turned, turned],
            scratch_shapes=[pltpu.VMEM((listed + WIN, width), F32)] * 2,
        ),
        out_shape=[jax.ShapeDtypeStruct((experts, listed, width), BF)] * 2
        + [jax.ShapeDtypeStruct((experts, width, listed), BF)] * 2,
        compiler_params=params(),
        cost_estimate=cost(8),
        name="gather",
    )(meta, routed, cot_pad, lrow, grow, *after)


def gelu_both(pre):
    bell = jnp.exp(-0.5 * (pre * pre))
    t = pl.reciprocal(1.0 + (0.3275911 * 2.0**-0.5) * jnp.abs(pre))
    tail = t * (0.127414796 + t * (-0.142248368 + t * (0.7107068705 + t * (-0.7265760135 + t * 0.5307027145))))
    tail = tail * bell
    phi = jnp.where(pre < 0.0, tail, 1.0 - tail)
    return pre * phi, phi + pre * bell * 0.3989422804014327


def expert_kernel(first, half, at_ref, *refs):
    rep = 4
    (r_ref, g_ref, rt_ref, gt_ref), w_refs, b_ref, refs = refs[:4], refs[4:12], refs[12], refs[13:]
    if first:
        refs = refs[2 * (half > 0) :]
        y_ref, d_ref, near_ref, far_ref, db_ref, obg_ref, y_all, d_all = refs
    else:
        (ob_ref, y_in, d_in), refs = refs[:3], refs[3 + 2 * (half > 0) :]
        y_ref, d_ref, near_ref, far_ref, db_ref, y_all, d_all = refs
    listed = r_ref.shape[1]
    step = pl.program_id(0)
    count = at_ref[2 + lax.bitwise_xor(expert_rank(step, half), at_ref[1])]

    def run(n):
        rows_t, grads_t = rt_ref[0, :, :n], gt_ref[0, :, :n]

        def weights(r):
            place = lax.bitwise_xor(at_ref[0], r)
            return place, w_refs[r][0, 0], w_refs[rep + r][0, 0]

        def enter_part(r):
            place, enter, leave = weights(r)
            pre = dot_nn(r_ref[0, :n, :], enter) + b_ref[0, pl.ds(place, 1), :]
            return pre, dot_nn(g_ref[0, :n, :], leave)

        def middle_part(pre, grad_act):
            act, slope = gelu_both(pre)
            return act.astype(BF), (grad_act * slope).astype(BF)

        def leave_part(r, act, grad_pre):
            place, enter, leave = weights(r)
            out = far_ref if r % 2 else near_ref
            out[r // 2, 0, 0] = dot_nn(rows_t, grad_pre).astype(BF)
            out[r // 2, 0, 1] = dot_nn(grads_t, act).astype(BF)
            db_ref[0, pl.ds(place, 1), :] = jnp.sum(grad_pre.astype(F32), axis=0, keepdims=True)
            y_part = dot_nt(act, leave)
            d_part = dot_nt(grad_pre, enter)
            if r == 0:
                y_all[:n, :] = y_part if first else y_part + y_in[0, :n, :]
                d_all[:n, :] = d_part if first else d_part + d_in[0, :n, :]
            else:
                y_all[:n, :] += y_part
                d_all[:n, :] += d_part

        held = enter_part(0)
        ready = None
        for r in range(rep):
            now = middle_part(*held)
            if r + 1 < rep:
                held = enter_part(r + 1)
            if ready is not None:
                leave_part(r - 1, *ready)
            ready = now
        leave_part(rep - 1, *ready)
        if not first:
            y_ref[0, :n, :] = (y_all[:n, :] + ob_ref[0]).astype(BF)
            d_ref[0, :n, :] = d_all[:n, :].astype(BF)
        else:
            y_ref[0, :n, :] = y_all[:n, :]
            d_ref[0, :n, :] = d_all[:n, :]
        if n < listed:
            y_ref[0, n:, :] = jnp.zeros((listed - n, y_ref.shape[2]), y_ref.dtype)
            d_ref[0, n:, :] = jnp.zeros((listed - n, y_ref.shape[2]), y_ref.dtype)

    if first:
        obg_ref[0] = jnp.sum(g_ref[0].astype(F32), axis=0, keepdims=True)
    short = listed * 3 // 4 // 16 * 16
    pl.when(count <= short)(lambda: run(short))
    pl.when(count > short)(lambda: run(listed))


def expert_rank(step, half):
    return lax.shift_left(lax.bitwise_and(step, 3), 1) + lax.shift_right_logical(step, 2) + half


def expert_pass(at, lists, weights, bias, out_bias=None, carried=None, half=0, done=None, after=()):
    first = carried is None
    rows = lists[0]
    experts, listed, width = rows.shape
    rep, cols = bias.shape[1], bias.shape[2]
    steps = experts // 2
    here = lambda e, at: lax.bitwise_xor(expert_rank(e, half), at[1])
    block = pl.BlockSpec((1, listed, width), lambda e, at: (here(e, at), 0, 0))
    turned = pl.BlockSpec((1, width, listed), lambda e, at: (here(e, at), 0, 0))
    out_w = pl.BlockSpec((rep // 2, 1, 2, width, cols), lambda e, at: (0, e, 0, 0, 0))
    in_specs = [
        block, block, turned, turned,
        *[pl.BlockSpec((1, 1, width, cols), lambda e, at, m=m: (m, e, 0, 0)) for _, m in weights],
        pl.BlockSpec((1, rep, cols), lambda e, at: (here(e, at), 0, 0)),
    ]
    args = list(lists) + [a for a, _ in weights] + [bias]
    kind = F32 if first else BF
    out_specs = [block, block, out_w, out_w, pl.BlockSpec((1, rep, cols), lambda e, at: (here(e, at), 0, 0))]
    out_shape = [
        jax.ShapeDtypeStruct(rows.shape, kind),
        jax.ShapeDtypeStruct(rows.shape, kind),
        jax.ShapeDtypeStruct((rep // 2, steps, 2, width, cols), BF),
        jax.ShapeDtypeStruct((rep // 2, steps, 2, width, cols), BF),
        jax.ShapeDtypeStruct((experts, rep, cols), F32),
    ]
    aliases = {}
    if first:
        out_specs.append(pl.BlockSpec((1, 1, width), lambda e, at: (here(e, at), 0, 0)))
        out_shape.append(jax.ShapeDtypeStruct((experts, 1, width), F32))
    else:
        in_specs += [pl.BlockSpec((1, 1, width), lambda e, at: (here(e, at), 0, 0)), block, block]
        args += [out_bias, *carried]
    if half:
        aliases = {len(args) + 1: 0, len(args) + 2: 1}
        in_specs += unread(done)
        args += list(done)
    kernel = behind(functools.partial(expert_kernel, first, half), len(args) + 1, after)
    return pl.pallas_call(
        kernel,
        grid_spec=pltpu.PrefetchScalarGridSpec(
            num_scalar_prefetch=1,
            grid=(steps,),
            in_specs=in_specs + unread(after),
            out_specs=out_specs,
            scratch_shapes=[pltpu.VMEM((listed, width), F32)] * 2,
        ),
        out_shape=out_shape,
        input_output_aliases=aliases,
        compiler_params=params(),
        cost_estimate=cost(4),
        name=f"experts_{0 if first else 1}{half}",
    )(at, *args, *after)


def combine_kernel(
    meta_ref, y_ref, d_ref, lcol_ref, gcol_ref, hidden_ref, cot_ref, mixed_ref, out_w_ref, router_ref, gains_ref,
    out_ref, gh_ref, gm_ref, dout_ref, drouter_ref, dscale_ref, y_acc, g_acc, d_acc,
):
    i = pl.program_id(0)
    images = pl.num_programs(0)
    experts, listed, width = y_ref.shape
    gates = gcol_ref[...]
    local = lcol_ref[...]
    go = cot_ref[...].astype(F32)
    lane = lane_iota(PAD, WIN).astype(F32)
    expert = lane_iota(PAD, experts)

    def window(e, q, base, shift):
        at = jnp.minimum(base + q * WIN, listed - WIN)
        moved = (at - base).astype(F32)
        spot = local[:, e : e + 1] + shift
        pick = jnp.logical_and(spot == lane + moved, local[:, e : e + 1] >= 0.0)
        pick = jnp.logical_and(pick, spot >= q * WIN)
        low = pick.astype(F32).astype(BF)
        where = pl.ds(pl.multiple_of(at, 16), WIN)
        return dot_nn(low, y_ref[e, where, :]), dot_nn(low, d_ref[e, where, :])

    y_sum = jnp.zeros((PAD, width), F32)
    d_sum = jnp.zeros((PAD, width), F32)
    grad_gates = jnp.zeros((PAD, experts), F32)
    bases = []
    for e in range(experts):
        start = meta_ref[i, e]
        base = lax.shift_left(lax.shift_right_logical(start, 4), 4)
        bases.append((start, base))
        y_tok, d_tok = window(e, 0, base, (start - base).astype(F32))
        y_sum += gates[:, e : e + 1] * y_tok
        d_sum += d_tok
        gg = jnp.sum(go * y_tok, axis=1, keepdims=True)
        grad_gates += jnp.where(expert == e, gg, 0.0)
    y_acc[...] = y_sum
    d_acc[...] = d_sum
    g_acc[...] = grad_gates
    for e in range(experts):
        start, base = bases[e]
        here = meta_ref[images + i, e]
        for q in range(1, window_count()):
            @pl.when(base + q * WIN < start + here)
            def _(e=e, q=q, base=base, start=start):
                y_tok, d_tok = window(e, q, base, (start - base).astype(F32))
                y_acc[...] += gates[:, e : e + 1] * y_tok
                d_acc[...] += d_tok
                gg = jnp.sum(go * y_tok, axis=1, keepdims=True)
                g_acc[...] += jnp.where(expert == e, gg, 0.0)
    hidden = hidden_ref[...]
    y_acc[...] += hidden
    store_image(out_ref, i, y_acc)
    grad_gates = g_acc[...]
    pick = gates * (grad_gates - jnp.sum(gates * grad_gates, axis=1, keepdims=True))
    logit_low = pick.astype(BF)
    grad_routed = d_acc[...] + dot_nn(logit_low, router_ref[...])
    normed, inverse = normalize(hidden)
    routed = (normed * gains_ref[2:3, :] + gains_ref[3:4, :]).astype(BF)
    grad_hidden = go + norm_back(grad_routed, normed, inverse, gains_ref[2:3, :])
    gh_ref[...] = grad_hidden
    grad_mix = grad_hidden.astype(BF)
    gm_ref[...] = dot_nt(grad_mix, out_w_ref[...]).astype(BF)

    @pl.when(i == 0)
    def _():
        dout_ref[...] = jnp.zeros_like(dout_ref)
        drouter_ref[...] = jnp.zeros_like(drouter_ref)
        dscale_ref[...] = jnp.zeros_like(dscale_ref)

    dout_ref[...] += dot_tn(mixed_ref[...], grad_mix)
    drouter_ref[...] += dot_tn(logit_low, routed)
    dscale_ref[2:3, :] += jnp.sum(grad_routed * normed, axis=0, keepdims=True)
    dscale_ref[3:4, :] += jnp.sum(grad_routed, axis=0, keepdims=True)
    dscale_ref[4:5, :] += jnp.sum(grad_hidden, axis=0, keepdims=True)


def combine(meta, y, d, lcol, gcol, hidden, cot_pad, mixed, out_matrix, router, gains, after=()):
    padded, width = hidden.shape
    images = padded // PAD
    experts = y.shape[0]
    row = lambda lanes: pl.BlockSpec((PAD, lanes), lambda i, m: (i, 0))
    once = lambda a: pl.BlockSpec(a.shape, lambda i, m: (0,) * a.ndim, pipeline_mode=pl.Buffered(1))
    return pl.pallas_call(
        behind(combine_kernel, 11, after),
        grid_spec=pltpu.PrefetchScalarGridSpec(
            num_scalar_prefetch=1,
            grid=(images,),
            in_specs=[
                once(y), once(d), row(experts), row(experts), row(width), row(width), row(width),
                once(out_matrix), once(router), once(gains), *unread(after),
            ],
            out_specs=[
                whole((images * SEQ, width)), row(width), row(width), whole((width, width)), whole((experts, width)),
                whole((8, width)),
            ],
            scratch_shapes=[
                pltpu.VMEM((PAD, width), F32), pltpu.VMEM((PAD, experts), F32), pltpu.VMEM((PAD, width), F32),
            ],
        ),
        out_shape=[
            jax.ShapeDtypeStruct((images * SEQ, width), F32),
            jax.ShapeDtypeStruct((padded, width), F32),
            jax.ShapeDtypeStruct((padded, width), BF),
            jax.ShapeDtypeStruct((width, width), F32),
            jax.ShapeDtypeStruct((experts, width), F32),
            jax.ShapeDtypeStruct((8, width), F32),
        ],
        compiler_params=params(),
        cost_estimate=cost(40),
        name="combine",
    )(meta, y, d, lcol, gcol, hidden, cot_pad, mixed, out_matrix, router, gains, *after)


def attention_back_kernel(
    place_ref, proj_ref, prob_ref, gm_ref, gh_ref, tpad_ref, in_ref, gains_ref, dout_ref, small_ref,
    grad_ref, near_ref, far_ref, din_ref, dscale_ref, line_ref, dproj, grad_all,
):
    i = pl.program_id(0)
    width = gm_ref.shape[1]
    pair = 2 * HEAD
    halves = lane_iota(PAD, pair) < HEAD
    factor = HEAD ** -0.5
    for p in range(HEADS // 2):
        cut = slice(pair * p, pair * (p + 1))
        q = proj_ref[:, cut]
        k = proj_ref[:, width + pair * p : width + pair * (p + 1)]
        v = proj_ref[:, 2 * width + pair * p : 2 * width + pair * (p + 1)]
        gm = gm_ref[:, cut]
        gms = split_halves(gm, halves)
        low = jnp.concatenate([prob_ref[0, 2 * p], prob_ref[0, 2 * p + 1]], axis=0)
        probs = low.astype(F32)
        grad_probs = dot_nt(gms, v)
        middle = jnp.sum(probs * grad_probs, axis=1, keepdims=True)
        grad_scores = (probs * (grad_probs - middle)).astype(BF)
        grad_q = dot_nn(grad_scores, k)
        dproj[:, cut] = (jnp.where(halves, grad_q[:PAD], grad_q[PAD:]) * factor).astype(BF)
        dproj[:, width + pair * p : width + pair * (p + 1)] = (
            dot_tn(grad_scores, split_halves(q, halves)) * factor
        ).astype(BF)
        dproj[:, 2 * width + pair * p : 2 * width + pair * (p + 1)] = dot_tn(low, gms).astype(BF)
    normed, inverse = normalize(tpad_ref[...].astype(F32))
    entry = (normed * gains_ref[0:1, :] + gains_ref[1:2, :]).astype(BF)
    grads = dproj[...]
    grad_entry = dot_nt(grads, in_ref[...])

    @pl.when(i == 0)
    def _():
        din_ref[...] = jnp.zeros_like(din_ref)
        dscale_ref[...] = jnp.zeros_like(dscale_ref)

    din_ref[...] += dot_tn(entry, grads)
    dscale_ref[0:1, :] += jnp.sum(grad_entry * normed, axis=0, keepdims=True)
    dscale_ref[1:2, :] += jnp.sum(grad_entry, axis=0, keepdims=True)
    grad = gh_ref[...] + norm_back(grad_entry, normed, inverse, gains_ref[0:1, :])
    grad_all[...] = grad
    store_image(grad_ref, i, grad_all)

    @pl.when(i == pl.num_programs(0) - 1)
    def _():
        blocks, rows = 2 * near_ref.shape[0], near_ref.shape[1]
        owner = lane_iota(blocks, width) // rows == row_iota(blocks, width)
        spot = row_iota(width, 128) % rows
        line = jnp.zeros((blocks, 128), F32)
        for s in range(2):
            spread = jnp.where(owner, dscale_ref[s : s + 1, :], 0.0)
            chosen = (lane_iota(width, 128) == spot + s * rows).astype(F32)
            line += lax.dot_general(
                spread, chosen, (((1,), (0,)), ((), ())),
                preferred_element_type=F32, precision=lax.Precision.HIGHEST,
            )
        line_ref[...] = line
        scale_row = row_iota(8, 128) == 6
        for side, out in ((0, near_ref), (1, far_ref)):
            def body(j, carry, side=side, out=out):
                place = place_ref[side * (blocks // 2) + j]
                here = pl.ds(pl.multiple_of(place * rows, rows), rows)
                out[j, :, : 3 * width] = din_ref[here, :].astype(BF)
                out[j, :, 3 * width : 4 * width] = dout_ref[here, :].astype(BF)
                small = small_ref[place] + jnp.where(scale_row, line_ref[pl.ds(place, 1), :], 0.0)
                out[j, :, 4 * width :] = resplit(small)
                return carry

            lax.fori_loop(0, blocks // 2, body, 0)


def attention_back(place, proj, probs, grad_mixed, grad_hidden, tok_pad, in_matrix, gains, grad_out, small, after=()):
    padded, width = grad_hidden.shape
    images = padded // PAD
    blocks = small.shape[0]
    rows = width // blocks
    row = lambda lanes: pl.BlockSpec((PAD, lanes), lambda i, m: (i, 0))
    once = lambda a: pl.BlockSpec(a.shape, lambda i, m: (0,) * a.ndim, pipeline_mode=pl.Buffered(1))
    half = (blocks // 2, rows, 4 * width + 128)
    return pl.pallas_call(
        behind(attention_back_kernel, 10, after),
        grid_spec=pltpu.PrefetchScalarGridSpec(
            num_scalar_prefetch=1,
            grid=(images,),
            in_specs=[
                row(3 * width), pl.BlockSpec((1, HEADS, PAD, PAD), lambda i, m: (i, 0, 0, 0)), row(width), row(width),
                row(width), once(in_matrix), once(gains), once(grad_out), once(small),
                *unread(after),
            ],
            out_specs=[whole((images * SEQ, width)), whole(half), whole(half)],
            scratch_shapes=[
                pltpu.VMEM((width, 3 * width), F32), pltpu.VMEM((8, width), F32), pltpu.VMEM((blocks, 128), F32),
                pltpu.VMEM((PAD, 3 * width), BF), pltpu.VMEM((PAD, width), F32),
            ],
        ),
        out_shape=[
            jax.ShapeDtypeStruct((images * SEQ, width), F32),
            jax.ShapeDtypeStruct(half, BF),
            jax.ShapeDtypeStruct(half, BF),
        ],
        compiler_params=params(),
        cost_estimate=cost(50),
        name="attention_back",
    )(place, proj, probs, grad_mixed, grad_hidden, tok_pad, in_matrix, gains, grad_out, small, *after)


X_BIT, CORE_BIT, Y_BIT = 16, 8, 1
Z_BITS = (2, 4, 6)
AXES = ("rep", "ep")


def swap(array, bits):
    devices = lax.axis_size("rep") * lax.axis_size("ep")
    return lax.ppermute(array, AXES, [(d, d ^ bits) for d in range(devices)])


def relative(position):
    c, x, y, z = position >> 4 & 1, position >> 3 & 1, position >> 2 & 1, position & 3
    return x * X_BIT + c * CORE_BIT + z * 2 + y * Y_BIT


def stack_kernel(count, *refs):
    for j in range(count):
        refs[count][j] = refs[j][...]


def stack(arrays, after=()):
    count = len(arrays)
    return pl.pallas_call(
        behind(functools.partial(stack_kernel, count), count, after),
        in_specs=[pl.BlockSpec(memory_space=pltpu.VMEM)] * count + unread(after),
        out_shape=jax.ShapeDtypeStruct((count,) + arrays[0].shape, arrays[0].dtype),
        compiler_params=params(),
        cost_estimate=cost(1),
        name="stack",
    )(*arrays, *after)


def turn_stack_kernel(*refs):
    for m in range(2):
        for j in range(4):
            refs[4][m, j] = refs[j][m]


def turn_stack(arrays, after=()):
    piece = arrays[0].shape
    return pl.pallas_call(
        behind(turn_stack_kernel, 4, after),
        in_specs=[pl.BlockSpec(memory_space=pltpu.VMEM)] * 4 + unread(after),
        out_shape=jax.ShapeDtypeStruct((2, 4) + piece[1:], arrays[0].dtype),
        compiler_params=params(),
        cost_estimate=cost(2),
        name="turn_stack",
    )(*arrays, *after)


def pick_kernel(far_x, far_y, x_in, x_out, y_out):
    x_in[0] = far_x[0]
    x_out[0] = far_x[1]
    y_out[0] = far_y[1]


def pick(far_x, far_y, after=()):
    shape = (1,) + far_x.shape[1:]
    return pl.pallas_call(
        behind(pick_kernel, 2, after),
        in_specs=[pl.BlockSpec(memory_space=pltpu.VMEM)] * 2 + unread(after),
        out_shape=[jax.ShapeDtypeStruct(shape, far_x.dtype)] * 3,
        compiler_params=params(),
        cost_estimate=cost(3),
        name="pick",
    )(far_x, far_y, *after)


def sum_everywhere(values):
    for bits in (CORE_BIT, Y_BIT, X_BIT, 2, 4):
        values = values + swap(values, bits)
    return values


def unsplit(block):
    return block[:8] + block[8:]


def resplit(small):
    twice = jnp.concatenate([small, small], axis=0)
    high = twice.astype(BF).astype(F32)
    return jnp.where(row_iota(16, 128) < 8, high, twice - high).astype(BF)


def block_sum_kernel(parts, terms, *refs):
    ins, outs = refs[:terms], refs[terms:]
    size = ins[0].shape[0] // parts
    lanes = ins[0].shape[2]
    for p in range(parts):
        for j in range(size):
            at = p * size + j
            total = ins[0][at].astype(F32)
            for t in ins[1:]:
                total = total + t[at].astype(F32)
            small = unsplit(total[:, lanes - 128 :])
            outs[p][j, :, : lanes - 128] = total[:, : lanes - 128].astype(BF)
            outs[p][j, :, lanes - 128 :] = resplit(small)


def block_sum(terms, parts):
    size = terms[0].shape[0] // parts
    shape = (size,) + terms[0].shape[1:]
    return pl.pallas_call(
        functools.partial(block_sum_kernel, parts, len(terms)),
        out_shape=[jax.ShapeDtypeStruct(shape, BF)] * parts,
        compiler_params=params(),
        cost_estimate=cost(0.1),
        name="block_sum",
    )(*terms)


def scatter_dense(near, far, beside):
    parts = block_sum([near, swap(far, CORE_BIT)], 4)
    got = [swap(parts[1], Y_BIT), swap(parts[2], X_BIT), swap(parts[3], X_BIT | Y_BIT)]
    keep, beside = lax.optimization_barrier((parts[0], beside))
    parts = block_sum([keep] + got, 4)
    return beside, [parts[0]] + [swap(parts[z], Z_BITS[z - 1]) for z in (1, 2, 3)]


def fold_cores_kernel(n0, n1, g0, g1, a_keep, b_keep, a_send, b_send):
    for x in range(2):
        a_keep[x, 0] = n0[x, 0, 0] + g0[x, 0, 0]
        a_send[x, 0] = n1[x, 0, 0] + g1[x, 0, 0]
        out = b_send if x else b_keep
        out[0, 0] = n0[x, 0, 1] + g0[x, 0, 1]
        out[1, 0] = n1[x, 0, 1] + g1[x, 0, 1]


def fold_cores(near, got):
    rows, cols = near[0].shape[3:]
    out = jax.ShapeDtypeStruct((2, 4, rows, cols), BF)
    return pl.pallas_call(
        fold_cores_kernel,
        grid=(4,),
        in_specs=[pl.BlockSpec((2, 1, 2, rows, cols), lambda z: (0, z, 0, 0, 0))] * 4,
        out_specs=[pl.BlockSpec((2, 1, rows, cols), lambda z: (0, z, 0, 0))] * 4,
        out_shape=[out] * 4,
        compiler_params=params(),
        cost_estimate=cost(7),
        name="fold_cores",
    )(*near, *got)


def fold_first_kernel(a_keep, b_keep, a_got, b_got, a_near, b_near, a_far, b_far):
    a_near[0] = a_keep[0, 0] + a_got[0, 0]
    b_near[0] = b_keep[0, 0] + b_got[0, 0]
    a_far[0] = a_keep[1, 0] + a_got[1, 0]
    b_far[0] = b_keep[1, 0] + b_got[1, 0]


def fold_first(a_keep, b_keep, a_got, b_got, after=()):
    rows, cols = a_keep.shape[2:]
    return pl.pallas_call(
        behind(fold_first_kernel, 4, after),
        grid=(4,),
        in_specs=[pl.BlockSpec((2, 1, rows, cols), lambda z: (0, z, 0, 0))] * 4 + unread(after),
        out_specs=[pl.BlockSpec((1, rows, cols), lambda z: (z, 0, 0))] * 4,
        out_shape=[jax.ShapeDtypeStruct((4, rows, cols), BF)] * 4,
        compiler_params=params(),
        cost_estimate=cost(4),
        name="fold_first",
    )(a_keep, b_keep, a_got, b_got, *after)


def fold_second_kernel(a_keep, b_keep, a_got, b_got, *parts):
    for z in range(4):
        parts[z][0] = a_keep[z] + a_got[z]
        parts[z][1] = b_keep[z] + b_got[z]


def fold_second(a_keep, b_keep, a_got, b_got):
    return pl.pallas_call(
        fold_second_kernel,
        out_shape=[jax.ShapeDtypeStruct((2,) + a_keep.shape[1:], BF)] * 4,
        compiler_params=params(),
        cost_estimate=cost(3),
        name="fold_second",
    )(a_keep, b_keep, a_got, b_got)


def total_of(array):
    return jnp.sum(jnp.sum(array, axis=1, keepdims=True), axis=0, keepdims=True)


def expert_update_kernel(given, *refs):
    parts, (wi, fi, si, wo, fo, so, before), refs = refs[:4], refs[4:11], refs[11:]
    outs, sums = refs[given : given + 6], refs[given + 6]
    lane = lane_iota(1, 128)
    kept, moved = before[0:1, :], before[1:2, :]
    for m, (weight, first, second, new) in enumerate(((wi, fi, si, outs[0:3]), (wo, fo, so, outs[3:6]))):
        grad = parts[0][m].astype(F32)
        for part in parts[1:]:
            grad = grad + part[m].astype(F32)
        if m:
            grad = grad.T
        state = moments(weight[0], grad, first[0], second[0])
        for ref, value in zip(new, state):
            ref[0] = value
        slot = lane == (10 if m else 8)
        kept += jnp.where(slot, total_of(weight[0] * weight[0]), 0.0)
        moved += jnp.where(slot, total_of(state[2] * state[2]), 0.0)
    sums[...] = jnp.zeros_like(sums)
    sums[0:1, :] = kept
    sums[1:2, :] = moved


def expert_update(parts, arrays, sums, slice_index, done=()):
    rows, cols = parts[0].shape[1:]
    part = pl.BlockSpec(parts[0].shape, lambda i: (0, 0, 0))
    enter = pl.BlockSpec((1, rows, cols), lambda i: (0, 0, slice_index))
    leave = pl.BlockSpec((1, cols, rows), lambda i: (0, slice_index, 0))
    total = pl.BlockSpec((8, 128), lambda i: (0, 0))
    shape = jax.ShapeDtypeStruct(arrays[0].shape, F32)
    return pl.pallas_call(
        functools.partial(expert_update_kernel, len(done)),
        grid=(1,),
        in_specs=[part] * 4 + [enter] * 3 + [leave] * 3 + [total] + unread(done),
        out_specs=[enter] * 3 + [leave] * 3 + [total],
        out_shape=[shape] * 6 + [jax.ShapeDtypeStruct((8, 128), F32)],
        input_output_aliases={11 + j: j for j in range(len(done))},
        compiler_params=params(),
        cost_estimate=cost(0.1),
        name=f"expert_update_{slice_index}",
    )(*parts, *arrays, sums, *done)


def narrow(row, columns, rows):
    spread = jnp.where(lane_iota(rows, 128) % rows == row_iota(rows, 128), row, 0.0)
    chosen = (row_iota(128, columns) // rows == lane_iota(128, columns)).astype(F32)
    return lax.dot_general(
        spread, chosen, (((1,), (0,)), ((), ())), preferred_element_type=F32, precision=lax.Precision.HIGHEST
    )


def dense_update_kernel(*refs):
    ins, sums, states, outs = refs[:4], refs[4], refs[5:23], refs[23:]
    width = ins[0].shape[2] - 128
    total = ins[0][0].astype(F32)
    for t in ins[1:]:
        total = total + t[0].astype(F32)
    small = unsplit(total[:, width:])
    experts, rows = states[6].shape[1], states[6].shape[0]
    bias_rows = states[12].shape[1] // 128
    grads = (
        total[:, : width * 3 // 4],
        total[:, width * 3 // 4 : width],
        narrow(small[bias_rows + 1 : bias_rows + 2], experts, rows),
        narrow(small[bias_rows + 2 : bias_rows + 3], 5, rows),
        jnp.concatenate([small[j : j + 1] for j in range(bias_rows)], axis=1),
        small[bias_rows : bias_rows + 1],
    )
    lane = lane_iota(1, 128)
    kept, moved = sums[0:1, :], sums[1:2, :]
    for j, grad in enumerate(grads):
        weight, first, second = (states[3 * j + k][...] for k in range(3))
        state = moments(weight, grad, first, second)
        for k in range(3):
            outs[3 * j + k][...] = state[k]
        for c, slot in enumerate({0: (0,), 1: (1,), 2: (2,), 3: (3, 4, 5, 6, 7), 4: (9,), 5: (11,)}[j]):
            cut = (slice(None), slice(c, c + 1)) if j == 3 else (slice(None), slice(None))
            kept += jnp.where(lane == slot, total_of(weight[cut] * weight[cut]), 0.0)
            moved += jnp.where(lane == slot, total_of(state[2][cut] * state[2][cut]), 0.0)
    outs[18][...] = jnp.zeros_like(outs[18])
    outs[18][0:1, :] = kept
    outs[18][1:2, :] = moved


def dense_update(terms, sums, states):
    return pl.pallas_call(
        dense_update_kernel,
        out_shape=[jax.ShapeDtypeStruct(a.shape, F32) for a in states] + [jax.ShapeDtypeStruct((8, 128), F32)],
        compiler_params=params(),
        cost_estimate=cost(0.1),
        name="dense_update",
    )(*terms, sums, *states)


def new_weights_kernel(sums, counts, *refs):
    weights, steps, outs, norms = refs[:8], refs[8:16], refs[16:24], refs[24]
    weight_rms = jnp.sqrt(sums[0:1, :] / counts[...])
    step_rms = jnp.sqrt(sums[1:2, :] / counts[...])
    trust = weight_rms / step_rms
    norms[...] = jnp.zeros_like(norms)
    norms[0:1, :] = weight_rms
    norms[1:2, :] = step_rms
    norms[2:3, :] = trust
    for j, begin in enumerate((0, 1, 2, 3, 8, 9, 10, 11)):
        scale = trust[:, 3:8] if j == 3 else trust[:, begin : begin + 1]
        if len(outs[j].shape) == 3:
            outs[j][0] = weights[j][0] - RATE * scale * steps[j][0]
        else:
            outs[j][...] = weights[j][...] - RATE * scale * steps[j][...]


def new_weights(sums, counts, weights, steps):
    return pl.pallas_call(
        new_weights_kernel,
        out_shape=[jax.ShapeDtypeStruct(a.shape, F32) for a in weights] + [jax.ShapeDtypeStruct((8, 128), F32)],
        compiler_params=params(),
        cost_estimate=cost(5),
        name="new_weights",
    )(sums, counts, *weights, *steps)


CHUNKS = 2


def replicate_plan(
    tokens, cotangent, expert_ids, priority,
    heads_in, heads_in_first, heads_in_second, heads_out, heads_out_first, heads_out_second,
    router, router_first, router_second, scales, scales_first, scales_second,
    expert_in, expert_in_first, expert_in_second, bias_in, bias_in_first, bias_in_second,
    expert_out, expert_out_first, expert_out_second, bias_out, bias_out_first, bias_out_second,
):
    count, width = tokens.shape
    images = count // SEQ
    experts = router.shape[1]
    rep, ep = lax.axis_size("rep"), lax.axis_size("ep")
    rep_me, ep_me = lax.axis_index("rep"), lax.axis_index("ep")
    me = (rep_me * ep + ep_me).astype(jnp.int32)
    at = jnp.stack([rep_me, ep_me]).astype(jnp.int32)
    capacity = (5 * expert_ids.shape[1] * count + 4 * experts - 1) // (4 * experts)
    listed = -(-capacity // 16) * 16
    hidden_part = FF // rep
    cols = hidden_part // CHUNKS

    enter_low = expert_in[0].astype(BF)
    leave_low = expert_out[0].astype(BF).T
    pieces = [
        jnp.stack([enter_low[:, k * cols : (k + 1) * cols], leave_low[:, k * cols : (k + 1) * cols]])
        for k in range(CHUNKS)
    ]

    rows_here = heads_in.shape[0]
    small = jnp.concatenate([router, scales], axis=1)
    small = jnp.pad(small, ((0, 0), (0, 128 - small.shape[1])))
    biases = jnp.concatenate([bias_in.reshape(-1, 128), bias_out.reshape(-1, 128)], axis=0)
    biases = jnp.pad(biases, ((0, rows_here - biases.shape[0]), (0, 0)))
    dense = jnp.concatenate([heads_in, heads_out, small, biases], axis=1).astype(BF)
    order = jnp.array([relative(p) for p in range(rep * ep)], jnp.int32)
    place = jnp.bitwise_xor(order, me)
    spread = lambda a, fill: jnp.pad(
        a.reshape(-1, images, SEQ), ((0, 0), (0, 0), (0, PAD - SEQ)), constant_values=fill
    ).reshape(-1, images * PAD)
    ids_rows = spread(expert_ids.T, -1)
    rows = jnp.concatenate([spread(priority, count), ids_rows], axis=0).astype(F32)
    rows = jnp.pad(rows, ((0, 5), (0, 0)))

    zs_got = [swap(dense, bits) for bits in Z_BITS]
    tok_pad, cot_pad = spread_rows(tokens, cotangent)
    zs = stack([dense] + zs_got, after=(tok_pad,))
    zs, pieces[0] = lax.optimization_barrier((zs, pieces[0]))
    others = [swap(zs, bits) for bits in (Y_BIT, X_BIT, X_BIT | Y_BIT)]
    lrow, lcol, meta = find_places(rows, rows.T, capacity, experts)
    piece_got = [swap(pieces[0], bits) for bits in Z_BITS]
    plane = stack([zs] + others, after=(lrow, piece_got[0]))
    in_matrix, out_matrix, router_matrix, gains, small_all = assemble(
        place, plane.reshape((16,) + dense.shape), swap(plane, CORE_BIT).reshape((16,) + dense.shape), experts
    )
    bias_all = small_all[:, 128:].reshape(rep, ep, rows_here, 128)
    in_rows = hidden_part // 128
    enter_bias = bias_all[:, :, :in_rows].reshape(rep, ep, hidden_part).astype(F32).transpose(1, 0, 2)
    leave_bias = bias_all[:, :, in_rows].astype(F32).transpose(1, 0, 2).reshape(ep, 1, width)

    proj, probs, mixed, hidden, routed, gcol, grow = attention(
        tok_pad, in_matrix, out_matrix, router_matrix, gains, ids_rows.T
    )
    near = turn_stack([pieces[0]] + piece_got, after=(gcol,))
    far_x, far_y = swap(near, X_BIT), swap(near, Y_BIT)
    near, pieces[1] = lax.optimization_barrier((near, pieces[1]))
    lists = gather(meta, routed, cot_pad, lrow, grow, listed, after=(near,))
    near_two = turn_stack([pieces[1]] + [swap(pieces[1], bits) for bits in Z_BITS], after=(lists[0],))

    totals_here = meta[images - 1] + meta[2 * images - 1]
    at = jnp.concatenate([at, totals_here])
    bias_cut = lambda k: enter_bias[:, :, k * cols : (k + 1) * cols]
    cross = lambda a: swap(a, CORE_BIT)

    def first_half(near, far_x, crossed):
        pairs = []
        for m in range(2):
            other = (crossed[1][m], 0) if isinstance(crossed[1], tuple) else (crossed[1], m)
            pairs += [(near, m), (crossed[0], m), (far_x, m), other]
        return pairs

    def other_half(far_y, far_xy, crossed):
        return [
            pair
            for m in range(2)
            for pair in ((far_y, m), (crossed[0], m), (far_xy[m], 0), (crossed[1 + m], 0))
        ]

    x_in, x_out, y_out = pick(far_x, far_y, after=(near_two,))
    far_xy = swap(x_in, Y_BIT), swap(y_out, X_BIT)
    near, x_in = lax.optimization_barrier((near, x_in))
    crossed = cross(near), (cross(x_in), cross(x_out))
    y_part, d_part, near_a, far_a, bias_a, leave_a = expert_pass(
        at, lists, first_half(near, far_x, crossed), bias_cut(0)
    )
    y_part, *far_xy = lax.optimization_barrier((y_part, *far_xy))
    far_x_two, far_y_two = swap(near_two, X_BIT), swap(near_two, Y_BIT)
    crossed = cross(far_y), cross(far_xy[0]), cross(far_xy[1])
    y_half, d_half, near_b, far_b, bias_b, leave_b = expert_pass(
        at, lists, other_half(far_y, far_xy, crossed), bias_cut(0), half=1, done=(y_part, d_part),
    )
    got_a = swap(far_a, CORE_BIT)
    near_two, bias_a = lax.optimization_barrier((near_two, bias_a))
    near_crossed = cross(near_two)
    far_b, far_x_two, far_y_two, near_crossed = lax.optimization_barrier((far_b, far_x_two, far_y_two, near_crossed))
    diagonal = far_x_two[0:1], far_y_two[1:2]
    crossed = near_crossed, cross(far_x_two)
    far_xy_two = swap(diagonal[0], Y_BIT), swap(diagonal[1], X_BIT)
    got_b = swap(far_b, CORE_BIT)
    one = fold_cores((near_a, near_b), (got_a, got_b))
    a_send, far_y_two = lax.optimization_barrier((one[2], far_y_two))
    one = (*one[:2], a_send, one[3])
    far_y_crossed = cross(far_y_two)
    even = lax.bitwise_xor(jnp.arange(ep, dtype=jnp.int32), ep_me)[:, None, None] % 2 == 0
    grad_bias = [jnp.where(even, bias_a, bias_b)]
    grad_leave_bias = jnp.where(even, leave_a, leave_b)
    one_got = swap(one[2], Y_BIT), swap(one[3], X_BIT)
    y_part, d_part, near_a, far_a, bias_a = expert_pass(
        at, lists, first_half(near_two, far_x_two, crossed), bias_cut(1), leave_bias, (y_half, d_half),
        after=one[2:],
    )
    y_part, *far_xy_two = lax.optimization_barrier((y_part, *far_xy_two))
    crossed = far_y_crossed, cross(far_xy_two[0]), cross(far_xy_two[1])
    got_a = swap(far_a, CORE_BIT)
    y, d, near_b, far_b, bias_b = expert_pass(
        at, lists, other_half(far_y_two, far_xy_two, crossed), bias_cut(1), leave_bias, (y_half, d_half), half=1,
        done=(y_part, d_part),
    )
    far_b, *one_got = lax.optimization_barrier((far_b, *one_got))
    one = fold_first(*one[:2], *one_got)
    one_got = swap(one[2], X_BIT), swap(one[3], Y_BIT)
    got_b = swap(far_b, CORE_BIT)
    two = fold_cores((near_a, near_b), (got_a, got_b))
    two_got = swap(two[2], Y_BIT), swap(two[3], X_BIT)
    output, grad_hidden, grad_mixed, grad_out, grad_router, grad_scale = combine(
        meta, y, d, lcol, gcol, hidden, cot_pad, mixed, out_matrix, router_matrix, gains,
        after=list(one) + list(two[2:]),
    )
    grad_mixed, *one_got = lax.optimization_barrier((grad_mixed, *one_got))
    one = fold_second(*one[:2], *one_got)
    one_got = [swap(one[z], Z_BITS[z - 1]) for z in (1, 2, 3)]
    two = fold_first(*two[:2], *two_got)
    two_got = swap(two[2], X_BIT), swap(two[3], Y_BIT)
    grad_bias.append(jnp.where(even, bias_a, bias_b))
    devices = rep * ep
    by_device = lambda a: jnp.pad(
        a.reshape(a.shape[0], devices, rows_here).transpose(1, 0, 2).reshape(devices, 1, -1),
        ((0, 0), (0, 0), (0, 128 - a.shape[0] * rows_here)),
    )
    small_grads = jnp.concatenate(
        [
            jnp.concatenate(grad_bias, axis=2).transpose(1, 0, 2).reshape(devices, in_rows, 128),
            grad_leave_bias.reshape(ep, rep, 128).transpose(1, 0, 2).reshape(devices, 1, 128),
            by_device(grad_router),
            by_device(grad_scale[:5]),
        ],
        axis=1,
    )
    small_grads = jnp.pad(small_grads, ((0, 0), (0, 8 - small_grads.shape[1]), (0, 0)))
    input_grad, near_dense, far_dense = attention_back(
        place, proj, probs, grad_mixed, grad_hidden, tok_pad, in_matrix, gains, grad_out, small_grads,
        after=list(one[1:]) + list(two[2:]),
    )
    far_dense, *got = lax.optimization_barrier((far_dense, *one_got, *two_got))
    one_got, two_got = got[:3], got[3:]
    two = fold_second(*two[:2], *two_got)
    far_dense, *two = lax.optimization_barrier((far_dense, *two))
    two_got = [swap(two[z], Z_BITS[z - 1]) for z in (1, 2, 3)]
    expert_states = (expert_in, expert_in_first, expert_in_second, expert_out, expert_out_first, expert_out_second)
    *expert_new, sums = expert_update([one[0]] + list(one_got), expert_states, jnp.zeros((8, 128), F32), 0)
    sums, dense_terms = scatter_dense(near_dense, far_dense, sums)
    dense_states = (
        heads_in, heads_in_first, heads_in_second, heads_out, heads_out_first, heads_out_second,
        router, router_first, router_second, scales, scales_first, scales_second,
        bias_in, bias_in_first, bias_in_second, bias_out, bias_out_first, bias_out_second,
    )
    *dense_new, sums = dense_update(dense_terms, sums, dense_states)
    sums, *two_got = lax.optimization_barrier((sums, *two_got))
    *expert_new, sums = expert_update([two[0]] + two_got, expert_states, sums, 1, done=expert_new)
    in_first, in_second, in_step, out_first, out_second, out_step = expert_new
    sums = sum_everywhere(sums)
    counts = jnp.array(
        [3 * width * width, width * width, width * experts]
        + [width] * 5
        + [experts * width * FF, experts * FF, experts * FF * width, experts * width]
        + [1] * (128 - 12),
        jnp.float32,
    )[None]
    trio = lambda j: tuple(dense_new[3 * j : 3 * j + 3])
    states = [
        trio(0), trio(1), trio(2), trio(3), (in_first, in_second, in_step), trio(4),
        (out_first, out_second, out_step), trio(5),
    ]
    weights_now = (heads_in, heads_out, router, scales, expert_in, bias_in, expert_out, bias_out)
    *fresh, norms = new_weights(sums, counts, weights_now, [state[2] for state in states])
    results = [output, input_grad]
    for state, weight in zip(states, fresh):
        results.extend([state[0], state[1], weight])
    results.append(norms[:3, :12])
    return tuple(results)


def expert_front(rows, enter_weight, enter_bias):
    pre = jnp.einsum("sjcd,jdf->sjcf", rows, enter_weight, preferred_element_type=jnp.float32)
    return pre + enter_bias.astype(jnp.float32)[None, :, None, :]


def exchange_plan(
    tokens,
    cotangent,
    expert_ids,
    priority,
    heads_in,
    heads_in_first,
    heads_in_second,
    heads_out,
    heads_out_first,
    heads_out_second,
    router,
    router_first,
    router_second,
    scales,
    scales_first,
    scales_second,
    expert_in,
    expert_in_first,
    expert_in_second,
    bias_in,
    bias_in_first,
    bias_in_second,
    expert_out,
    expert_out_first,
    expert_out_second,
    bias_out,
    bias_out_first,
    bias_out_second,
):
    in_matrix, out_matrix, router_matrix, scale_table = (
        lax.all_gather(heads_in.astype(jnp.bfloat16), ("rep", "ep"), axis=0, tiled=True),
        lax.all_gather(heads_out.astype(jnp.bfloat16), ("rep", "ep"), axis=0, tiled=True),
        lax.all_gather(router.astype(jnp.bfloat16), ("rep", "ep"), axis=0, tiled=True),
        lax.all_gather(scales.astype(jnp.bfloat16), ("rep", "ep"), axis=0, tiled=True),
    )
    enter_weight, enter_bias, leave_weight, leave_bias = (
        lax.all_gather(expert_in.astype(jnp.bfloat16), "rep", axis=2, tiled=True),
        lax.all_gather(bias_in.astype(jnp.bfloat16), "rep", axis=1, tiled=True),
        lax.all_gather(expert_out.astype(jnp.bfloat16), "rep", axis=1, tiled=True),
        lax.all_gather(bias_out.astype(jnp.bfloat16), "rep", axis=1, tiled=True),
    )
    gains = scale_table.astype(jnp.float32)
    inputs = tokens.astype(jnp.float32)
    count, width = inputs.shape
    images = count // SEQ
    factor = HEAD ** (-0.5)
    normed_one, inverse_one = normalize(inputs)
    entry = (normed_one * gains[:, 0] + gains[:, 1]).astype(jnp.bfloat16)
    projected = jnp.dot(entry, in_matrix, preferred_element_type=jnp.float32).astype(jnp.bfloat16)
    grid = projected.reshape(images, SEQ, 3, HEADS, HEAD)
    query = grid[:, :, 0]
    keyed = grid[:, :, 1]
    valued = grid[:, :, 2]
    scores = attention_scores(query, keyed, factor)
    peak = jnp.max(scores, axis=-1, keepdims=True)
    log_total = peak + jnp.log(jnp.sum(jnp.exp(scores - peak), axis=-1, keepdims=True))
    weights = jnp.exp(scores - log_total).astype(jnp.bfloat16)
    mixed = jnp.einsum("bhqk,bkhd->bqhd", weights, valued, preferred_element_type=jnp.float32)
    mixed = mixed.reshape(count, width).astype(jnp.bfloat16)
    hidden = inputs + jnp.dot(mixed, out_matrix, preferred_element_type=jnp.float32) + gains[:, 4]
    normed_two, inverse_two = normalize(hidden)
    routed = (normed_two * gains[:, 2] + gains[:, 3]).astype(jnp.bfloat16)
    logits = jnp.dot(routed, router_matrix, preferred_element_type=jnp.float32)
    experts = logits.shape[1]
    top = expert_ids.shape[1]
    choose = (expert_ids[:, :, None] == jnp.arange(experts, dtype=jnp.int32)[None, None, :]).astype(
        jnp.float32
    )
    picked = jnp.sum(choose * logits[:, None, :], axis=2)
    gates = jax.nn.softmax(picked, axis=1)
    places = route_places(expert_ids, priority[0], experts)
    capacity = (5 * top * count + 4 * experts - 1) // (4 * experts)
    groups = lax.axis_size("ep")
    local = experts // groups
    slots = experts * capacity
    slot = jnp.where(places < capacity, expert_ids * capacity + places, slots)
    pair_of_slot = (
        jnp.full((slots,), count * top, jnp.int32)
        .at[slot.reshape(-1)]
        .set(jnp.arange(count * top, dtype=jnp.int32), mode="drop")
    )
    token_of_slot = pair_of_slot // top
    padded_rows = jnp.concatenate([routed, jnp.zeros((1, width), jnp.bfloat16)], axis=0)
    outgoing = padded_rows[token_of_slot].reshape(groups, local, capacity, width)
    arrived = lax.all_to_all(outgoing, "ep", split_axis=0, concat_axis=0, tiled=True)
    pre = expert_front(arrived, enter_weight, enter_bias)
    act, gelu_back = jax.vjp(exact_gelu, pre)
    act_low = act.astype(jnp.bfloat16)
    result = jnp.einsum("sjcf,jfd->sjcd", act_low, leave_weight, preferred_element_type=jnp.float32)
    result = (result + leave_bias.astype(jnp.float32)[None, :, None, :]).astype(jnp.bfloat16)
    returned = lax.all_to_all(result, "ep", split_axis=0, concat_axis=0, tiled=True).reshape(
        slots, width
    )
    padded_back = jnp.concatenate([returned, jnp.zeros((1, width), jnp.bfloat16)], axis=0)
    picked_rows = padded_back[slot].astype(jnp.float32)
    output = hidden + jnp.sum(gates[:, :, None] * picked_rows, axis=1)
    grad_output = cotangent.astype(jnp.float32)
    grad_gates = jnp.sum(picked_rows * grad_output[:, None, :], axis=2)
    gate_list = jnp.concatenate([gates.reshape(-1), jnp.zeros((1,), jnp.float32)])
    padded_grad = jnp.concatenate([grad_output, jnp.zeros((1, width), jnp.float32)], axis=0)
    grad_slots = (padded_grad[token_of_slot] * gate_list[pair_of_slot][:, None]).astype(
        jnp.bfloat16
    )
    grad_arrived = lax.all_to_all(
        grad_slots.reshape(groups, local, capacity, width),
        "ep",
        split_axis=0,
        concat_axis=0,
        tiled=True,
    )
    grad_act = jnp.einsum(
        "sjcd,jfd->sjcf", grad_arrived, leave_weight, preferred_element_type=jnp.float32
    )
    grad_pre = gelu_back(grad_act)[0].astype(jnp.bfloat16)
    grad_leave = jnp.einsum(
        "sjcf,sjcd->jfd", act_low, grad_arrived, preferred_element_type=jnp.float32
    )
    grad_leave_bias = jnp.sum(grad_arrived, axis=(0, 2), dtype=jnp.float32)
    grad_enter = jnp.einsum("sjcd,sjcf->jdf", arrived, grad_pre, preferred_element_type=jnp.float32)
    grad_enter_bias = jnp.sum(grad_pre, axis=(0, 2), dtype=jnp.float32)
    grad_rows = jnp.einsum(
        "sjcf,jdf->sjcd", grad_pre, enter_weight, preferred_element_type=jnp.float32
    ).astype(jnp.bfloat16)
    grad_back = lax.all_to_all(grad_rows, "ep", split_axis=0, concat_axis=0, tiled=True).reshape(
        slots, width
    )
    padded_grad_back = jnp.concatenate([grad_back, jnp.zeros((1, width), jnp.bfloat16)], axis=0)
    grad_routed = jnp.sum(padded_grad_back[slot], axis=1, dtype=jnp.float32)
    grad_picked = gates * (grad_gates - jnp.sum(gates * grad_gates, axis=1, keepdims=True))
    grad_logits = jnp.sum(choose * grad_picked[:, :, None], axis=1).astype(jnp.bfloat16)
    grad_router = jnp.einsum("td,te->de", routed, grad_logits, preferred_element_type=jnp.float32)
    grad_routed = grad_routed + jnp.einsum(
        "te,de->td", grad_logits, router_matrix, preferred_element_type=jnp.float32
    )
    grad_gain_two = jnp.sum(grad_routed * normed_two, axis=0)
    grad_shift_two = jnp.sum(grad_routed, axis=0)
    grad_hidden = grad_output + norm_back(grad_routed, normed_two, inverse_two, gains[:, 2])
    grad_shift_out = jnp.sum(grad_hidden, axis=0)
    grad_mix_out = grad_hidden.astype(jnp.bfloat16)
    grad_out_matrix = jnp.einsum(
        "td,te->de", mixed, grad_mix_out, preferred_element_type=jnp.float32
    )
    grad_mixed = jnp.einsum(
        "te,de->td", grad_mix_out, out_matrix, preferred_element_type=jnp.float32
    )
    grad_mixed = grad_mixed.astype(jnp.bfloat16).reshape(images, SEQ, HEADS, HEAD)
    probs = jnp.exp(attention_scores(query, keyed, factor) - log_total)
    weights_again = probs.astype(jnp.bfloat16)
    grad_valued = jnp.einsum(
        "bhqk,bqhd->bkhd", weights_again, grad_mixed, preferred_element_type=jnp.float32
    )
    grad_probs = jnp.einsum(
        "bqhd,bkhd->bhqk", grad_mixed, valued, preferred_element_type=jnp.float32
    )
    grad_scores = (
        probs * (grad_probs - jnp.sum(probs * grad_probs, axis=-1, keepdims=True))
    ).astype(jnp.bfloat16)
    grad_query = (
        jnp.einsum("bhqk,bkhd->bqhd", grad_scores, keyed, preferred_element_type=jnp.float32)
        * factor
    )
    grad_keyed = (
        jnp.einsum("bhqk,bqhd->bkhd", grad_scores, query, preferred_element_type=jnp.float32)
        * factor
    )
    grad_projected = (
        jnp.stack([grad_query, grad_keyed, grad_valued], axis=2)
        .reshape(count, 3 * width)
        .astype(jnp.bfloat16)
    )
    grad_in_matrix = jnp.einsum(
        "td,te->de", entry, grad_projected, preferred_element_type=jnp.float32
    )
    grad_entry = jnp.einsum(
        "te,de->td", grad_projected, in_matrix, preferred_element_type=jnp.float32
    )
    grad_gain_one = jnp.sum(grad_entry * normed_one, axis=0)
    grad_shift_one = jnp.sum(grad_entry, axis=0)
    input_grad = grad_hidden + norm_back(grad_entry, normed_one, inverse_one, gains[:, 0])
    grad_scales = jnp.stack(
        [grad_gain_one, grad_shift_one, grad_gain_two, grad_shift_two, grad_shift_out], axis=1
    )
    summed_dense = (
        lax.psum_scatter(grad_in_matrix, ("rep", "ep"), scatter_dimension=0, tiled=True),
        lax.psum_scatter(grad_out_matrix, ("rep", "ep"), scatter_dimension=0, tiled=True),
        lax.psum_scatter(grad_router, ("rep", "ep"), scatter_dimension=0, tiled=True),
        lax.psum_scatter(grad_scales, ("rep", "ep"), scatter_dimension=0, tiled=True),
    )
    summed_expert = (
        lax.psum_scatter(
            grad_enter.astype(jnp.bfloat16), "rep", scatter_dimension=2, tiled=True
        ).astype(jnp.float32),
        lax.psum_scatter(
            grad_enter_bias.astype(jnp.bfloat16), "rep", scatter_dimension=1, tiled=True
        ).astype(jnp.float32),
        lax.psum_scatter(
            grad_leave.astype(jnp.bfloat16), "rep", scatter_dimension=1, tiled=True
        ).astype(jnp.float32),
        lax.psum_scatter(
            grad_leave_bias.astype(jnp.bfloat16), "rep", scatter_dimension=1, tiled=True
        ).astype(jnp.float32),
    )
    weights_now = (heads_in, heads_out, router, scales, expert_in, bias_in, expert_out, bias_out)
    grads_now = tuple(summed_dense) + tuple(summed_expert)
    firsts = (
        heads_in_first,
        heads_out_first,
        router_first,
        scales_first,
        expert_in_first,
        bias_in_first,
        expert_out_first,
        bias_out_first,
    )
    seconds = (
        heads_in_second,
        heads_out_second,
        router_second,
        scales_second,
        expert_in_second,
        bias_in_second,
        expert_out_second,
        bias_out_second,
    )
    states = [moments(w, g, f, s) for w, g, f, s in zip(weights_now, grads_now, firsts, seconds)]
    weight_terms = jnp.concatenate([squares(w, index == 3) for index, w in enumerate(weights_now)])
    step_terms = jnp.concatenate(
        [squares(state[2], index == 3) for index, state in enumerate(states)]
    )
    totals = lax.psum(jnp.stack([weight_terms, step_terms]), ("rep", "ep"))
    return (output, input_grad) + finish(totals, weights_now, states, width, experts)


def solution(mesh):
    in_specs = (
        P(("rep", "ep"), None),
        P(("rep", "ep"), None),
        P(("rep", "ep"), None),
        P(("rep", "ep"), None),
        P(("rep", "ep"), None),
        P(("rep", "ep"), None),
        P(("rep", "ep"), None),
        P(("rep", "ep"), None),
        P(("rep", "ep"), None),
        P(("rep", "ep"), None),
        P(("rep", "ep"), None),
        P(("rep", "ep"), None),
        P(("rep", "ep"), None),
        P(("rep", "ep"), None),
        P(("rep", "ep"), None),
        P(("rep", "ep"), None),
        P("ep", None, "rep"),
        P("ep", None, "rep"),
        P("ep", None, "rep"),
        P("ep", "rep"),
        P("ep", "rep"),
        P("ep", "rep"),
        P("ep", "rep", None),
        P("ep", "rep", None),
        P("ep", "rep", None),
        P("ep", "rep"),
        P("ep", "rep"),
        P("ep", "rep"),
    )
    out_specs = (
        P(("rep", "ep"), None),
        P(("rep", "ep"), None),
        P(("rep", "ep"), None),
        P(("rep", "ep"), None),
        P(("rep", "ep"), None),
        P(("rep", "ep"), None),
        P(("rep", "ep"), None),
        P(("rep", "ep"), None),
        P(("rep", "ep"), None),
        P(("rep", "ep"), None),
        P(("rep", "ep"), None),
        P(("rep", "ep"), None),
        P(("rep", "ep"), None),
        P(("rep", "ep"), None),
        P("ep", None, "rep"),
        P("ep", None, "rep"),
        P("ep", None, "rep"),
        P("ep", "rep"),
        P("ep", "rep"),
        P("ep", "rep"),
        P("ep", "rep", None),
        P("ep", "rep", None),
        P("ep", "rep", None),
        P("ep", "rep"),
        P("ep", "rep"),
        P("ep", "rep"),
        P(),
    )
    replicated = mesh.shape["rep"] == 4 and mesh.shape["ep"] == 8
    return jax.shard_map(
        replicate_plan if replicated else exchange_plan,
        mesh=mesh,
        in_specs=in_specs,
        out_specs=out_specs,
        check_vma=False,
    )
```

```python
import functools

import jax
import jax.numpy as jnp
from jax import lax
from jax.experimental import pallas as pl
from jax.experimental.pallas import tpu as pltpu
from jax.sharding import PartitionSpec as P

HEADS = 8
HEAD = 64
FF = 2048
SEQ = 197
STEP = 5


BETA = 0.5
RATE = 0.3
DECAY = 0.01
EPSILON = 1e-06


def normalize(rows):
    centred = rows - jnp.mean(rows, axis=-1, keepdims=True)
    inverse = lax.rsqrt(jnp.mean(centred * centred, axis=-1, keepdims=True) + 1e-06)
    return (centred * inverse, inverse)


def norm_back(grad_rows, normed, inverse, gain):
    scaled = grad_rows * gain
    return inverse * (
        scaled
        - jnp.mean(scaled, axis=-1, keepdims=True)
        - normed * jnp.mean(scaled * normed, axis=-1, keepdims=True)
    )


def exact_gelu(values):
    return jax.nn.gelu(values, approximate=False)


def route_places(block_ids, ranking, experts):
    count = block_ids.shape[0]
    keys = jnp.arange(block_ids.shape[1], dtype=jnp.int32)[None, :] * count + ranking[:, None]
    ordered = (
        jnp.zeros((block_ids.size,), jnp.int32).at[keys.reshape(-1)].set(block_ids.reshape(-1))
    )
    hits = (ordered[:, None] == jnp.arange(experts, dtype=jnp.int32)[None, :]).astype(jnp.int32)
    before = jnp.cumsum(hits, axis=0) - hits
    place = jnp.sum(before * hits, axis=1)
    return place[keys]


def attention_scores(query, keyed, factor):
    return jnp.einsum("bqhd,bkhd->bhqk", query, keyed, preferred_element_type=jnp.float32) * factor


def moments(weight, grad, first, second):
    first_new = BETA * first + (1.0 - BETA) * grad
    second_new = BETA * second + (1.0 - BETA) * grad * grad
    step = (
        first_new / (1.0 - BETA**STEP) / (jnp.sqrt(second_new / (1.0 - BETA**STEP)) + EPSILON)
        + DECAY * weight
    )
    return (first_new, second_new, step)


def squares(array, per_column):
    if per_column:
        return jnp.sum(array * array, axis=0)
    return jnp.sum(array * array)[None]


def finish(totals, weights_now, states, width, experts):
    counts = jnp.array(
        [3 * width * width, width * width, width * experts]
        + [width] * 5
        + [experts * width * FF, experts * FF, experts * FF * width, experts * width],
        jnp.float32,
    )
    weight_rms = jnp.sqrt(totals[0] / counts)
    step_rms = jnp.sqrt(totals[1] / counts)
    trust = weight_rms / step_rms
    bounds = [(0, 1), (1, 2), (2, 3), (3, 8), (8, 9), (9, 10), (10, 11), (11, 12)]
    results = []
    for weight, state, bound in zip(weights_now, states, bounds):
        results.extend([state[0], state[1], weight - RATE * trust[bound[0] : bound[1]] * state[2]])
    results.append(jnp.stack([weight_rms, step_rms, trust]))
    return tuple(results)


PAD = 208
WIN = 96
VMEM = 60 * 1024 * 1024
BF = jnp.bfloat16
F32 = jnp.float32


def dot_nn(a, b):
    return lax.dot_general(a, b, (((1,), (0,)), ((), ())), preferred_element_type=F32)


def dot_nt(a, b):
    return lax.dot_general(a, b, (((1,), (1,)), ((), ())), preferred_element_type=F32)


def dot_tn(a, b):
    return lax.dot_general(a, b, (((0,), (0,)), ((), ())), preferred_element_type=F32)


def lane_iota(rows, lanes):
    return lax.broadcasted_iota(jnp.int32, (rows, lanes), 1)


def row_iota(rows, lanes):
    return lax.broadcasted_iota(jnp.int32, (rows, lanes), 0)


def whole(shape):
    return pl.BlockSpec(shape, lambda *_: (0,) * len(shape))


def cost(micros):
    return pl.CostEstimate(flops=int(micros * 1e9), bytes_accessed=int(micros * 1e5), transcendentals=0)


def params(**kw):
    return pltpu.CompilerParams(vmem_limit_bytes=VMEM, **kw)


def behind(kernel, inputs, after):
    def body(*refs):
        return kernel(*refs[:inputs], *refs[inputs + len(after) :])

    return body


def unread(after):
    return [pl.BlockSpec(memory_space=pl.ANY)] * len(after)


def assemble_kernel(place_ref, near_ref, far_ref, in_ref, out_ref, router_ref, gains_ref, small_ref):
    copies, rows = near_ref.shape[0], near_ref.shape[1]
    width = out_ref.shape[1]
    for side, got_ref in enumerate((near_ref, far_ref)):
        for j in range(copies):
            place = pl.multiple_of(place_ref[side * copies + j] * rows, rows)
            in_ref[pl.ds(place, rows), :] = got_ref[j, :, : 3 * width]
            out_ref[pl.ds(place, rows), :] = got_ref[j, :, 3 * width : 4 * width]
            small_ref[pl.ds(place, rows), :] = got_ref[j, :, 4 * width :]
    turned = small_ref[:, :128].astype(F32).T
    experts = router_ref.shape[0]
    router_ref[...] = turned[:experts].astype(BF)
    gains_ref[...] = turned[experts : experts + 8]


def assemble(place, near, far, experts):
    copies, rows, lanes = near.shape
    width = 2 * copies * rows
    return pl.pallas_call(
        assemble_kernel,
        grid_spec=pltpu.PrefetchScalarGridSpec(
            num_scalar_prefetch=1,
            grid=(1,),
            in_specs=[whole(near.shape)] * 2,
            out_specs=[
                whole((width, 3 * width)),
                whole((width, width)),
                whole((experts, width)),
                whole((8, width)),
                whole((width, lanes - 4 * width)),
            ],
        ),
        out_shape=[
            jax.ShapeDtypeStruct((width, 3 * width), BF),
            jax.ShapeDtypeStruct((width, width), BF),
            jax.ShapeDtypeStruct((experts, width), BF),
            jax.ShapeDtypeStruct((8, width), F32),
            jax.ShapeDtypeStruct((width, lanes - 4 * width), BF),
        ],
        compiler_params=params(),
        cost_estimate=cost(1),
        name="assemble",
    )(place, near, far)


def places_kernel(capacity, rows_ref, cols_ref, lrow_ref, lcol_ref, meta_ref):
    count = cols_ref.shape[0]
    images = count // PAD
    experts = lcol_ref.shape[1]
    expert = lane_iota(count, experts).astype(F32)
    first = (cols_ref[:, 1:2] == expert).astype(F32)
    second = (cols_ref[:, 2:3] == expert).astype(F32)
    first_low = first.astype(BF)
    second_low = second.astype(BF)
    total_first = jnp.sum(first, axis=0, keepdims=True)
    lower = (lane_iota(PAD, PAD) < row_iota(PAD, PAD)).astype(F32).astype(BF)
    ranking = rows_ref[0:1, :]
    begin = jnp.zeros((1, experts), F32)
    for i in range(images):
        span = slice(i * PAD, (i + 1) * PAD)
        ahead = (ranking < cols_ref[span, 0:1]).astype(F32).astype(BF)
        rank_first = dot_nn(ahead, first_low)
        rank_second = dot_nn(ahead, second_low) + total_first
        place = first[span] * rank_first + second[span] * rank_second
        kept = (first[span] + second[span]) * (place < capacity).astype(F32)
        local = dot_nn(lower, kept.astype(BF))
        local = jnp.where(kept > 0.0, local, -1.0)
        lcol_ref[span, :] = local
        lrow_ref[i] = local.T
        here = jnp.sum(kept, axis=0, keepdims=True)
        meta_ref[i : i + 1, :] = begin.astype(jnp.int32)
        meta_ref[images + i : images + i + 1, :] = here.astype(jnp.int32)
        begin = begin + here


def find_places(rows, cols, capacity, experts):
    count = cols.shape[0]
    images = count // PAD
    return pl.pallas_call(
        functools.partial(places_kernel, capacity),
        out_shape=[
            jax.ShapeDtypeStruct((images, experts, PAD), F32),
            jax.ShapeDtypeStruct((count, experts), F32),
            jax.ShapeDtypeStruct((2 * images, experts), jnp.int32),
        ],
        compiler_params=params(),
        cost_estimate=cost(2),
        name="places",
    )(rows, cols)


def spread_kernel(tok_ref, cot_ref, tpad_ref, cpad_ref):
    count, width = tok_ref.shape
    for source, target in ((tok_ref, tpad_ref), (cot_ref, cpad_ref)):
        for i in range(count // SEQ):
            rows = source[SEQ * i : SEQ * (i + 1), :].astype(F32)
            rows = jnp.concatenate([rows, jnp.zeros((PAD - SEQ, width), F32)], axis=0)
            target[PAD * i : PAD * (i + 1), :] = rows.astype(BF)


def spread_rows(tokens, cotangent):
    count, width = tokens.shape
    shape = jax.ShapeDtypeStruct((count // SEQ * PAD, width), BF)
    return pl.pallas_call(
        spread_kernel, out_shape=[shape, shape], compiler_params=params(), cost_estimate=cost(5), name="spread_rows"
    )(tokens, cotangent)


def store_image(target, i, values):
    for image in range(target.shape[0] // SEQ):

        @pl.when(i == image)
        def _(image=image):
            target[SEQ * image : SEQ * (image + 1), :] = values[0:SEQ, :]


def split_halves(block, halves):
    zero = jnp.zeros_like(block)
    return jnp.concatenate([jnp.where(halves, block, zero), jnp.where(halves, zero, block)], axis=0)


def attention_kernel(
    tok_ref, in_ref, out_ref, router_ref, gains_ref, ids_ref,
    proj_ref, prob_ref, mixed_ref, hidden_ref, routed_ref, gcol_ref, grow_ref, mixed_all,
):
    width = tok_ref.shape[1]
    x = tok_ref[...].astype(F32)
    normed, _ = normalize(x)
    entry = (normed * gains_ref[0:1, :] + gains_ref[1:2, :]).astype(BF)
    proj_ref[...] = dot_nn(entry, in_ref[...]).astype(BF)
    pair = 2 * HEAD
    halves = lane_iota(PAD, pair) < HEAD
    key_there = lane_iota(2 * PAD, PAD) < SEQ
    for p in range(HEADS // 2):
        q = proj_ref[:, pair * p : pair * (p + 1)] * jnp.asarray(HEAD ** -0.5, BF)
        k = proj_ref[:, width + pair * p : width + pair * (p + 1)]
        v = proj_ref[:, 2 * width + pair * p : 2 * width + pair * (p + 1)]
        scores = dot_nt(split_halves(q, halves), k)
        scores = jnp.where(key_there, scores, -1e30)
        peak = jnp.max(scores, axis=1, keepdims=True)
        raised = jnp.exp(scores - peak)
        total = jnp.sum(raised, axis=1, keepdims=True)
        weights = (raised * (1.0 / total)).astype(BF)
        prob_ref[0, 2 * p] = weights[:PAD]
        prob_ref[0, 2 * p + 1] = weights[PAD:]
        out = dot_nn(weights, v)
        mixed_all[:, pair * p : pair * (p + 1)] = jnp.where(halves, out[:PAD], out[PAD:]).astype(BF)
    mixed = mixed_all[...]
    mixed_ref[...] = mixed
    hidden = x + dot_nn(mixed, out_ref[...]) + gains_ref[4:5, :]
    hidden_ref[...] = hidden
    normed_two, _ = normalize(hidden)
    routed = (normed_two * gains_ref[2:3, :] + gains_ref[3:4, :]).astype(BF)
    routed_ref[...] = routed
    logits = dot_nt(routed, router_ref[...])
    experts = logits.shape[1]
    expert = lane_iota(PAD, experts)
    chosen = jnp.logical_or(ids_ref[:, 0:1] == expert, ids_ref[:, 1:2] == expert)
    top = jnp.max(jnp.where(chosen, logits, -1e30), axis=1, keepdims=True)
    raised = jnp.where(chosen, jnp.exp(jnp.where(chosen, logits - top, 0.0)), 0.0)
    total = jnp.sum(raised, axis=1, keepdims=True)
    gates = raised / jnp.where(total > 0.0, total, 1.0)
    gcol_ref[...] = gates
    grow_ref[0] = gates.T


def attention(tok_pad, in_matrix, out_matrix, router, gains, ids_col, after=()):
    padded, width = tok_pad.shape
    images = padded // PAD
    experts = router.shape[0]
    row = lambda lanes: pl.BlockSpec((PAD, lanes), lambda i: (i, 0))
    once = lambda a: pl.BlockSpec(a.shape, lambda i: (0, 0), pipeline_mode=pl.Buffered(1))
    return pl.pallas_call(
        behind(attention_kernel, 6, after),
        grid=(images,),
        in_specs=[row(width), once(in_matrix), once(out_matrix), once(router), once(gains), row(2)] + unread(after),
        out_specs=[
            row(3 * width),
            pl.BlockSpec((1, HEADS, PAD, PAD), lambda i: (i, 0, 0, 0)),
            row(width), row(width), row(width), row(experts),
            pl.BlockSpec((1, experts, PAD), lambda i: (i, 0, 0)),
        ],
        out_shape=[
            jax.ShapeDtypeStruct((padded, 3 * width), BF),
            jax.ShapeDtypeStruct((images, HEADS, PAD, PAD), BF),
            jax.ShapeDtypeStruct((padded, width), BF),
            jax.ShapeDtypeStruct((padded, width), F32),
            jax.ShapeDtypeStruct((padded, width), BF),
            jax.ShapeDtypeStruct((padded, experts), F32),
            jax.ShapeDtypeStruct((images, experts, PAD), F32),
        ],
        scratch_shapes=[pltpu.VMEM((PAD, width), BF)],
        compiler_params=params(),
        cost_estimate=cost(8),
        name="attention",
    )(tok_pad, in_matrix, out_matrix, router, gains, ids_col, *after)


def window_count():
    return -(-(15 + SEQ) // WIN)


def gather_kernel(meta_ref, routed_ref, cot_ref, lrow_ref, grow_ref, r_ref, g_ref, rt_ref, gt_ref, r_all, g_all):
    e = pl.program_id(0)
    images = lrow_ref.shape[0]
    listed = r_ref.shape[1]
    r_all[...] = jnp.zeros_like(r_all)
    g_all[...] = jnp.zeros_like(g_all)
    row = row_iota(WIN, PAD).astype(F32)
    for i in range(images):
        start, here = meta_ref[i, e], meta_ref[images + i, e]
        base = lax.shift_left(lax.shift_right_logical(start, 4), 4)
        shift = (start - base).astype(F32)
        local = lrow_ref[i, pl.ds(e, 1), :]
        gate = grow_ref[i, pl.ds(e, 1), :]
        for q in range(window_count()):
            @pl.when(jnp.logical_and(here > 0, base + q * WIN < start + here))
            def _(i=i, q=q, base=base, shift=shift, local=local, gate=gate):
                pick = jnp.logical_and(local >= 0.0, local + (shift - q * WIN) == row)
                low = pick.astype(F32).astype(BF)
                slot_gate = jnp.sum(jnp.where(pick, gate, 0.0), axis=1, keepdims=True)
                where = pl.ds(pl.multiple_of(base + q * WIN, 16), WIN)
                r_all[where, :] += dot_nn(low, routed_ref[i * PAD : (i + 1) * PAD, :])
                g_all[where, :] += slot_gate * dot_nn(low, cot_ref[i * PAD : (i + 1) * PAD, :])
    r_ref[0] = r_all[0:listed, :].astype(BF)
    g_ref[0] = g_all[0:listed, :].astype(BF)
    rt_ref[0] = r_all[0:listed, :].T.astype(BF)
    gt_ref[0] = g_all[0:listed, :].astype(BF).astype(F32).T.astype(BF)


def gather(meta, routed, cot_pad, lrow, grow, listed, after=()):
    width = routed.shape[1]
    experts = lrow.shape[1]
    once = lambda a: pl.BlockSpec(a.shape, lambda e, m: (0,) * a.ndim, pipeline_mode=pl.Buffered(1))
    block = pl.BlockSpec((1, listed, width), lambda e, m: (e, 0, 0))
    turned = pl.BlockSpec((1, width, listed), lambda e, m: (e, 0, 0))
    return pl.pallas_call(
        behind(gather_kernel, 5, after),
        grid_spec=pltpu.PrefetchScalarGridSpec(
            num_scalar_prefetch=1,
            grid=(experts,),
            in_specs=[once(routed), once(cot_pad), once(lrow), once(grow)] + unread(after),
            out_specs=[block, block, turned, turned],
            scratch_shapes=[pltpu.VMEM((listed + WIN, width), F32)] * 2,
        ),
        out_shape=[jax.ShapeDtypeStruct((experts, listed, width), BF)] * 2
        + [jax.ShapeDtypeStruct((experts, width, listed), BF)] * 2,
        compiler_params=params(),
        cost_estimate=cost(8),
        name="gather",
    )(meta, routed, cot_pad, lrow, grow, *after)


def gelu_both(pre):
    bell = jnp.exp(-0.5 * (pre * pre))
    t = pl.reciprocal(1.0 + (0.3275911 * 2.0**-0.5) * jnp.abs(pre))
    tail = t * (0.127414796 + t * (-0.142248368 + t * (0.7107068705 + t * (-0.7265760135 + t * 0.5307027145))))
    tail = tail * bell
    phi = jnp.where(pre < 0.0, tail, 1.0 - tail)
    return pre * phi, phi + pre * bell * 0.3989422804014327


def expert_kernel(first, half, at_ref, *refs):
    rep = 4
    (r_ref, g_ref, rt_ref, gt_ref), w_refs, b_ref, refs = refs[:4], refs[4:12], refs[12], refs[13:]
    if first:
        refs = refs[2 * (half > 0) :]
        y_ref, d_ref, near_ref, far_ref, db_ref, obg_ref, y_all, d_all = refs
    else:
        (ob_ref, y_in, d_in), refs = refs[:3], refs[3 + 2 * (half > 0) :]
        y_ref, d_ref, near_ref, far_ref, db_ref, y_all, d_all = refs
    listed = r_ref.shape[1]
    step = pl.program_id(0)
    count = at_ref[2 + lax.bitwise_xor(expert_rank(step, half), at_ref[1])]

    def run(n):
        rows_t, grads_t = rt_ref[0, :, :n], gt_ref[0, :, :n]

        def weights(r):
            place = lax.bitwise_xor(at_ref[0], r)
            return place, w_refs[r][0, 0], w_refs[rep + r][0, 0]

        def enter_part(r):
            place, enter, leave = weights(r)
            pre = dot_nn(r_ref[0, :n, :], enter) + b_ref[0, pl.ds(place, 1), :]
            return pre, dot_nn(g_ref[0, :n, :], leave)

        def middle_part(pre, grad_act):
            act, slope = gelu_both(pre)
            return act.astype(BF), (grad_act * slope).astype(BF)

        def leave_part(r, act, grad_pre):
            place, enter, leave = weights(r)
            out = far_ref if r % 2 else near_ref
            out[r // 2, 0, 0] = dot_nn(rows_t, grad_pre).astype(BF)
            out[r // 2, 0, 1] = dot_nn(grads_t, act).astype(BF)
            db_ref[0, pl.ds(place, 1), :] = jnp.sum(grad_pre.astype(F32), axis=0, keepdims=True)
            y_part = dot_nt(act, leave)
            d_part = dot_nt(grad_pre, enter)
            if r == 0:
                y_all[:n, :] = y_part if first else y_part + y_in[0, :n, :]
                d_all[:n, :] = d_part if first else d_part + d_in[0, :n, :]
            else:
                y_all[:n, :] += y_part
                d_all[:n, :] += d_part

        held = enter_part(0)
        ready = None
        for r in range(rep):
            now = middle_part(*held)
            if r + 1 < rep:
                held = enter_part(r + 1)
            if ready is not None:
                leave_part(r - 1, *ready)
            ready = now
        leave_part(rep - 1, *ready)
        if not first:
            y_ref[0, :n, :] = (y_all[:n, :] + ob_ref[0]).astype(BF)
            d_ref[0, :n, :] = d_all[:n, :].astype(BF)
        else:
            y_ref[0, :n, :] = y_all[:n, :]
            d_ref[0, :n, :] = d_all[:n, :]
        if n < listed:
            y_ref[0, n:, :] = jnp.zeros((listed - n, y_ref.shape[2]), y_ref.dtype)
            d_ref[0, n:, :] = jnp.zeros((listed - n, y_ref.shape[2]), y_ref.dtype)

    if first:
        obg_ref[0] = jnp.sum(g_ref[0].astype(F32), axis=0, keepdims=True)
    short = listed * 3 // 4 // 16 * 16
    pl.when(count <= short)(lambda: run(short))
    pl.when(count > short)(lambda: run(listed))


def expert_rank(step, half):
    return lax.shift_left(lax.bitwise_and(step, 3), 1) + lax.shift_right_logical(step, 2) + half


def expert_pass(at, lists, weights, bias, out_bias=None, carried=None, half=0, done=None, after=()):
    first = carried is None
    rows = lists[0]
    experts, listed, width = rows.shape
    rep, cols = bias.shape[1], bias.shape[2]
    steps = experts // 2
    here = lambda e, at: lax.bitwise_xor(expert_rank(e, half), at[1])
    block = pl.BlockSpec((1, listed, width), lambda e, at: (here(e, at), 0, 0))
    turned = pl.BlockSpec((1, width, listed), lambda e, at: (here(e, at), 0, 0))
    out_w = pl.BlockSpec((rep // 2, 1, 2, width, cols), lambda e, at: (0, e, 0, 0, 0))
    in_specs = [
        block, block, turned, turned,
        *[pl.BlockSpec((1, 1, width, cols), lambda e, at, m=m: (m, e, 0, 0)) for _, m in weights],
        pl.BlockSpec((1, rep, cols), lambda e, at: (here(e, at), 0, 0)),
    ]
    args = list(lists) + [a for a, _ in weights] + [bias]
    kind = F32 if first else BF
    out_specs = [block, block, out_w, out_w, pl.BlockSpec((1, rep, cols), lambda e, at: (here(e, at), 0, 0))]
    out_shape = [
        jax.ShapeDtypeStruct(rows.shape, kind),
        jax.ShapeDtypeStruct(rows.shape, kind),
        jax.ShapeDtypeStruct((rep // 2, steps, 2, width, cols), BF),
        jax.ShapeDtypeStruct((rep // 2, steps, 2, width, cols), BF),
        jax.ShapeDtypeStruct((experts, rep, cols), F32),
    ]
    aliases = {}
    if first:
        out_specs.append(pl.BlockSpec((1, 1, width), lambda e, at: (here(e, at), 0, 0)))
        out_shape.append(jax.ShapeDtypeStruct((experts, 1, width), F32))
    else:
        in_specs += [pl.BlockSpec((1, 1, width), lambda e, at: (here(e, at), 0, 0)), block, block]
        args += [out_bias, *carried]
    if half:
        aliases = {len(args) + 1: 0, len(args) + 2: 1}
        in_specs += unread(done)
        args += list(done)
    kernel = behind(functools.partial(expert_kernel, first, half), len(args) + 1, after)
    return pl.pallas_call(
        kernel,
        grid_spec=pltpu.PrefetchScalarGridSpec(
            num_scalar_prefetch=1,
            grid=(steps,),
            in_specs=in_specs + unread(after),
            out_specs=out_specs,
            scratch_shapes=[pltpu.VMEM((listed, width), F32)] * 2,
        ),
        out_shape=out_shape,
        input_output_aliases=aliases,
        compiler_params=params(),
        cost_estimate=cost(4),
        name=f"experts_{0 if first else 1}{half}",
    )(at, *args, *after)


def combine_kernel(
    meta_ref, y_ref, d_ref, lcol_ref, gcol_ref, hidden_ref, cot_ref, mixed_ref, out_w_ref, router_ref, gains_ref,
    out_ref, gh_ref, gm_ref, dout_ref, drouter_ref, dscale_ref, y_acc, g_acc, d_acc,
):
    i = pl.program_id(0)
    images = pl.num_programs(0)
    experts, listed, width = y_ref.shape
    gates = gcol_ref[...]
    local = lcol_ref[...]
    go = cot_ref[...].astype(F32)
    lane = lane_iota(PAD, WIN).astype(F32)
    expert = lane_iota(PAD, experts)

    def window(e, q, base, shift):
        at = jnp.minimum(base + q * WIN, listed - WIN)
        moved = (at - base).astype(F32)
        spot = local[:, e : e + 1] + shift
        pick = jnp.logical_and(spot == lane + moved, local[:, e : e + 1] >= 0.0)
        pick = jnp.logical_and(pick, spot >= q * WIN)
        low = pick.astype(F32).astype(BF)
        where = pl.ds(pl.multiple_of(at, 16), WIN)
        return dot_nn(low, y_ref[e, where, :]), dot_nn(low, d_ref[e, where, :])

    y_sum = jnp.zeros((PAD, width), F32)
    d_sum = jnp.zeros((PAD, width), F32)
    grad_gates = jnp.zeros((PAD, experts), F32)
    bases = []
    for e in range(experts):
        start = meta_ref[i, e]
        base = lax.shift_left(lax.shift_right_logical(start, 4), 4)
        bases.append((start, base))
        y_tok, d_tok = window(e, 0, base, (start - base).astype(F32))
        y_sum += gates[:, e : e + 1] * y_tok
        d_sum += d_tok
        gg = jnp.sum(go * y_tok, axis=1, keepdims=True)
        grad_gates += jnp.where(expert == e, gg, 0.0)
    y_acc[...] = y_sum
    d_acc[...] = d_sum
    g_acc[...] = grad_gates
    for e in range(experts):
        start, base = bases[e]
        here = meta_ref[images + i, e]
        for q in range(1, window_count()):
            @pl.when(base + q * WIN < start + here)
            def _(e=e, q=q, base=base, start=start):
                y_tok, d_tok = window(e, q, base, (start - base).astype(F32))
                y_acc[...] += gates[:, e : e + 1] * y_tok
                d_acc[...] += d_tok
                gg = jnp.sum(go * y_tok, axis=1, keepdims=True)
                g_acc[...] += jnp.where(expert == e, gg, 0.0)
    hidden = hidden_ref[...]
    y_acc[...] += hidden
    store_image(out_ref, i, y_acc)
    grad_gates = g_acc[...]
    pick = gates * (grad_gates - jnp.sum(gates * grad_gates, axis=1, keepdims=True))
    logit_low = pick.astype(BF)
    grad_routed = d_acc[...] + dot_nn(logit_low, router_ref[...])
    normed, inverse = normalize(hidden)
    routed = (normed * gains_ref[2:3, :] + gains_ref[3:4, :]).astype(BF)
    grad_hidden = go + norm_back(grad_routed, normed, inverse, gains_ref[2:3, :])
    gh_ref[...] = grad_hidden
    grad_mix = grad_hidden.astype(BF)
    gm_ref[...] = dot_nt(grad_mix, out_w_ref[...]).astype(BF)

    @pl.when(i == 0)
    def _():
        dout_ref[...] = jnp.zeros_like(dout_ref)
        drouter_ref[...] = jnp.zeros_like(drouter_ref)
        dscale_ref[...] = jnp.zeros_like(dscale_ref)

    dout_ref[...] += dot_tn(mixed_ref[...], grad_mix)
    drouter_ref[...] += dot_tn(logit_low, routed)
    dscale_ref[2:3, :] += jnp.sum(grad_routed * normed, axis=0, keepdims=True)
    dscale_ref[3:4, :] += jnp.sum(grad_routed, axis=0, keepdims=True)
    dscale_ref[4:5, :] += jnp.sum(grad_hidden, axis=0, keepdims=True)


def combine(meta, y, d, lcol, gcol, hidden, cot_pad, mixed, out_matrix, router, gains, after=()):
    padded, width = hidden.shape
    images = padded // PAD
    experts = y.shape[0]
    row = lambda lanes: pl.BlockSpec((PAD, lanes), lambda i, m: (i, 0))
    once = lambda a: pl.BlockSpec(a.shape, lambda i, m: (0,) * a.ndim, pipeline_mode=pl.Buffered(1))
    return pl.pallas_call(
        behind(combine_kernel, 11, after),
        grid_spec=pltpu.PrefetchScalarGridSpec(
            num_scalar_prefetch=1,
            grid=(images,),
            in_specs=[
                once(y), once(d), row(experts), row(experts), row(width), row(width), row(width),
                once(out_matrix), once(router), once(gains), *unread(after),
            ],
            out_specs=[
                whole((images * SEQ, width)), row(width), row(width), whole((width, width)), whole((experts, width)),
                whole((8, width)),
            ],
            scratch_shapes=[
                pltpu.VMEM((PAD, width), F32), pltpu.VMEM((PAD, experts), F32), pltpu.VMEM((PAD, width), F32),
            ],
        ),
        out_shape=[
            jax.ShapeDtypeStruct((images * SEQ, width), F32),
            jax.ShapeDtypeStruct((padded, width), F32),
            jax.ShapeDtypeStruct((padded, width), BF),
            jax.ShapeDtypeStruct((width, width), F32),
            jax.ShapeDtypeStruct((experts, width), F32),
            jax.ShapeDtypeStruct((8, width), F32),
        ],
        compiler_params=params(),
        cost_estimate=cost(40),
        name="combine",
    )(meta, y, d, lcol, gcol, hidden, cot_pad, mixed, out_matrix, router, gains, *after)


def attention_back_kernel(
    place_ref, proj_ref, prob_ref, gm_ref, gh_ref, tpad_ref, in_ref, gains_ref, dout_ref, small_ref,
    grad_ref, near_ref, far_ref, din_ref, dscale_ref, line_ref, dproj, grad_all,
):
    i = pl.program_id(0)
    width = gm_ref.shape[1]
    pair = 2 * HEAD
    halves = lane_iota(PAD, pair) < HEAD
    factor = HEAD ** -0.5
    for p in range(HEADS // 2):
        cut = slice(pair * p, pair * (p + 1))
        q = proj_ref[:, cut]
        k = proj_ref[:, width + pair * p : width + pair * (p + 1)]
        v = proj_ref[:, 2 * width + pair * p : 2 * width + pair * (p + 1)]
        gm = gm_ref[:, cut]
        gms = split_halves(gm, halves)
        low = jnp.concatenate([prob_ref[0, 2 * p], prob_ref[0, 2 * p + 1]], axis=0)
        probs = low.astype(F32)
        grad_probs = dot_nt(gms, v)
        middle = jnp.sum(probs * grad_probs, axis=1, keepdims=True)
        grad_scores = (probs * (grad_probs - middle)).astype(BF)
        grad_q = dot_nn(grad_scores, k)
        dproj[:, cut] = (jnp.where(halves, grad_q[:PAD], grad_q[PAD:]) * factor).astype(BF)
        dproj[:, width + pair * p : width + pair * (p + 1)] = (
            dot_tn(grad_scores, split_halves(q, halves)) * factor
        ).astype(BF)
        dproj[:, 2 * width + pair * p : 2 * width + pair * (p + 1)] = dot_tn(low, gms).astype(BF)
    normed, inverse = normalize(tpad_ref[...].astype(F32))
    entry = (normed * gains_ref[0:1, :] + gains_ref[1:2, :]).astype(BF)
    grads = dproj[...]
    grad_entry = dot_nt(grads, in_ref[...])

    @pl.when(i == 0)
    def _():
        din_ref[...] = jnp.zeros_like(din_ref)
        dscale_ref[...] = jnp.zeros_like(dscale_ref)

    din_ref[...] += dot_tn(entry, grads)
    dscale_ref[0:1, :] += jnp.sum(grad_entry * normed, axis=0, keepdims=True)
    dscale_ref[1:2, :] += jnp.sum(grad_entry, axis=0, keepdims=True)
    grad = gh_ref[...] + norm_back(grad_entry, normed, inverse, gains_ref[0:1, :])
    grad_all[...] = grad
    store_image(grad_ref, i, grad_all)

    @pl.when(i == pl.num_programs(0) - 1)
    def _():
        blocks, rows = 2 * near_ref.shape[0], near_ref.shape[1]
        owner = lane_iota(blocks, width) // rows == row_iota(blocks, width)
        spot = row_iota(width, 128) % rows
        line = jnp.zeros((blocks, 128), F32)
        for s in range(2):
            spread = jnp.where(owner, dscale_ref[s : s + 1, :], 0.0)
            chosen = (lane_iota(width, 128) == spot + s * rows).astype(F32)
            line += lax.dot_general(
                spread, chosen, (((1,), (0,)), ((), ())),
                preferred_element_type=F32, precision=lax.Precision.HIGHEST,
            )
        line_ref[...] = line
        scale_row = row_iota(8, 128) == 6
        for side, out in ((0, near_ref), (1, far_ref)):
            def body(j, carry, side=side, out=out):
                place = place_ref[side * (blocks // 2) + j]
                here = pl.ds(pl.multiple_of(place * rows, rows), rows)
                out[j, :, : 3 * width] = din_ref[here, :].astype(BF)
                out[j, :, 3 * width : 4 * width] = dout_ref[here, :].astype(BF)
                small = small_ref[place] + jnp.where(scale_row, line_ref[pl.ds(place, 1), :], 0.0)
                out[j, :, 4 * width :] = resplit(small)
                return carry

            lax.fori_loop(0, blocks // 2, body, 0)


def attention_back(place, proj, probs, grad_mixed, grad_hidden, tok_pad, in_matrix, gains, grad_out, small, after=()):
    padded, width = grad_hidden.shape
    images = padded // PAD
    blocks = small.shape[0]
    rows = width // blocks
    row = lambda lanes: pl.BlockSpec((PAD, lanes), lambda i, m: (i, 0))
    once = lambda a: pl.BlockSpec(a.shape, lambda i, m: (0,) * a.ndim, pipeline_mode=pl.Buffered(1))
    half = (blocks // 2, rows, 4 * width + 128)
    return pl.pallas_call(
        behind(attention_back_kernel, 10, after),
        grid_spec=pltpu.PrefetchScalarGridSpec(
            num_scalar_prefetch=1,
            grid=(images,),
            in_specs=[
                row(3 * width), pl.BlockSpec((1, HEADS, PAD, PAD), lambda i, m: (i, 0, 0, 0)), row(width), row(width),
                row(width), once(in_matrix), once(gains), once(grad_out), once(small),
                *unread(after),
            ],
            out_specs=[whole((images * SEQ, width)), whole(half), whole(half)],
            scratch_shapes=[
                pltpu.VMEM((width, 3 * width), F32), pltpu.VMEM((8, width), F32), pltpu.VMEM((blocks, 128), F32),
                pltpu.VMEM((PAD, 3 * width), BF), pltpu.VMEM((PAD, width), F32),
            ],
        ),
        out_shape=[
            jax.ShapeDtypeStruct((images * SEQ, width), F32),
            jax.ShapeDtypeStruct(half, BF),
            jax.ShapeDtypeStruct(half, BF),
        ],
        compiler_params=params(),
        cost_estimate=cost(50),
        name="attention_back",
    )(place, proj, probs, grad_mixed, grad_hidden, tok_pad, in_matrix, gains, grad_out, small, *after)


X_BIT, CORE_BIT, Y_BIT = 16, 8, 1
Z_BITS = (2, 4, 6)
AXES = ("rep", "ep")


def swap(array, bits):
    devices = lax.axis_size("rep") * lax.axis_size("ep")
    return lax.ppermute(array, AXES, [(d, d ^ bits) for d in range(devices)])


def relative(position):
    c, x, y, z = position >> 4 & 1, position >> 3 & 1, position >> 2 & 1, position & 3
    return x * X_BIT + c * CORE_BIT + z * 2 + y * Y_BIT


def stack_kernel(count, *refs):
    for j in range(count):
        refs[count][j] = refs[j][...]


def stack(arrays, after=()):
    count = len(arrays)
    return pl.pallas_call(
        behind(functools.partial(stack_kernel, count), count, after),
        in_specs=[pl.BlockSpec(memory_space=pltpu.VMEM)] * count + unread(after),
        out_shape=jax.ShapeDtypeStruct((count,) + arrays[0].shape, arrays[0].dtype),
        compiler_params=params(),
        cost_estimate=cost(1),
        name="stack",
    )(*arrays, *after)


def turn_stack_kernel(*refs):
    for m in range(2):
        for j in range(4):
            refs[4][m, j] = refs[j][m]


def turn_stack(arrays, after=()):
    piece = arrays[0].shape
    return pl.pallas_call(
        behind(turn_stack_kernel, 4, after),
        in_specs=[pl.BlockSpec(memory_space=pltpu.VMEM)] * 4 + unread(after),
        out_shape=jax.ShapeDtypeStruct((2, 4) + piece[1:], arrays[0].dtype),
        compiler_params=params(),
        cost_estimate=cost(2),
        name="turn_stack",
    )(*arrays, *after)


def pick_kernel(far_x, far_y, x_in, x_out, y_out):
    x_in[0] = far_x[0]
    x_out[0] = far_x[1]
    y_out[0] = far_y[1]


def pick(far_x, far_y, after=()):
    shape = (1,) + far_x.shape[1:]
    return pl.pallas_call(
        behind(pick_kernel, 2, after),
        in_specs=[pl.BlockSpec(memory_space=pltpu.VMEM)] * 2 + unread(after),
        out_shape=[jax.ShapeDtypeStruct(shape, far_x.dtype)] * 3,
        compiler_params=params(),
        cost_estimate=cost(3),
        name="pick",
    )(far_x, far_y, *after)


def sum_everywhere(values):
    for bits in (CORE_BIT, Y_BIT, X_BIT, 2, 4):
        values = values + swap(values, bits)
    return values


def unsplit(block):
    return block[:8] + block[8:]


def resplit(small):
    twice = jnp.concatenate([small, small], axis=0)
    high = twice.astype(BF).astype(F32)
    return jnp.where(row_iota(16, 128) < 8, high, twice - high).astype(BF)


def block_sum_kernel(parts, terms, *refs):
    ins, outs = refs[:terms], refs[terms:]
    size = ins[0].shape[0] // parts
    lanes = ins[0].shape[2]
    for p in range(parts):
        for j in range(size):
            at = p * size + j
            total = ins[0][at].astype(F32)
            for t in ins[1:]:
                total = total + t[at].astype(F32)
            small = unsplit(total[:, lanes - 128 :])
            outs[p][j, :, : lanes - 128] = total[:, : lanes - 128].astype(BF)
            outs[p][j, :, lanes - 128 :] = resplit(small)


def block_sum(terms, parts):
    size = terms[0].shape[0] // parts
    shape = (size,) + terms[0].shape[1:]
    return pl.pallas_call(
        functools.partial(block_sum_kernel, parts, len(terms)),
        out_shape=[jax.ShapeDtypeStruct(shape, BF)] * parts,
        compiler_params=params(),
        cost_estimate=cost(0.1),
        name="block_sum",
    )(*terms)


def scatter_dense(near, far, beside):
    parts = block_sum([near, swap(far, CORE_BIT)], 4)
    got = [swap(parts[1], Y_BIT), swap(parts[2], X_BIT), swap(parts[3], X_BIT | Y_BIT)]
    keep, beside = lax.optimization_barrier((parts[0], beside))
    parts = block_sum([keep] + got, 4)
    return beside, [parts[0]] + [swap(parts[z], Z_BITS[z - 1]) for z in (1, 2, 3)]


def fold_cores_kernel(n0, n1, g0, g1, a_keep, b_keep, a_send, b_send):
    for x in range(2):
        a_keep[x, 0] = n0[x, 0, 0] + g0[x, 0, 0]
        a_send[x, 0] = n1[x, 0, 0] + g1[x, 0, 0]
        out = b_send if x else b_keep
        out[0, 0] = n0[x, 0, 1] + g0[x, 0, 1]
        out[1, 0] = n1[x, 0, 1] + g1[x, 0, 1]


def fold_cores(near, got):
    rows, cols = near[0].shape[3:]
    out = jax.ShapeDtypeStruct((2, 4, rows, cols), BF)
    return pl.pallas_call(
        fold_cores_kernel,
        grid=(4, 2),
        in_specs=[pl.BlockSpec((2, 1, 2, rows // 2, cols), lambda z, r: (0, z, 0, r, 0))] * 4,
        out_specs=[pl.BlockSpec((2, 1, rows // 2, cols), lambda z, r: (0, z, r, 0))] * 4,
        out_shape=[out] * 4,
        compiler_params=params(),
        cost_estimate=cost(7),
        name="fold_cores",
    )(*near, *got)


def fold_first_kernel(a_keep, b_keep, a_got, b_got, a_near, b_near, a_far, b_far):
    a_near[0] = a_keep[0, 0] + a_got[0, 0]
    b_near[0] = b_keep[0, 0] + b_got[0, 0]
    a_far[0] = a_keep[1, 0] + a_got[1, 0]
    b_far[0] = b_keep[1, 0] + b_got[1, 0]


def fold_first(a_keep, b_keep, a_got, b_got, after=()):
    rows, cols = a_keep.shape[2:]
    return pl.pallas_call(
        behind(fold_first_kernel, 4, after),
        grid=(4,),
        in_specs=[pl.BlockSpec((2, 1, rows, cols), lambda z: (0, z, 0, 0))] * 4 + unread(after),
        out_specs=[pl.BlockSpec((1, rows, cols), lambda z: (z, 0, 0))] * 4,
        out_shape=[jax.ShapeDtypeStruct((4, rows, cols), BF)] * 4,
        compiler_params=params(),
        cost_estimate=cost(4),
        name="fold_first",
    )(a_keep, b_keep, a_got, b_got, *after)


def fold_second_kernel(a_keep, b_keep, a_got, b_got, *parts):
    for z in range(4):
        parts[z][0] = a_keep[z] + a_got[z]
        parts[z][1] = b_keep[z] + b_got[z]


def fold_second(a_keep, b_keep, a_got, b_got):
    return pl.pallas_call(
        fold_second_kernel,
        out_shape=[jax.ShapeDtypeStruct((2,) + a_keep.shape[1:], BF)] * 4,
        compiler_params=params(),
        cost_estimate=cost(3),
        name="fold_second",
    )(a_keep, b_keep, a_got, b_got)


def total_of(array):
    return jnp.sum(jnp.sum(array, axis=1, keepdims=True), axis=0, keepdims=True)


def expert_update_kernel(given, *refs):
    parts, (wi, fi, si, wo, fo, so, before), refs = refs[:4], refs[4:11], refs[11:]
    outs, sums = refs[given : given + 6], refs[given + 6]
    lane = lane_iota(1, 128)
    kept, moved = before[0:1, :], before[1:2, :]
    for m, (weight, first, second, new) in enumerate(((wi, fi, si, outs[0:3]), (wo, fo, so, outs[3:6]))):
        grad = parts[0][m].astype(F32)
        for part in parts[1:]:
            grad = grad + part[m].astype(F32)
        if m:
            grad = grad.T
        state = moments(weight[0], grad, first[0], second[0])
        for ref, value in zip(new, state):
            ref[0] = value
        slot = lane == (10 if m else 8)
        kept += jnp.where(slot, total_of(weight[0] * weight[0]), 0.0)
        moved += jnp.where(slot, total_of(state[2] * state[2]), 0.0)
    sums[...] = jnp.zeros_like(sums)
    sums[0:1, :] = kept
    sums[1:2, :] = moved


def expert_update(parts, arrays, sums, slice_index, done=()):
    rows, cols = parts[0].shape[1:]
    part = pl.BlockSpec(parts[0].shape, lambda i: (0, 0, 0))
    enter = pl.BlockSpec((1, rows, cols), lambda i: (0, 0, slice_index))
    leave = pl.BlockSpec((1, cols, rows), lambda i: (0, slice_index, 0))
    total = pl.BlockSpec((8, 128), lambda i: (0, 0))
    shape = jax.ShapeDtypeStruct(arrays[0].shape, F32)
    return pl.pallas_call(
        functools.partial(expert_update_kernel, len(done)),
        grid=(1,),
        in_specs=[part] * 4 + [enter] * 3 + [leave] * 3 + [total] + unread(done),
        out_specs=[enter] * 3 + [leave] * 3 + [total],
        out_shape=[shape] * 6 + [jax.ShapeDtypeStruct((8, 128), F32)],
        input_output_aliases={11 + j: j for j in range(len(done))},
        compiler_params=params(),
        cost_estimate=cost(0.1),
        name=f"expert_update_{slice_index}",
    )(*parts, *arrays, sums, *done)


def narrow(row, columns, rows):
    spread = jnp.where(lane_iota(rows, 128) % rows == row_iota(rows, 128), row, 0.0)
    chosen = (row_iota(128, columns) // rows == lane_iota(128, columns)).astype(F32)
    return lax.dot_general(
        spread, chosen, (((1,), (0,)), ((), ())), preferred_element_type=F32, precision=lax.Precision.HIGHEST
    )


def dense_update_kernel(*refs):
    ins, sums, states, outs = refs[:4], refs[4], refs[5:23], refs[23:]
    width = ins[0].shape[2] - 128
    total = ins[0][0].astype(F32)
    for t in ins[1:]:
        total = total + t[0].astype(F32)
    small = unsplit(total[:, width:])
    experts, rows = states[6].shape[1], states[6].shape[0]
    bias_rows = states[12].shape[1] // 128
    grads = (
        total[:, : width * 3 // 4],
        total[:, width * 3 // 4 : width],
        narrow(small[bias_rows + 1 : bias_rows + 2], experts, rows),
        narrow(small[bias_rows + 2 : bias_rows + 3], 5, rows),
        jnp.concatenate([small[j : j + 1] for j in range(bias_rows)], axis=1),
        small[bias_rows : bias_rows + 1],
    )
    lane = lane_iota(1, 128)
    kept, moved = sums[0:1, :], sums[1:2, :]
    for j, grad in enumerate(grads):
        weight, first, second = (states[3 * j + k][...] for k in range(3))
        state = moments(weight, grad, first, second)
        for k in range(3):
            outs[3 * j + k][...] = state[k]
        for c, slot in enumerate({0: (0,), 1: (1,), 2: (2,), 3: (3, 4, 5, 6, 7), 4: (9,), 5: (11,)}[j]):
            cut = (slice(None), slice(c, c + 1)) if j == 3 else (slice(None), slice(None))
            kept += jnp.where(lane == slot, total_of(weight[cut] * weight[cut]), 0.0)
            moved += jnp.where(lane == slot, total_of(state[2][cut] * state[2][cut]), 0.0)
    outs[18][...] = jnp.zeros_like(outs[18])
    outs[18][0:1, :] = kept
    outs[18][1:2, :] = moved


def dense_update(terms, sums, states):
    return pl.pallas_call(
        dense_update_kernel,
        out_shape=[jax.ShapeDtypeStruct(a.shape, F32) for a in states] + [jax.ShapeDtypeStruct((8, 128), F32)],
        compiler_params=params(),
        cost_estimate=cost(0.1),
        name="dense_update",
    )(*terms, sums, *states)


def new_weights_kernel(sums, counts, *refs):
    weights, steps, outs, norms = refs[:8], refs[8:16], refs[16:24], refs[24]
    weight_rms = jnp.sqrt(sums[0:1, :] / counts[...])
    step_rms = jnp.sqrt(sums[1:2, :] / counts[...])
    trust = weight_rms / step_rms
    norms[...] = jnp.zeros_like(norms)
    norms[0:1, :] = weight_rms
    norms[1:2, :] = step_rms
    norms[2:3, :] = trust
    for j, begin in enumerate((0, 1, 2, 3, 8, 9, 10, 11)):
        scale = trust[:, 3:8] if j == 3 else trust[:, begin : begin + 1]
        if len(outs[j].shape) == 3:
            outs[j][0] = weights[j][0] - RATE * scale * steps[j][0]
        else:
            outs[j][...] = weights[j][...] - RATE * scale * steps[j][...]


def new_weights(sums, counts, weights, steps):
    return pl.pallas_call(
        new_weights_kernel,
        out_shape=[jax.ShapeDtypeStruct(a.shape, F32) for a in weights] + [jax.ShapeDtypeStruct((8, 128), F32)],
        compiler_params=params(),
        cost_estimate=cost(5),
        name="new_weights",
    )(sums, counts, *weights, *steps)


CHUNKS = 2


def replicate_plan(
    tokens, cotangent, expert_ids, priority,
    heads_in, heads_in_first, heads_in_second, heads_out, heads_out_first, heads_out_second,
    router, router_first, router_second, scales, scales_first, scales_second,
    expert_in, expert_in_first, expert_in_second, bias_in, bias_in_first, bias_in_second,
    expert_out, expert_out_first, expert_out_second, bias_out, bias_out_first, bias_out_second,
):
    count, width = tokens.shape
    images = count // SEQ
    experts = router.shape[1]
    rep, ep = lax.axis_size("rep"), lax.axis_size("ep")
    rep_me, ep_me = lax.axis_index("rep"), lax.axis_index("ep")
    me = (rep_me * ep + ep_me).astype(jnp.int32)
    at = jnp.stack([rep_me, ep_me]).astype(jnp.int32)
    capacity = (5 * expert_ids.shape[1] * count + 4 * experts - 1) // (4 * experts)
    listed = -(-capacity // 16) * 16
    hidden_part = FF // rep
    cols = hidden_part // CHUNKS

    enter_low = expert_in[0].astype(BF)
    leave_low = expert_out[0].astype(BF).T
    pieces = [
        jnp.stack([enter_low[:, k * cols : (k + 1) * cols], leave_low[:, k * cols : (k + 1) * cols]])
        for k in range(CHUNKS)
    ]

    rows_here = heads_in.shape[0]
    small = jnp.concatenate([router, scales], axis=1)
    small = jnp.pad(small, ((0, 0), (0, 128 - small.shape[1])))
    biases = jnp.concatenate([bias_in.reshape(-1, 128), bias_out.reshape(-1, 128)], axis=0)
    biases = jnp.pad(biases, ((0, rows_here - biases.shape[0]), (0, 0)))
    dense = jnp.concatenate([heads_in, heads_out, small, biases], axis=1).astype(BF)
    order = jnp.array([relative(p) for p in range(rep * ep)], jnp.int32)
    place = jnp.bitwise_xor(order, me)
    spread = lambda a, fill: jnp.pad(
        a.reshape(-1, images, SEQ), ((0, 0), (0, 0), (0, PAD - SEQ)), constant_values=fill
    ).reshape(-1, images * PAD)
    ids_rows = spread(expert_ids.T, -1)
    rows = jnp.concatenate([spread(priority, count), ids_rows], axis=0).astype(F32)
    rows = jnp.pad(rows, ((0, 5), (0, 0)))

    zs_got = [swap(dense, bits) for bits in Z_BITS]
    tok_pad, cot_pad = spread_rows(tokens, cotangent)
    zs = stack([dense] + zs_got, after=(tok_pad,))
    zs, pieces[0] = lax.optimization_barrier((zs, pieces[0]))
    others = [swap(zs, bits) for bits in (Y_BIT, X_BIT, X_BIT | Y_BIT)]
    lrow, lcol, meta = find_places(rows, rows.T, capacity, experts)
    piece_got = [swap(pieces[0], bits) for bits in Z_BITS]
    plane = stack([zs] + others, after=(lrow, piece_got[0]))
    in_matrix, out_matrix, router_matrix, gains, small_all = assemble(
        place, plane.reshape((16,) + dense.shape), swap(plane, CORE_BIT).reshape((16,) + dense.shape), experts
    )
    bias_all = small_all[:, 128:].reshape(rep, ep, rows_here, 128)
    in_rows = hidden_part // 128
    enter_bias = bias_all[:, :, :in_rows].reshape(rep, ep, hidden_part).astype(F32).transpose(1, 0, 2)
    leave_bias = bias_all[:, :, in_rows].astype(F32).transpose(1, 0, 2).reshape(ep, 1, width)

    proj, probs, mixed, hidden, routed, gcol, grow = attention(
        tok_pad, in_matrix, out_matrix, router_matrix, gains, ids_rows.T
    )
    near = turn_stack([pieces[0]] + piece_got, after=(gcol,))
    far_x, far_y = swap(near, X_BIT), swap(near, Y_BIT)
    near, pieces[1] = lax.optimization_barrier((near, pieces[1]))
    lists = gather(meta, routed, cot_pad, lrow, grow, listed, after=(near,))
    near_two = turn_stack([pieces[1]] + [swap(pieces[1], bits) for bits in Z_BITS], after=(lists[0],))

    totals_here = meta[images - 1] + meta[2 * images - 1]
    at = jnp.concatenate([at, totals_here])
    bias_cut = lambda k: enter_bias[:, :, k * cols : (k + 1) * cols]
    cross = lambda a: swap(a, CORE_BIT)

    def first_half(near, far_x, crossed):
        pairs = []
        for m in range(2):
            other = (crossed[1][m], 0) if isinstance(crossed[1], tuple) else (crossed[1], m)
            pairs += [(near, m), (crossed[0], m), (far_x, m), other]
        return pairs

    def other_half(far_y, far_xy, crossed):
        return [
            pair
            for m in range(2)
            for pair in ((far_y, m), (crossed[0], m), (far_xy[m], 0), (crossed[1 + m], 0))
        ]

    x_in, x_out, y_out = pick(far_x, far_y, after=(near_two,))
    far_xy = swap(x_in, Y_BIT), swap(y_out, X_BIT)
    near, x_in = lax.optimization_barrier((near, x_in))
    crossed = cross(near), (cross(x_in), cross(x_out))
    y_part, d_part, near_a, far_a, bias_a, leave_a = expert_pass(
        at, lists, first_half(near, far_x, crossed), bias_cut(0)
    )
    y_part, *far_xy = lax.optimization_barrier((y_part, *far_xy))
    far_x_two, far_y_two = swap(near_two, X_BIT), swap(near_two, Y_BIT)
    crossed = cross(far_y), cross(far_xy[0]), cross(far_xy[1])
    y_half, d_half, near_b, far_b, bias_b, leave_b = expert_pass(
        at, lists, other_half(far_y, far_xy, crossed), bias_cut(0), half=1, done=(y_part, d_part),
    )
    got_a = swap(far_a, CORE_BIT)
    near_two, bias_a = lax.optimization_barrier((near_two, bias_a))
    near_crossed = cross(near_two)
    far_b, far_x_two, far_y_two, near_crossed = lax.optimization_barrier((far_b, far_x_two, far_y_two, near_crossed))
    diagonal = far_x_two[0:1], far_y_two[1:2]
    crossed = near_crossed, cross(far_x_two)
    far_xy_two = swap(diagonal[0], Y_BIT), swap(diagonal[1], X_BIT)
    got_b = swap(far_b, CORE_BIT)
    one = fold_cores((near_a, near_b), (got_a, got_b))
    a_send, far_y_two = lax.optimization_barrier((one[2], far_y_two))
    one = (*one[:2], a_send, one[3])
    far_y_crossed = cross(far_y_two)
    even = lax.bitwise_xor(jnp.arange(ep, dtype=jnp.int32), ep_me)[:, None, None] % 2 == 0
    grad_bias = [jnp.where(even, bias_a, bias_b)]
    grad_leave_bias = jnp.where(even, leave_a, leave_b)
    one_got = swap(one[2], Y_BIT), swap(one[3], X_BIT)
    y_part, d_part, near_a, far_a, bias_a = expert_pass(
        at, lists, first_half(near_two, far_x_two, crossed), bias_cut(1), leave_bias, (y_half, d_half),
        after=one[2:],
    )
    y_part, *far_xy_two = lax.optimization_barrier((y_part, *far_xy_two))
    crossed = far_y_crossed, cross(far_xy_two[0]), cross(far_xy_two[1])
    got_a = swap(far_a, CORE_BIT)
    y, d, near_b, far_b, bias_b = expert_pass(
        at, lists, other_half(far_y_two, far_xy_two, crossed), bias_cut(1), leave_bias, (y_half, d_half), half=1,
        done=(y_part, d_part),
    )
    far_b, *one_got = lax.optimization_barrier((far_b, *one_got))
    one = fold_first(*one[:2], *one_got)
    one_got = swap(one[2], X_BIT), swap(one[3], Y_BIT)
    got_b = swap(far_b, CORE_BIT)
    two = fold_cores((near_a, near_b), (got_a, got_b))
    two_got = swap(two[2], Y_BIT), swap(two[3], X_BIT)
    output, grad_hidden, grad_mixed, grad_out, grad_router, grad_scale = combine(
        meta, y, d, lcol, gcol, hidden, cot_pad, mixed, out_matrix, router_matrix, gains,
        after=list(one) + list(two[2:]),
    )
    grad_mixed, *one_got = lax.optimization_barrier((grad_mixed, *one_got))
    one = fold_second(*one[:2], *one_got)
    one_got = [swap(one[z], Z_BITS[z - 1]) for z in (1, 2, 3)]
    two = fold_first(*two[:2], *two_got)
    two_got = swap(two[2], X_BIT), swap(two[3], Y_BIT)
    grad_bias.append(jnp.where(even, bias_a, bias_b))
    devices = rep * ep
    by_device = lambda a: jnp.pad(
        a.reshape(a.shape[0], devices, rows_here).transpose(1, 0, 2).reshape(devices, 1, -1),
        ((0, 0), (0, 0), (0, 128 - a.shape[0] * rows_here)),
    )
    small_grads = jnp.concatenate(
        [
            jnp.concatenate(grad_bias, axis=2).transpose(1, 0, 2).reshape(devices, in_rows, 128),
            grad_leave_bias.reshape(ep, rep, 128).transpose(1, 0, 2).reshape(devices, 1, 128),
            by_device(grad_router),
            by_device(grad_scale[:5]),
        ],
        axis=1,
    )
    small_grads = jnp.pad(small_grads, ((0, 0), (0, 8 - small_grads.shape[1]), (0, 0)))
    input_grad, near_dense, far_dense = attention_back(
        place, proj, probs, grad_mixed, grad_hidden, tok_pad, in_matrix, gains, grad_out, small_grads,
        after=list(one[1:]) + list(two[2:]),
    )
    far_dense, *got = lax.optimization_barrier((far_dense, *one_got, *two_got))
    one_got, two_got = got[:3], got[3:]
    two = fold_second(*two[:2], *two_got)
    far_dense, *two = lax.optimization_barrier((far_dense, *two))
    two_got = [swap(two[z], Z_BITS[z - 1]) for z in (1, 2, 3)]
    expert_states = (expert_in, expert_in_first, expert_in_second, expert_out, expert_out_first, expert_out_second)
    *expert_new, sums = expert_update([one[0]] + list(one_got), expert_states, jnp.zeros((8, 128), F32), 0)
    sums, dense_terms = scatter_dense(near_dense, far_dense, sums)
    dense_states = (
        heads_in, heads_in_first, heads_in_second, heads_out, heads_out_first, heads_out_second,
        router, router_first, router_second, scales, scales_first, scales_second,
        bias_in, bias_in_first, bias_in_second, bias_out, bias_out_first, bias_out_second,
    )
    *dense_new, sums = dense_update(dense_terms, sums, dense_states)
    sums, *two_got = lax.optimization_barrier((sums, *two_got))
    *expert_new, sums = expert_update([two[0]] + two_got, expert_states, sums, 1, done=expert_new)
    in_first, in_second, in_step, out_first, out_second, out_step = expert_new
    sums = sum_everywhere(sums)
    counts = jnp.array(
        [3 * width * width, width * width, width * experts]
        + [width] * 5
        + [experts * width * FF, experts * FF, experts * FF * width, experts * width]
        + [1] * (128 - 12),
        jnp.float32,
    )[None]
    trio = lambda j: tuple(dense_new[3 * j : 3 * j + 3])
    states = [
        trio(0), trio(1), trio(2), trio(3), (in_first, in_second, in_step), trio(4),
        (out_first, out_second, out_step), trio(5),
    ]
    weights_now = (heads_in, heads_out, router, scales, expert_in, bias_in, expert_out, bias_out)
    *fresh, norms = new_weights(sums, counts, weights_now, [state[2] for state in states])
    results = [output, input_grad]
    for state, weight in zip(states, fresh):
        results.extend([state[0], state[1], weight])
    results.append(norms[:3, :12])
    return tuple(results)


def expert_front(rows, enter_weight, enter_bias):
    pre = jnp.einsum("sjcd,jdf->sjcf", rows, enter_weight, preferred_element_type=jnp.float32)
    return pre + enter_bias.astype(jnp.float32)[None, :, None, :]


def exchange_plan(
    tokens,
    cotangent,
    expert_ids,
    priority,
    heads_in,
    heads_in_first,
    heads_in_second,
    heads_out,
    heads_out_first,
    heads_out_second,
    router,
    router_first,
    router_second,
    scales,
    scales_first,
    scales_second,
    expert_in,
    expert_in_first,
    expert_in_second,
    bias_in,
    bias_in_first,
    bias_in_second,
    expert_out,
    expert_out_first,
    expert_out_second,
    bias_out,
    bias_out_first,
    bias_out_second,
):
    in_matrix, out_matrix, router_matrix, scale_table = (
        lax.all_gather(heads_in.astype(jnp.bfloat16), ("rep", "ep"), axis=0, tiled=True),
        lax.all_gather(heads_out.astype(jnp.bfloat16), ("rep", "ep"), axis=0, tiled=True),
        lax.all_gather(router.astype(jnp.bfloat16), ("rep", "ep"), axis=0, tiled=True),
        lax.all_gather(scales.astype(jnp.bfloat16), ("rep", "ep"), axis=0, tiled=True),
    )
    enter_weight, enter_bias, leave_weight, leave_bias = (
        lax.all_gather(expert_in.astype(jnp.bfloat16), "rep", axis=2, tiled=True),
        lax.all_gather(bias_in.astype(jnp.bfloat16), "rep", axis=1, tiled=True),
        lax.all_gather(expert_out.astype(jnp.bfloat16), "rep", axis=1, tiled=True),
        lax.all_gather(bias_out.astype(jnp.bfloat16), "rep", axis=1, tiled=True),
    )
    gains = scale_table.astype(jnp.float32)
    inputs = tokens.astype(jnp.float32)
    count, width = inputs.shape
    images = count // SEQ
    factor = HEAD ** (-0.5)
    normed_one, inverse_one = normalize(inputs)
    entry = (normed_one * gains[:, 0] + gains[:, 1]).astype(jnp.bfloat16)
    projected = jnp.dot(entry, in_matrix, preferred_element_type=jnp.float32).astype(jnp.bfloat16)
    grid = projected.reshape(images, SEQ, 3, HEADS, HEAD)
    query = grid[:, :, 0]
    keyed = grid[:, :, 1]
    valued = grid[:, :, 2]
    scores = attention_scores(query, keyed, factor)
    peak = jnp.max(scores, axis=-1, keepdims=True)
    log_total = peak + jnp.log(jnp.sum(jnp.exp(scores - peak), axis=-1, keepdims=True))
    weights = jnp.exp(scores - log_total).astype(jnp.bfloat16)
    mixed = jnp.einsum("bhqk,bkhd->bqhd", weights, valued, preferred_element_type=jnp.float32)
    mixed = mixed.reshape(count, width).astype(jnp.bfloat16)
    hidden = inputs + jnp.dot(mixed, out_matrix, preferred_element_type=jnp.float32) + gains[:, 4]
    normed_two, inverse_two = normalize(hidden)
    routed = (normed_two * gains[:, 2] + gains[:, 3]).astype(jnp.bfloat16)
    logits = jnp.dot(routed, router_matrix, preferred_element_type=jnp.float32)
    experts = logits.shape[1]
    top = expert_ids.shape[1]
    choose = (expert_ids[:, :, None] == jnp.arange(experts, dtype=jnp.int32)[None, None, :]).astype(
        jnp.float32
    )
    picked = jnp.sum(choose * logits[:, None, :], axis=2)
    gates = jax.nn.softmax(picked, axis=1)
    places = route_places(expert_ids, priority[0], experts)
    capacity = (5 * top * count + 4 * experts - 1) // (4 * experts)
    groups = lax.axis_size("ep")
    local = experts // groups
    slots = experts * capacity
    slot = jnp.where(places < capacity, expert_ids * capacity + places, slots)
    pair_of_slot = (
        jnp.full((slots,), count * top, jnp.int32)
        .at[slot.reshape(-1)]
        .set(jnp.arange(count * top, dtype=jnp.int32), mode="drop")
    )
    token_of_slot = pair_of_slot // top
    padded_rows = jnp.concatenate([routed, jnp.zeros((1, width), jnp.bfloat16)], axis=0)
    outgoing = padded_rows[token_of_slot].reshape(groups, local, capacity, width)
    arrived = lax.all_to_all(outgoing, "ep", split_axis=0, concat_axis=0, tiled=True)
    pre = expert_front(arrived, enter_weight, enter_bias)
    act, gelu_back = jax.vjp(exact_gelu, pre)
    act_low = act.astype(jnp.bfloat16)
    result = jnp.einsum("sjcf,jfd->sjcd", act_low, leave_weight, preferred_element_type=jnp.float32)
    result = (result + leave_bias.astype(jnp.float32)[None, :, None, :]).astype(jnp.bfloat16)
    returned = lax.all_to_all(result, "ep", split_axis=0, concat_axis=0, tiled=True).reshape(
        slots, width
    )
    padded_back = jnp.concatenate([returned, jnp.zeros((1, width), jnp.bfloat16)], axis=0)
    picked_rows = padded_back[slot].astype(jnp.float32)
    output = hidden + jnp.sum(gates[:, :, None] * picked_rows, axis=1)
    grad_output = cotangent.astype(jnp.float32)
    grad_gates = jnp.sum(picked_rows * grad_output[:, None, :], axis=2)
    gate_list = jnp.concatenate([gates.reshape(-1), jnp.zeros((1,), jnp.float32)])
    padded_grad = jnp.concatenate([grad_output, jnp.zeros((1, width), jnp.float32)], axis=0)
    grad_slots = (padded_grad[token_of_slot] * gate_list[pair_of_slot][:, None]).astype(
        jnp.bfloat16
    )
    grad_arrived = lax.all_to_all(
        grad_slots.reshape(groups, local, capacity, width),
        "ep",
        split_axis=0,
        concat_axis=0,
        tiled=True,
    )
    grad_act = jnp.einsum(
        "sjcd,jfd->sjcf", grad_arrived, leave_weight, preferred_element_type=jnp.float32
    )
    grad_pre = gelu_back(grad_act)[0].astype(jnp.bfloat16)
    grad_leave = jnp.einsum(
        "sjcf,sjcd->jfd", act_low, grad_arrived, preferred_element_type=jnp.float32
    )
    grad_leave_bias = jnp.sum(grad_arrived, axis=(0, 2), dtype=jnp.float32)
    grad_enter = jnp.einsum("sjcd,sjcf->jdf", arrived, grad_pre, preferred_element_type=jnp.float32)
    grad_enter_bias = jnp.sum(grad_pre, axis=(0, 2), dtype=jnp.float32)
    grad_rows = jnp.einsum(
        "sjcf,jdf->sjcd", grad_pre, enter_weight, preferred_element_type=jnp.float32
    ).astype(jnp.bfloat16)
    grad_back = lax.all_to_all(grad_rows, "ep", split_axis=0, concat_axis=0, tiled=True).reshape(
        slots, width
    )
    padded_grad_back = jnp.concatenate([grad_back, jnp.zeros((1, width), jnp.bfloat16)], axis=0)
    grad_routed = jnp.sum(padded_grad_back[slot], axis=1, dtype=jnp.float32)
    grad_picked = gates * (grad_gates - jnp.sum(gates * grad_gates, axis=1, keepdims=True))
    grad_logits = jnp.sum(choose * grad_picked[:, :, None], axis=1).astype(jnp.bfloat16)
    grad_router = jnp.einsum("td,te->de", routed, grad_logits, preferred_element_type=jnp.float32)
    grad_routed = grad_routed + jnp.einsum(
        "te,de->td", grad_logits, router_matrix, preferred_element_type=jnp.float32
    )
    grad_gain_two = jnp.sum(grad_routed * normed_two, axis=0)
    grad_shift_two = jnp.sum(grad_routed, axis=0)
    grad_hidden = grad_output + norm_back(grad_routed, normed_two, inverse_two, gains[:, 2])
    grad_shift_out = jnp.sum(grad_hidden, axis=0)
    grad_mix_out = grad_hidden.astype(jnp.bfloat16)
    grad_out_matrix = jnp.einsum(
        "td,te->de", mixed, grad_mix_out, preferred_element_type=jnp.float32
    )
    grad_mixed = jnp.einsum(
        "te,de->td", grad_mix_out, out_matrix, preferred_element_type=jnp.float32
    )
    grad_mixed = grad_mixed.astype(jnp.bfloat16).reshape(images, SEQ, HEADS, HEAD)
    probs = jnp.exp(attention_scores(query, keyed, factor) - log_total)
    weights_again = probs.astype(jnp.bfloat16)
    grad_valued = jnp.einsum(
        "bhqk,bqhd->bkhd", weights_again, grad_mixed, preferred_element_type=jnp.float32
    )
    grad_probs = jnp.einsum(
        "bqhd,bkhd->bhqk", grad_mixed, valued, preferred_element_type=jnp.float32
    )
    grad_scores = (
        probs * (grad_probs - jnp.sum(probs * grad_probs, axis=-1, keepdims=True))
    ).astype(jnp.bfloat16)
    grad_query = (
        jnp.einsum("bhqk,bkhd->bqhd", grad_scores, keyed, preferred_element_type=jnp.float32)
        * factor
    )
    grad_keyed = (
        jnp.einsum("bhqk,bqhd->bkhd", grad_scores, query, preferred_element_type=jnp.float32)
        * factor
    )
    grad_projected = (
        jnp.stack([grad_query, grad_keyed, grad_valued], axis=2)
        .reshape(count, 3 * width)
        .astype(jnp.bfloat16)
    )
    grad_in_matrix = jnp.einsum(
        "td,te->de", entry, grad_projected, preferred_element_type=jnp.float32
    )
    grad_entry = jnp.einsum(
        "te,de->td", grad_projected, in_matrix, preferred_element_type=jnp.float32
    )
    grad_gain_one = jnp.sum(grad_entry * normed_one, axis=0)
    grad_shift_one = jnp.sum(grad_entry, axis=0)
    input_grad = grad_hidden + norm_back(grad_entry, normed_one, inverse_one, gains[:, 0])
    grad_scales = jnp.stack(
        [grad_gain_one, grad_shift_one, grad_gain_two, grad_shift_two, grad_shift_out], axis=1
    )
    summed_dense = (
        lax.psum_scatter(grad_in_matrix, ("rep", "ep"), scatter_dimension=0, tiled=True),
        lax.psum_scatter(grad_out_matrix, ("rep", "ep"), scatter_dimension=0, tiled=True),
        lax.psum_scatter(grad_router, ("rep", "ep"), scatter_dimension=0, tiled=True),
        lax.psum_scatter(grad_scales, ("rep", "ep"), scatter_dimension=0, tiled=True),
    )
    summed_expert = (
        lax.psum_scatter(
            grad_enter.astype(jnp.bfloat16), "rep", scatter_dimension=2, tiled=True
        ).astype(jnp.float32),
        lax.psum_scatter(
            grad_enter_bias.astype(jnp.bfloat16), "rep", scatter_dimension=1, tiled=True
        ).astype(jnp.float32),
        lax.psum_scatter(
            grad_leave.astype(jnp.bfloat16), "rep", scatter_dimension=1, tiled=True
        ).astype(jnp.float32),
        lax.psum_scatter(
            grad_leave_bias.astype(jnp.bfloat16), "rep", scatter_dimension=1, tiled=True
        ).astype(jnp.float32),
    )
    weights_now = (heads_in, heads_out, router, scales, expert_in, bias_in, expert_out, bias_out)
    grads_now = tuple(summed_dense) + tuple(summed_expert)
    firsts = (
        heads_in_first,
        heads_out_first,
        router_first,
        scales_first,
        expert_in_first,
        bias_in_first,
        expert_out_first,
        bias_out_first,
    )
    seconds = (
        heads_in_second,
        heads_out_second,
        router_second,
        scales_second,
        expert_in_second,
        bias_in_second,
        expert_out_second,
        bias_out_second,
    )
    states = [moments(w, g, f, s) for w, g, f, s in zip(weights_now, grads_now, firsts, seconds)]
    weight_terms = jnp.concatenate([squares(w, index == 3) for index, w in enumerate(weights_now)])
    step_terms = jnp.concatenate(
        [squares(state[2], index == 3) for index, state in enumerate(states)]
    )
    totals = lax.psum(jnp.stack([weight_terms, step_terms]), ("rep", "ep"))
    return (output, input_grad) + finish(totals, weights_now, states, width, experts)


def solution(mesh):
    in_specs = (
        P(("rep", "ep"), None),
        P(("rep", "ep"), None),
        P(("rep", "ep"), None),
        P(("rep", "ep"), None),
        P(("rep", "ep"), None),
        P(("rep", "ep"), None),
        P(("rep", "ep"), None),
        P(("rep", "ep"), None),
        P(("rep", "ep"), None),
        P(("rep", "ep"), None),
        P(("rep", "ep"), None),
        P(("rep", "ep"), None),
        P(("rep", "ep"), None),
        P(("rep", "ep"), None),
        P(("rep", "ep"), None),
        P(("rep", "ep"), None),
        P("ep", None, "rep"),
        P("ep", None, "rep"),
        P("ep", None, "rep"),
        P("ep", "rep"),
        P("ep", "rep"),
        P("ep", "rep"),
        P("ep", "rep", None),
        P("ep", "rep", None),
        P("ep", "rep", None),
        P("ep", "rep"),
        P("ep", "rep"),
        P("ep", "rep"),
    )
    out_specs = (
        P(("rep", "ep"), None),
        P(("rep", "ep"), None),
        P(("rep", "ep"), None),
        P(("rep", "ep"), None),
        P(("rep", "ep"), None),
        P(("rep", "ep"), None),
        P(("rep", "ep"), None),
        P(("rep", "ep"), None),
        P(("rep", "ep"), None),
        P(("rep", "ep"), None),
        P(("rep", "ep"), None),
        P(("rep", "ep"), None),
        P(("rep", "ep"), None),
        P(("rep", "ep"), None),
        P("ep", None, "rep"),
        P("ep", None, "rep"),
        P("ep", None, "rep"),
        P("ep", "rep"),
        P("ep", "rep"),
        P("ep", "rep"),
        P("ep", "rep", None),
        P("ep", "rep", None),
        P("ep", "rep", None),
        P("ep", "rep"),
        P("ep", "rep"),
        P("ep", "rep"),
        P(),
    )
    replicated = mesh.shape["rep"] == 4 and mesh.shape["ep"] == 8
    return jax.shard_map(
        replicate_plan if replicated else exchange_plan,
        mesh=mesh,
        in_specs=in_specs,
        out_specs=out_specs,
        check_vma=False,
    )
```
